32 devices in a mesh: rep: 8 (over z, y), shard: 4 (over x, core).
Axes of the slice: x: 2, y: 2, z: 4, core: 2. Of those that a mesh axis runs over, the one named last changes fastest.
Arguments:
- inputs: bfloat16 [64, 1024, 512], P(('rep', 'shard')), may hold values from -6 to 6
- lengths: int32 [64], P(('rep', 'shard')), may hold values from 256 to 1024, as said below
- w_qkv: bfloat16 [512, 1536], P('shard'), may hold values from -0.25 to 0.25
- w_out: bfloat16 [512, 512], P('shard'), may hold values from -2 to 2
- w_in: bfloat16 [512, 2048], P('shard'), may hold values from -0.25 to 0.25
- w_back: bfloat16 [2048, 512], P('shard'), may hold values from -0.125 to 0.125
- vectors: bfloat16 [32, 512], P('shard'), may hold values from -5 to 5
- cotangent: bfloat16 [64, 1024, 512], P(('rep', 'shard')), may hold values from -6 to 6
Outputs:
- output: bfloat16 [64, 1024, 512], P(('rep', 'shard'))
- grad_inputs: bfloat16 [64, 1024, 512], P(('rep', 'shard'))
- grad_qkv: float32 [512, 1536], P('shard')
- grad_out: float32 [512, 512], P('shard')
- grad_in: float32 [512, 2048], P('shard')
- grad_back: float32 [2048, 512], P('shard')
- grad_vectors: float32 [32, 512], P('shard')
The draws below stay inside these ranges and needn't reach their ends.
Inputs may be any that keep to these rules, and one draw needn't show every extreme that they name: `lengths`: valid tokens are a sequence's first slots; some sequence has exactly 1024 and some exactly 256.
All inputs are finite; a program needn't handle non-finite values.
Results may differ from the reference program's by a relative error of at most 0.019.
Values may be sent and summed in bfloat16 or wider, within the bound.
No kernel may reach another device: no remote copies, remote signals or barrier semaphores. Data moves between devices by JAX's collectives and lax.ppermute only.
A program may use at most 192 MiB of HBM per device.

```python
import jax
import jax.numpy as jnp
from jax import lax

D = 512
HEADS = 8
HDIM = 64
FF = 2048
MEM = 20
SEQ_LEN = 1024
MIN_LEN = 256
SEQS = 64


def draw_lengths(key, part):
    values = jax.random.randint(key, (SEQS,), MIN_LEN, SEQ_LEN + 1, dtype=jnp.int32)
    return values.at[0].set(SEQ_LEN).at[1].set(MIN_LEN)


def draw_vectors(key, part):
    rows = MEM + 8 + FF // D
    base = jnp.clip(jax.random.normal(key, (rows, D), jnp.float32), -5.0, 5.0)
    index = jnp.arange(rows)[:, None]
    gain_rows = (index == MEM + 4 + FF // D) | (index == MEM + 6 + FF // D)
    factor = jnp.where(index < MEM, 1.0, 0.2)
    values = jnp.where(gain_rows, 1.0 + 0.15 * base, factor * base)
    return values.astype(jnp.bfloat16)


def level_of(key, shape, cuts, least, high):
    def one(position, blocks):
        heights = jax.random.uniform(jax.random.fold_in(jax.random.fold_in(key, 6), position), (blocks,), jnp.float32, least / len(cuts), high / len(cuts))
        return jnp.repeat(jnp.exp(heights), shape[position] // blocks).reshape((-1,) + (1,) * (len(shape) - position - 1))

    factor_of = one(*cuts[0])
    for cut in cuts[1:]:
        factor_of = factor_of * one(*cut)
    return factor_of


def scatter_about(rng, dims, width, bound, split=(), held_as=jnp.bfloat16):
    drawn = jax.random.normal(rng, dims, jnp.float32) * width
    if len(split) > 0:
        drawn = level_of(rng, dims, split, -0.22, 0.18) * drawn
    return jnp.clip(drawn, min=-bound, max=bound).astype(held_as)


def setup_inputs(seed: int = 0) -> dict:
    streams_of = jax.random.split(jax.random.key(seed), 9)
    return {
        "inputs": scatter_about(streams_of[0], (SEQS, SEQ_LEN, D), 1.0, 6.0, ((0, 32),)),
        "lengths": draw_lengths(jax.random.fold_in(streams_of[8], 71), 0),
        "w_qkv": scatter_about(streams_of[2], (D, 3 * D), D ** -0.5, 0.25, ((0, 4),)),
        "w_out": scatter_about(streams_of[3], (D, D), (max(D // 64, 8)) ** -0.5, 2.0, ((0, 4),)),
        "w_in": scatter_about(streams_of[4], (D, FF), D ** -0.5, 0.25, ((0, 4),)),
        "w_back": scatter_about(streams_of[5], (FF, D), FF ** -0.5, 0.125, ((0, 4),)),
        "vectors": draw_vectors(jax.random.fold_in(streams_of[8], 71), 0),
        "cotangent": scatter_about(streams_of[7], (SEQS, SEQ_LEN, D), 1.0, 6.0, ((0, 32),)),
    }


@jax.custom_vjp
def low(v):
    return lax.optimization_barrier(v.astype(jnp.bfloat16)).astype(jnp.float32)

@jax.custom_vjp
def low_back(v):
    return v

def low_keep(v):
    return (low(v), None)

def low_pass(kept, grad):
    return (grad,)

def back_keep(v):
    return (v, None)

def back_low(kept, grad):
    return (low(grad),)
low.defvjp(low_keep, low_pass)
low_back.defvjp(back_keep, back_low)

def layer_norm(values, gains, shifts):
    center = values - lax.optimization_barrier(jnp.mean(values, axis=-1, keepdims=True))
    spread = lax.optimization_barrier(jnp.mean(center * center, axis=-1, keepdims=True))
    return center * lax.rsqrt(spread + 1e-05) * gains + shifts

def layer_seq(tokens, length, weight_qkv, weight_out, weight_in, weight_back, vector_rows):
    blocks = FF // D
    highest = lax.Precision.HIGHEST
    memory = vector_rows[:MEM]
    bias_query = vector_rows[MEM]
    bias_value = vector_rows[MEM + 1]
    bias_out = vector_rows[MEM + 2]
    bias_in = vector_rows[MEM + 3:MEM + 3 + blocks].reshape(FF)
    bias_back = vector_rows[MEM + 3 + blocks]
    gain_one = vector_rows[MEM + 4 + blocks]
    shift_one = vector_rows[MEM + 5 + blocks]
    gain_two = vector_rows[MEM + 6 + blocks]
    shift_two = vector_rows[MEM + 7 + blocks]
    seq_rows = tokens.shape[0]
    joined = jnp.concatenate([memory, tokens], 0)
    qkv_bias = jnp.concatenate([bias_query, jnp.zeros_like(bias_query), bias_value])
    projected = low(low_back(jnp.dot(joined, weight_qkv, precision=highest) + qkv_bias))
    queries = projected[MEM:, :D].reshape(seq_rows, HEADS, HDIM)
    keys_all = projected[:, D:2 * D].reshape(MEM + seq_rows, HEADS, HDIM)
    values_all = projected[:, 2 * D:].reshape(MEM + seq_rows, HEADS, HDIM)
    scores = low_back(jnp.einsum('qhd,khd->hqk', queries, keys_all, precision=highest) * HDIM ** (-0.5))
    key_mask = jnp.arange(MEM + seq_rows, dtype=jnp.int32) < MEM + length
    scores = jnp.where(key_mask[None, None, :], scores, -1e+30)
    probs = low(jax.nn.softmax(scores, axis=-1))
    mixed = jnp.einsum('hqk,khd->qhd', probs, values_all, precision=highest).reshape(seq_rows, D)
    mixed = low(low_back(mixed))
    attn = low_back(jnp.dot(mixed, weight_out, precision=highest) + bias_out)
    first = layer_norm(tokens + attn, gain_one, shift_one)
    up_value = low_back(jnp.dot(low(first), weight_in, precision=highest) + bias_in)
    active = low(jax.nn.gelu(up_value, approximate=True))
    down_value = low_back(jnp.dot(active, weight_back, precision=highest) + bias_back)
    result = layer_norm(first + down_value, gain_two, shift_two)
    valid = jnp.arange(seq_rows, dtype=jnp.int32) < length
    return jnp.where(valid[:, None], result, 0.0)

def reference(inputs, lengths, w_qkv, w_out, w_in, w_back, vectors, cotangent):
    params = (w_qkv.astype(jnp.float32), w_out.astype(jnp.float32), w_in.astype(jnp.float32), w_back.astype(jnp.float32), vectors.astype(jnp.float32))
    tokens_all = inputs.astype(jnp.float32)
    seq_layer = jax.checkpoint(layer_seq)

    def forward(token_rows, weight_qkv, weight_out, weight_in, weight_back, vector_rows):

        def step(carry, item):
            return (carry, seq_layer(item[0], item[1], weight_qkv, weight_out, weight_in, weight_back, vector_rows))
        unused, stacked = lax.scan(step, jnp.zeros((), jnp.float32), (token_rows, lengths))
        return stacked
    result, pull = jax.vjp(forward, tokens_all, *params)
    grads = pull(cotangent.astype(jnp.float32))
    return (result.astype(jnp.bfloat16), grads[0].astype(jnp.bfloat16), grads[1], grads[2], grads[3], grads[4], grads[5])
```

```python
import math
from functools import partial

import jax
import jax.numpy as jnp
from jax import lax
from jax.experimental import pallas as pl
from jax.experimental.pallas import tpu as pltpu
from jax.sharding import PartitionSpec as P

D = 512
HEADS = 8
HDIM = 64
FF = 2048
MEM = 20
TILE = 256
PAIRS = HEADS // 2
SCALE = HDIM**-0.5
QSCALE = SCALE * math.log2(math.e)
LN2 = math.log(2.0)
F32 = jnp.float32
BF16 = jnp.bfloat16
VROWS = 80
VMEM_LIMIT = 62 * 2**20


def nn(a, b):
    return lax.dot_general(a, b, (((1,), (0,)), ((), ())), preferred_element_type=F32)


def nt(a, b):
    return lax.dot_general(a, b, (((1,), (1,)), ((), ())), preferred_element_type=F32)


def tn(a, b):
    return lax.dot_general(a, b, (((0,), (0,)), ((), ())), preferred_element_type=F32)


def key_sizes(seq_rows):
    top = -(-(seq_rows + MEM) // 32) * 32
    return [rows for rows in range(384, top, 128)] + [top]


def cdiv(a, b):
    return (a + b - 1) // b


def joined_rows(x_ref, memory, length, chunk, seq_rows):
    start = chunk * TILE
    row = lax.broadcasted_iota(jnp.int32, (TILE, 1), 0) + start
    pick = (
        lax.broadcasted_iota(jnp.int32, (TILE, 32), 0)
        + (start - length)
        == lax.broadcasted_iota(jnp.int32, (TILE, 32), 1)
    )
    placed = nn(jnp.where(pick, 1.0, 0.0).astype(BF16), memory)
    at = pl.multiple_of(jnp.minimum(start, seq_rows - TILE), TILE)
    tokens = x_ref[pl.ds(at, TILE), :].astype(F32)
    return jnp.where(row < length, tokens, placed).astype(BF16)


def fwd_kernel(
    seq_rows, len_ref, x_ref, w_ref, vec_ref, e_hbm, qt_ref, mixt_ref, inv_ref,
    wqt, wvt, keys, vt, qpad, ebuf, sems,
):
    length = len_ref[0]
    total = length + MEM
    sizes = key_sizes(seq_rows)
    memory = jnp.where(
        lax.broadcasted_iota(jnp.int32, (32, D), 0) < MEM, vec_ref[...].astype(F32), 0.0
    ).astype(BF16)
    vec_cols = vec_ref[...].astype(F32).T
    bias_q = vec_cols[:, MEM : MEM + 1]
    bias_v = vec_cols[:, MEM + 1 : MEM + 2]
    wqt[...] = w_ref[:, :D].T
    wvt[...] = w_ref[:, 2 * D :].T
    mixt_ref[...] = jnp.zeros(mixt_ref.shape, BF16)
    inv_ref[...] = jnp.zeros(inv_ref.shape, F32)
    qpad[...] = jnp.zeros(qpad.shape, BF16)
    vt[:, HDIM:, :] = jnp.ones((HEADS, VROWS - HDIM, vt.shape[2]), BF16)

    def project(chunk, _):
        rows = joined_rows(x_ref, memory, length, chunk, seq_rows)
        at = pl.multiple_of(chunk * TILE, TILE)
        here = pl.ds(at, TILE)
        key_rows = nn(rows, w_ref[:, D : 2 * D]).astype(BF16)
        for pair in range(PAIRS):
            keys[pair, here, :] = key_rows[:, pair * 128 : pair * 128 + 128]
        values = (nt(wvt[...], rows) + bias_v).astype(BF16)
        for head in range(HEADS):
            vt[head, :HDIM, here] = values[head * HDIM : (head + 1) * HDIM]

        @pl.when(at < seq_rows)
        def _():
            queries = ((nt(wqt[...], rows) + bias_q) * QSCALE).astype(BF16)
            qt_ref[:, here] = queries
            for head in range(HEADS):
                low = (head % 2) * HDIM
                qpad[head, low : low + HDIM, here] = queries[head * HDIM : (head + 1) * HDIM]

        return 0

    lax.fori_loop(0, cdiv(total, TILE), project, 0)
    n_tiles = cdiv(length, TILE)

    def attend(kr):
        tail = kr - 128 if kr % 128 == 0 else kr - kr % 128
        row = lax.broadcasted_iota(jnp.int32, (kr - tail, TILE), 0) + tail
        mask = row < total

        def copies(unit, slot):
            tile, pair = unit // PAIRS, unit % PAIRS
            return pltpu.make_async_copy(
                ebuf.at[slot, :, pl.ds(0, kr), :],
                e_hbm.at[tile, pl.ds(pair * 2, 2), pl.ds(0, kr), :],
                sems.at[slot],
            )

        def step(unit, _):
            slot = unit % 2
            tile, pair = unit // PAIRS, unit % PAIRS
            here = pl.ds(pl.multiple_of(tile * TILE, TILE), TILE)

            @pl.when(unit >= 2)
            def _():
                copies(unit - 2, slot).wait()

            slab = keys[pair, :kr, :]
            for sub in range(2):
                head = pair * 2 + sub
                scores = nn(slab, qpad[head, :, here])
                scores = jnp.concatenate(
                    [scores[:tail], jnp.where(mask, scores[tail:], -1e30)], 0
                )
                top = jnp.max(scores, axis=0, keepdims=True)
                expo = jnp.exp2(scores - top).astype(BF16)
                ebuf[slot, sub, :kr, :] = expo
                mixed = nn(vt[head, :, :kr], expo)
                inverse = 1.0 / mixed[HDIM : HDIM + 1]
                mixt_ref[pl.ds(pl.multiple_of(head * HDIM, HDIM), HDIM), here] = (
                    mixed[:HDIM] * inverse
                ).astype(BF16)
                inv_ref[pl.ds(head, 1), here] = inverse
            copies(unit, slot).start()
            return 0

        units = n_tiles * PAIRS
        lax.fori_loop(0, units, step, 0)
        copies(units - 2, units % 2).wait()
        copies(units - 1, (units - 1) % 2).wait()

    for index, kr in enumerate(sizes):
        least = sizes[index - 1] if index else 0

        @pl.when(jnp.logical_and(total > least, total <= kr))
        def _():
            attend(kr)


def attention_forward(length, x, w_qkv, vectors):
    seq_rows = x.shape[0]
    top = key_sizes(seq_rows)[-1]
    padded = cdiv(seq_rows + MEM, TILE) * TILE
    tiles = seq_rows // TILE
    vm = pl.BlockSpec(memory_space=pltpu.VMEM)
    return pl.pallas_call(
        partial(fwd_kernel, seq_rows),
        out_shape=(
            jax.ShapeDtypeStruct((tiles, HEADS, top, TILE), BF16),
            jax.ShapeDtypeStruct((D, seq_rows), BF16),
            jax.ShapeDtypeStruct((D, seq_rows), BF16),
            jax.ShapeDtypeStruct((HEADS, seq_rows), F32),
        ),
        in_specs=[pl.BlockSpec(memory_space=pltpu.SMEM), vm, vm, vm],
        out_specs=(pl.BlockSpec(memory_space=pl.ANY), vm, vm, vm),
        scratch_shapes=[
            pltpu.VMEM((D, D), BF16),
            pltpu.VMEM((D, D), BF16),
            pltpu.VMEM((PAIRS, padded, 128), BF16),
            pltpu.VMEM((HEADS, VROWS, padded), BF16),
            pltpu.VMEM((HEADS, 128, seq_rows), BF16),
            pltpu.VMEM((2, 2, top, TILE), BF16),
            pltpu.SemaphoreType.DMA((2,)),
        ],
        compiler_params=pltpu.CompilerParams(vmem_limit_bytes=VMEM_LIMIT),
        cost_estimate=pl.CostEstimate(
            flops=8 * 10**9, bytes_accessed=24 * 10**6, transcendentals=8 * 10**6
        ),
        name="attention_forward",
    )(length, x, w_qkv, vectors)


def norm_forward(values):
    center = values - jnp.mean(values, axis=-1, keepdims=True)
    inverse = lax.rsqrt(jnp.mean(center * center, axis=-1, keepdims=True) + 1e-05)
    return center * inverse, inverse


def norm_backward(grad, normed, inverse):
    return inverse * (
        grad
        - jnp.mean(grad, axis=-1, keepdims=True)
        - normed * jnp.mean(grad * normed, axis=-1, keepdims=True)
    )


def col_sum(values):
    return jnp.sum(values, axis=0, keepdims=True)


GELU_A = math.sqrt(2.0 / math.pi)
GELU_B = GELU_A * 0.044715
BLOCKS = FF // D


def ffn_kernel(
    seq_rows, len_ref, x_ref, cot_ref, mixt_ref, inv_ref, wo_ref, wi_ref, wb_ref, vec_ref,
    out_ref, gh_ref, dot_ref, gwo_ref, gwi_ref, gwb_ref, sums_ref,
    acc_o, acc_i, acc_b, slopes, actives,
):
    half = TILE // 2
    len0, len1 = len_ref[0], len_ref[1]
    n0, n1 = cdiv(len0, half), cdiv(len1, half)
    full = seq_rows // half
    n_all = n0 + n1
    out_ref[...] = jnp.zeros(out_ref.shape, BF16)
    gh_ref[...] = jnp.zeros(gh_ref.shape, F32)
    dot_ref[...] = jnp.zeros(dot_ref.shape, BF16)
    acc_o[...] = jnp.zeros(acc_o.shape, F32)
    acc_i[...] = jnp.zeros(acc_i.shape, F32)
    acc_b[...] = jnp.zeros(acc_b.shape, F32)
    sums_ref[...] = jnp.zeros(sums_ref.shape, F32)

    def vec(index):
        return vec_ref[index : index + 1, :].astype(F32)

    bias_out = vec(MEM + 2)
    bias_back = vec(MEM + 3 + BLOCKS)
    gain_one = vec(MEM + 4 + BLOCKS)
    shift_one = vec(MEM + 5 + BLOCKS)
    gain_two = vec(MEM + 6 + BLOCKS)
    shift_two = vec(MEM + 7 + BLOCKS)

    def place(chunk):
        second = chunk >= n0
        inside = jnp.where(second, chunk - n0, chunk)
        spare = chunk >= n_all
        seq = jnp.where(spare, jnp.where(n1 < full, 1, 0), jnp.where(second, 1, 0))
        inside = jnp.where(spare, jnp.where(n1 < full, n1, n0), inside)
        return seq, pl.multiple_of(inside * half, half), jnp.where(seq == 1, len1, len0)

    def step(index, _):
        spots = [place(index * 2), place(index * 2 + 1)]

        def rows_of(ref):
            return jnp.concatenate([ref[s, pl.ds(r, half), :] for s, r, _ in spots], 0)

        def lanes_of(ref):
            return jnp.concatenate([ref[s, :, pl.ds(r, half)] for s, r, _ in spots], 1)

        def put_rows(ref, value):
            for i, (s, r, _) in enumerate(spots):
                ref[s, pl.ds(r, half), :] = value[i * half : (i + 1) * half]

        def put_lanes(ref, value):
            for i, (s, r, _) in enumerate(spots):
                ref[s, :, pl.ds(r, half)] = value[:, i * half : (i + 1) * half]

        iota = lax.broadcasted_iota(jnp.int32, (half, 1), 0)
        valid = jnp.concatenate(
            [jnp.where(iota + r < count, 1.0, 0.0) for _, r, count in spots], 0
        )
        mixt = lanes_of(mixt_ref)
        attn = nn(mixt.T, wo_ref[...]) + bias_out
        normed_one, inverse_one = norm_forward(rows_of(x_ref).astype(F32) + attn)
        first = normed_one * gain_one + shift_one
        first_low = first.astype(BF16)
        second = first + bias_back
        for j in range(BLOCKS):
            cols = slice(j * D, (j + 1) * D)
            up = nn(first_low, wi_ref[:, cols]) + vec(MEM + 3 + j)
            square = up * up
            half_gate = 0.5 + 0.5 * jnp.tanh(up * (GELU_A + GELU_B * square))
            active = up * half_gate
            slopes[:, cols] = half_gate + active * (2.0 - 2.0 * half_gate) * (
                GELU_A + 3.0 * GELU_B * square
            )
            actives[:, cols] = active.astype(BF16)
            second = second + nn(active.astype(BF16), wb_ref[cols, :])
        normed_two, inverse_two = norm_forward(second)
        put_rows(out_ref, ((normed_two * gain_two + shift_two) * valid).astype(BF16))
        grad_out = rows_of(cot_ref).astype(F32) * valid
        sums_ref[MEM + 6 + BLOCKS : MEM + 7 + BLOCKS] += col_sum(grad_out * normed_two)
        sums_ref[MEM + 7 + BLOCKS : MEM + 8 + BLOCKS] += col_sum(grad_out)
        grad_second = norm_backward(grad_out * gain_two, normed_two, inverse_two)
        grad_down = grad_second.astype(BF16)
        sums_ref[MEM + 3 + BLOCKS : MEM + 4 + BLOCKS] += col_sum(grad_down.astype(F32))
        grad_first = grad_second
        first_t = first_low.T
        for j in range(BLOCKS):
            cols = slice(j * D, (j + 1) * D)
            acc_b[cols, :] += tn(actives[:, cols], grad_down)
            grad_up = (nt(grad_down, wb_ref[cols, :]) * slopes[:, cols]).astype(BF16)
            sums_ref[MEM + 3 + j : MEM + 4 + j] += col_sum(grad_up.astype(F32))
            acc_i[:, cols] += nn(first_t, grad_up)
            grad_first = grad_first + nt(grad_up, wi_ref[:, cols])
        sums_ref[MEM + 4 + BLOCKS : MEM + 5 + BLOCKS] += col_sum(grad_first * normed_one)
        sums_ref[MEM + 5 + BLOCKS : MEM + 6 + BLOCKS] += col_sum(grad_first)
        grad_one = norm_backward(grad_first * gain_one, normed_one, inverse_one)
        put_rows(gh_ref, grad_one)
        grad_attn = grad_one.astype(BF16)
        sums_ref[MEM + 2 : MEM + 3] += col_sum(grad_attn.astype(F32))
        acc_o[...] += nn(mixt, grad_attn)
        grad_mixed = nt(wo_ref[...], grad_attn)
        inverse = lanes_of(inv_ref)
        scaled = jnp.concatenate(
            [
                grad_mixed[h * HDIM : (h + 1) * HDIM] * inverse[h : h + 1]
                for h in range(HEADS)
            ],
            0,
        )
        put_lanes(dot_ref, scaled.astype(BF16))
        return 0

    lax.fori_loop(0, cdiv(n_all, 2), step, 0)
    gwo_ref[...] = acc_o[...].astype(BF16)
    gwi_ref[...] = acc_i[...].astype(BF16)
    gwb_ref[...] = acc_b[...].astype(BF16)


def feed_forward(lengths, x, cot, mixt, inv, w_out, w_in, w_back, vectors):
    count, seq_rows = x.shape[:2]
    vm = pl.BlockSpec(memory_space=pltpu.VMEM)
    return pl.pallas_call(
        partial(ffn_kernel, seq_rows),
        out_shape=(
            jax.ShapeDtypeStruct((count, seq_rows, D), BF16),
            jax.ShapeDtypeStruct((count, seq_rows, D), F32),
            jax.ShapeDtypeStruct((count, D, seq_rows), BF16),
            jax.ShapeDtypeStruct((D, D), BF16),
            jax.ShapeDtypeStruct((D, FF), BF16),
            jax.ShapeDtypeStruct((FF, D), BF16),
            jax.ShapeDtypeStruct((32, D), F32),
        ),
        in_specs=[pl.BlockSpec(memory_space=pltpu.SMEM)] + [vm] * 8,
        out_specs=(vm,) * 7,
        scratch_shapes=[
            pltpu.VMEM((D, D), F32),
            pltpu.VMEM((D, FF), F32),
            pltpu.VMEM((FF, D), F32),
            pltpu.VMEM((TILE, FF), F32),
            pltpu.VMEM((TILE, FF), BF16),
        ],
        compiler_params=pltpu.CompilerParams(vmem_limit_bytes=VMEM_LIMIT),
        cost_estimate=pl.CostEstimate(
            flops=27 * 10**9, bytes_accessed=24 * 10**6, transcendentals=4 * 10**6
        ),
        name="feed_forward",
    )(lengths, x, cot, mixt, inv, w_out, w_in, w_back, vectors)


def bwd_kernel(
    seq_rows, groups, group, n_seqs, *refs,
):
    gp = PAIRS // groups
    gcols = gp * 128
    len_ref, x_ref, w_ref, vec_ref, qt_ref, mixt_ref, dot_ref = refs[:7]
    e_refs = refs[7 : 7 + n_seqs]
    dw_ref, proj_ref, sums_ref = refs[7 + n_seqs : 10 + n_seqs]
    wkt, kt, values, qpad, dpad, dqt, dk, dv, ebuf, acc, sems = refs[10 + n_seqs :]
    sizes = key_sizes(seq_rows)
    base = group * gcols
    memory = jnp.where(
        lax.broadcasted_iota(jnp.int32, (32, D), 0) < MEM, vec_ref[...].astype(F32), 0.0
    ).astype(BF16)
    bias_v = vec_ref[MEM + 1 : MEM + 2, base : base + gcols].astype(F32)
    wkt[...] = w_ref[:, D + base : D + base + gcols].T
    acc[...] = jnp.zeros(acc.shape, F32)
    proj_ref[...] = jnp.zeros(proj_ref.shape, BF16)
    sums_ref[...] = jnp.zeros(sums_ref.shape, F32)
    qpad[...] = jnp.zeros(qpad.shape, BF16)
    dpad[...] = jnp.zeros(dpad.shape, BF16)

    for seq in range(n_seqs):
        length = len_ref[seq]
        total = length + MEM
        chunks = cdiv(total, TILE)
        n_tiles = cdiv(length, TILE)
        e_hbm = e_refs[seq]

        def project(chunk, _):
            rows = joined_rows(x_ref.at[seq], memory, length, chunk, seq_rows)
            here = pl.ds(pl.multiple_of(chunk * TILE, TILE), TILE)
            value_rows = (
                nn(rows, w_ref[:, 2 * D + base : 2 * D + base + gcols]) + bias_v
            ).astype(BF16)
            for pair in range(gp):
                values[pair, here, :] = value_rows[:, pair * 128 : pair * 128 + 128]
            kt[:, here] = nt(wkt[...], rows).astype(BF16)
            dqt[:, here] = jnp.zeros((gcols, TILE), BF16)
            for pair in range(gp):
                dk[pair, here, :] = jnp.zeros((TILE, 128), F32)
                dv[pair, here, :] = jnp.zeros((TILE, 128), F32)
            return 0

        lax.fori_loop(0, chunks, project, 0)

        def attend(kr):
            def copies(unit, slot):
                pair, tile = unit // n_tiles, unit % n_tiles
                return pltpu.make_async_copy(
                    e_hbm.at[tile, pl.ds((group * gp + pair) * 2, 2), pl.ds(0, kr), :],
                    ebuf.at[slot, :, pl.ds(0, kr), :],
                    sems.at[slot],
                )

            units = n_tiles * gp
            copies(0, 0).start()

            def step(unit, _):
                slot = unit % 2
                pair, tile = unit // n_tiles, unit % n_tiles
                here = pl.ds(pl.multiple_of(tile * TILE, TILE), TILE)

                @pl.when(unit + 1 < units)
                def _():
                    copies(unit + 1, (unit + 1) % 2).start()

                copies(unit, slot).wait()
                slab = values[pair, :kr, :]
                grads, expos = [], []
                for sub in range(2):
                    low = sub * HDIM
                    local = pl.ds(pl.multiple_of(pair * 128 + low, HDIM), HDIM)
                    spot = pl.ds(pl.multiple_of(base + pair * 128 + low, HDIM), HDIM)
                    outer = dot_ref[seq, spot, here]
                    dpad[sub, low : low + HDIM, :] = outer
                    qpad[sub, low : low + HDIM, :] = qt_ref[seq, spot, here]
                    inner = col_sum(
                        outer.astype(F32) * mixt_ref[seq, spot, here].astype(F32)
                    )
                    expo = ebuf[slot, sub, :kr, :]
                    grad = (
                        expo.astype(F32) * (nn(slab, dpad[sub]) - inner)
                    ).astype(BF16)
                    dqt[local, here] = (nn(kt[local, :kr], grad) * SCALE).astype(BF16)
                    grads.append(grad)
                    expos.append(expo)
                dk[pair, :kr, :] += nt(
                    jnp.concatenate(grads, 1), jnp.concatenate([qpad[0], qpad[1]], 1)
                )
                dv[pair, :kr, :] += nt(
                    jnp.concatenate(expos, 1), jnp.concatenate([dpad[0], dpad[1]], 1)
                )
                return 0

            lax.fori_loop(0, units, step, 0)

        for index, kr in enumerate(sizes):
            least = sizes[index - 1] if index else 0

            @pl.when(jnp.logical_and(total > least, total <= kr))
            def _():
                attend(kr)

        def finish(chunk, _):
            rows = joined_rows(x_ref.at[seq], memory, length, chunk, seq_rows)
            here = pl.ds(pl.multiple_of(chunk * TILE, TILE), TILE)
            parts = [dqt[:, here].T]
            parts += [(dk[pair, here, :] * LN2).astype(BF16) for pair in range(gp)]
            parts += [dv[pair, here, :].astype(BF16) for pair in range(gp)]
            grad = jnp.concatenate(parts, 1)
            proj_ref[seq, here, :] = grad
            acc[...] += tn(rows, grad)
            sums_ref[0:1, :] += col_sum(grad.astype(F32))
            return 0

        lax.fori_loop(0, chunks, finish, 0)

    dw_ref[...] = acc[...].astype(BF16)


def attention_backward(group, groups, lengths, x, w_qkv, vectors, qt, mixt, dot, expos):
    count, seq_rows = x.shape[:2]
    top = key_sizes(seq_rows)[-1]
    padded = cdiv(seq_rows + MEM, TILE) * TILE
    gp = PAIRS // groups
    gcols = gp * 128
    vm = pl.BlockSpec(memory_space=pltpu.VMEM)
    return pl.pallas_call(
        partial(bwd_kernel, seq_rows, groups, group, count),
        out_shape=(
            jax.ShapeDtypeStruct((D, 3 * gcols), BF16),
            jax.ShapeDtypeStruct((count, padded, 3 * gcols), BF16),
            jax.ShapeDtypeStruct((8, 3 * gcols), F32),
        ),
        in_specs=[pl.BlockSpec(memory_space=pltpu.SMEM)]
        + [vm] * 6
        + [pl.BlockSpec(memory_space=pl.ANY)] * count,
        out_specs=(vm, vm, vm),
        scratch_shapes=[
            pltpu.VMEM((gcols, D), BF16),
            pltpu.VMEM((gcols, padded), BF16),
            pltpu.VMEM((gp, padded, 128), BF16),
            pltpu.VMEM((2, 128, TILE), BF16),
            pltpu.VMEM((2, 128, TILE), BF16),
            pltpu.VMEM((gcols, padded), BF16),
            pltpu.VMEM((gp, padded, 128), F32),
            pltpu.VMEM((gp, padded, 128), F32),
            pltpu.VMEM((2, 2, top, TILE), BF16),
            pltpu.VMEM((D, 3 * gcols), F32),
            pltpu.SemaphoreType.DMA((2,)),
        ],
        compiler_params=pltpu.CompilerParams(vmem_limit_bytes=VMEM_LIMIT),
        cost_estimate=pl.CostEstimate(
            flops=16 * 10**9, bytes_accessed=30 * 10**6, transcendentals=0
        ),
        name="attention_backward",
    )(lengths, x, w_qkv, vectors, qt, mixt, dot, *expos)


def input_kernel(seq_rows, groups, len_ref, w_ref, gh_ref, *refs):
    projs = refs[:groups]
    gx_ref, mem_ref = refs[groups:]
    gcols = D // groups
    gx_ref[...] = jnp.zeros(gx_ref.shape, BF16)
    mem_ref[...] = jnp.zeros(mem_ref.shape, F32)

    def joint(seq, here):
        parts = [
            projs[g][seq, here, kind * gcols : (kind + 1) * gcols]
            for kind in range(3)
            for g in range(groups)
        ]
        return jnp.concatenate(parts, 1)

    for seq in range(gx_ref.shape[0]):
        length = len_ref[seq]

        def step(chunk, _):
            start = pl.multiple_of(chunk * TILE, TILE)
            here = pl.ds(start, TILE)
            grad = nt(joint(seq, here), w_ref[...])
            row = lax.broadcasted_iota(jnp.int32, (TILE, 1), 0) + start

            @pl.when(start < seq_rows)
            def _():
                gx_ref[seq, here, :] = jnp.where(
                    row < length, grad + gh_ref[seq, pl.ds(start, TILE), :], 0.0
                ).astype(BF16)

            @pl.when(start + TILE > length)
            def _():
                pick = (
                    lax.broadcasted_iota(jnp.int32, (32, TILE), 1) + (start - length)
                    == lax.broadcasted_iota(jnp.int32, (32, TILE), 0)
                )
                pick = jnp.logical_and(pick, lax.broadcasted_iota(jnp.int32, (32, TILE), 0) < MEM)
                mem_ref[...] += nn(jnp.where(pick, 1.0, 0.0).astype(BF16), grad.astype(BF16))

            return 0

        lax.fori_loop(0, cdiv(length + MEM, TILE), step, 0)


def input_gradient(lengths, w_qkv, gh, projs):
    count, seq_rows = gh.shape[:2]
    vm = pl.BlockSpec(memory_space=pltpu.VMEM)
    return pl.pallas_call(
        partial(input_kernel, seq_rows, len(projs)),
        out_shape=(
            jax.ShapeDtypeStruct((count, seq_rows, D), BF16),
            jax.ShapeDtypeStruct((32, D), F32),
        ),
        in_specs=[pl.BlockSpec(memory_space=pltpu.SMEM)] + [vm] * (2 + len(projs)),
        out_specs=(vm, vm),
        compiler_params=pltpu.CompilerParams(vmem_limit_bytes=VMEM_LIMIT),
        cost_estimate=pl.CostEstimate(
            flops=3 * 10**9, bytes_accessed=14 * 10**6, transcendentals=0
        ),
        name="input_gradient",
    )(lengths, w_qkv, gh, *projs)


GROUPS = 2


def local_layer(lengths, x, w_qkv, w_out, w_in, w_back, vectors, cot):
    count = x.shape[0]
    fwd = [
        attention_forward(lax.slice(lengths, (s,), (s + 1,)), x[s], w_qkv, vectors)
        for s in range(count)
    ]
    qt = jnp.stack([f[1] for f in fwd])
    mixt = jnp.stack([f[2] for f in fwd])
    inv = jnp.stack([f[3] for f in fwd])
    out, gh, dot, gwo, gwi, gwb, sums = feed_forward(
        lengths, x, cot, mixt, inv, w_out, w_in, w_back, vectors
    )
    back = [
        attention_backward(
            g, GROUPS, lengths, x, w_qkv, vectors, qt, mixt, dot, [f[0] for f in fwd]
        )
        for g in range(GROUPS)
    ]
    gx, mem = input_gradient(lengths, w_qkv, gh, [b[1] for b in back])
    gcols = D // GROUPS
    dw = jnp.concatenate(
        [b[0][:, k * gcols : (k + 1) * gcols] for k in range(3) for b in back], 1
    )
    psum = jnp.concatenate(
        [b[2][0, k * gcols : (k + 1) * gcols] for k in range(3) for b in back], 0
    )
    rows = sums.at[:MEM].set(mem[:MEM]).at[MEM].set(psum[:D]).at[MEM + 1].set(psum[2 * D :])
    return out, gx, dw, gwo, gwi, gwb, rows


def bits_of(size):
    bit, bits = size // 2, []
    while bit:
        bits.append(bit)
        bit //= 2
    return bits


def exchange(value, axis, size, bit):
    return lax.ppermute(value, axis, [(i, i ^ bit) for i in range(size)])


def gather_pieces(value, axis, size):
    pieces = {0: value}
    for bit in bits_of(size):
        for mask in sorted(pieces):
            pieces[mask | bit] = exchange(pieces[mask], axis, size, bit)
    return [pieces[mask] for mask in range(size)]


def gather_rows(value, axis, size):
    me = lax.axis_index(axis)
    rows = value.shape[0]
    whole = jnp.zeros((size * rows,) + value.shape[1:], value.dtype)
    for mask, piece in enumerate(gather_pieces(value, axis, size)):
        whole = lax.dynamic_update_slice_in_dim(whole, piece, (me ^ mask) * rows, 0)
    return whole


def add_low(a, b):
    return (a.astype(F32) + b.astype(F32)).astype(BF16)


def reduce_shard(blocks, axis, size):
    me = lax.axis_index(axis)
    parts = [lax.dynamic_index_in_dim(blocks, me ^ m, 0, False) for m in range(size)]
    live = {m: parts[m] for m in range(size)}
    bit = 1
    while bit < size:
        live = {
            m: add_low(live[m], exchange(live[m | bit], axis, size, bit))
            for m in live
            if not m & bit
        }
        bit *= 2
    return live[0]


def reduce_rep(value, axis, size):
    me = lax.axis_index(axis)
    steps = []
    bit = 1
    while bit < size:
        steps.append(bit)
        bit *= 2
    for bit in steps:
        half = value.shape[0] // 2
        high = (me & bit) != 0
        low_part, high_part = value[:half], value[half:]
        send = jnp.where(high, low_part, high_part)
        keep = jnp.where(high, high_part, low_part)
        value = add_low(keep, exchange(send, axis, size, bit))
    for bit in reversed(steps):
        high = (me & bit) != 0
        other = exchange(value, axis, size, bit)
        value = jnp.where(
            high, jnp.concatenate([other, value], 0), jnp.concatenate([value, other], 0)
        )
    return value


def body(sizes, inputs, lengths, w_qkv, w_out, w_in, w_back, vectors, cotangent):
    reps, shards = sizes
    full = [gather_rows(w, "shard", shards) for w in (w_qkv, w_out, w_in, w_back, vectors)]
    out, gx, dw, gwo, gwi, gwb, rows = local_layer(lengths, inputs, *full, cotangent)

    def split(grad):
        grad = grad.astype(BF16)
        grad = grad.reshape(shards, grad.shape[0] // shards, grad.shape[1])
        return grad.reshape(shards, -1, D)

    grads = (dw, gwo, gwi, gwb, rows)
    blocks = jnp.concatenate([split(g) for g in grads], 1)
    spare = -blocks.shape[1] % (16 * reps)
    blocks = jnp.pad(blocks, ((0, 0), (0, spare), (0, 0)))
    total = reduce_rep(reduce_shard(blocks, "shard", shards), "rep", reps).astype(F32)
    outs, at = [], 0
    for g in grads:
        count = g.size // shards // D
        outs.append(total[at : at + count].reshape(g.shape[0] // shards, g.shape[1]))
        at += count
    return (out, gx, *outs)


def solution(mesh):
    data = P(("rep", "shard"), None, None)
    rows = P("shard", None)
    return jax.shard_map(
        partial(body, (mesh.shape["rep"], mesh.shape["shard"])),
        mesh=mesh,
        in_specs=(data, P(("rep", "shard")), rows, rows, rows, rows, rows, data),
        out_specs=(data, data, rows, rows, rows, rows, rows),
        check_vma=False,
    )
```

```python
import math
from functools import partial

import jax
import jax.numpy as jnp
from jax import lax
from jax.experimental import pallas as pl
from jax.experimental.pallas import tpu as pltpu
from jax.sharding import PartitionSpec as P

D = 512
HEADS = 8
HDIM = 64
FF = 2048
MEM = 20
TILE = 256
PAIRS = HEADS // 2
SCALE = HDIM**-0.5
QSCALE = SCALE * math.log2(math.e)
LN2 = math.log(2.0)
F32 = jnp.float32
BF16 = jnp.bfloat16
VROWS = 80
VMEM_LIMIT = 62 * 2**20


def nn(a, b):
    return lax.dot_general(a, b, (((1,), (0,)), ((), ())), preferred_element_type=F32)


def nt(a, b):
    return lax.dot_general(a, b, (((1,), (1,)), ((), ())), preferred_element_type=F32)


def tn(a, b):
    return lax.dot_general(a, b, (((0,), (0,)), ((), ())), preferred_element_type=F32)


def key_sizes(seq_rows):
    top = -(-(seq_rows + MEM) // 32) * 32
    return [rows for rows in range(384, top, 128)] + [top]


def column_max(values):
    parts = [values[i : i + 128] for i in range(0, values.shape[0] - 127, 128)]
    while len(parts) > 1:
        odd = parts[len(parts) - len(parts) % 2 :]
        parts = [jnp.maximum(a, b) for a, b in zip(parts[::2], parts[1::2])] + odd
    top = jnp.max(parts[0], axis=0, keepdims=True)
    rest = values.shape[0] % 128
    if rest:
        top = jnp.maximum(top, jnp.max(values[-rest:], axis=0, keepdims=True))
    return top


AHEAD = 2
BODY_HEADS = 4


def cdiv(a, b):
    return (a + b - 1) // b


def pick_memory(rows_ref, memory, length, kr):
    start = kr - TILE
    row = lax.broadcasted_iota(jnp.int32, (TILE, 1), 0) + start
    lane = lax.broadcasted_iota(jnp.int32, (TILE, 32), 1)
    pick = lax.broadcasted_iota(jnp.int32, (TILE, 32), 0) + (start - length) == lane
    placed = nn(jnp.where(pick, 1.0, 0.0).astype(BF16), memory)
    tokens = rows_ref[start:kr, :].astype(F32)
    rows_ref[start:kr, :] = jnp.where(row < length, tokens, placed).astype(BF16)


def memory_rows(vec_ref):
    inside = lax.broadcasted_iota(jnp.int32, (32, D), 0) < MEM
    return jnp.where(inside, vec_ref[...].astype(F32), 0.0).astype(BF16)


def for_size(seq_rows, total, run):
    sizes = key_sizes(seq_rows)
    for index, kr in enumerate(sizes):
        least = sizes[index - 1] if index else 0

        @pl.when(jnp.logical_and(total > least, total <= kr))
        def _(kr=kr):
            run(kr)


def prepare_kernel(shards, me_ref, *refs):
    w_p, v_p = refs[:shards], refs[shards : 2 * shards]
    w_ref, wqt_ref, wvt_ref, vec_ref, sems = refs[2 * shards :]
    me = me_ref[0]
    copies = []
    part, few = D // shards, 32 // shards
    for m in range(shards):
        at = pl.multiple_of((me ^ m) * part, part)
        copies.append(
            pltpu.make_async_copy(w_p[m], w_ref.at[pl.ds(at, part), :], sems.at[m])
        )
    for copy in copies:
        copy.start()
    for m in range(shards):
        values = v_p[m][...].astype(F32)
        spread = jnp.concatenate([values] * shards, 0)
        owner = lax.broadcasted_iota(jnp.int32, (32, D), 0) // few
        if m == 0:
            rows = spread
        else:
            rows = jnp.where(owner == (me ^ m), spread, rows)
    vec_ref[...] = rows.astype(BF16)
    for copy in copies:
        copy.wait()
    wqt_ref[...] = w_ref[:, :D].T
    wvt_ref[...] = w_ref[:, 2 * D :].T


def prepare(me, w_qkv, vectors):
    shards = len(w_qkv)
    vm = pl.BlockSpec(memory_space=pltpu.VMEM)
    return pl.pallas_call(
        partial(prepare_kernel, shards),
        out_shape=(
            jax.ShapeDtypeStruct((D, 3 * D), BF16),
            jax.ShapeDtypeStruct((D, D), BF16),
            jax.ShapeDtypeStruct((D, D), BF16),
            jax.ShapeDtypeStruct((32, D), BF16),
        ),
        in_specs=[pl.BlockSpec(memory_space=pltpu.SMEM)]
        + [pl.BlockSpec(memory_space=pl.ANY)] * shards
        + [vm] * shards,
        out_specs=(vm, vm, vm, vm),
        scratch_shapes=[pltpu.SemaphoreType.DMA((shards,))],
        compiler_params=pltpu.CompilerParams(vmem_limit_bytes=VMEM_LIMIT),
        name="prepare",
    )(me, *w_qkv, *vectors)


def fwd_kernel(
    seq_rows, seq, len_ref, x_hbm, wk_ref, wqt_ref, wvt_ref, vec_ref,
    e_hbm, qt_hbm, mixt_hbm, inv_ref,
    rows, keys, vt, qpad, queries, mixed_t, ebuf, sems, io_sems,
):
    length = len_ref[seq]
    total = length + MEM
    load = pltpu.make_async_copy(x_hbm.at[seq], rows.at[pl.ds(0, seq_rows), :], io_sems.at[0])
    load.start()
    memory = memory_rows(vec_ref)
    vec_cols = vec_ref[...].astype(F32).T
    bias_q = vec_cols[:, MEM : MEM + 1]
    bias_v = vec_cols[:, MEM + 1 : MEM + 2]
    mixed_t[...] = jnp.zeros(mixed_t.shape, BF16)
    inv_ref[...] = jnp.zeros(inv_ref.shape, F32)
    for head in range(HEADS):
        spare = HDIM * (1 - head % 2)
        qpad[head, spare : spare + HDIM, :] = jnp.zeros((HDIM, seq_rows), BF16)
    vt[:, HDIM:, :] = jnp.ones((HEADS, VROWS - HDIM, vt.shape[2]), BF16)
    n_tiles = cdiv(length, TILE)
    load.wait()

    def attend(kr):
        pick_memory(rows, memory, length, kr)
        joined = rows[:kr, :]
        key_rows = nn(joined, wk_ref[...]).astype(BF16)
        for pair in range(PAIRS):
            keys[pair, :kr, :] = key_rows[:, pair * 128 : pair * 128 + 128]
        wide = min(cdiv(kr, TILE) * TILE, seq_rows)
        found = ((nt(wqt_ref[...], rows[:wide, :]) + bias_q) * QSCALE).astype(BF16)
        queries[:, :wide] = found
        for head in range(HEADS):
            low = (head % 2) * HDIM
            qpad[head, low : low + HDIM, :wide] = found[head * HDIM : (head + 1) * HDIM]
        save = pltpu.make_async_copy(queries, qt_hbm, io_sems.at[1])
        save.start()
        values = (nt(wvt_ref[...], joined) + bias_v).astype(BF16)
        for head in range(HEADS):
            vt[head, :HDIM, :kr] = values[head * HDIM : (head + 1) * HDIM]

        tail = kr - 128 if kr % 128 == 0 else kr - kr % 128
        row = lax.broadcasted_iota(jnp.int32, (kr - tail, TILE), 0) + tail
        mask = row < total

        def copies(tile, pair):
            return pltpu.make_async_copy(
                ebuf.at[pair, :, pl.ds(0, kr), :],
                e_hbm.at[tile, pl.ds(pair * 2, 2), pl.ds(0, kr), :],
                sems.at[pair],
            )

        turns = HEADS // BODY_HEADS

        def step(unit, _):
            tile, turn = unit // turns, unit % turns
            here = pl.ds(pl.multiple_of(tile * TILE, TILE), TILE)
            base = turn * BODY_HEADS

            def score(i):
                pair = turn * (BODY_HEADS // 2) + i // 2
                scores = nn(keys[pair, :kr, :], qpad[base + i, :, here])
                scores = jnp.concatenate(
                    [scores[:tail], jnp.where(mask, scores[tail:], -1e30)], 0
                )
                return scores, column_max(scores)

            live = {i: score(i) for i in range(AHEAD)}
            for i in range(BODY_HEADS):
                pair, sub = turn * (BODY_HEADS // 2) + i // 2, i % 2
                scores, top = live.pop(i)
                if sub == 0:
                    copies(tile, pair).wait()
                if i + AHEAD < BODY_HEADS:
                    live[i + AHEAD] = score(i + AHEAD)
                expo = jnp.exp2(scores - top).astype(BF16)
                ebuf[pair, sub, :kr, :] = expo
                mixed = nn(vt[base + i, :, :kr], expo)
                inverse = 1.0 / mixed[HDIM : HDIM + 1]
                spot = pl.ds(pl.multiple_of((base + i) * HDIM, HDIM), HDIM)
                mixed_t[spot, here] = (mixed[:HDIM] * inverse).astype(BF16)
                inv_ref[pl.ds(base + i, 1), here] = inverse
                if sub == 1:
                    copies(tile, pair).start()
            return 0

        for pair in range(PAIRS):
            copies(0, pair).start()
        lax.fori_loop(0, n_tiles * turns, step, 0)
        out = pltpu.make_async_copy(mixed_t, mixt_hbm, io_sems.at[2])
        out.start()
        for pair in range(PAIRS):
            copies(n_tiles - 1, pair).wait()
        save.wait()
        out.wait()

    for_size(seq_rows, total, attend)


def attention_forward(seq, lengths, x, w_qkv, wqt, wvt, vectors):
    seq_rows = x.shape[1]
    top = key_sizes(seq_rows)[-1]
    padded = cdiv(seq_rows + MEM, TILE) * TILE
    tiles = seq_rows // TILE
    vm = pl.BlockSpec(memory_space=pltpu.VMEM)
    hbm = pl.BlockSpec(memory_space=pl.ANY)
    return pl.pallas_call(
        partial(fwd_kernel, seq_rows, seq),
        out_shape=(
            jax.ShapeDtypeStruct((tiles, HEADS, top, TILE), BF16),
            jax.ShapeDtypeStruct((D, seq_rows), BF16),
            jax.ShapeDtypeStruct((D, seq_rows), BF16),
            jax.ShapeDtypeStruct((HEADS, seq_rows), F32),
        ),
        grid=(1,),
        in_specs=[
            pl.BlockSpec(memory_space=pltpu.SMEM),
            hbm,
            pl.BlockSpec((D, D), lambda i: (0, 1)),
            vm,
            vm,
            vm,
        ],
        out_specs=(hbm, hbm, hbm, vm),
        scratch_shapes=[
            pltpu.VMEM((padded, D), BF16),
            pltpu.VMEM((PAIRS, padded, 128), BF16),
            pltpu.VMEM((HEADS, VROWS, padded), BF16),
            pltpu.VMEM((HEADS, 128, seq_rows), BF16),
            pltpu.VMEM((D, seq_rows), BF16),
            pltpu.VMEM((D, seq_rows), BF16),
            pltpu.VMEM((PAIRS, 2, top, TILE), BF16),
            pltpu.SemaphoreType.DMA((PAIRS,)),
            pltpu.SemaphoreType.DMA((3,)),
        ],
        compiler_params=pltpu.CompilerParams(vmem_limit_bytes=VMEM_LIMIT),
        cost_estimate=pl.CostEstimate(
            flops=8 * 10**9, bytes_accessed=24 * 10**6, transcendentals=8 * 10**6
        ),
        name="attention_forward",
    )(lengths, x, w_qkv, wqt, wvt, vectors)


def norm_forward(values):
    center = values - jnp.mean(values, axis=-1, keepdims=True)
    inverse = lax.rsqrt(jnp.mean(center * center, axis=-1, keepdims=True) + 1e-05)
    return center * inverse, inverse


def norm_backward(grad, normed, inverse):
    return inverse * (
        grad
        - jnp.mean(grad, axis=-1, keepdims=True)
        - normed * jnp.mean(grad * normed, axis=-1, keepdims=True)
    )


def col_sum(values):
    return jnp.sum(values, axis=0, keepdims=True)


GELU_A = math.sqrt(2.0 / math.pi)
GELU_B = GELU_A * 0.044715
BLOCKS = FF // D


def piece_order(shards):
    bits = shards.bit_length() - 1
    return [int(format(i, "b").zfill(bits)[::-1], 2) if bits else 0 for i in range(shards)]


def piece_spots(pair, shards, rows):
    half = max(shards // 2, 1)
    for index, m in enumerate(piece_order(shards)):
        yield m, pair[index // half], index % half * rows


def ffn_kernel(
    seq_rows, shards, len_ref, me_ref, x_hbm, cot_hbm, mixt0, mixt1, inv0, inv1, *refs,
):
    wo_p, wi_p, wb_p = refs[:shards], refs[shards : 2 * shards], refs[2 * shards : 3 * shards]
    vec_ref, out_hbm, gh_hbm, dot_hbm = refs[3 * shards : 3 * shards + 4]
    grads = refs[3 * shards + 4 : 3 * shards + 8]
    (
        sums_ref, x_ref, cot_ref, mixt_ref, inv_ref, wo_ref, wi_ref, wb_ref,
        out_ref, gh_ref, dot_ref, acc_o, acc_i, acc_b, slopes, actives,
        s_normed1, s_first, s_gsecond, ups, sems, out_sems,
    ) = refs[3 * shards + 8 :]
    half = TILE // 2
    len0, len1 = len_ref[0], len_ref[1]
    me = me_ref[0]
    n0, n1 = cdiv(len0, half), cdiv(len1, half)
    full = seq_rows // half
    n_all = n0 + n1

    def rows_at(piece, rows):
        return pl.ds(pl.multiple_of((me ^ piece) * rows, rows), rows)

    loads = []

    def load(src, dst):
        copy = pltpu.make_async_copy(src, dst, sems.at[len(loads)])
        loads.append(copy)
        copy.start()
        return copy

    first_loads = [load(mixt0, mixt_ref.at[0]), load(mixt1, mixt_ref.at[1])]
    first_loads += [load(inv0, inv_ref.at[0]), load(inv1, inv_ref.at[1])]
    first_loads += [load(p, wo_ref.at[rows_at(i, D // shards), :]) for i, p in enumerate(wo_p)]
    first_loads += [load(x_hbm.at[s], x_ref.at[s]) for s in range(2)]
    second_loads = [load(p, wi_ref.at[rows_at(i, D // shards), :]) for i, p in enumerate(wi_p)]
    second_loads += [load(p, wb_ref.at[rows_at(i, FF // shards), :]) for i, p in enumerate(wb_p)]
    third_loads = [load(cot_hbm.at[s], cot_ref.at[s]) for s in range(2)]

    out_ref[...] = jnp.zeros(out_ref.shape, BF16)
    gh_ref[...] = jnp.zeros(gh_ref.shape, BF16)
    dot_ref[...] = jnp.zeros(dot_ref.shape, BF16)
    acc_o[...] = jnp.zeros(acc_o.shape, F32)
    acc_i[...] = jnp.zeros(acc_i.shape, F32)
    acc_b[...] = jnp.zeros(acc_b.shape, F32)
    sums_ref[...] = jnp.zeros(sums_ref.shape, F32)

    def vec(index):
        return vec_ref[index : index + 1, :].astype(F32)

    bias_out = vec(MEM + 2)
    bias_back = vec(MEM + 3 + BLOCKS)
    gain_one = vec(MEM + 4 + BLOCKS)
    shift_one = vec(MEM + 5 + BLOCKS)
    gain_two = vec(MEM + 6 + BLOCKS)
    shift_two = vec(MEM + 7 + BLOCKS)

    spare_one = jnp.logical_and(n_all % 2 == 1, n1 < full)
    spare_zero = jnp.logical_and(n_all % 2 == 1, n1 >= full)

    def place(chunk):
        second = chunk >= n0
        inside = jnp.where(second, chunk - n0, chunk)
        spare = chunk >= n_all
        seq = jnp.where(spare, jnp.where(n1 < full, 1, 0), jnp.where(second, 1, 0))
        inside = jnp.where(spare, jnp.where(n1 < full, n1, n0), inside)
        return seq, pl.multiple_of(inside * half, half), jnp.where(seq == 1, len1, len0)

    def rows_of(ref, spots):
        return jnp.concatenate([ref[s, pl.ds(r, half), :] for s, r, _ in spots], 0)

    def lanes_of(ref, spots):
        return jnp.concatenate([ref[s, :, pl.ds(r, half)] for s, r, _ in spots], 1)

    def put_rows(ref, value, spots):
        for i, (s, r, _) in enumerate(spots):
            ref[s, pl.ds(r, half), :] = value[i * half : (i + 1) * half]

    def put_lanes(ref, value, spots):
        for i, (s, r, _) in enumerate(spots):
            ref[s, :, pl.ds(r, half)] = value[:, i * half : (i + 1) * half]

    def valid_of(spots):
        iota = lax.broadcasted_iota(jnp.int32, (half, 1), 0)
        return jnp.concatenate(
            [jnp.where(iota + r < count, 1.0, 0.0) for _, r, count in spots], 0
        )

    def add_sum(row, value):
        sums_ref[row : row + 1] += col_sum(value)

    def whole_tile(spots):
        count = half * len(spots)
        here = slice(0, count)
        valid = valid_of(spots)
        mixt = lanes_of(mixt_ref, spots)
        attn = nn(mixt.T, wo_ref[...]) + bias_out
        normed_one, inverse_one = norm_forward(rows_of(x_ref, spots).astype(F32) + attn)
        first = normed_one * gain_one + shift_one
        s_normed1[here] = normed_one
        low = first.astype(BF16)
        s_first[here] = low
        second = first + bias_back
        for j in range(BLOCKS):
            cols = slice(j * D, (j + 1) * D)
            up = nn(low, wi_ref[:, cols]) + vec(MEM + 3 + j)
            square = up * up
            gate = 0.5 + 0.5 * jnp.tanh(up * (GELU_A + GELU_B * square))
            active = up * gate
            slopes[here, cols] = (
                gate + active * (2.0 - 2.0 * gate) * (GELU_A + 3.0 * GELU_B * square)
            ).astype(slopes.dtype)
            actives[here, cols] = active.astype(BF16)
        second = second + nn(actives[here, :], wb_ref[...])
        normed_two, inverse_two = norm_forward(second)
        put_rows(out_ref, ((normed_two * gain_two + shift_two) * valid).astype(BF16), spots)
        grad_out = rows_of(cot_ref, spots).astype(F32) * valid
        add_sum(MEM + 6 + BLOCKS, grad_out * normed_two)
        add_sum(MEM + 7 + BLOCKS, grad_out)
        grad_second = norm_backward(grad_out * gain_two, normed_two, inverse_two)
        s_gsecond[here] = grad_second
        down = grad_second.astype(BF16)
        add_sum(MEM + 3 + BLOCKS, down.astype(F32))
        low_t = s_first[here, :].T
        for j in range(BLOCKS):
            cols = slice(j * D, (j + 1) * D)
            grad_up = (
                nt(down, wb_ref[cols, :]) * slopes[here, cols].astype(F32)
            ).astype(BF16)
            acc_b[cols, :] += tn(actives[here, cols], down)
            ups[here, cols] = grad_up
            add_sum(MEM + 3 + j, grad_up.astype(F32))
            acc_i[:, cols] += nn(low_t, grad_up)
        grad_first = s_gsecond[here] + nt(ups[here, :], wi_ref[...])
        normed_one = s_normed1[here]
        add_sum(MEM + 4 + BLOCKS, grad_first * normed_one)
        add_sum(MEM + 5 + BLOCKS, grad_first)
        grad_one = norm_backward(grad_first * gain_one, normed_one, inverse_one)
        low = grad_one.astype(BF16)
        put_rows(gh_ref, low, spots)
        add_sum(MEM + 2, low.astype(F32))
        acc_o[...] += nn(mixt, low)
        grad_mixed = nt(wo_ref[...], low)
        inverse = lanes_of(inv_ref, spots)
        scaled = [
            grad_mixed[h * HDIM : (h + 1) * HDIM] * inverse[h : h + 1] for h in range(HEADS)
        ]
        put_lanes(dot_ref, jnp.concatenate(scaled, 0).astype(BF16), spots)

    def send(ref, hbm, sem, seq, row, lanes=False):
        here = pl.ds(row, half)
        src = ref.at[seq, :, here] if lanes else ref.at[seq, here, :]
        dst = hbm.at[seq, :, here] if lanes else hbm.at[seq, here, :]
        pltpu.make_async_copy(src, dst, out_sems.at[sem]).start()

    def send_all(seq, row):
        send(out_ref, out_hbm, 0, seq, row)
        send(gh_ref, gh_hbm, 1, seq, row)
        send(dot_ref, dot_hbm, 2, seq, row, True)

    for copy in first_loads + second_loads + third_loads:
        copy.wait()

    def step(index, _):
        spots = [place(index * 4 + i) for i in range(4)]
        whole_tile(spots)
        for seq, row, _ in spots:
            send_all(seq, row)
        return 0

    left = lax.rem(n_all, 4)
    bigs = n_all // 4 + jnp.where(left == 3, 1, 0)
    lax.fori_loop(0, bigs, step, 0)

    @pl.when(jnp.logical_or(left == 1, left == 2))
    def _():
        spots = [place(bigs * 4 + i) for i in range(2)]
        whole_tile(spots)
        for seq, row, _ in spots:
            send_all(seq, row)

    def rest(seq):
        def one(chunk, _):
            send_all(seq, pl.multiple_of(chunk * half, half))
            return 0

        return one

    lax.fori_loop(n0 + jnp.where(spare_zero, 1, 0), full, rest(0), 0)
    lax.fori_loop(n1 + jnp.where(spare_one, 1, 0), full, rest(1), 0)

    part = D // shards
    deep = FF // shards
    block = part * (1 + BLOCKS)
    for m, piece, row in piece_spots(grads[:2], shards, block):
        at = pl.multiple_of((me ^ m) * part, part)
        piece[row : row + part, :] = acc_o[pl.ds(at, part), :].astype(BF16)
        for j in range(BLOCKS):
            row += part
            piece[row : row + part, :] = acc_i[
                pl.ds(at, part), j * D : (j + 1) * D
            ].astype(BF16)
    for m, piece, row in piece_spots(grads[2:], shards, deep):
        at = pl.multiple_of((me ^ m) * deep, deep)
        piece[row : row + deep, :] = acc_b[pl.ds(at, deep), :].astype(BF16)
    for ref, hbm, sem in ((out_ref, out_hbm, 0), (gh_ref, gh_hbm, 1), (dot_ref, dot_hbm, 2)):
        pltpu.make_async_copy(ref, hbm, out_sems.at[sem]).wait()


def feed_forward(lengths, me, x, cot, mixts, invs, w_out, w_in, w_back, vectors):
    count, seq_rows = x.shape[:2]
    shards = len(w_out)
    vm = pl.BlockSpec(memory_space=pltpu.VMEM)
    hbm = pl.BlockSpec(memory_space=pl.ANY)
    smem = pl.BlockSpec(memory_space=pltpu.SMEM)
    return pl.pallas_call(
        partial(ffn_kernel, seq_rows, shards),
        out_shape=(
            jax.ShapeDtypeStruct((count, seq_rows, D), BF16),
            jax.ShapeDtypeStruct((count, seq_rows, D), BF16),
            jax.ShapeDtypeStruct((count, D, seq_rows), BF16),
            *[
                jax.ShapeDtypeStruct((rows, D), BF16)
                for rows in (D * (1 + BLOCKS) // 2, FF // 2)
                for _ in range(2)
            ],
            jax.ShapeDtypeStruct((32, D), F32),
        ),
        in_specs=[smem, smem] + [hbm] * (6 + 3 * shards) + [vm],
        out_specs=(hbm, hbm, hbm) + (vm,) * 5,
        scratch_shapes=[
            pltpu.VMEM((count, seq_rows, D), BF16),
            pltpu.VMEM((count, seq_rows, D), BF16),
            pltpu.VMEM((count, D, seq_rows), BF16),
            pltpu.VMEM((count, HEADS, seq_rows), F32),
            pltpu.VMEM((D, D), BF16),
            pltpu.VMEM((D, FF), BF16),
            pltpu.VMEM((FF, D), BF16),
            pltpu.VMEM((count, seq_rows, D), BF16),
            pltpu.VMEM((count, seq_rows, D), BF16),
            pltpu.VMEM((count, D, seq_rows), BF16),
            pltpu.VMEM((D, D), F32),
            pltpu.VMEM((D, FF), F32),
            pltpu.VMEM((FF, D), F32),
            pltpu.VMEM((2 * TILE, FF), F32),
            pltpu.VMEM((2 * TILE, FF), BF16),
            pltpu.VMEM((2 * TILE, D), F32),
            pltpu.VMEM((2 * TILE, D), BF16),
            pltpu.VMEM((2 * TILE, D), F32),
            pltpu.VMEM((2 * TILE, FF), BF16),
            pltpu.SemaphoreType.DMA((8 + 3 * shards,)),
            pltpu.SemaphoreType.DMA((3,)),
        ],
        compiler_params=pltpu.CompilerParams(vmem_limit_bytes=VMEM_LIMIT),
        cost_estimate=pl.CostEstimate(
            flops=27 * 10**9, bytes_accessed=24 * 10**6, transcendentals=4 * 10**6
        ),
        name="feed_forward",
    )(lengths, me, x, cot, *mixts, *invs, *w_out, *w_in, *w_back, vectors)


def bwd_kernel(seq_rows, groups, group, seq, shards, chained, closing, waits, *refs):
    gp = PAIRS // groups
    gcols = gp * 128
    width = 3 * gcols
    refs = list(refs)
    len_ref, me_ref, wk_ref, wv_ref, vec_ref = refs[:5]
    x_hbm, dot_hbm, qt_hbm, mixt_hbm, e_hbm = refs[5:10]
    refs = refs[10:]
    acc_in, extra_in = (refs.pop(0), refs.pop(0)) if chained else (None, None)
    other_rows = [refs.pop(0) for _ in range(closing)]
    refs = refs[waits:]
    proj_hbm = refs.pop(0)
    last = chained
    if last:
        pieces = [refs.pop(0), refs.pop(0)]
    else:
        acc_hbm = refs.pop(0)
    extra_ref = None if closing else refs.pop(0)
    (
        rows, qts, mixts, dots, wkt, kt, values, qpad, dpad, dqt, dk, dv, ebuf, acc, proj,
        extra, table, sems, io_sems, out_sem, acc_sem,
    ) = refs
    base = group * gcols
    mine = pl.ds(base, gcols)
    length = len_ref[seq]
    total = length + MEM
    n_tiles = cdiv(length, TILE)
    chunks = cdiv(total, TILE)
    pairs = [
        (x_hbm.at[seq], rows.at[pl.ds(0, seq_rows), :]),
        (qt_hbm.at[mine, :], qts),
        (mixt_hbm.at[mine, :], mixts),
        (dot_hbm.at[seq, mine, :], dots),
    ]
    loads = [pltpu.make_async_copy(a, b, io_sems.at[i]) for i, (a, b) in enumerate(pairs)]

    def copies_of(kr):
        def copies(tile, slot):
            return pltpu.make_async_copy(
                e_hbm.at[tile, pl.ds(group * gp * 2, gp * 2), pl.ds(0, kr), :],
                ebuf.at[slot, :, pl.ds(0, kr), :],
                sems.at[slot],
            )

        return copies

    for copy in loads:
        copy.start()
    if chained:
        fetch = pltpu.make_async_copy(acc_in, acc, acc_sem)
        fetch.start()
    for_size(seq_rows, total, lambda kr: copies_of(kr)(0, 0).start())
    memory = memory_rows(vec_ref)
    bias_v = vec_ref[MEM + 1 : MEM + 2, base : base + gcols].astype(F32)
    wkt[...] = wk_ref[...].T
    if chained:
        extra[...] = extra_in[...]
        for other in other_rows:
            extra[...] += other[...]
    else:
        acc[...] = jnp.zeros(acc.shape, F32)
        extra[...] = jnp.zeros(extra.shape, F32)
    for head in range(gp * 2):
        spare = HDIM * (1 - head % 2)
        qpad[head, spare : spare + HDIM, :] = jnp.zeros((HDIM, TILE), BF16)
        dpad[head, spare : spare + HDIM, :] = jnp.zeros((HDIM, TILE), BF16)
    rows[seq_rows:, :] = jnp.zeros((rows.shape[0] - seq_rows, D), BF16)
    loads[0].wait()
    edge = pl.multiple_of(length // 128 * 128, 128)
    fix = pl.ds(edge, TILE)
    row = lax.broadcasted_iota(jnp.int32, (TILE, 1), 0) + edge
    pick = (
        lax.broadcasted_iota(jnp.int32, (TILE, 32), 0) + (edge - length)
        == lax.broadcasted_iota(jnp.int32, (TILE, 32), 1)
    )
    placed = nn(jnp.where(pick, 1.0, 0.0).astype(BF16), memory)
    rows[fix, :] = jnp.where(row < length, rows[fix, :].astype(F32), placed).astype(BF16)

    def project(chunk, _):
        here = pl.ds(pl.multiple_of(chunk * TILE, TILE), TILE)
        joined = rows[here, :]
        value_rows = (nn(joined, wv_ref[...]) + bias_v).astype(BF16)
        for pair in range(gp):
            values[pair, here, :] = value_rows[:, pair * 128 : pair * 128 + 128]
            dk[pair, here, :] = jnp.zeros((TILE, 128), F32)
            dv[pair, here, :] = jnp.zeros((TILE, 128), F32)
        kt[:, here] = nt(wkt[...], joined).astype(BF16)
        dqt[:, here] = jnp.zeros((gcols, TILE), BF16)
        return 0

    lax.fori_loop(0, chunks, project, 0)
    for copy in loads[1:]:
        copy.wait()

    def attend(kr):
        copies = copies_of(kr)

        def step(tile, _):
            slot = lax.rem(tile, 2)
            here = pl.ds(pl.multiple_of(tile * TILE, TILE), TILE)

            @pl.when(tile + 1 < n_tiles)
            def _():
                copies(tile + 1, 1 - slot).start()

            copies(tile, slot).wait()
            inners = []
            for head in range(gp * 2):
                low = (head % 2) * HDIM
                local = slice(head * HDIM, (head + 1) * HDIM)
                outer = dots[local, here]
                dpad[head, low : low + HDIM, :] = outer
                qpad[head, low : low + HDIM, :] = qts[local, here]
                inners.append(col_sum(outer.astype(F32) * mixts[local, here].astype(F32)))

            def outer_product(head):
                return nn(values[head // 2, :kr, :], dpad[head])

            live = {head: outer_product(head) for head in range(AHEAD)}
            grads = []
            for head in range(gp * 2):
                pair = head // 2
                product = live.pop(head)
                if head + AHEAD < gp * 2:
                    live[head + AHEAD] = outer_product(head + AHEAD)
                local = slice(head * HDIM, (head + 1) * HDIM)
                grad = (
                    ebuf[slot, head, :kr, :].astype(F32) * (product - inners[head])
                ).astype(BF16)
                grads.append(grad)
                dqt[local, here] = (nn(kt[local, :kr], grad) * SCALE).astype(BF16)
                if head % 2:
                    both = [ebuf[slot, h, :kr, :] for h in (head - 1, head)]
                    dv[pair, :kr, :] += nt(
                        jnp.concatenate(both, 1),
                        jnp.concatenate([dpad[head - 1], dpad[head]], 1),
                    )
                    dk[pair, :kr, :] += nt(
                        jnp.concatenate(grads[-2:], 1),
                        jnp.concatenate([qpad[head - 1], qpad[head]], 1),
                    )
            return 0

        lax.fori_loop(0, n_tiles, step, 0)

    for_size(seq_rows, total, attend)
    if chained:
        fetch.wait()

    def send(chunk):
        here = pl.ds(pl.multiple_of(chunk * TILE, TILE), TILE)
        return pltpu.make_async_copy(proj.at[here, :], proj_hbm.at[here, :], out_sem)

    def finish(chunk, sums):
        here = pl.ds(pl.multiple_of(chunk * TILE, TILE), TILE)
        parts = [dqt[:, here].T]
        parts += [(dk[pair, here, :] * LN2).astype(BF16) for pair in range(gp)]
        parts += [dv[pair, here, :].astype(BF16) for pair in range(gp)]
        grad = jnp.concatenate(parts, 1)
        proj[here, :] = grad
        send(chunk).start()
        acc[...] += tn(rows[here, :], grad)
        return sums + col_sum(grad.astype(F32))

    sums = lax.fori_loop(0, chunks, finish, jnp.zeros((1, width), F32))
    extra[MEM : MEM + 1, base : base + gcols] += sums[:, :gcols]
    extra[MEM + 1 : MEM + 2, base : base + gcols] += sums[:, 2 * gcols :]
    turned = (
        lax.broadcasted_iota(jnp.int32, (32, TILE), 1) + (edge - length)
        == lax.broadcasted_iota(jnp.int32, (32, TILE), 0)
    )
    turned = jnp.logical_and(turned, lax.broadcasted_iota(jnp.int32, (32, TILE), 0) < MEM)
    turned = jnp.where(turned, 1.0, 0.0).astype(BF16)
    found_k = jnp.concatenate([dk[pair, fix, :] * LN2 for pair in range(gp)], 1)
    found_v = jnp.concatenate([dv[pair, fix, :] for pair in range(gp)], 1)
    grad_memory = nt(nn(turned, found_k.astype(BF16)).astype(BF16), wk_ref[...])
    grad_memory += nt(nn(turned, found_v.astype(BF16)).astype(BF16), wv_ref[...])
    extra[...] += grad_memory

    if last:
        me = me_ref[0]
        part, few = D // shards, 32 // shards
        if closing:
            for s in range(shards):
                table[s, :few, :] = extra[s * few : (s + 1) * few]
        for m, piece, row in piece_spots(pieces, shards, part):
            spot = slice(row, row + part)
            at = pl.multiple_of((me ^ m) * part, part)
            piece[spot, :width] = acc[pl.ds(at, part), :].astype(BF16)
            if closing:
                mine_rows = table[me ^ m]
                lanes = [mine_rows[:, j : j + 128] for j in range(0, D, 128)]
                empty = part - mine_rows.shape[0] * len(lanes)
                if empty:
                    lanes.append(jnp.zeros((empty, 128), F32))
                piece[spot, width:] = jnp.concatenate(lanes, 0).astype(BF16)
    else:
        store = pltpu.make_async_copy(acc, acc_hbm, acc_sem)
        store.start()
        store.wait()
    if extra_ref is not None:
        extra_ref[...] = extra[...]

    def drain(chunk, _):
        send(chunk).wait()
        return 0

    lax.fori_loop(0, chunks, drain, 0)


def attention_backward(
    seq, group, groups, shards, lengths, me, w_qkv, vectors, x, dot, qt, mixt, expo,
    chain=(), others=(), after=(),
):
    seq_rows = x.shape[1]
    top = key_sizes(seq_rows)[-1]
    padded = cdiv(seq_rows + MEM, TILE) * TILE
    gp = PAIRS // groups
    gcols = gp * 128
    width = 3 * gcols
    vm = pl.BlockSpec(memory_space=pltpu.VMEM)
    hbm = pl.BlockSpec(memory_space=pl.ANY)
    smem = pl.BlockSpec(memory_space=pltpu.SMEM)
    out_shape = [jax.ShapeDtypeStruct((padded, width), BF16)]
    out_specs = [hbm]
    if chain:
        wide = width + (128 if others else 0)
        out_shape += [jax.ShapeDtypeStruct((D // 2, wide), BF16)] * 2
        out_specs += [vm] * 2
    else:
        out_shape += [jax.ShapeDtypeStruct((D, width), F32)]
        out_specs += [hbm]
    if not others:
        out_shape += [jax.ShapeDtypeStruct((32, D), F32)]
        out_specs += [vm]
    return pl.pallas_call(
        partial(
            bwd_kernel, seq_rows, groups, group, seq, shards, bool(chain), len(others),
            len(after),
        ),
        out_shape=tuple(out_shape),
        grid=(1,),
        in_specs=[
            smem,
            smem,
            pl.BlockSpec((D, gcols), lambda i: (0, groups + group)),
            pl.BlockSpec((D, gcols), lambda i: (0, 2 * groups + group)),
            vm,
        ]
        + [hbm] * 5
        + ([hbm, vm] if chain else [])
        + [vm] * len(others)
        + [hbm] * len(after),
        out_specs=tuple(out_specs),
        scratch_shapes=[
            pltpu.VMEM((padded, D), BF16),
            pltpu.VMEM((gcols, seq_rows), BF16),
            pltpu.VMEM((gcols, seq_rows), BF16),
            pltpu.VMEM((gcols, seq_rows), BF16),
            pltpu.VMEM((gcols, D), BF16),
            pltpu.VMEM((gcols, padded), BF16),
            pltpu.VMEM((gp, padded, 128), BF16),
            pltpu.VMEM((gp * 2, 128, TILE), BF16),
            pltpu.VMEM((gp * 2, 128, TILE), BF16),
            pltpu.VMEM((gcols, padded), BF16),
            pltpu.VMEM((gp, padded, 128), F32),
            pltpu.VMEM((gp, padded, 128), F32),
            pltpu.VMEM((2, gp * 2, top, TILE), BF16),
            pltpu.VMEM((D, width), F32),
            pltpu.VMEM((padded, width), BF16),
            pltpu.VMEM((32, D), F32),
            pltpu.VMEM((shards, max(8, 32 // shards), D), F32),
            pltpu.SemaphoreType.DMA((2,)),
            pltpu.SemaphoreType.DMA((4,)),
            pltpu.SemaphoreType.DMA,
            pltpu.SemaphoreType.DMA,
        ],
        compiler_params=pltpu.CompilerParams(vmem_limit_bytes=VMEM_LIMIT),
        cost_estimate=pl.CostEstimate(
            flops=8 * 10**9, bytes_accessed=15 * 10**6, transcendentals=0
        ),
        name="attention_backward",
    )(lengths, me, w_qkv, w_qkv, vectors, x, dot, qt, mixt, expo, *chain, *others, *after)


def input_kernel(seq_rows, groups, seq, len_ref, w_ref, gh_hbm, *refs):
    projs = refs[:groups]
    gx_ref, gh, blocks, sems = refs[-4:]
    gcols = D // groups
    length = len_ref[seq]
    chunks = cdiv(length, TILE)

    def fetch(chunk):
        here = pl.ds(pl.multiple_of(chunk * TILE, TILE), TILE)
        slot = lax.rem(chunk, 2)
        return [
            pltpu.make_async_copy(gh_hbm.at[seq, here, :], gh.at[slot], sems.at[slot, 0])
        ] + [
            pltpu.make_async_copy(p.at[here, :], blocks.at[slot, i], sems.at[slot, 1 + i])
            for i, p in enumerate(projs)
        ]

    for copy in fetch(0):
        copy.start()
    gx_ref[...] = jnp.zeros(gx_ref.shape, BF16)

    def step(chunk, _):
        start = pl.multiple_of(chunk * TILE, TILE)
        slot = lax.rem(chunk, 2)

        @pl.when(chunk + 1 < chunks)
        def _():
            for copy in fetch(chunk + 1):
                copy.start()

        for copy in fetch(chunk):
            copy.wait()
        joint = jnp.concatenate(
            [
                blocks[slot, g, :, kind * gcols : (kind + 1) * gcols]
                for kind in range(3)
                for g in range(groups)
            ],
            1,
        )
        grad = nt(joint, w_ref[...])
        row = lax.broadcasted_iota(jnp.int32, (TILE, 1), 0) + start
        gx_ref[0, pl.ds(start, TILE), :] = jnp.where(
            row < length, grad + gh[slot].astype(F32), 0.0
        ).astype(BF16)
        return 0

    lax.fori_loop(0, chunks, step, 0)


def input_gradient(seq, lengths, w_qkv, gh, projs, after=(), base=None):
    count, seq_rows = gh.shape[:2]
    groups = len(projs)
    hbm = pl.BlockSpec(memory_space=pl.ANY)
    base = () if base is None else (base,)
    return pl.pallas_call(
        partial(input_kernel, seq_rows, groups, seq),
        out_shape=jax.ShapeDtypeStruct((count, seq_rows, D), BF16),
        grid=(1,),
        in_specs=[
            pl.BlockSpec(memory_space=pltpu.SMEM),
            pl.BlockSpec(memory_space=pltpu.VMEM),
        ]
        + [hbm] * (1 + groups + len(after) + len(base)),
        out_specs=pl.BlockSpec((1, seq_rows, D), lambda i: (seq, 0, 0)),
        input_output_aliases={3 + groups + len(after): 0} if base else {},
        scratch_shapes=[
            pltpu.VMEM((2, TILE, D), BF16),
            pltpu.VMEM((2, groups, TILE, 3 * D // groups), BF16),
            pltpu.SemaphoreType.DMA((2, 1 + groups)),
        ],
        compiler_params=pltpu.CompilerParams(vmem_limit_bytes=VMEM_LIMIT),
        cost_estimate=pl.CostEstimate(
            flops=2 * 10**9, bytes_accessed=7 * 10**6, transcendentals=0
        ),
        name="input_gradient",
    )(lengths, w_qkv, gh, *projs, *after, *base)


GROUPS = 2


def powers(size):
    return [1 << i for i in range(size.bit_length() - 1)]


def exchange(value, axis, size, bit):
    return lax.ppermute(value, axis, [(i, i ^ bit) for i in range(size)])


def gather_pieces(value, axis, size):
    pieces = {0: value}
    for bit in reversed(powers(size)):
        for mask in sorted(pieces):
            pieces[mask | bit] = exchange(pieces[mask], axis, size, bit)
    return [pieces[mask] for mask in range(size)]


def combine_kernel(counts, modes, waits, place_ref, *refs):
    refs = list(refs)
    arrays = [[[refs.pop(0) for _ in range(c)] for c in group] for group in counts]
    refs = refs[waits:]
    total = refs.pop()
    place = place_ref[0]
    for groups, (mode, stacked, cols) in zip(arrays, modes):
        rows = 0
        for group in groups:
            more, wide = group[0].shape
            value = group[0][...].astype(F32)
            for other in group[1:]:
                value = value + other[...].astype(F32)
            total[rows : rows + more, :wide] = value
            if wide < cols:
                total[rows : rows + more, wide:cols] = jnp.zeros((more, cols - wide), F32)
            rows += more
        if mode == "halves":
            refs.pop(0)[...] = total[: rows // 2, :cols].astype(BF16)
            refs.pop(0)[...] = total[rows // 2 : rows, :cols].astype(BF16)
        elif mode == "parts":
            one = rows // stacked
            part = one // GROUP
            for m in range(GROUP):
                target = refs.pop(0)
                at = pl.multiple_of((place ^ m) * part, part)
                for i in range(stacked):
                    target[i * part : (i + 1) * part, :] = total[
                        pl.ds(at + i * one, part), :cols
                    ].astype(BF16)
        else:
            refs.pop(0)[...] = total[:rows, :cols].astype(BF16)


def combine(place, items, after):
    vm = pl.BlockSpec(memory_space=pltpu.VMEM)
    shapes, flat, modes, most = [], [], [], 0
    for groups, mode, stacked in items:
        rows = sum(arrays[0].shape[0] for arrays in groups)
        cols = max(arrays[0].shape[1] for arrays in groups)
        flat += [a for arrays in groups for a in arrays]
        modes.append((mode, stacked, cols))
        most = max(most, rows)
        if mode == "halves":
            shapes += [(rows // 2, cols)] * 2
        elif mode == "parts":
            shapes += [(rows // GROUP, cols)] * GROUP
        else:
            shapes += [(rows, cols)]
    size = sum(a.size for a in flat) * 2
    outs = pl.pallas_call(
        partial(combine_kernel, [[len(g) for g in i[0]] for i in items], modes, len(after)),
        out_shape=tuple(jax.ShapeDtypeStruct(s, BF16) for s in shapes),
        in_specs=[pl.BlockSpec(memory_space=pltpu.SMEM)]
        + [vm] * len(flat)
        + [pl.BlockSpec(memory_space=pl.ANY)] * len(after),
        out_specs=(vm,) * len(shapes),
        scratch_shapes=[pltpu.VMEM((most, max(m[2] for m in modes)), F32)],
        compiler_params=pltpu.CompilerParams(vmem_limit_bytes=24 * 2**20),
        cost_estimate=pl.CostEstimate(flops=size, bytes_accessed=2 * size, transcendentals=0),
        name="combine",
    )(place, *flat, *after)
    outs, results = list(outs), []
    for mode, _, _ in modes:
        taken = {"halves": 2, "parts": GROUP, "whole": 1}[mode]
        results.append([outs.pop(0) for _ in range(taken)])
    return results


GROUP = 4


class Stream:
    def __init__(self, value, sizes, steps, stacked=None):
        self.value, self.steps = list(value), list(steps)
        self.reps, self.shards = sizes
        self.stacked = stacked or max(self.shards // 2, 1)

    def exchange(self):
        kind, bit = self.steps.pop(0)
        value = self.value
        if kind == "fold":
            arrays = [value[0], exchange(value[1], "shard", self.shards, bit)]
        elif kind == "group":
            arrays = [value[0]] + [
                exchange(value[j], "rep", self.reps, j) for j in range(1, GROUP)
            ]
        else:
            arrays = [value[0], exchange(value[0], "rep", self.reps, bit)]
        follow = self.steps[0][0] if self.steps else "end"
        item = ([arrays], {"fold": "halves", "group": "parts"}.get(follow, "whole"), self.stacked)
        if follow == "fold":
            self.stacked //= 2
        return item

    def alone(self, place, after=()):
        self.value = combine(place, [self.exchange()], after)[0]


def advance(place, streams, items, after):
    results = combine(place, items, after)
    for stream, result in zip(streams, results):
        stream.value = result
    return [r for result in results for r in result]


def whole_parts(stream):
    own = stream.value[0]
    return [own] + [exchange(own, "rep", stream.reps, j) for j in range(1, GROUP)]


def spread_kernel(counts, shards, place_ref, *refs):
    refs = list(refs)
    arrays = [[refs.pop(0) for _ in range(GROUP)] for _ in counts]
    qkv_ref, out_ref, in_ref, back_ref, vec_ref, table = refs
    place = place_ref[0]

    def put(target, parts, cols, first=0, count=None):
        part = count or parts[0].shape[0]
        for m in range(GROUP):
            at = pl.multiple_of((place ^ m) * part, part)
            target[pl.ds(at, part), :cols] = parts[m][first : first + part, :].astype(F32)

    part = D // shards
    tall = part * (1 + BLOCKS) // GROUP
    put(back_ref, arrays[0], D, tall, FF // shards // GROUP)
    put(table, arrays[0], D, 0, tall)
    out_ref[...] = table[:part, :D]
    for j in range(BLOCKS):
        in_ref[:, j * D : (j + 1) * D] = table[(1 + j) * part : (2 + j) * part, :D]
    gcols = D // GROUPS
    for g in range(GROUPS):
        put(table, arrays[1], 3 * gcols + 128, g * part // GROUP, part // GROUP)
        for kind in range(3):
            at = kind * D + g * gcols
            qkv_ref[:, at : at + gcols] = table[:part, kind * gcols : (kind + 1) * gcols]
    few = 32 // shards
    width = 3 * gcols
    step = max(8, few)
    for j in range(D // 128):
        vec_ref[:, j * 128 : (j + 1) * 128] = table[j * step : j * step + few, width : width + 128]


def spread(place, shards, streams):
    parts = [p for stream in streams for p in whole_parts(stream)]
    part = D // shards
    vm = pl.BlockSpec(memory_space=pltpu.VMEM)
    shapes = ((part, 3 * D), (part, D), (part, FF), (FF // shards, D), (32 // shards, D))
    most = max(part * (1 + BLOCKS), part), max(p.shape[1] for p in parts)
    return pl.pallas_call(
        partial(spread_kernel, [GROUP] * len(streams), shards),
        out_shape=tuple(jax.ShapeDtypeStruct(s, F32) for s in shapes),
        in_specs=[pl.BlockSpec(memory_space=pltpu.SMEM)] + [vm] * len(parts),
        out_specs=(vm,) * len(shapes),
        scratch_shapes=[pltpu.VMEM(most, F32)],
        compiler_params=pltpu.CompilerParams(vmem_limit_bytes=24 * 2**20),
        name="spread",
    )(place, *parts)


def body(sizes, inputs, lengths, w_qkv, w_out, w_in, w_back, vectors, cotangent):
    reps, shards = sizes
    count = inputs.shape[0]
    me = lax.axis_index("shard").astype(jnp.int32).reshape(1)

    def collect(value):
        return gather_pieces(value, "shard", shards)

    whole, wqt, wvt, table = prepare(me, collect(w_qkv), collect(vectors))
    fwd = [
        attention_forward(s, lengths, inputs, whole, wqt, wvt, table) for s in range(count)
    ]
    out, gh, dot, *grads, sums = feed_forward(
        lengths, me, inputs, cotangent, [f[2] for f in fwd], [f[3] for f in fwd],
        collect(w_out), collect(w_in), collect(w_back), table,
    )
    place = (lax.axis_index("rep") % GROUP).astype(jnp.int32).reshape(1)
    folds = [("fold", bit) for bit in powers(shards)]
    group = [("group", 0)]
    rest = [("full", bit) for bit in powers(reps) if bit >= GROUP]
    tall = Stream(grads[:2], sizes, folds + group + rest)
    deep = Stream(grads[2:], sizes, folds[:1] + group + folds[1:] + rest)
    projs = [[None] * GROUPS for _ in range(count)]
    quarters = [None] * GROUPS
    extras, after, calls = [], [], []
    for g in range(GROUPS):
        chain = ()
        for s in range(count):
            closing = [sums] + extras if s == count - 1 and g == GROUPS - 1 else ()
            busy = [(tall, deep), (tall, deep), (tall, quarters[0]), (deep, quarters[0])][
                len(calls)
            ]
            items = [stream.exchange() for stream in busy]
            res = attention_backward(
                s, g, GROUPS, shards, lengths, me, whole, table, inputs, dot, fwd[s][1],
                fwd[s][2], fwd[s][0], chain, closing, after,
            )
            after = advance(place, busy, items, [res[0]])
            projs[s][g] = res[0]
            calls.append(res)
            chain = res[1:]
        quarters[g] = Stream(chain[:2], sizes, folds + [("stop", 0)])
        extras += chain[2:]
    early, last = quarters
    last.value = list(lax.optimization_barrier((*last.value, after[0])))[:2]
    for stream in (early, tall, deep):
        left = 1 if stream is early else len(rest) and 1
        while len(stream.steps) > left:
            stream.alone(place)
    ends = [stream.exchange()[0][0] for stream in (tall, deep)]
    while len(last.steps) > 2:
        last.alone(place)
    gx = input_gradient(0, lengths, whole, gh, projs[0], last.value)
    final = last.exchange()[0]
    both = Stream([], sizes, group + rest, stacked=GROUPS)
    after = advance(place, [both], [([early.value] + final, "parts", GROUPS)], [gx])
    for seq in range(1, count):
        gx = input_gradient(seq, lengths, whole, gh, projs[seq], after, gx)
    joined = Stream([], sizes, [])
    advance(place, [both, joined], [both.exchange(), (ends, "whole", 1)], [gx])
    while both.steps:
        both.alone(place)
    return (out, gx, *spread(place, shards, [joined, both]))


def solution(mesh):
    data = P(("rep", "shard"), None, None)
    rows = P("shard", None)
    return jax.shard_map(
        partial(body, (mesh.shape["rep"], mesh.shape["shard"])),
        mesh=mesh,
        in_specs=(data, P(("rep", "shard")), rows, rows, rows, rows, rows, data),
        out_specs=(data, data, rows, rows, rows, rows, rows),
        check_vma=False,
    )
```

```python
import math
from functools import partial

import jax
import jax.numpy as jnp
from jax import lax
from jax.experimental import pallas as pl
from jax.experimental.pallas import tpu as pltpu
from jax.sharding import PartitionSpec as P

D = 512
HEADS = 8
HDIM = 64
FF = 2048
MEM = 20
TILE = 256
PAIRS = HEADS // 2
SCALE = HDIM**-0.5
QSCALE = SCALE * math.log2(math.e)
LN2 = math.log(2.0)
F32 = jnp.float32
BF16 = jnp.bfloat16
VROWS = 80
VMEM_LIMIT = 62 * 2**20


def nn(a, b):
    return lax.dot_general(a, b, (((1,), (0,)), ((), ())), preferred_element_type=F32)


def nt(a, b):
    return lax.dot_general(a, b, (((1,), (1,)), ((), ())), preferred_element_type=F32)


def tn(a, b):
    return lax.dot_general(a, b, (((0,), (0,)), ((), ())), preferred_element_type=F32)


def key_sizes(seq_rows):
    top = -(-(seq_rows + MEM) // 32) * 32
    return [rows for rows in range(512, top, 256)] + [top]


def column_max(values):
    parts = [values[i : i + 128] for i in range(0, values.shape[0] - 127, 128)]
    while len(parts) > 1:
        odd = parts[len(parts) - len(parts) % 2 :]
        parts = [jnp.maximum(a, b) for a, b in zip(parts[::2], parts[1::2])] + odd
    top = jnp.max(parts[0], axis=0, keepdims=True)
    rest = values.shape[0] % 128
    if rest:
        top = jnp.maximum(top, jnp.max(values[-rest:], axis=0, keepdims=True))
    return top


AHEAD = 2
BODY_HEADS = 4


def cdiv(a, b):
    return (a + b - 1) // b


def pick_memory(rows_ref, memory, length):
    edge = pl.multiple_of(length // 128 * 128, 128)
    fix = pl.ds(edge, TILE)
    row = lax.broadcasted_iota(jnp.int32, (TILE, 1), 0) + edge
    lane = lax.broadcasted_iota(jnp.int32, (TILE, 32), 1)
    pick = lax.broadcasted_iota(jnp.int32, (TILE, 32), 0) + (edge - length) == lane
    placed = nn(jnp.where(pick, 1.0, 0.0).astype(BF16), memory)
    rows_ref[fix, :] = jnp.where(row < length, rows_ref[fix, :].astype(F32), placed).astype(BF16)


def memory_rows(vec_ref):
    inside = lax.broadcasted_iota(jnp.int32, (32, D), 0) < MEM
    return jnp.where(inside, vec_ref[...].astype(F32), 0.0).astype(BF16)


def for_size(seq_rows, total, run):
    sizes = key_sizes(seq_rows)
    for index, kr in enumerate(sizes):
        least = sizes[index - 1] if index else 0

        @pl.when(jnp.logical_and(total > least, total <= kr))
        def _(kr=kr):
            run(kr)


def prepare_kernel(shards, me_ref, *refs):
    pieces = refs[:shards]
    w_ref, wqt_ref, wvt_ref, vec_ref, few_rows, sems = refs[shards:]
    me = me_ref[0]
    part, few = D // shards, 32 // shards
    copies, small = [], []
    for m in range(shards):
        at = pl.multiple_of((me ^ m) * part, part)
        small.append(
            pltpu.make_async_copy(
                pieces[m].at[pl.ds(part, SPARE), pl.ds(0, D)], few_rows.at[m], sems.at[m, 1]
            )
        )
        copies.append(
            pltpu.make_async_copy(
                pieces[m].at[pl.ds(0, part), :], w_ref.at[pl.ds(at, part), :], sems.at[m, 0]
            )
        )
    for copy in small + copies:
        copy.start()
    for copy in small:
        copy.wait()
    owner = lax.broadcasted_iota(jnp.int32, (32, D), 0) // few
    rows = jnp.zeros((32, D), F32)
    for m in range(shards):
        values = few_rows[m].astype(F32)[:few]
        rows = jnp.where(owner == (me ^ m), jnp.concatenate([values] * shards, 0), rows)
    vec_ref[...] = rows.astype(BF16)
    for copy in copies:
        copy.wait()
    wqt_ref[...] = w_ref[:, :D].T
    wvt_ref[...] = w_ref[:, 2 * D :].T


SPARE = 16


def pack(w_qkv, vectors):
    below = ((0, SPARE - vectors.shape[0]), (0, w_qkv.shape[1] - vectors.shape[1]))
    return jnp.concatenate([w_qkv, jnp.pad(vectors, below)], 0)


def prepare(me, pieces):
    shards = len(pieces)
    vm = pl.BlockSpec(memory_space=pltpu.VMEM)
    return pl.pallas_call(
        partial(prepare_kernel, shards),
        out_shape=(
            jax.ShapeDtypeStruct((D, 3 * D), BF16),
            jax.ShapeDtypeStruct((D, D), BF16),
            jax.ShapeDtypeStruct((D, D), BF16),
            jax.ShapeDtypeStruct((32, D), BF16),
        ),
        in_specs=[pl.BlockSpec(memory_space=pltpu.SMEM)]
        + [pl.BlockSpec(memory_space=pl.ANY)] * shards,
        out_specs=(vm, vm, vm, vm),
        scratch_shapes=[
            pltpu.VMEM((shards, SPARE, D), BF16),
            pltpu.SemaphoreType.DMA((shards, 2)),
        ],
        compiler_params=pltpu.CompilerParams(vmem_limit_bytes=24 * 2**20),
        name="prepare",
    )(me, *pieces)


def fwd_kernel(
    seq_rows, seq, len_ref, x_hbm, wk_ref, wqt_ref, wvt_ref, vec_ref,
    e_hbm, qt_hbm, mixt_hbm, inv_ref,
    rows, keys, vt, qpad, queries, mixed_t, ebuf, sems, io_sems,
):
    length = len_ref[seq]
    total = length + MEM
    load = pltpu.make_async_copy(x_hbm.at[seq], rows.at[pl.ds(0, seq_rows), :], io_sems.at[0])
    load.start()
    memory = memory_rows(vec_ref)
    vec_cols = vec_ref[...].astype(F32).T
    bias_q = vec_cols[:, MEM : MEM + 1]
    bias_v = vec_cols[:, MEM + 1 : MEM + 2]
    mixed_t[...] = jnp.zeros(mixed_t.shape, BF16)
    inv_ref[...] = jnp.zeros(inv_ref.shape, F32)
    for head in range(HEADS):
        spare = HDIM * (1 - head % 2)
        qpad[head, spare : spare + HDIM, :] = jnp.zeros((HDIM, qpad.shape[2]), BF16)
    vt[:, HDIM:, :] = jnp.ones((HEADS, VROWS - HDIM, vt.shape[2]), BF16)
    n_tiles = cdiv(length, TILE)
    chunks = cdiv(total, TILE)
    load.wait()

    rows[seq_rows:, :] = jnp.zeros((rows.shape[0] - seq_rows, D), BF16)
    pick_memory(rows, memory, length)

    def project(chunk, _):
        here = pl.ds(pl.multiple_of(chunk * TILE, TILE), TILE)
        joined = rows[here, :]
        key_rows = nn(joined, wk_ref[...]).astype(BF16)
        for pair in range(PAIRS):
            keys[pair, here, :] = key_rows[:, pair * 128 : pair * 128 + 128]
        values = (nt(wvt_ref[...], joined) + bias_v).astype(BF16)
        found = ((nt(wqt_ref[...], joined) + bias_q) * QSCALE).astype(BF16)
        queries[:, here] = found
        for head in range(HEADS):
            low = (head % 2) * HDIM
            vt[head, :HDIM, here] = values[head * HDIM : (head + 1) * HDIM]
            qpad[head, low : low + HDIM, here] = found[head * HDIM : (head + 1) * HDIM]
        return 0

    lax.fori_loop(0, chunks, project, 0)
    save = pltpu.make_async_copy(queries.at[:, pl.ds(0, seq_rows)], qt_hbm, io_sems.at[1])
    save.start()

    def attend(kr):
        tail = kr - TILE if kr % TILE == 0 else kr - kr % TILE
        row = lax.broadcasted_iota(jnp.int32, (kr - tail, TILE), 0) + tail
        mask = row < total

        def copies(tile, pair):
            return pltpu.make_async_copy(
                ebuf.at[pair, :, pl.ds(0, kr), :],
                e_hbm.at[tile, pl.ds(pair * 2, 2), pl.ds(0, kr), :],
                sems.at[pair],
            )

        turns = HEADS // BODY_HEADS

        def step(unit, _):
            tile, turn = unit // turns, unit % turns
            here = pl.ds(pl.multiple_of(tile * TILE, TILE), TILE)
            base = turn * BODY_HEADS

            def score(i):
                pair = turn * (BODY_HEADS // 2) + i // 2
                scores = nn(keys[pair, :kr, :], qpad[base + i, :, here])
                scores = jnp.concatenate(
                    [scores[:tail], jnp.where(mask, scores[tail:], -1e30)], 0
                )
                return scores, column_max(scores)

            live = {i: score(i) for i in range(AHEAD)}
            for i in range(BODY_HEADS):
                pair, sub = turn * (BODY_HEADS // 2) + i // 2, i % 2
                scores, top = live.pop(i)
                if sub == 0:
                    copies(tile, pair).wait()
                if i + AHEAD < BODY_HEADS:
                    live[i + AHEAD] = score(i + AHEAD)
                expo = jnp.exp2(scores - top).astype(BF16)
                ebuf[pair, sub, :kr, :] = expo
                mixed = nn(vt[base + i, :, :kr], expo)
                inverse = 1.0 / mixed[HDIM : HDIM + 1]
                spot = pl.ds(pl.multiple_of((base + i) * HDIM, HDIM), HDIM)
                mixed_t[spot, here] = (mixed[:HDIM] * inverse).astype(BF16)
                inv_ref[pl.ds(base + i, 1), here] = inverse
                if sub == 1:
                    copies(tile, pair).start()
            return 0

        for pair in range(PAIRS):
            copies(0, pair).start()
        lax.fori_loop(0, n_tiles * turns, step, 0)
        out = pltpu.make_async_copy(mixed_t, mixt_hbm, io_sems.at[2])
        out.start()
        for pair in range(PAIRS):
            copies(n_tiles - 1, pair).wait()
        save.wait()
        out.wait()

    for_size(seq_rows, total, attend)


def attention_forward(seq, lengths, x, w_qkv, wqt, wvt, vectors):
    seq_rows = x.shape[1]
    top = key_sizes(seq_rows)[-1]
    padded = cdiv(seq_rows + MEM, TILE) * TILE
    tiles = seq_rows // TILE
    vm = pl.BlockSpec(memory_space=pltpu.VMEM)
    hbm = pl.BlockSpec(memory_space=pl.ANY)
    return pl.pallas_call(
        partial(fwd_kernel, seq_rows, seq),
        out_shape=(
            jax.ShapeDtypeStruct((tiles, HEADS, top, TILE), BF16),
            jax.ShapeDtypeStruct((D, seq_rows), BF16),
            jax.ShapeDtypeStruct((D, seq_rows), BF16),
            jax.ShapeDtypeStruct((HEADS, seq_rows), F32),
        ),
        grid=(1,),
        in_specs=[
            pl.BlockSpec(memory_space=pltpu.SMEM),
            hbm,
            pl.BlockSpec((D, D), lambda i: (0, 1)),
            vm,
            vm,
            vm,
        ],
        out_specs=(hbm, hbm, hbm, vm),
        scratch_shapes=[
            pltpu.VMEM((padded, D), BF16),
            pltpu.VMEM((PAIRS, padded, 128), BF16),
            pltpu.VMEM((HEADS, VROWS, padded), BF16),
            pltpu.VMEM((HEADS, 128, padded), BF16),
            pltpu.VMEM((D, padded), BF16),
            pltpu.VMEM((D, seq_rows), BF16),
            pltpu.VMEM((PAIRS, 2, top, TILE), BF16),
            pltpu.SemaphoreType.DMA((PAIRS,)),
            pltpu.SemaphoreType.DMA((3,)),
        ],
        compiler_params=pltpu.CompilerParams(vmem_limit_bytes=VMEM_LIMIT),
        cost_estimate=pl.CostEstimate(
            flops=8 * 10**9, bytes_accessed=24 * 10**6, transcendentals=8 * 10**6
        ),
        name="attention_forward",
    )(lengths, x, w_qkv, wqt, wvt, vectors)


def norm_forward(values):
    center = values - jnp.mean(values, axis=-1, keepdims=True)
    inverse = lax.rsqrt(jnp.mean(center * center, axis=-1, keepdims=True) + 1e-05)
    return center * inverse, inverse


def norm_backward(grad, normed, inverse):
    return inverse * (
        grad
        - jnp.mean(grad, axis=-1, keepdims=True)
        - normed * jnp.mean(grad * normed, axis=-1, keepdims=True)
    )


def col_sum(values):
    return jnp.sum(values, axis=0, keepdims=True)


GELU_A = math.sqrt(2.0 / math.pi)
GELU_B = GELU_A * 0.044715
BLOCKS = FF // D


def piece_order(shards):
    bits = shards.bit_length() - 1
    return [int(format(i, "b").zfill(bits)[::-1], 2) if bits else 0 for i in range(shards)]


def piece_spots(pair, shards, rows):
    half = max(shards // 2, 1)
    for index, m in enumerate(piece_order(shards)):
        yield m, pair[index // half], index % half * rows


def ffn_kernel(
    seq_rows, shards, len_ref, me_ref, x_hbm, cot_hbm, mixt0, mixt1, inv0, inv1, *refs,
):
    wi_p, wb_p = refs[:shards], refs[shards : 2 * shards]
    vec_ref, out_hbm, gh_hbm, dot_hbm = refs[2 * shards : 2 * shards + 4]
    grads = refs[2 * shards + 4 : 2 * shards + 8]
    (
        sums_ref, x_ref, cot_ref, mixt_ref, inv_ref, wo_ref, wi_ref, wb_ref,
        out_ref, gh_ref, dot_ref, acc_o, acc_i, acc_b, slopes, actives,
        s_normed1, s_first, s_gsecond, ups, sems, out_sems,
    ) = refs[2 * shards + 8 :]
    half = TILE // 2
    len0, len1 = len_ref[0], len_ref[1]
    me = me_ref[0]
    n0, n1 = cdiv(len0, half), cdiv(len1, half)
    full = seq_rows // half
    n_all = n0 + n1

    def rows_at(piece, rows):
        return pl.ds(pl.multiple_of((me ^ piece) * rows, rows), rows)

    loads = []

    def load(src, dst):
        copy = pltpu.make_async_copy(src, dst, sems.at[len(loads)])
        loads.append(copy)
        copy.start()
        return copy

    first_loads = [load(mixt0, mixt_ref.at[0]), load(mixt1, mixt_ref.at[1])]
    first_loads += [load(inv0, inv_ref.at[0]), load(inv1, inv_ref.at[1])]
    part = D // shards
    first_loads += [
        load(p.at[:, pl.ds(0, D)], wo_ref.at[rows_at(i, part), :]) for i, p in enumerate(wi_p)
    ]
    first_loads += [load(x_hbm.at[s], x_ref.at[s]) for s in range(2)]
    second_loads = [
        load(p.at[:, pl.ds(D, FF)], wi_ref.at[rows_at(i, part), :]) for i, p in enumerate(wi_p)
    ]
    second_loads += [load(p, wb_ref.at[rows_at(i, FF // shards), :]) for i, p in enumerate(wb_p)]
    third_loads = [load(cot_hbm.at[s], cot_ref.at[s]) for s in range(2)]

    out_ref[...] = jnp.zeros(out_ref.shape, BF16)
    gh_ref[...] = jnp.zeros(gh_ref.shape, BF16)
    dot_ref[...] = jnp.zeros(dot_ref.shape, BF16)
    acc_o[...] = jnp.zeros(acc_o.shape, F32)
    acc_i[...] = jnp.zeros(acc_i.shape, F32)
    acc_b[...] = jnp.zeros(acc_b.shape, F32)
    sums_ref[...] = jnp.zeros(sums_ref.shape, F32)

    def vec(index):
        return vec_ref[index : index + 1, :].astype(F32)

    bias_out = vec(MEM + 2)
    bias_back = vec(MEM + 3 + BLOCKS)
    gain_one = vec(MEM + 4 + BLOCKS)
    shift_one = vec(MEM + 5 + BLOCKS)
    gain_two = vec(MEM + 6 + BLOCKS)
    shift_two = vec(MEM + 7 + BLOCKS)

    spare_one = jnp.logical_and(n_all % 2 == 1, n1 < full)
    spare_zero = jnp.logical_and(n_all % 2 == 1, n1 >= full)

    def place(chunk):
        second = chunk >= n0
        inside = jnp.where(second, chunk - n0, chunk)
        spare = chunk >= n_all
        seq = jnp.where(spare, jnp.where(n1 < full, 1, 0), jnp.where(second, 1, 0))
        inside = jnp.where(spare, jnp.where(n1 < full, n1, n0), inside)
        return seq, pl.multiple_of(inside * half, half), jnp.where(seq == 1, len1, len0)

    def rows_of(ref, spots):
        return jnp.concatenate([ref[s, pl.ds(r, half), :] for s, r, _ in spots], 0)

    def lanes_of(ref, spots):
        return jnp.concatenate([ref[s, :, pl.ds(r, half)] for s, r, _ in spots], 1)

    def put_rows(ref, value, spots):
        for i, (s, r, _) in enumerate(spots):
            ref[s, pl.ds(r, half), :] = value[i * half : (i + 1) * half]

    def put_lanes(ref, value, spots):
        for i, (s, r, _) in enumerate(spots):
            ref[s, :, pl.ds(r, half)] = value[:, i * half : (i + 1) * half]

    def valid_of(spots):
        iota = lax.broadcasted_iota(jnp.int32, (half, 1), 0)
        return jnp.concatenate(
            [jnp.where(iota + r < count, 1.0, 0.0) for _, r, count in spots], 0
        )

    def add_sum(row, value):
        sums_ref[row : row + 1] += col_sum(value)

    def whole_tile(spots):
        count = half * len(spots)
        here = slice(0, count)
        valid = valid_of(spots)
        mixt = lanes_of(mixt_ref, spots)
        attn = nn(mixt.T, wo_ref[...]) + bias_out
        normed_one, inverse_one = norm_forward(rows_of(x_ref, spots).astype(F32) + attn)
        first = normed_one * gain_one + shift_one
        s_normed1[here] = normed_one
        low = first.astype(BF16)
        s_first[here] = low
        second = first + bias_back
        for j in range(BLOCKS):
            cols = slice(j * D, (j + 1) * D)
            up = nn(low, wi_ref[:, cols]) + vec(MEM + 3 + j)
            square = up * up
            gate = 0.5 + 0.5 * jnp.tanh(up * (GELU_A + GELU_B * square))
            active = up * gate
            slopes[here, cols] = (
                gate + active * (2.0 - 2.0 * gate) * (GELU_A + 3.0 * GELU_B * square)
            ).astype(slopes.dtype)
            actives[here, cols] = active.astype(BF16)
        second = second + nn(actives[here, :], wb_ref[...])
        normed_two, inverse_two = norm_forward(second)
        put_rows(out_ref, ((normed_two * gain_two + shift_two) * valid).astype(BF16), spots)
        grad_out = rows_of(cot_ref, spots).astype(F32) * valid
        add_sum(MEM + 6 + BLOCKS, grad_out * normed_two)
        add_sum(MEM + 7 + BLOCKS, grad_out)
        grad_second = norm_backward(grad_out * gain_two, normed_two, inverse_two)
        s_gsecond[here] = grad_second
        down = grad_second.astype(BF16)
        add_sum(MEM + 3 + BLOCKS, down.astype(F32))
        low_t = s_first[here, :].T
        for j in range(BLOCKS):
            cols = slice(j * D, (j + 1) * D)
            grad_up = (
                nt(down, wb_ref[cols, :]) * slopes[here, cols].astype(F32)
            ).astype(BF16)
            acc_b[cols, :] += tn(actives[here, cols], down)
            ups[here, cols] = grad_up
            add_sum(MEM + 3 + j, grad_up.astype(F32))
            acc_i[:, cols] += nn(low_t, grad_up)
        grad_first = s_gsecond[here] + nt(ups[here, :], wi_ref[...])
        normed_one = s_normed1[here]
        add_sum(MEM + 4 + BLOCKS, grad_first * normed_one)
        add_sum(MEM + 5 + BLOCKS, grad_first)
        grad_one = norm_backward(grad_first * gain_one, normed_one, inverse_one)
        low = grad_one.astype(BF16)
        put_rows(gh_ref, low, spots)
        add_sum(MEM + 2, low.astype(F32))
        acc_o[...] += nn(mixt, low)
        grad_mixed = nt(wo_ref[...], low)
        inverse = lanes_of(inv_ref, spots)
        scaled = [
            grad_mixed[h * HDIM : (h + 1) * HDIM] * inverse[h : h + 1] for h in range(HEADS)
        ]
        put_lanes(dot_ref, jnp.concatenate(scaled, 0).astype(BF16), spots)

    def send(ref, hbm, sem, seq, row, lanes=False):
        here = pl.ds(row, half)
        src = ref.at[seq, :, here] if lanes else ref.at[seq, here, :]
        dst = hbm.at[seq, :, here] if lanes else hbm.at[seq, here, :]
        pltpu.make_async_copy(src, dst, out_sems.at[sem]).start()

    def send_all(seq, row):
        send(out_ref, out_hbm, 0, seq, row)
        send(gh_ref, gh_hbm, 1, seq, row)
        send(dot_ref, dot_hbm, 2, seq, row, True)

    for copy in first_loads + second_loads + third_loads:
        copy.wait()

    def step(index, _):
        spots = [place(index * 4 + i) for i in range(4)]
        whole_tile(spots)
        for seq, row, _ in spots:
            send_all(seq, row)
        return 0

    left = lax.rem(n_all, 4)
    bigs = n_all // 4 + jnp.where(left == 3, 1, 0)
    lax.fori_loop(0, bigs, step, 0)

    @pl.when(jnp.logical_or(left == 1, left == 2))
    def _():
        spots = [place(bigs * 4 + i) for i in range(2)]
        whole_tile(spots)
        for seq, row, _ in spots:
            send_all(seq, row)

    def rest(seq):
        def one(chunk, _):
            send_all(seq, pl.multiple_of(chunk * half, half))
            return 0

        return one

    lax.fori_loop(n0 + jnp.where(spare_zero, 1, 0), full, rest(0), 0)
    lax.fori_loop(n1 + jnp.where(spare_one, 1, 0), full, rest(1), 0)

    part = D // shards
    deep = FF // shards
    block = part * (1 + BLOCKS)
    for m, piece, row in piece_spots(grads[:2], shards, block):
        at = pl.multiple_of((me ^ m) * part, part)
        piece[row : row + part, :] = acc_o[pl.ds(at, part), :].astype(BF16)
        for j in range(BLOCKS):
            row += part
            piece[row : row + part, :] = acc_i[
                pl.ds(at, part), j * D : (j + 1) * D
            ].astype(BF16)
    for m, piece, row in piece_spots(grads[2:], shards, deep):
        at = pl.multiple_of((me ^ m) * deep, deep)
        piece[row : row + deep, :] = acc_b[pl.ds(at, deep), :].astype(BF16)
    for ref, hbm, sem in ((out_ref, out_hbm, 0), (gh_ref, gh_hbm, 1), (dot_ref, dot_hbm, 2)):
        pltpu.make_async_copy(ref, hbm, out_sems.at[sem]).wait()


def feed_forward(lengths, me, x, cot, mixts, invs, w_up, w_back, vectors):
    count, seq_rows = x.shape[:2]
    shards = len(w_up)
    vm = pl.BlockSpec(memory_space=pltpu.VMEM)
    hbm = pl.BlockSpec(memory_space=pl.ANY)
    smem = pl.BlockSpec(memory_space=pltpu.SMEM)
    return pl.pallas_call(
        partial(ffn_kernel, seq_rows, shards),
        out_shape=(
            jax.ShapeDtypeStruct((count, seq_rows, D), BF16),
            jax.ShapeDtypeStruct((count, seq_rows, D), BF16),
            jax.ShapeDtypeStruct((count, D, seq_rows), BF16),
            *[
                jax.ShapeDtypeStruct((rows, D), BF16)
                for rows in (D * (1 + BLOCKS) // 2, FF // 2)
                for _ in range(2)
            ],
            jax.ShapeDtypeStruct((32, D), F32),
        ),
        in_specs=[smem, smem] + [hbm] * (6 + 2 * shards) + [vm],
        out_specs=(hbm, hbm, hbm) + (vm,) * 5,
        scratch_shapes=[
            pltpu.VMEM((count, seq_rows, D), BF16),
            pltpu.VMEM((count, seq_rows, D), BF16),
            pltpu.VMEM((count, D, seq_rows), BF16),
            pltpu.VMEM((count, HEADS, seq_rows), F32),
            pltpu.VMEM((D, D), BF16),
            pltpu.VMEM((D, FF), BF16),
            pltpu.VMEM((FF, D), BF16),
            pltpu.VMEM((count, seq_rows, D), BF16),
            pltpu.VMEM((count, seq_rows, D), BF16),
            pltpu.VMEM((count, D, seq_rows), BF16),
            pltpu.VMEM((D, D), F32),
            pltpu.VMEM((D, FF), F32),
            pltpu.VMEM((FF, D), F32),
            pltpu.VMEM((2 * TILE, FF), F32),
            pltpu.VMEM((2 * TILE, FF), BF16),
            pltpu.VMEM((2 * TILE, D), F32),
            pltpu.VMEM((2 * TILE, D), BF16),
            pltpu.VMEM((2 * TILE, D), F32),
            pltpu.VMEM((2 * TILE, FF), BF16),
            pltpu.SemaphoreType.DMA((8 + 3 * shards,)),
            pltpu.SemaphoreType.DMA((3,)),
        ],
        compiler_params=pltpu.CompilerParams(vmem_limit_bytes=VMEM_LIMIT),
        cost_estimate=pl.CostEstimate(
            flops=27 * 10**9, bytes_accessed=24 * 10**6, transcendentals=4 * 10**6
        ),
        name="feed_forward",
    )(lengths, me, x, cot, *mixts, *invs, *w_up, *w_back, vectors)


def bwd_kernel(seq_rows, groups, group, seq, shards, chained, closing, waits, *refs):
    gp = PAIRS // groups
    gcols = gp * 128
    width = 3 * gcols
    refs = list(refs)
    len_ref, me_ref, wk_ref, wv_ref, vec_ref = refs[:5]
    x_hbm, dot_hbm, qt_hbm, mixt_hbm, e_hbm = refs[5:10]
    refs = refs[10:]
    acc_in, extra_in = (refs.pop(0), refs.pop(0)) if chained else (None, None)
    other_rows = [refs.pop(0) for _ in range(closing)]
    refs = refs[waits:]
    proj_hbm = refs.pop(0)
    last = chained
    if last:
        pieces = [refs.pop(0), refs.pop(0)]
    else:
        acc_hbm = refs.pop(0)
    extra_ref = None if closing else refs.pop(0)
    token = refs.pop(0)
    token[...] = jnp.zeros(token.shape, F32)
    (
        rows, qts, mixts, dots, wkt, kt, values, qpad, dpad, dqt, dk, dv, ebuf, acc, proj,
        extra, table, sems, io_sems, out_sem, acc_sem,
    ) = refs
    base = group * gcols
    mine = pl.ds(base, gcols)
    length = len_ref[seq]
    total = length + MEM
    n_tiles = cdiv(length, TILE)
    chunks = cdiv(total, TILE)
    pairs = [
        (x_hbm.at[seq], rows.at[pl.ds(0, seq_rows), :]),
        (qt_hbm.at[mine, :], qts),
        (mixt_hbm.at[mine, :], mixts),
        (dot_hbm.at[seq, mine, :], dots),
    ]
    loads = [pltpu.make_async_copy(a, b, io_sems.at[i]) for i, (a, b) in enumerate(pairs)]

    def copies_of(kr):
        def copies(tile, slot):
            return pltpu.make_async_copy(
                e_hbm.at[tile, pl.ds(group * gp * 2, gp * 2), pl.ds(0, kr), :],
                ebuf.at[slot, :, pl.ds(0, kr), :],
                sems.at[slot],
            )

        return copies

    for copy in loads:
        copy.start()
    if chained:
        fetch = pltpu.make_async_copy(acc_in, acc, acc_sem)
        fetch.start()
    for_size(seq_rows, total, lambda kr: copies_of(kr)(0, 0).start())
    memory = memory_rows(vec_ref)
    bias_v = vec_ref[MEM + 1 : MEM + 2, base : base + gcols].astype(F32)
    wkt[...] = wk_ref[...].T
    if chained:
        extra[...] = extra_in[...]
        for other in other_rows:
            extra[...] += other[...]
    else:
        acc[...] = jnp.zeros(acc.shape, F32)
        extra[...] = jnp.zeros(extra.shape, F32)
    for head in range(gp * 2):
        spare = HDIM * (1 - head % 2)
        qpad[head, spare : spare + HDIM, :] = jnp.zeros((HDIM, TILE), BF16)
        dpad[head, spare : spare + HDIM, :] = jnp.zeros((HDIM, TILE), BF16)
    rows[seq_rows:, :] = jnp.zeros((rows.shape[0] - seq_rows, D), BF16)
    loads[0].wait()
    edge = pl.multiple_of(length // 128 * 128, 128)
    fix = pl.ds(edge, TILE)
    pick_memory(rows, memory, length)

    def project(chunk, _):
        here = pl.ds(pl.multiple_of(chunk * TILE, TILE), TILE)
        joined = rows[here, :]
        value_rows = (nn(joined, wv_ref[...]) + bias_v).astype(BF16)
        for pair in range(gp):
            values[pair, here, :] = value_rows[:, pair * 128 : pair * 128 + 128]
            dk[pair, here, :] = jnp.zeros((TILE, 128), F32)
            dv[pair, here, :] = jnp.zeros((TILE, 128), F32)
        kt[:, here] = nt(wkt[...], joined).astype(BF16)
        dqt[:, here] = jnp.zeros((gcols, TILE), BF16)
        return 0

    lax.fori_loop(0, chunks, project, 0)
    for copy in loads[1:]:
        copy.wait()

    def attend(kr):
        copies = copies_of(kr)

        def step(tile, _):
            slot = lax.rem(tile, 2)
            here = pl.ds(pl.multiple_of(tile * TILE, TILE), TILE)

            @pl.when(tile + 1 < n_tiles)
            def _():
                copies(tile + 1, 1 - slot).start()

            copies(tile, slot).wait()
            inners = []
            for head in range(gp * 2):
                low = (head % 2) * HDIM
                local = slice(head * HDIM, (head + 1) * HDIM)
                outer = dots[local, here]
                dpad[head, low : low + HDIM, :] = outer
                qpad[head, low : low + HDIM, :] = qts[local, here]
                inners.append(col_sum(outer.astype(F32) * mixts[local, here].astype(F32)))

            def outer_product(head):
                return nn(values[head // 2, :kr, :], dpad[head])

            live = {head: outer_product(head) for head in range(AHEAD)}
            grads = []
            for head in range(gp * 2):
                pair = head // 2
                product = live.pop(head)
                if head + AHEAD < gp * 2:
                    live[head + AHEAD] = outer_product(head + AHEAD)
                local = slice(head * HDIM, (head + 1) * HDIM)
                grad = (
                    ebuf[slot, head, :kr, :].astype(F32) * (product - inners[head])
                ).astype(BF16)
                grads.append(grad)
                dqt[local, here] = (nn(kt[local, :kr], grad) * SCALE).astype(BF16)
                if head % 2:
                    both = [ebuf[slot, h, :kr, :] for h in (head - 1, head)]
                    dv[pair, :kr, :] += nt(
                        jnp.concatenate(both, 1),
                        jnp.concatenate([dpad[head - 1], dpad[head]], 1),
                    )
                    dk[pair, :kr, :] += nt(
                        jnp.concatenate(grads[-2:], 1),
                        jnp.concatenate([qpad[head - 1], qpad[head]], 1),
                    )
            return 0

        lax.fori_loop(0, n_tiles, step, 0)

    for_size(seq_rows, total, attend)
    if chained:
        fetch.wait()

    def send(chunk):
        here = pl.ds(pl.multiple_of(chunk * TILE, TILE), TILE)
        return pltpu.make_async_copy(proj.at[here, :], proj_hbm.at[here, :], out_sem)

    def finish(chunk, sums):
        here = pl.ds(pl.multiple_of(chunk * TILE, TILE), TILE)
        parts = [dqt[:, here].T]
        parts += [(dk[pair, here, :] * LN2).astype(BF16) for pair in range(gp)]
        parts += [dv[pair, here, :].astype(BF16) for pair in range(gp)]
        grad = jnp.concatenate(parts, 1)
        proj[here, :] = grad
        send(chunk).start()
        acc[...] += tn(rows[here, :], grad)
        return sums + col_sum(grad.astype(F32))

    sums = lax.fori_loop(0, chunks, finish, jnp.zeros((1, width), F32))
    extra[MEM : MEM + 1, base : base + gcols] += sums[:, :gcols]
    extra[MEM + 1 : MEM + 2, base : base + gcols] += sums[:, 2 * gcols :]
    turned = (
        lax.broadcasted_iota(jnp.int32, (32, TILE), 1) + (edge - length)
        == lax.broadcasted_iota(jnp.int32, (32, TILE), 0)
    )
    turned = jnp.logical_and(turned, lax.broadcasted_iota(jnp.int32, (32, TILE), 0) < MEM)
    turned = jnp.where(turned, 1.0, 0.0).astype(BF16)
    found_k = jnp.concatenate([dk[pair, fix, :] * LN2 for pair in range(gp)], 1)
    found_v = jnp.concatenate([dv[pair, fix, :] for pair in range(gp)], 1)
    grad_memory = nt(nn(turned, found_k.astype(BF16)).astype(BF16), wk_ref[...])
    grad_memory += nt(nn(turned, found_v.astype(BF16)).astype(BF16), wv_ref[...])
    extra[...] += grad_memory

    if last:
        me = me_ref[0]
        part, few = D // shards, 32 // shards
        if closing:
            for s in range(shards):
                table[s, :few, :] = extra[s * few : (s + 1) * few]
        for m, piece, row in piece_spots(pieces, shards, part):
            spot = slice(row, row + part)
            at = pl.multiple_of((me ^ m) * part, part)
            piece[spot, :width] = acc[pl.ds(at, part), :].astype(BF16)
            if closing:
                mine_rows = table[me ^ m]
                lanes = [mine_rows[:, j : j + 128] for j in range(0, D, 128)]
                empty = part - mine_rows.shape[0] * len(lanes)
                if empty:
                    lanes.append(jnp.zeros((empty, 128), F32))
                piece[spot, width:] = jnp.concatenate(lanes, 0).astype(BF16)
    else:
        store = pltpu.make_async_copy(acc, acc_hbm, acc_sem)
        store.start()
        store.wait()
    if extra_ref is not None:
        extra_ref[...] = extra[...]

    def drain(chunk, _):
        send(chunk).wait()
        return 0

    lax.fori_loop(0, chunks, drain, 0)


def attention_backward(
    seq, group, groups, shards, lengths, me, w_qkv, vectors, x, dot, qt, mixt, expo,
    chain=(), others=(), after=(),
):
    seq_rows = x.shape[1]
    top = key_sizes(seq_rows)[-1]
    padded = cdiv(seq_rows + MEM, TILE) * TILE
    gp = PAIRS // groups
    gcols = gp * 128
    width = 3 * gcols
    vm = pl.BlockSpec(memory_space=pltpu.VMEM)
    hbm = pl.BlockSpec(memory_space=pl.ANY)
    smem = pl.BlockSpec(memory_space=pltpu.SMEM)
    out_shape = [jax.ShapeDtypeStruct((padded, width), BF16)]
    out_specs = [hbm]
    if chain:
        wide = width + (128 if others else 0)
        out_shape += [jax.ShapeDtypeStruct((D // 2, wide), BF16)] * 2
        out_specs += [vm] * 2
    else:
        out_shape += [jax.ShapeDtypeStruct((D, width), F32)]
        out_specs += [hbm]
    if not others:
        out_shape += [jax.ShapeDtypeStruct((32, D), F32)]
        out_specs += [vm]
    out_shape += [jax.ShapeDtypeStruct((8, 128), F32)]
    out_specs += [vm]
    return pl.pallas_call(
        partial(
            bwd_kernel, seq_rows, groups, group, seq, shards, bool(chain), len(others),
            len(after),
        ),
        out_shape=tuple(out_shape),
        grid=(1,),
        in_specs=[
            smem,
            smem,
            pl.BlockSpec((D, gcols), lambda i: (0, groups + group)),
            pl.BlockSpec((D, gcols), lambda i: (0, 2 * groups + group)),
            vm,
        ]
        + [hbm] * 5
        + ([hbm, vm] if chain else [])
        + [vm] * len(others)
        + [hbm] * len(after),
        out_specs=tuple(out_specs),
        scratch_shapes=[
            pltpu.VMEM((padded, D), BF16),
            pltpu.VMEM((gcols, seq_rows), BF16),
            pltpu.VMEM((gcols, seq_rows), BF16),
            pltpu.VMEM((gcols, seq_rows), BF16),
            pltpu.VMEM((gcols, D), BF16),
            pltpu.VMEM((gcols, padded), BF16),
            pltpu.VMEM((gp, padded, 128), BF16),
            pltpu.VMEM((gp * 2, 128, TILE), BF16),
            pltpu.VMEM((gp * 2, 128, TILE), BF16),
            pltpu.VMEM((gcols, padded), BF16),
            pltpu.VMEM((gp, padded, 128), F32),
            pltpu.VMEM((gp, padded, 128), F32),
            pltpu.VMEM((2, gp * 2, top, TILE), BF16),
            pltpu.VMEM((D, width), F32),
            pltpu.VMEM((padded, width), BF16),
            pltpu.VMEM((32, D), F32),
            pltpu.VMEM((shards, max(8, 32 // shards), D), F32),
            pltpu.SemaphoreType.DMA((2,)),
            pltpu.SemaphoreType.DMA((4,)),
            pltpu.SemaphoreType.DMA,
            pltpu.SemaphoreType.DMA,
        ],
        compiler_params=pltpu.CompilerParams(vmem_limit_bytes=VMEM_LIMIT),
        cost_estimate=pl.CostEstimate(
            flops=8 * 10**9, bytes_accessed=15 * 10**6, transcendentals=0
        ),
        name="attention_backward",
    )(lengths, me, w_qkv, w_qkv, vectors, x, dot, qt, mixt, expo, *chain, *others, *after)


def input_kernel(seq_rows, groups, seq, len_ref, w_ref, gh_hbm, *refs):
    projs = refs[:groups]
    gx_ref, token, gh, blocks, sems = refs[-5:]
    token[...] = jnp.zeros(token.shape, F32)
    gcols = D // groups
    length = len_ref[seq]
    chunks = cdiv(length, TILE)

    def fetch(chunk):
        here = pl.ds(pl.multiple_of(chunk * TILE, TILE), TILE)
        slot = lax.rem(chunk, 2)
        return [
            pltpu.make_async_copy(gh_hbm.at[seq, here, :], gh.at[slot], sems.at[slot, 0])
        ] + [
            pltpu.make_async_copy(p.at[here, :], blocks.at[slot, i], sems.at[slot, 1 + i])
            for i, p in enumerate(projs)
        ]

    for copy in fetch(0):
        copy.start()
    gx_ref[...] = jnp.zeros(gx_ref.shape, BF16)

    def step(chunk, _):
        start = pl.multiple_of(chunk * TILE, TILE)
        slot = lax.rem(chunk, 2)

        @pl.when(chunk + 1 < chunks)
        def _():
            for copy in fetch(chunk + 1):
                copy.start()

        for copy in fetch(chunk):
            copy.wait()
        joint = jnp.concatenate(
            [
                blocks[slot, g, :, kind * gcols : (kind + 1) * gcols]
                for kind in range(3)
                for g in range(groups)
            ],
            1,
        )
        grad = nt(joint, w_ref[...])
        row = lax.broadcasted_iota(jnp.int32, (TILE, 1), 0) + start
        gx_ref[0, pl.ds(start, TILE), :] = jnp.where(
            row < length, grad + gh[slot].astype(F32), 0.0
        ).astype(BF16)
        return 0

    lax.fori_loop(0, chunks, step, 0)


def input_gradient(seq, lengths, w_qkv, gh, projs, after=(), base=None):
    count, seq_rows = gh.shape[:2]
    groups = len(projs)
    hbm = pl.BlockSpec(memory_space=pl.ANY)
    base = () if base is None else (base,)
    return pl.pallas_call(
        partial(input_kernel, seq_rows, groups, seq),
        out_shape=(
            jax.ShapeDtypeStruct((count, seq_rows, D), BF16),
            jax.ShapeDtypeStruct((8, 128), F32),
        ),
        grid=(1,),
        in_specs=[
            pl.BlockSpec(memory_space=pltpu.SMEM),
            pl.BlockSpec(memory_space=pltpu.VMEM),
        ]
        + [hbm] * (1 + groups + len(after) + len(base)),
        out_specs=(
            pl.BlockSpec((1, seq_rows, D), lambda i: (seq, 0, 0)),
            pl.BlockSpec(memory_space=pltpu.VMEM),
        ),
        input_output_aliases={3 + groups + len(after): 0} if base else {},
        scratch_shapes=[
            pltpu.VMEM((2, TILE, D), BF16),
            pltpu.VMEM((2, groups, TILE, 3 * D // groups), BF16),
            pltpu.SemaphoreType.DMA((2, 1 + groups)),
        ],
        compiler_params=pltpu.CompilerParams(vmem_limit_bytes=VMEM_LIMIT),
        cost_estimate=pl.CostEstimate(
            flops=2 * 10**9, bytes_accessed=7 * 10**6, transcendentals=0
        ),
        name="input_gradient",
    )(lengths, w_qkv, gh, *projs, *after, *base)


GROUPS = 2


def powers(size):
    return [1 << i for i in range(size.bit_length() - 1)]


def exchange(value, axis, size, bit):
    return lax.ppermute(value, axis, [(i, i ^ bit) for i in range(size)])


def far_pieces(value, axis, size):
    pieces = {0: value}
    for bit in reversed(powers(size)[1:]):
        for mask in sorted(pieces):
            pieces[mask | bit] = exchange(pieces[mask], axis, size, bit)
    return pieces


def near_pieces(pieces, axis, size):
    pieces = dict(pieces)
    for mask in sorted(pieces):
        pieces[mask | 1] = exchange(pieces[mask], axis, size, 1)
    return [pieces[mask] for mask in range(size)]


def held_until(pieces, event):
    keys = list(pieces)
    return dict(zip(keys, lax.optimization_barrier((*[pieces[k] for k in keys], event))))


def combine_kernel(counts, modes, waits, place_ref, *refs):
    refs = list(refs)
    arrays = [[[refs.pop(0) for _ in range(c)] for c in group] for group in counts]
    refs = refs[waits:]
    total, token = refs.pop(), refs.pop(-1)
    token[...] = jnp.zeros(token.shape, F32)
    place = place_ref[0]
    for groups, (mode, stacked, cols) in zip(arrays, modes):
        rows = 0
        for group in groups:
            more, wide = group[0].shape
            value = group[0][...].astype(F32)
            for other in group[1:]:
                value = value + other[...].astype(F32)
            total[rows : rows + more, :wide] = value
            if wide < cols:
                total[rows : rows + more, wide:cols] = jnp.zeros((more, cols - wide), F32)
            rows += more
        if mode == "halves":
            refs.pop(0)[...] = total[: rows // 2, :cols].astype(BF16)
            refs.pop(0)[...] = total[rows // 2 : rows, :cols].astype(BF16)
        elif mode == "parts":
            one = rows // stacked
            part = one // GROUP
            for m in range(GROUP):
                target = refs.pop(0)
                at = pl.multiple_of((place ^ m) * part, part)
                for i in range(stacked):
                    target[i * part : (i + 1) * part, :] = total[
                        pl.ds(at + i * one, part), :cols
                    ].astype(BF16)
        else:
            refs.pop(0)[...] = total[:rows, :cols].astype(BF16)


def combine(place, items, after):
    vm = pl.BlockSpec(memory_space=pltpu.VMEM)
    shapes, flat, modes, most = [], [], [], 0
    for groups, mode, stacked in items:
        rows = sum(arrays[0].shape[0] for arrays in groups)
        cols = max(arrays[0].shape[1] for arrays in groups)
        flat += [a for arrays in groups for a in arrays]
        modes.append((mode, stacked, cols))
        most = max(most, rows)
        if mode == "halves":
            shapes += [(rows // 2, cols)] * 2
        elif mode == "parts":
            shapes += [(rows // GROUP, cols)] * GROUP
        else:
            shapes += [(rows, cols)]
    size = sum(a.size for a in flat) * 2
    outs = pl.pallas_call(
        partial(combine_kernel, [[len(g) for g in i[0]] for i in items], modes, len(after)),
        out_shape=tuple(jax.ShapeDtypeStruct(s, BF16) for s in shapes)
        + (jax.ShapeDtypeStruct((8, 128), F32),),
        in_specs=[pl.BlockSpec(memory_space=pltpu.SMEM)]
        + [vm] * len(flat)
        + [pl.BlockSpec(memory_space=pl.ANY)] * len(after),
        out_specs=(vm,) * (len(shapes) + 1),
        scratch_shapes=[pltpu.VMEM((most, max(m[2] for m in modes)), F32)],
        compiler_params=pltpu.CompilerParams(vmem_limit_bytes=24 * 2**20),
        cost_estimate=pl.CostEstimate(flops=size, bytes_accessed=2 * size, transcendentals=0),
        name="combine",
    )(place, *flat, *after)
    outs, token, results = list(outs[:-1]), outs[-1], []
    for mode, _, _ in modes:
        taken = {"halves": 2, "parts": GROUP, "whole": 1}[mode]
        results.append([outs.pop(0) for _ in range(taken)])
    return results, token


GROUP = 4


class Stream:
    def __init__(self, value, sizes, steps, stacked=None):
        self.value, self.steps = list(value), list(steps)
        self.reps, self.shards = sizes
        self.stacked = stacked or max(self.shards // 2, 1)

    def exchange(self):
        kind, bit = self.steps.pop(0)
        value = self.value
        if kind == "fold":
            arrays = [value[0], exchange(value[1], "shard", self.shards, bit)]
        elif kind == "group":
            arrays = [value[0]] + [
                exchange(value[j], "rep", self.reps, j) for j in range(1, GROUP)
            ]
        else:
            arrays = [value[0], exchange(value[0], "rep", self.reps, bit)]
        follow = self.steps[0][0] if self.steps else "end"
        item = ([arrays], {"fold": "halves", "group": "parts"}.get(follow, "whole"), self.stacked)
        if follow == "fold":
            self.stacked //= 2
        return item

    def alone(self, place, after=()):
        (self.value,), token = combine(place, [self.exchange()], after)
        return [token]


def advance(place, streams, items, after):
    results, token = combine(place, items, after)
    for stream, result in zip(streams, results):
        stream.value = result
    return [token]


def whole_parts(stream):
    own = stream.value[0]
    return [own] + [exchange(own, "rep", stream.reps, j) for j in range(1, GROUP)]


def spread_kernel(shards, place_ref, *refs):
    refs = list(refs)
    arrays = [[refs.pop(0) for _ in range(GROUP)] for _ in range(3)]
    qkv_ref, out_ref, in_ref, back_ref, vec_ref, table = refs
    place = place_ref[0]

    def put(target, parts, cols, first=0, count=None):
        part = count or parts[0].shape[0]
        for m in range(GROUP):
            at = pl.multiple_of((place ^ m) * part, part)
            target[pl.ds(at, part), :cols] = parts[m][first : first + part, :].astype(F32)

    part = D // shards
    put(back_ref, arrays[1], D)
    put(table, arrays[0], D)
    out_ref[...] = table[:part, :D]
    for j in range(BLOCKS):
        in_ref[:, j * D : (j + 1) * D] = table[(1 + j) * part : (2 + j) * part, :D]
    gcols = D // GROUPS
    for g in range(GROUPS):
        put(table, arrays[2], 3 * gcols + 128, g * part // GROUP, part // GROUP)
        for kind in range(3):
            at = kind * D + g * gcols
            qkv_ref[:, at : at + gcols] = table[:part, kind * gcols : (kind + 1) * gcols]
    few = 32 // shards
    width = 3 * gcols
    step = max(8, few)
    for j in range(D // 128):
        vec_ref[:, j * 128 : (j + 1) * 128] = table[j * step : j * step + few, width : width + 128]


def spread(place, shards, parts):
    part = D // shards
    vm = pl.BlockSpec(memory_space=pltpu.VMEM)
    shapes = ((part, 3 * D), (part, D), (part, FF), (FF // shards, D), (32 // shards, D))
    most = max(part * (1 + BLOCKS), part), max(p.shape[1] for p in parts)
    return pl.pallas_call(
        partial(spread_kernel, shards),
        out_shape=tuple(jax.ShapeDtypeStruct(s, F32) for s in shapes),
        in_specs=[pl.BlockSpec(memory_space=pltpu.SMEM)] + [vm] * len(parts),
        out_specs=(vm,) * len(shapes),
        scratch_shapes=[pltpu.VMEM(most, F32)],
        compiler_params=pltpu.CompilerParams(vmem_limit_bytes=24 * 2**20),
        name="spread",
    )(place, *parts)


def body(sizes, inputs, lengths, w_qkv, w_out, w_in, w_back, vectors, cotangent):
    reps, shards = sizes
    count = inputs.shape[0]
    me = lax.axis_index("shard").astype(jnp.int32).reshape(1)

    axis = ("shard", shards)
    far = far_pieces(pack(w_qkv, vectors), *axis)
    start = held_until(
        {0: jnp.concatenate([w_out, w_in], 1), 1: w_back}, far[max(far)]
    )
    far_up, far_back = far_pieces(start[0], *axis), far_pieces(start[1], *axis)
    whole, wqt, wvt, table = prepare(me, near_pieces(far, *axis))
    fwd = [
        attention_forward(s, lengths, inputs, whole, wqt, wvt, table) for s in range(count)
    ]
    far_up, far_back = held_until(far_up, fwd[-1][3]), held_until(far_back, fwd[-1][3])
    out, gh, dot, *grads, sums = feed_forward(
        lengths, me, inputs, cotangent, [f[2] for f in fwd], [f[3] for f in fwd],
        near_pieces(far_up, *axis), near_pieces(far_back, *axis), table,
    )
    place = (lax.axis_index("rep") % GROUP).astype(jnp.int32).reshape(1)
    folds = [("fold", bit) for bit in powers(shards)]
    group = [("group", 0)]
    rest = [("full", bit) for bit in powers(reps) if bit >= GROUP]
    tall = Stream(grads[:2], sizes, folds + group + rest)
    deep = Stream(grads[2:], sizes, folds[:1] + group + folds[1:] + rest)
    projs = [[None] * GROUPS for _ in range(count)]
    quarters = [None] * GROUPS
    extras, after, calls = [], [], []
    for g in range(GROUPS):
        chain = ()
        for s in range(count):
            closing = [sums] + extras if s == count - 1 and g == GROUPS - 1 else ()
            busy = [
                (tall, deep), (tall, deep), (tall, quarters[0]), (deep, quarters[0], tall)
            ][len(calls)]
            items = [stream.exchange() for stream in busy]
            res = attention_backward(
                s, g, GROUPS, shards, lengths, me, whole, table, inputs, dot, fwd[s][1],
                fwd[s][2], fwd[s][0], chain, closing, after,
            )
            after = advance(place, busy, items, [res[-1]])
            projs[s][g] = res[0]
            calls.append(res)
            chain = res[1:-1]
        quarters[g] = Stream(chain[:2], sizes, folds + [("stop", 0)])
        extras += chain[2:]
    early, last = quarters
    last.value[1] = last.value[1] + after[0][0, 0].astype(BF16)
    for stream, left in ((early, 1), (tall, 0), (deep, 1)):
        while len(stream.steps) > left:
            stream.alone(place)
    tall_parts = whole_parts(tall)
    end = deep.exchange()
    after = []
    while len(last.steps) > 2:
        after = last.alone(place)
    gx, token = input_gradient(0, lengths, whole, gh, projs[0], after)
    final = last.exchange()[0]
    both = Stream([], sizes, group + rest, stacked=GROUPS)
    after = advance(
        place, [both, deep], [([early.value] + final, "parts", GROUPS), end], [token]
    )
    for seq in range(1, count):
        gx, token = input_gradient(seq, lengths, whole, gh, projs[seq], after, gx)
    both.alone(place, [token] + tall_parts[1:])
    deep_parts = whole_parts(deep)
    while both.steps:
        both.alone(place)
    return (out, gx, *spread(place, shards, tall_parts + deep_parts + whole_parts(both)))


def solution(mesh):
    data = P(("rep", "shard"), None, None)
    rows = P("shard", None)
    return jax.shard_map(
        partial(body, (mesh.shape["rep"], mesh.shape["shard"])),
        mesh=mesh,
        in_specs=(data, P(("rep", "shard")), rows, rows, rows, rows, rows, data),
        out_specs=(data, data, rows, rows, rows, rows, rows),
        check_vma=False,
    )
```

```python
import math
from functools import partial

import jax
import jax.numpy as jnp
from jax import lax
from jax.experimental import pallas as pl
from jax.experimental.pallas import tpu as pltpu
from jax.sharding import PartitionSpec as P

D = 512
HEADS = 8
HDIM = 64
FF = 2048
MEM = 20
TILE = 256
PAIRS = HEADS // 2
SCALE = HDIM**-0.5
QSCALE = SCALE * math.log2(math.e)
LN2 = math.log(2.0)
F32 = jnp.float32
BF16 = jnp.bfloat16
VROWS = 80
VMEM_LIMIT = 62 * 2**20


def nn(a, b):
    return lax.dot_general(a, b, (((1,), (0,)), ((), ())), preferred_element_type=F32)


def nt(a, b):
    return lax.dot_general(a, b, (((1,), (1,)), ((), ())), preferred_element_type=F32)


def tn(a, b):
    return lax.dot_general(a, b, (((0,), (0,)), ((), ())), preferred_element_type=F32)


def key_sizes(seq_rows):
    top = -(-(seq_rows + MEM) // 32) * 32
    return [rows for rows in range(512, top, 256)] + [top]


def column_max(values):
    parts = [values[i : i + 128] for i in range(0, values.shape[0] - 127, 128)]
    while len(parts) > 1:
        odd = parts[len(parts) - len(parts) % 2 :]
        parts = [jnp.maximum(a, b) for a, b in zip(parts[::2], parts[1::2])] + odd
    top = jnp.max(parts[0], axis=0, keepdims=True)
    rest = values.shape[0] % 128
    if rest:
        top = jnp.maximum(top, jnp.max(values[-rest:], axis=0, keepdims=True))
    return top


AHEAD = 2
BODY_HEADS = 4


def cdiv(a, b):
    return (a + b - 1) // b


def pick_memory(rows_ref, memory, length):
    edge = pl.multiple_of(length // 128 * 128, 128)
    fix = pl.ds(edge, TILE)
    row = lax.broadcasted_iota(jnp.int32, (TILE, 1), 0) + edge
    lane = lax.broadcasted_iota(jnp.int32, (TILE, 32), 1)
    pick = lax.broadcasted_iota(jnp.int32, (TILE, 32), 0) + (edge - length) == lane
    placed = nn(jnp.where(pick, 1.0, 0.0).astype(BF16), memory)
    rows_ref[fix, :] = jnp.where(row < length, rows_ref[fix, :].astype(F32), placed).astype(BF16)


def memory_rows(vec_ref):
    inside = lax.broadcasted_iota(jnp.int32, (32, D), 0) < MEM
    return jnp.where(inside, vec_ref[...].astype(F32), 0.0).astype(BF16)


def for_size(seq_rows, total, run):
    sizes = key_sizes(seq_rows)
    for index, kr in enumerate(sizes):
        least = sizes[index - 1] if index else 0

        @pl.when(jnp.logical_and(total > least, total <= kr))
        def _(kr=kr):
            run(kr)


def prepare_kernel(shards, me_ref, *refs):
    pieces = refs[:shards]
    w_ref, wqt_ref, wvt_ref, vec_ref, few_rows, sems = refs[shards:]
    me = me_ref[0]
    part, few = D // shards, 32 // shards
    copies, small = [], []
    for m in range(shards):
        at = pl.multiple_of((me ^ m) * part, part)
        small.append(
            pltpu.make_async_copy(
                pieces[m].at[pl.ds(part, SPARE), pl.ds(0, D)], few_rows.at[m], sems.at[m, 1]
            )
        )
        copies.append(
            pltpu.make_async_copy(
                pieces[m].at[pl.ds(0, part), :], w_ref.at[pl.ds(at, part), :], sems.at[m, 0]
            )
        )
    for copy in small + copies:
        copy.start()
    for copy in small:
        copy.wait()
    owner = lax.broadcasted_iota(jnp.int32, (32, D), 0) // few
    rows = jnp.zeros((32, D), F32)
    for m in range(shards):
        values = few_rows[m].astype(F32)[:few]
        rows = jnp.where(owner == (me ^ m), jnp.concatenate([values] * shards, 0), rows)
    vec_ref[...] = rows.astype(BF16)
    for copy in copies:
        copy.wait()
    wqt_ref[...] = w_ref[:, :D].T
    wvt_ref[...] = w_ref[:, 2 * D :].T


SPARE = 16


def pack(w_qkv, vectors):
    below = ((0, SPARE - vectors.shape[0]), (0, w_qkv.shape[1] - vectors.shape[1]))
    return jnp.concatenate([w_qkv, jnp.pad(vectors, below)], 0)


def prepare(me, pieces):
    shards = len(pieces)
    vm = pl.BlockSpec(memory_space=pltpu.VMEM)
    return pl.pallas_call(
        partial(prepare_kernel, shards),
        out_shape=(
            jax.ShapeDtypeStruct((D, 3 * D), BF16),
            jax.ShapeDtypeStruct((D, D), BF16),
            jax.ShapeDtypeStruct((D, D), BF16),
            jax.ShapeDtypeStruct((32, D), BF16),
        ),
        in_specs=[pl.BlockSpec(memory_space=pltpu.SMEM)]
        + [pl.BlockSpec(memory_space=pl.ANY)] * shards,
        out_specs=(vm, vm, vm, vm),
        scratch_shapes=[
            pltpu.VMEM((shards, SPARE, D), BF16),
            pltpu.SemaphoreType.DMA((shards, 2)),
        ],
        compiler_params=pltpu.CompilerParams(vmem_limit_bytes=24 * 2**20),
        name="prepare",
    )(me, *pieces)


def fwd_kernel(
    seq_rows, seq, len_ref, x_hbm, wk_ref, wqt_ref, wvt_ref, vec_ref,
    e_hbm, qt_hbm, mixt_hbm, inv_ref,
    rows, keys, vt, qpad, queries, mixed_t, ebuf, sems, io_sems,
):
    length = len_ref[seq]
    total = length + MEM
    load = pltpu.make_async_copy(x_hbm.at[seq], rows.at[pl.ds(0, seq_rows), :], io_sems.at[0])
    load.start()
    memory = memory_rows(vec_ref)
    vec_cols = vec_ref[...].astype(F32).T
    bias_q = vec_cols[:, MEM : MEM + 1]
    bias_v = vec_cols[:, MEM + 1 : MEM + 2]
    mixed_t[...] = jnp.zeros(mixed_t.shape, BF16)
    inv_ref[...] = jnp.zeros(inv_ref.shape, F32)
    for head in range(HEADS):
        spare = HDIM * (1 - head % 2)
        qpad[head, spare : spare + HDIM, :] = jnp.zeros((HDIM, qpad.shape[2]), BF16)
    vt[:, HDIM:, :] = jnp.ones((HEADS, VROWS - HDIM, vt.shape[2]), BF16)
    n_tiles = cdiv(length, TILE)
    chunks = cdiv(total, TILE)
    load.wait()

    rows[seq_rows:, :] = jnp.zeros((rows.shape[0] - seq_rows, D), BF16)
    pick_memory(rows, memory, length)

    def project(chunk, _):
        here = pl.ds(pl.multiple_of(chunk * TILE, TILE), TILE)
        joined = rows[here, :]
        key_rows = nn(joined, wk_ref[...]).astype(BF16)
        for pair in range(PAIRS):
            keys[pair, here, :] = key_rows[:, pair * 128 : pair * 128 + 128]
        values = (nt(wvt_ref[...], joined) + bias_v).astype(BF16)
        found = ((nt(wqt_ref[...], joined) + bias_q) * QSCALE).astype(BF16)
        queries[:, here] = found
        for head in range(HEADS):
            low = (head % 2) * HDIM
            vt[head, :HDIM, here] = values[head * HDIM : (head + 1) * HDIM]
            qpad[head, low : low + HDIM, here] = found[head * HDIM : (head + 1) * HDIM]
        return 0

    lax.fori_loop(0, chunks, project, 0)
    save = pltpu.make_async_copy(queries.at[:, pl.ds(0, seq_rows)], qt_hbm, io_sems.at[1])
    save.start()

    def attend(kr):
        tail = kr - TILE if kr % TILE == 0 else kr - kr % TILE
        row = lax.broadcasted_iota(jnp.int32, (kr - tail, TILE), 0) + tail
        mask = row < total

        def copies(tile, pair):
            return pltpu.make_async_copy(
                ebuf.at[pair, :, pl.ds(0, kr), :],
                e_hbm.at[tile, pl.ds(pair * 2, 2), pl.ds(0, kr), :],
                sems.at[pair],
            )

        turns = HEADS // BODY_HEADS

        def step(unit, _):
            tile, turn = unit // turns, unit % turns
            here = pl.ds(pl.multiple_of(tile * TILE, TILE), TILE)
            base = turn * BODY_HEADS

            def score(i):
                pair = turn * (BODY_HEADS // 2) + i // 2
                scores = nn(keys[pair, :kr, :], qpad[base + i, :, here])
                scores = jnp.concatenate(
                    [scores[:tail], jnp.where(mask, scores[tail:], -1e30)], 0
                )
                return scores, column_max(scores)

            live = {i: score(i) for i in range(AHEAD)}
            for i in range(BODY_HEADS):
                pair, sub = turn * (BODY_HEADS // 2) + i // 2, i % 2
                scores, top = live.pop(i)
                if sub == 0:
                    copies(tile, pair).wait()
                if i + AHEAD < BODY_HEADS:
                    live[i + AHEAD] = score(i + AHEAD)
                expo = jnp.exp2(scores - top).astype(BF16)
                ebuf[pair, sub, :kr, :] = expo
                mixed = nn(vt[base + i, :, :kr], expo)
                inverse = 1.0 / mixed[HDIM : HDIM + 1]
                spot = pl.ds(pl.multiple_of((base + i) * HDIM, HDIM), HDIM)
                mixed_t[spot, here] = (mixed[:HDIM] * inverse).astype(BF16)
                inv_ref[pl.ds(base + i, 1), here] = inverse
                if sub == 1:
                    copies(tile, pair).start()
            return 0

        for pair in range(PAIRS):
            copies(0, pair).start()
        lax.fori_loop(0, n_tiles * turns, step, 0)
        out = pltpu.make_async_copy(mixed_t, mixt_hbm, io_sems.at[2])
        out.start()
        for pair in range(PAIRS):
            copies(n_tiles - 1, pair).wait()
        save.wait()
        out.wait()

    for_size(seq_rows, total, attend)


def attention_forward(seq, lengths, x, w_qkv, wqt, wvt, vectors):
    seq_rows = x.shape[1]
    top = key_sizes(seq_rows)[-1]
    padded = cdiv(seq_rows + MEM, TILE) * TILE
    tiles = seq_rows // TILE
    vm = pl.BlockSpec(memory_space=pltpu.VMEM)
    hbm = pl.BlockSpec(memory_space=pl.ANY)
    return pl.pallas_call(
        partial(fwd_kernel, seq_rows, seq),
        out_shape=(
            jax.ShapeDtypeStruct((tiles, HEADS, top, TILE), BF16),
            jax.ShapeDtypeStruct((D, seq_rows), BF16),
            jax.ShapeDtypeStruct((D, seq_rows), BF16),
            jax.ShapeDtypeStruct((HEADS, seq_rows), F32),
        ),
        grid=(1,),
        in_specs=[
            pl.BlockSpec(memory_space=pltpu.SMEM),
            hbm,
            pl.BlockSpec((D, D), lambda i: (0, 1)),
            vm,
            vm,
            vm,
        ],
        out_specs=(hbm, hbm, hbm, vm),
        scratch_shapes=[
            pltpu.VMEM((padded, D), BF16),
            pltpu.VMEM((PAIRS, padded, 128), BF16),
            pltpu.VMEM((HEADS, VROWS, padded), BF16),
            pltpu.VMEM((HEADS, 128, padded), BF16),
            pltpu.VMEM((D, padded), BF16),
            pltpu.VMEM((D, seq_rows), BF16),
            pltpu.VMEM((PAIRS, 2, top, TILE), BF16),
            pltpu.SemaphoreType.DMA((PAIRS,)),
            pltpu.SemaphoreType.DMA((3,)),
        ],
        compiler_params=pltpu.CompilerParams(vmem_limit_bytes=VMEM_LIMIT),
        cost_estimate=pl.CostEstimate(
            flops=8 * 10**9, bytes_accessed=24 * 10**6, transcendentals=8 * 10**6
        ),
        name="attention_forward",
    )(lengths, x, w_qkv, wqt, wvt, vectors)


def norm_forward(values):
    center = values - jnp.mean(values, axis=-1, keepdims=True)
    inverse = lax.rsqrt(jnp.mean(center * center, axis=-1, keepdims=True) + 1e-05)
    return center * inverse, inverse


def norm_backward(grad, normed, inverse):
    return inverse * (
        grad
        - jnp.mean(grad, axis=-1, keepdims=True)
        - normed * jnp.mean(grad * normed, axis=-1, keepdims=True)
    )


def col_sum(values):
    return jnp.sum(values, axis=0, keepdims=True)


GELU_A = math.sqrt(2.0 / math.pi)
GELU_B = GELU_A * 0.044715
BLOCKS = FF // D


def piece_order(shards):
    bits = shards.bit_length() - 1
    return [int(format(i, "b").zfill(bits)[::-1], 2) if bits else 0 for i in range(shards)]


def piece_spots(pair, shards, rows):
    half = max(shards // 2, 1)
    for index, m in enumerate(piece_order(shards)):
        yield m, pair[index // half], index % half * rows


def ffn_kernel(
    seq_rows, shards, len_ref, me_ref, x_hbm, cot_hbm, mixt0, mixt1, inv0, inv1, *refs,
):
    wi_p, wb_p = refs[:shards], refs[shards : 2 * shards]
    vec_ref, out_hbm, gh_hbm, dot_hbm = refs[2 * shards : 2 * shards + 4]
    grads = refs[2 * shards + 4 : 2 * shards + 8]
    (
        sums_ref, x_ref, cot_ref, mixt_ref, inv_ref, wo_ref, wi_ref, wb_ref,
        out_ref, gh_ref, dot_ref, acc_o, acc_i, acc_b, slopes, actives,
        s_normed1, s_first, s_gsecond, ups, sems, out_sems,
    ) = refs[2 * shards + 8 :]
    half = TILE // 2
    len0, len1 = len_ref[0], len_ref[1]
    me = me_ref[0]
    n0, n1 = cdiv(len0, half), cdiv(len1, half)
    full = seq_rows // half
    n_all = n0 + n1

    def rows_at(piece, rows):
        return pl.ds(pl.multiple_of((me ^ piece) * rows, rows), rows)

    loads = []

    def load(src, dst):
        copy = pltpu.make_async_copy(src, dst, sems.at[len(loads)])
        loads.append(copy)
        copy.start()
        return copy

    first_loads = [load(mixt0, mixt_ref.at[0]), load(mixt1, mixt_ref.at[1])]
    first_loads += [load(inv0, inv_ref.at[0]), load(inv1, inv_ref.at[1])]
    part = D // shards
    first_loads += [
        load(p.at[:, pl.ds(0, D)], wo_ref.at[rows_at(i, part), :]) for i, p in enumerate(wi_p)
    ]
    first_loads += [load(x_hbm.at[s], x_ref.at[s]) for s in range(2)]
    second_loads = [
        load(p.at[:, pl.ds(D, FF)], wi_ref.at[rows_at(i, part), :]) for i, p in enumerate(wi_p)
    ]
    second_loads += [load(p, wb_ref.at[rows_at(i, FF // shards), :]) for i, p in enumerate(wb_p)]
    third_loads = [load(cot_hbm.at[s], cot_ref.at[s]) for s in range(2)]

    out_ref[...] = jnp.zeros(out_ref.shape, BF16)
    gh_ref[...] = jnp.zeros(gh_ref.shape, BF16)
    dot_ref[...] = jnp.zeros(dot_ref.shape, BF16)
    acc_o[...] = jnp.zeros(acc_o.shape, F32)
    acc_i[...] = jnp.zeros(acc_i.shape, F32)
    acc_b[...] = jnp.zeros(acc_b.shape, F32)
    sums_ref[...] = jnp.zeros(sums_ref.shape, F32)

    def vec(index):
        return vec_ref[index : index + 1, :].astype(F32)

    bias_out = vec(MEM + 2)
    bias_back = vec(MEM + 3 + BLOCKS)
    gain_one = vec(MEM + 4 + BLOCKS)
    shift_one = vec(MEM + 5 + BLOCKS)
    gain_two = vec(MEM + 6 + BLOCKS)
    shift_two = vec(MEM + 7 + BLOCKS)

    spare_one = jnp.logical_and(n_all % 2 == 1, n1 < full)
    spare_zero = jnp.logical_and(n_all % 2 == 1, n1 >= full)

    def place(chunk):
        second = chunk >= n0
        inside = jnp.where(second, chunk - n0, chunk)
        spare = chunk >= n_all
        seq = jnp.where(spare, jnp.where(n1 < full, 1, 0), jnp.where(second, 1, 0))
        inside = jnp.where(spare, jnp.where(n1 < full, n1, n0), inside)
        return seq, pl.multiple_of(inside * half, half), jnp.where(seq == 1, len1, len0)

    def rows_of(ref, spots):
        return jnp.concatenate([ref[s, pl.ds(r, half), :] for s, r, _ in spots], 0)

    def lanes_of(ref, spots):
        return jnp.concatenate([ref[s, :, pl.ds(r, half)] for s, r, _ in spots], 1)

    def put_rows(ref, value, spots):
        for i, (s, r, _) in enumerate(spots):
            ref[s, pl.ds(r, half), :] = value[i * half : (i + 1) * half]

    def put_lanes(ref, value, spots):
        for i, (s, r, _) in enumerate(spots):
            ref[s, :, pl.ds(r, half)] = value[:, i * half : (i + 1) * half]

    def valid_of(spots):
        iota = lax.broadcasted_iota(jnp.int32, (half, 1), 0)
        return jnp.concatenate(
            [jnp.where(iota + r < count, 1.0, 0.0) for _, r, count in spots], 0
        )

    def add_sum(row, value):
        sums_ref[row : row + 1] += col_sum(value)

    def whole_tile(spots):
        count = half * len(spots)
        here = slice(0, count)
        valid = valid_of(spots)
        mixt = lanes_of(mixt_ref, spots)
        attn = nn(mixt.T, wo_ref[...]) + bias_out
        normed_one, inverse_one = norm_forward(rows_of(x_ref, spots).astype(F32) + attn)
        first = normed_one * gain_one + shift_one
        s_normed1[here] = normed_one
        low = first.astype(BF16)
        s_first[here] = low
        second = first + bias_back
        for j in range(BLOCKS):
            cols = slice(j * D, (j + 1) * D)
            up = nn(low, wi_ref[:, cols]) + vec(MEM + 3 + j)
            square = up * up
            gate = 0.5 + 0.5 * jnp.tanh(up * (GELU_A + GELU_B * square))
            active = up * gate
            slopes[here, cols] = (
                gate + active * (2.0 - 2.0 * gate) * (GELU_A + 3.0 * GELU_B * square)
            ).astype(slopes.dtype)
            actives[here, cols] = active.astype(BF16)
        second = second + nn(actives[here, :], wb_ref[...])
        normed_two, inverse_two = norm_forward(second)
        put_rows(out_ref, ((normed_two * gain_two + shift_two) * valid).astype(BF16), spots)
        grad_out = rows_of(cot_ref, spots).astype(F32) * valid
        add_sum(MEM + 6 + BLOCKS, grad_out * normed_two)
        add_sum(MEM + 7 + BLOCKS, grad_out)
        grad_second = norm_backward(grad_out * gain_two, normed_two, inverse_two)
        s_gsecond[here] = grad_second
        down = grad_second.astype(BF16)
        add_sum(MEM + 3 + BLOCKS, down.astype(F32))
        low_t = s_first[here, :].T
        for j in range(BLOCKS):
            cols = slice(j * D, (j + 1) * D)
            grad_up = (
                nt(down, wb_ref[cols, :]) * slopes[here, cols].astype(F32)
            ).astype(BF16)
            acc_b[cols, :] += tn(actives[here, cols], down)
            ups[here, cols] = grad_up
            add_sum(MEM + 3 + j, grad_up.astype(F32))
            acc_i[:, cols] += nn(low_t, grad_up)
        grad_first = s_gsecond[here] + nt(ups[here, :], wi_ref[...])
        normed_one = s_normed1[here]
        add_sum(MEM + 4 + BLOCKS, grad_first * normed_one)
        add_sum(MEM + 5 + BLOCKS, grad_first)
        grad_one = norm_backward(grad_first * gain_one, normed_one, inverse_one)
        low = grad_one.astype(BF16)
        put_rows(gh_ref, low, spots)
        add_sum(MEM + 2, low.astype(F32))
        acc_o[...] += nn(mixt, low)
        grad_mixed = nt(wo_ref[...], low)
        inverse = lanes_of(inv_ref, spots)
        scaled = [
            grad_mixed[h * HDIM : (h + 1) * HDIM] * inverse[h : h + 1] for h in range(HEADS)
        ]
        put_lanes(dot_ref, jnp.concatenate(scaled, 0).astype(BF16), spots)

    def send(ref, hbm, sem, seq, row, lanes=False):
        here = pl.ds(row, half)
        src = ref.at[seq, :, here] if lanes else ref.at[seq, here, :]
        dst = hbm.at[seq, :, here] if lanes else hbm.at[seq, here, :]
        pltpu.make_async_copy(src, dst, out_sems.at[sem]).start()

    def send_all(seq, row):
        send(out_ref, out_hbm, 0, seq, row)
        send(gh_ref, gh_hbm, 1, seq, row)
        send(dot_ref, dot_hbm, 2, seq, row, True)

    for copy in first_loads + second_loads + third_loads:
        copy.wait()

    def step(index, _):
        spots = [place(index * 4 + i) for i in range(4)]
        whole_tile(spots)
        for seq, row, _ in spots:
            send_all(seq, row)
        return 0

    left = lax.rem(n_all, 4)
    bigs = n_all // 4 + jnp.where(left == 3, 1, 0)
    lax.fori_loop(0, bigs, step, 0)

    @pl.when(jnp.logical_or(left == 1, left == 2))
    def _():
        spots = [place(bigs * 4 + i) for i in range(2)]
        whole_tile(spots)
        for seq, row, _ in spots:
            send_all(seq, row)

    def rest(seq):
        def one(chunk, _):
            send_all(seq, pl.multiple_of(chunk * half, half))
            return 0

        return one

    lax.fori_loop(n0 + jnp.where(spare_zero, 1, 0), full, rest(0), 0)
    lax.fori_loop(n1 + jnp.where(spare_one, 1, 0), full, rest(1), 0)

    part = D // shards
    deep = FF // shards
    block = part * (1 + BLOCKS)
    for m, piece, row in piece_spots(grads[:2], shards, block):
        at = pl.multiple_of((me ^ m) * part, part)
        piece[row : row + part, :] = acc_o[pl.ds(at, part), :].astype(BF16)
        for j in range(BLOCKS):
            row += part
            piece[row : row + part, :] = acc_i[
                pl.ds(at, part), j * D : (j + 1) * D
            ].astype(BF16)
    for m, piece, row in piece_spots(grads[2:], shards, deep):
        at = pl.multiple_of((me ^ m) * deep, deep)
        piece[row : row + deep, :] = acc_b[pl.ds(at, deep), :].astype(BF16)
    for ref, hbm, sem in ((out_ref, out_hbm, 0), (gh_ref, gh_hbm, 1), (dot_ref, dot_hbm, 2)):
        pltpu.make_async_copy(ref, hbm, out_sems.at[sem]).wait()


def feed_forward(lengths, me, x, cot, mixts, invs, w_up, w_back, vectors):
    count, seq_rows = x.shape[:2]
    shards = len(w_up)
    vm = pl.BlockSpec(memory_space=pltpu.VMEM)
    hbm = pl.BlockSpec(memory_space=pl.ANY)
    smem = pl.BlockSpec(memory_space=pltpu.SMEM)
    return pl.pallas_call(
        partial(ffn_kernel, seq_rows, shards),
        out_shape=(
            jax.ShapeDtypeStruct((count, seq_rows, D), BF16),
            jax.ShapeDtypeStruct((count, seq_rows, D), BF16),
            jax.ShapeDtypeStruct((count, D, seq_rows), BF16),
            *[
                jax.ShapeDtypeStruct((rows, D), BF16)
                for rows in (D * (1 + BLOCKS) // 2, FF // 2)
                for _ in range(2)
            ],
            jax.ShapeDtypeStruct((32, D), F32),
        ),
        in_specs=[smem, smem] + [hbm] * (6 + 2 * shards) + [vm],
        out_specs=(hbm, hbm, hbm) + (vm,) * 5,
        scratch_shapes=[
            pltpu.VMEM((count, seq_rows, D), BF16),
            pltpu.VMEM((count, seq_rows, D), BF16),
            pltpu.VMEM((count, D, seq_rows), BF16),
            pltpu.VMEM((count, HEADS, seq_rows), F32),
            pltpu.VMEM((D, D), BF16),
            pltpu.VMEM((D, FF), BF16),
            pltpu.VMEM((FF, D), BF16),
            pltpu.VMEM((count, seq_rows, D), BF16),
            pltpu.VMEM((count, seq_rows, D), BF16),
            pltpu.VMEM((count, D, seq_rows), BF16),
            pltpu.VMEM((D, D), F32),
            pltpu.VMEM((D, FF), F32),
            pltpu.VMEM((FF, D), F32),
            pltpu.VMEM((2 * TILE, FF), F32),
            pltpu.VMEM((2 * TILE, FF), BF16),
            pltpu.VMEM((2 * TILE, D), F32),
            pltpu.VMEM((2 * TILE, D), BF16),
            pltpu.VMEM((2 * TILE, D), F32),
            pltpu.VMEM((2 * TILE, FF), BF16),
            pltpu.SemaphoreType.DMA((8 + 3 * shards,)),
            pltpu.SemaphoreType.DMA((3,)),
        ],
        compiler_params=pltpu.CompilerParams(vmem_limit_bytes=VMEM_LIMIT),
        cost_estimate=pl.CostEstimate(
            flops=27 * 10**9, bytes_accessed=24 * 10**6, transcendentals=4 * 10**6
        ),
        name="feed_forward",
    )(lengths, me, x, cot, *mixts, *invs, *w_up, *w_back, vectors)


def bwd_kernel(seq_rows, groups, group, seq, shards, chained, closing, waits, *refs):
    gp = PAIRS // groups
    gcols = gp * 128
    width = 3 * gcols
    refs = list(refs)
    len_ref, me_ref, wk_ref, wv_ref, vec_ref = refs[:5]
    x_hbm, dot_hbm, qt_hbm, mixt_hbm, e_hbm = refs[5:10]
    refs = refs[10:]
    acc_in, extra_in = (refs.pop(0), refs.pop(0)) if chained else (None, None)
    other_rows = [refs.pop(0) for _ in range(closing)]
    refs = refs[waits:]
    proj_hbm = refs.pop(0)
    last = chained
    if last:
        pieces = [refs.pop(0), refs.pop(0)]
    else:
        acc_hbm = refs.pop(0)
    extra_ref = None if closing else refs.pop(0)
    token = refs.pop(0)
    token[...] = jnp.zeros(token.shape, F32)
    (
        rows, qts, mixts, dots, wkt, kt, values, qpad, dpad, dqt, dk, dv, ebuf, acc, proj,
        extra, table, sems, io_sems, out_sem, acc_sem,
    ) = refs
    base = group * gcols
    mine = pl.ds(base, gcols)
    length = len_ref[seq]
    total = length + MEM
    n_tiles = cdiv(length, TILE)
    chunks = cdiv(total, TILE)
    pairs = [
        (x_hbm.at[seq], rows.at[pl.ds(0, seq_rows), :]),
        (qt_hbm.at[mine, :], qts),
        (mixt_hbm.at[mine, :], mixts),
        (dot_hbm.at[seq, mine, :], dots),
    ]
    loads = [pltpu.make_async_copy(a, b, io_sems.at[i]) for i, (a, b) in enumerate(pairs)]

    def copies_of(kr):
        def copies(tile, slot):
            return pltpu.make_async_copy(
                e_hbm.at[tile, pl.ds(group * gp * 2, gp * 2), pl.ds(0, kr), :],
                ebuf.at[slot, :, pl.ds(0, kr), :],
                sems.at[slot],
            )

        return copies

    for copy in loads:
        copy.start()
    if chained:
        fetch = pltpu.make_async_copy(acc_in, acc, acc_sem)
        fetch.start()
    for_size(seq_rows, total, lambda kr: copies_of(kr)(0, 0).start())
    memory = memory_rows(vec_ref)
    bias_v = vec_ref[MEM + 1 : MEM + 2, base : base + gcols].astype(F32)
    wkt[...] = wk_ref[...].T
    if chained:
        extra[...] = extra_in[...]
        for other in other_rows:
            extra[...] += other[...]
    else:
        acc[...] = jnp.zeros(acc.shape, F32)
        extra[...] = jnp.zeros(extra.shape, F32)
    for head in range(gp * 2):
        spare = HDIM * (1 - head % 2)
        qpad[head, spare : spare + HDIM, :] = jnp.zeros((HDIM, TILE), BF16)
        dpad[head, spare : spare + HDIM, :] = jnp.zeros((HDIM, TILE), BF16)
    rows[seq_rows:, :] = jnp.zeros((rows.shape[0] - seq_rows, D), BF16)
    loads[0].wait()
    edge = pl.multiple_of(length // 128 * 128, 128)
    fix = pl.ds(edge, TILE)
    pick_memory(rows, memory, length)

    def project(chunk, _):
        here = pl.ds(pl.multiple_of(chunk * TILE, TILE), TILE)
        joined = rows[here, :]
        value_rows = (nn(joined, wv_ref[...]) + bias_v).astype(BF16)
        for pair in range(gp):
            values[pair, here, :] = value_rows[:, pair * 128 : pair * 128 + 128]
            dk[pair, here, :] = jnp.zeros((TILE, 128), F32)
            dv[pair, here, :] = jnp.zeros((TILE, 128), F32)
        kt[:, here] = nt(wkt[...], joined).astype(BF16)
        dqt[:, here] = jnp.zeros((gcols, TILE), BF16)
        return 0

    lax.fori_loop(0, chunks, project, 0)
    for copy in loads[1:]:
        copy.wait()

    def attend(kr):
        copies = copies_of(kr)

        def step(tile, _):
            slot = lax.rem(tile, 2)
            here = pl.ds(pl.multiple_of(tile * TILE, TILE), TILE)

            @pl.when(tile + 1 < n_tiles)
            def _():
                copies(tile + 1, 1 - slot).start()

            copies(tile, slot).wait()
            inners = []
            for head in range(gp * 2):
                low = (head % 2) * HDIM
                local = slice(head * HDIM, (head + 1) * HDIM)
                outer = dots[local, here]
                dpad[head, low : low + HDIM, :] = outer
                qpad[head, low : low + HDIM, :] = qts[local, here]
                inners.append(col_sum(outer.astype(F32) * mixts[local, here].astype(F32)))

            def outer_product(head):
                return nn(values[head // 2, :kr, :], dpad[head])

            live = {head: outer_product(head) for head in range(AHEAD)}
            grads = []
            for head in range(gp * 2):
                pair = head // 2
                product = live.pop(head)
                if head + AHEAD < gp * 2:
                    live[head + AHEAD] = outer_product(head + AHEAD)
                local = slice(head * HDIM, (head + 1) * HDIM)
                grad = (
                    ebuf[slot, head, :kr, :].astype(F32) * (product - inners[head])
                ).astype(BF16)
                grads.append(grad)
                dqt[local, here] = (nn(kt[local, :kr], grad) * SCALE).astype(BF16)
                if head % 2:
                    both = [ebuf[slot, h, :kr, :] for h in (head - 1, head)]
                    dv[pair, :kr, :] += nt(
                        jnp.concatenate(both, 1),
                        jnp.concatenate([dpad[head - 1], dpad[head]], 1),
                    )
                    dk[pair, :kr, :] += nt(
                        jnp.concatenate(grads[-2:], 1),
                        jnp.concatenate([qpad[head - 1], qpad[head]], 1),
                    )
            return 0

        lax.fori_loop(0, n_tiles, step, 0)

    for_size(seq_rows, total, attend)
    if chained:
        fetch.wait()

    def send(chunk):
        here = pl.ds(pl.multiple_of(chunk * TILE, TILE), TILE)
        return pltpu.make_async_copy(proj.at[here, :], proj_hbm.at[here, :], out_sem)

    def finish(chunk, sums):
        here = pl.ds(pl.multiple_of(chunk * TILE, TILE), TILE)
        parts = [dqt[:, here].T]
        parts += [(dk[pair, here, :] * LN2).astype(BF16) for pair in range(gp)]
        parts += [dv[pair, here, :].astype(BF16) for pair in range(gp)]
        grad = jnp.concatenate(parts, 1)
        proj[here, :] = grad
        send(chunk).start()
        acc[...] += tn(rows[here, :], grad)
        return sums + col_sum(grad.astype(F32))

    sums = lax.fori_loop(0, chunks, finish, jnp.zeros((1, width), F32))
    if not last:
        store = pltpu.make_async_copy(acc, acc_hbm, acc_sem)
        store.start()
    extra[MEM : MEM + 1, base : base + gcols] += sums[:, :gcols]
    extra[MEM + 1 : MEM + 2, base : base + gcols] += sums[:, 2 * gcols :]
    turned = (
        lax.broadcasted_iota(jnp.int32, (32, TILE), 1) + (edge - length)
        == lax.broadcasted_iota(jnp.int32, (32, TILE), 0)
    )
    turned = jnp.logical_and(turned, lax.broadcasted_iota(jnp.int32, (32, TILE), 0) < MEM)
    turned = jnp.where(turned, 1.0, 0.0).astype(BF16)
    found_k = jnp.concatenate([dk[pair, fix, :] * LN2 for pair in range(gp)], 1)
    found_v = jnp.concatenate([dv[pair, fix, :] for pair in range(gp)], 1)
    grad_memory = nt(nn(turned, found_k.astype(BF16)).astype(BF16), wk_ref[...])
    grad_memory += nt(nn(turned, found_v.astype(BF16)).astype(BF16), wv_ref[...])
    extra[...] += grad_memory

    if last:
        me = me_ref[0]
        part, few = D // shards, 32 // shards
        if closing:
            for s in range(shards):
                table[s, :few, :] = extra[s * few : (s + 1) * few]
        for m, piece, row in piece_spots(pieces, shards, part):
            spot = slice(row, row + part)
            at = pl.multiple_of((me ^ m) * part, part)
            piece[spot, :width] = acc[pl.ds(at, part), :].astype(BF16)
            if closing:
                mine_rows = table[me ^ m]
                lanes = [mine_rows[:, j : j + 128] for j in range(0, D, 128)]
                empty = part - mine_rows.shape[0] * len(lanes)
                if empty:
                    lanes.append(jnp.zeros((empty, 128), F32))
                piece[spot, width:] = jnp.concatenate(lanes, 0).astype(BF16)
    else:
        store.wait()
    if extra_ref is not None:
        extra_ref[...] = extra[...]

    def drain(chunk, _):
        send(chunk).wait()
        return 0

    lax.fori_loop(0, chunks, drain, 0)


def attention_backward(
    seq, group, groups, shards, lengths, me, w_qkv, vectors, x, dot, qt, mixt, expo,
    chain=(), others=(), after=(),
):
    seq_rows = x.shape[1]
    top = key_sizes(seq_rows)[-1]
    padded = cdiv(seq_rows + MEM, TILE) * TILE
    gp = PAIRS // groups
    gcols = gp * 128
    width = 3 * gcols
    vm = pl.BlockSpec(memory_space=pltpu.VMEM)
    hbm = pl.BlockSpec(memory_space=pl.ANY)
    smem = pl.BlockSpec(memory_space=pltpu.SMEM)
    out_shape = [jax.ShapeDtypeStruct((padded, width), BF16)]
    out_specs = [hbm]
    if chain:
        wide = width + (128 if others else 0)
        out_shape += [jax.ShapeDtypeStruct((D // 2, wide), BF16)] * 2
        out_specs += [vm] * 2
    else:
        out_shape += [jax.ShapeDtypeStruct((D, width), F32)]
        out_specs += [hbm]
    if not others:
        out_shape += [jax.ShapeDtypeStruct((32, D), F32)]
        out_specs += [vm]
    out_shape += [jax.ShapeDtypeStruct((8, 128), F32)]
    out_specs += [vm]
    return pl.pallas_call(
        partial(
            bwd_kernel, seq_rows, groups, group, seq, shards, bool(chain), len(others),
            len(after),
        ),
        out_shape=tuple(out_shape),
        grid=(1,),
        in_specs=[
            smem,
            smem,
            pl.BlockSpec((D, gcols), lambda i: (0, groups + group)),
            pl.BlockSpec((D, gcols), lambda i: (0, 2 * groups + group)),
            vm,
        ]
        + [hbm] * 5
        + ([hbm, vm] if chain else [])
        + [vm] * len(others)
        + [hbm] * len(after),
        out_specs=tuple(out_specs),
        scratch_shapes=[
            pltpu.VMEM((padded, D), BF16),
            pltpu.VMEM((gcols, seq_rows), BF16),
            pltpu.VMEM((gcols, seq_rows), BF16),
            pltpu.VMEM((gcols, seq_rows), BF16),
            pltpu.VMEM((gcols, D), BF16),
            pltpu.VMEM((gcols, padded), BF16),
            pltpu.VMEM((gp, padded, 128), BF16),
            pltpu.VMEM((gp * 2, 128, TILE), BF16),
            pltpu.VMEM((gp * 2, 128, TILE), BF16),
            pltpu.VMEM((gcols, padded), BF16),
            pltpu.VMEM((gp, padded, 128), F32),
            pltpu.VMEM((gp, padded, 128), F32),
            pltpu.VMEM((2, gp * 2, top, TILE), BF16),
            pltpu.VMEM((D, width), F32),
            pltpu.VMEM((padded, width), BF16),
            pltpu.VMEM((32, D), F32),
            pltpu.VMEM((shards, max(8, 32 // shards), D), F32),
            pltpu.SemaphoreType.DMA((2,)),
            pltpu.SemaphoreType.DMA((4,)),
            pltpu.SemaphoreType.DMA,
            pltpu.SemaphoreType.DMA,
        ],
        compiler_params=pltpu.CompilerParams(vmem_limit_bytes=VMEM_LIMIT),
        cost_estimate=pl.CostEstimate(
            flops=8 * 10**9, bytes_accessed=15 * 10**6, transcendentals=0
        ),
        name="attention_backward",
    )(lengths, me, w_qkv, w_qkv, vectors, x, dot, qt, mixt, expo, *chain, *others, *after)


def input_kernel(seq_rows, groups, seq, len_ref, w_ref, gh_hbm, *refs):
    projs = refs[:groups]
    gx_hbm, token, gh, blocks, rows, sems, out_sem = refs[-7:]
    token[...] = jnp.zeros(token.shape, F32)
    gcols = D // groups
    length = len_ref[seq]
    chunks = cdiv(length, TILE)
    whole = seq_rows // TILE

    def spot(chunk):
        return pl.ds(pl.multiple_of(chunk * TILE, TILE), TILE)

    def fetch(chunk):
        here = spot(chunk)
        return [pltpu.make_async_copy(gh_hbm.at[seq, here, :], gh.at[here, :], sems.at[chunk, 0])] + [
            pltpu.make_async_copy(p.at[here, :], blocks.at[i, here, :], sems.at[chunk, 1 + i])
            for i, p in enumerate(projs)
        ]

    def send(chunk):
        here = spot(chunk)
        return pltpu.make_async_copy(rows.at[here, :], gx_hbm.at[seq, here, :], out_sem)

    def begin(chunk, _):
        for copy in fetch(chunk):
            copy.start()
        return 0

    lax.fori_loop(0, chunks, begin, 0)

    def empty(chunk, _):
        rows[spot(chunk), :] = jnp.zeros((TILE, D), BF16)
        send(chunk).start()
        return 0

    lax.fori_loop(chunks, whole, empty, 0)

    def step(chunk, _):
        here = spot(chunk)
        for copy in fetch(chunk):
            copy.wait()
        joint = jnp.concatenate(
            [
                blocks[g, here, kind * gcols : (kind + 1) * gcols]
                for kind in range(3)
                for g in range(groups)
            ],
            1,
        )
        grad = nt(joint, w_ref[...])
        row = lax.broadcasted_iota(jnp.int32, (TILE, 1), 0) + chunk * TILE
        rows[here, :] = jnp.where(row < length, grad + gh[here, :].astype(F32), 0.0).astype(BF16)
        send(chunk).start()
        return 0

    lax.fori_loop(0, chunks, step, 0)
    pltpu.make_async_copy(rows, gx_hbm.at[seq], out_sem).wait()


def input_gradient(seq, lengths, w_qkv, gh, projs, after=(), base=None):
    count, seq_rows = gh.shape[:2]
    groups = len(projs)
    hbm = pl.BlockSpec(memory_space=pl.ANY)
    vm = pl.BlockSpec(memory_space=pltpu.VMEM)
    base = () if base is None else (base,)
    return pl.pallas_call(
        partial(input_kernel, seq_rows, groups, seq),
        out_shape=(
            jax.ShapeDtypeStruct((count, seq_rows, D), BF16),
            jax.ShapeDtypeStruct((8, 128), F32),
        ),
        in_specs=[pl.BlockSpec(memory_space=pltpu.SMEM), vm]
        + [hbm] * (1 + groups + len(after) + len(base)),
        out_specs=(hbm, vm),
        input_output_aliases={3 + groups + len(after): 0} if base else {},
        scratch_shapes=[
            pltpu.VMEM((seq_rows, D), BF16),
            pltpu.VMEM((groups, seq_rows, 3 * D // groups), BF16),
            pltpu.VMEM((seq_rows, D), BF16),
            pltpu.SemaphoreType.DMA((seq_rows // TILE, 1 + groups)),
            pltpu.SemaphoreType.DMA,
        ],
        compiler_params=pltpu.CompilerParams(vmem_limit_bytes=VMEM_LIMIT),
        cost_estimate=pl.CostEstimate(
            flops=2 * 10**9, bytes_accessed=7 * 10**6, transcendentals=0
        ),
        name="input_gradient",
    )(lengths, w_qkv, gh, *projs, *after, *base)


GROUPS = 2


def powers(size):
    return [1 << i for i in range(size.bit_length() - 1)]


def exchange(value, axis, size, bit):
    return lax.ppermute(value, axis, [(i, i ^ bit) for i in range(size)])


def far_pieces(value, axis, size):
    pieces = {0: value}
    for bit in reversed(powers(size)[1:]):
        for mask in sorted(pieces):
            pieces[mask | bit] = exchange(pieces[mask], axis, size, bit)
    return pieces


def near_pieces(pieces, axis, size):
    pieces = dict(pieces)
    for mask in sorted(pieces):
        pieces[mask | 1] = exchange(pieces[mask], axis, size, 1)
    return [pieces[mask] for mask in range(size)]


def held_until(pieces, event):
    keys = list(pieces)
    return dict(zip(keys, lax.optimization_barrier((*[pieces[k] for k in keys], event))))


def combine_kernel(counts, modes, waits, carried, place_ref, *refs):
    refs = list(refs)
    arrays = [[[refs.pop(0) for _ in range(c)] for c in group] for group in counts]
    refs = refs[waits:]
    total = refs.pop()
    refs = refs[: len(refs) - carried]
    token = refs.pop()
    token[...] = jnp.zeros(token.shape, F32)
    place = place_ref[0]
    for groups, (mode, stacked, cols) in zip(arrays, modes):
        rows = sum(group[0].shape[0] for group in groups)
        if mode == "halves":
            half = rows // 2
            for side in range(2):
                add_rows(groups[0], side * half, half, refs.pop(0), 0, cols)
        elif mode == "parts":
            base = 0
            for group in groups:
                more = group[0].shape[0]
                add_rows(group, 0, more, total, base, cols)
                base += more
            one = rows // stacked
            part = one // GROUP
            for m in range(GROUP):
                target = refs.pop(0)
                at = pl.multiple_of((place ^ m) * part, part)
                for i in range(stacked):
                    target[i * part : (i + 1) * part, :] = total[
                        pl.ds(at + i * one, part), :cols
                    ].astype(BF16)
        else:
            add_rows(groups[0], 0, rows, refs.pop(0), 0, cols)


def add_rows(group, start, rows, target, base, cols):
    wide = group[0].shape[1]
    step = next((s for s in (64, 32, 16) if not (rows % s or start % s or base % s)), rows)

    def add(index, _):
        def at(first):
            if step == rows:
                return pl.ds(first, rows)
            return pl.ds(pl.multiple_of(first + index * step, step), step)

        value = group[0][at(start), :].astype(F32)
        for other in group[1:]:
            value = value + other[at(start), :].astype(F32)
        target[at(base), :wide] = value.astype(target.dtype)
        if wide < cols:
            target[at(base), wide:cols] = jnp.zeros((step, cols - wide), target.dtype)
        return 0

    lax.fori_loop(0, rows // step, add, 0)


def combine(place, items, after, carry=()):
    vm = pl.BlockSpec(memory_space=pltpu.VMEM)
    shapes, flat, modes, most = [], [], [], 0
    for groups, mode, stacked in items:
        rows = sum(arrays[0].shape[0] for arrays in groups)
        cols = max(arrays[0].shape[1] for arrays in groups)
        flat += [a for arrays in groups for a in arrays]
        modes.append((mode, stacked, cols))
        most = max(most, rows)
        if mode == "halves":
            shapes += [(rows // 2, cols)] * 2
        elif mode == "parts":
            shapes += [(rows // GROUP, cols)] * GROUP
        else:
            shapes += [(rows, cols)]
    size = sum(a.size for a in flat) * 2
    outs = pl.pallas_call(
        partial(
            combine_kernel,
            [[len(g) for g in i[0]] for i in items],
            modes,
            len(after) + len(carry),
            len(carry),
        ),
        out_shape=tuple(jax.ShapeDtypeStruct(s, BF16) for s in shapes)
        + (jax.ShapeDtypeStruct((8, 128), F32),)
        + tuple(jax.ShapeDtypeStruct(a.shape, a.dtype) for a in carry),
        in_specs=[pl.BlockSpec(memory_space=pltpu.SMEM)]
        + [vm] * len(flat)
        + [pl.BlockSpec(memory_space=pl.ANY)] * (len(after) + len(carry)),
        out_specs=(vm,) * (len(shapes) + 1)
        + (pl.BlockSpec(memory_space=pl.ANY),) * len(carry),
        input_output_aliases={
            1 + len(flat) + len(after) + i: len(shapes) + 1 + i for i in range(len(carry))
        },
        scratch_shapes=[pltpu.VMEM((most, max(m[2] for m in modes)), F32)],
        compiler_params=pltpu.CompilerParams(vmem_limit_bytes=24 * 2**20),
        cost_estimate=pl.CostEstimate(flops=size, bytes_accessed=2 * size, transcendentals=0),
        name="combine",
    )(place, *flat, *after, *carry)
    held = list(outs[len(shapes) + 1 :])
    outs, token, results = list(outs[: len(shapes)]), outs[len(shapes)], []
    for mode, _, _ in modes:
        taken = {"halves": 2, "parts": GROUP, "whole": 1}[mode]
        results.append([outs.pop(0) for _ in range(taken)])
    return results, [token, *held]


GROUP = 4


class Stream:
    def __init__(self, value, sizes, steps, stacked=None):
        self.value, self.steps = list(value), list(steps)
        self.reps, self.shards = sizes
        self.stacked = stacked or max(self.shards // 2, 1)

    def exchange(self):
        kind, bit = self.steps.pop(0)
        value = self.value
        if kind == "fold":
            arrays = [value[0], exchange(value[1], "shard", self.shards, bit)]
        elif kind == "group":
            arrays = [value[0]] + [
                exchange(value[j], "rep", self.reps, j) for j in range(1, GROUP)
            ]
        else:
            arrays = [value[0], exchange(value[0], "rep", self.reps, bit)]
        follow = self.steps[0][0] if self.steps else "end"
        item = ([arrays], {"fold": "halves", "group": "parts"}.get(follow, "whole"), self.stacked)
        if follow == "fold":
            self.stacked //= 2
        return item

    def alone(self, place, after=()):
        (self.value,), token = combine(place, [self.exchange()], after)
        return token


def advance(place, streams, items, after, carry=()):
    results, token = combine(place, items, after, carry)
    for stream, result in zip(streams, results):
        stream.value = result
    return token


def whole_parts(stream):
    own = stream.value[0]
    return [own] + [exchange(own, "rep", stream.reps, j) for j in range(1, GROUP)]


def spread_kernel(shards, place_ref, *refs):
    refs = list(refs)
    arrays = [[refs.pop(0) for _ in range(GROUP)] for _ in range(3)]
    qkv_ref, out_ref, in_ref, back_ref, vec_ref, table = refs
    place = place_ref[0]

    def put(target, parts, cols, first=0, count=None):
        part = count or parts[0].shape[0]
        for m in range(GROUP):
            at = pl.multiple_of((place ^ m) * part, part)
            target[pl.ds(at, part), :cols] = parts[m][first : first + part, :].astype(F32)

    part = D // shards
    put(back_ref, arrays[1], D)
    put(table, arrays[0], D)
    out_ref[...] = table[:part, :D]
    for j in range(BLOCKS):
        in_ref[:, j * D : (j + 1) * D] = table[(1 + j) * part : (2 + j) * part, :D]
    gcols = D // GROUPS
    for g in range(GROUPS):
        put(table, arrays[2], 3 * gcols + 128, g * part // GROUP, part // GROUP)
        for kind in range(3):
            at = kind * D + g * gcols
            qkv_ref[:, at : at + gcols] = table[:part, kind * gcols : (kind + 1) * gcols]
    few = 32 // shards
    width = 3 * gcols
    step = max(8, few)
    for j in range(D // 128):
        vec_ref[:, j * 128 : (j + 1) * 128] = table[j * step : j * step + few, width : width + 128]


def spread(place, shards, parts):
    part = D // shards
    vm = pl.BlockSpec(memory_space=pltpu.VMEM)
    shapes = ((part, 3 * D), (part, D), (part, FF), (FF // shards, D), (32 // shards, D))
    most = max(part * (1 + BLOCKS), part), max(p.shape[1] for p in parts)
    return pl.pallas_call(
        partial(spread_kernel, shards),
        out_shape=tuple(jax.ShapeDtypeStruct(s, F32) for s in shapes),
        in_specs=[pl.BlockSpec(memory_space=pltpu.SMEM)] + [vm] * len(parts),
        out_specs=(vm,) * len(shapes),
        scratch_shapes=[pltpu.VMEM(most, F32)],
        compiler_params=pltpu.CompilerParams(vmem_limit_bytes=24 * 2**20),
        name="spread",
    )(place, *parts)


def body(sizes, inputs, lengths, w_qkv, w_out, w_in, w_back, vectors, cotangent):
    reps, shards = sizes
    count = inputs.shape[0]
    me = lax.axis_index("shard").astype(jnp.int32).reshape(1)

    axis = ("shard", shards)
    far = far_pieces(pack(w_qkv, vectors), *axis)
    start = held_until(
        {0: jnp.concatenate([w_out, w_in], 1), 1: w_back}, far[max(far)]
    )
    far_up, far_back = far_pieces(start[0], *axis), far_pieces(start[1], *axis)
    whole, wqt, wvt, table = prepare(me, near_pieces(far, *axis))
    fwd = [
        attention_forward(s, lengths, inputs, whole, wqt, wvt, table) for s in range(count)
    ]
    far_up, far_back = held_until(far_up, fwd[-1][3]), held_until(far_back, fwd[-1][3])
    out, gh, dot, *grads, sums = feed_forward(
        lengths, me, inputs, cotangent, [f[2] for f in fwd], [f[3] for f in fwd],
        near_pieces(far_up, *axis), near_pieces(far_back, *axis), table,
    )
    place = (lax.axis_index("rep") % GROUP).astype(jnp.int32).reshape(1)
    folds = [("fold", bit) for bit in powers(shards)]
    group = [("group", 0)]
    rest = [("full", bit) for bit in powers(reps) if bit >= GROUP]
    tall = Stream(grads[:2], sizes, folds + group + rest)
    deep = Stream(grads[2:], sizes, folds[:1] + group + folds[1:] + rest)
    projs = [[None] * GROUPS for _ in range(count)]
    quarters = [None] * GROUPS
    extras, after, calls = [], [], []
    for g in range(GROUPS):
        chain = ()
        for s in range(count):
            closing = [sums] + extras if s == count - 1 and g == GROUPS - 1 else ()
            busy = [
                (tall, deep), (tall, deep), (tall, quarters[0]), (deep, quarters[0], tall)
            ][len(calls)]
            items = [stream.exchange() for stream in busy]
            res = attention_backward(
                s, g, GROUPS, shards, lengths, me, whole, table, inputs, dot, fwd[s][1],
                fwd[s][2], fwd[s][0], chain, closing, after,
            )
            chain = list(res[1:-1])
            carry = chain[1:2] if len(calls) == 3 else []
            after, *held = advance(place, busy, items, [res[-1]], carry)
            after = [after]
            chain[1 : 1 + len(held)] = held
            projs[s][g] = res[0]
            calls.append(res)
        quarters[g] = Stream(chain[:2], sizes, folds + [("stop", 0)])
        extras += chain[2:]
    early, last = quarters
    for stream, left in ((early, 1), (tall, 0), (deep, 1)):
        while len(stream.steps) > left:
            stream.alone(place)
    tall_parts = whole_parts(tall)
    end = deep.exchange()
    after = []
    while len(last.steps) > 2:
        after = last.alone(place)
    gx, token = input_gradient(0, lengths, whole, gh, projs[0], after)
    final = last.exchange()[0]
    both = Stream([], sizes, group + rest, stacked=GROUPS)
    after = advance(
        place, [both, deep], [([early.value] + final, "parts", GROUPS), end], [token]
    )
    for seq in range(1, count):
        gx, token = input_gradient(seq, lengths, whole, gh, projs[seq], after, gx)
    both.alone(place, [token] + tall_parts[1:])
    deep_parts = whole_parts(deep)
    while both.steps:
        both.alone(place)
    return (out, gx, *spread(place, shards, tall_parts + deep_parts + whole_parts(both)))


def solution(mesh):
    data = P(("rep", "shard"), None, None)
    rows = P("shard", None)
    return jax.shard_map(
        partial(body, (mesh.shape["rep"], mesh.shape["shard"])),
        mesh=mesh,
        in_specs=(data, P(("rep", "shard")), rows, rows, rows, rows, rows, data),
        out_specs=(data, data, rows, rows, rows, rows, rows),
        check_vma=False,
    )
```

```python
import math
from functools import partial

import jax
import jax.numpy as jnp
from jax import lax
from jax.experimental import pallas as pl
from jax.experimental.pallas import tpu as pltpu
from jax.sharding import PartitionSpec as P

D = 512
HEADS = 8
HDIM = 64
FF = 2048
MEM = 20
TILE = 256
PAIRS = HEADS // 2
SCALE = HDIM**-0.5
QSCALE = SCALE * math.log2(math.e)
LN2 = math.log(2.0)
F32 = jnp.float32
BF16 = jnp.bfloat16
VROWS = 80
VMEM_LIMIT = 62 * 2**20


def nn(a, b):
    return lax.dot_general(a, b, (((1,), (0,)), ((), ())), preferred_element_type=F32)


def nt(a, b):
    return lax.dot_general(a, b, (((1,), (1,)), ((), ())), preferred_element_type=F32)


def tn(a, b):
    return lax.dot_general(a, b, (((0,), (0,)), ((), ())), preferred_element_type=F32)


def key_sizes(seq_rows):
    top = -(-(seq_rows + MEM) // 32) * 32
    return [rows for rows in range(512, top, 256)] + [top]


def column_max(values):
    parts = [values[i : i + 128] for i in range(0, values.shape[0] - 127, 128)]
    while len(parts) > 1:
        odd = parts[len(parts) - len(parts) % 2 :]
        parts = [jnp.maximum(a, b) for a, b in zip(parts[::2], parts[1::2])] + odd
    top = jnp.max(parts[0], axis=0, keepdims=True)
    rest = values.shape[0] % 128
    if rest:
        top = jnp.maximum(top, jnp.max(values[-rest:], axis=0, keepdims=True))
    return top


AHEAD = 2
BODY_HEADS = 4


def cdiv(a, b):
    return (a + b - 1) // b


def pick_memory(rows_ref, memory, length):
    edge = pl.multiple_of(length // 128 * 128, 128)
    fix = pl.ds(edge, TILE)
    row = lax.broadcasted_iota(jnp.int32, (TILE, 1), 0) + edge
    lane = lax.broadcasted_iota(jnp.int32, (TILE, 32), 1)
    pick = lax.broadcasted_iota(jnp.int32, (TILE, 32), 0) + (edge - length) == lane
    placed = nn(jnp.where(pick, 1.0, 0.0).astype(BF16), memory)
    rows_ref[fix, :] = jnp.where(row < length, rows_ref[fix, :].astype(F32), placed).astype(BF16)


def memory_rows(vec_ref):
    inside = lax.broadcasted_iota(jnp.int32, (32, D), 0) < MEM
    return jnp.where(inside, vec_ref[...].astype(F32), 0.0).astype(BF16)


def for_size(seq_rows, total, run):
    sizes = key_sizes(seq_rows)
    for index, kr in enumerate(sizes):
        least = sizes[index - 1] if index else 0

        @pl.when(jnp.logical_and(total > least, total <= kr))
        def _(kr=kr):
            run(kr)


def prepare_kernel(shards, me_ref, *refs):
    pieces = refs[:shards]
    w_ref, wqt_ref, wvt_ref, vec_ref, few_rows, sems = refs[shards:]
    me = me_ref[0]
    part, few = D // shards, 32 // shards
    copies, small = [], []
    for m in range(shards):
        at = pl.multiple_of((me ^ m) * part, part)
        small.append(
            pltpu.make_async_copy(
                pieces[m].at[pl.ds(part, SPARE), pl.ds(0, D)], few_rows.at[m], sems.at[m, 1]
            )
        )
        copies.append(
            pltpu.make_async_copy(
                pieces[m].at[pl.ds(0, part), :], w_ref.at[pl.ds(at, part), :], sems.at[m, 0]
            )
        )
    for copy in small + copies:
        copy.start()
    for copy in small:
        copy.wait()
    owner = lax.broadcasted_iota(jnp.int32, (32, D), 0) // few
    rows = jnp.zeros((32, D), F32)
    for m in range(shards):
        values = few_rows[m].astype(F32)[:few]
        rows = jnp.where(owner == (me ^ m), jnp.concatenate([values] * shards, 0), rows)
    vec_ref[...] = rows.astype(BF16)
    for copy in copies:
        copy.wait()
    wqt_ref[...] = w_ref[:, :D].T
    wvt_ref[...] = w_ref[:, 2 * D :].T


SPARE = 16


def pack(w_qkv, vectors):
    below = ((0, SPARE - vectors.shape[0]), (0, w_qkv.shape[1] - vectors.shape[1]))
    return jnp.concatenate([w_qkv, jnp.pad(vectors, below)], 0)


def prepare(me, pieces):
    shards = len(pieces)
    vm = pl.BlockSpec(memory_space=pltpu.VMEM)
    return pl.pallas_call(
        partial(prepare_kernel, shards),
        out_shape=(
            jax.ShapeDtypeStruct((D, 3 * D), BF16),
            jax.ShapeDtypeStruct((D, D), BF16),
            jax.ShapeDtypeStruct((D, D), BF16),
            jax.ShapeDtypeStruct((32, D), BF16),
        ),
        in_specs=[pl.BlockSpec(memory_space=pltpu.SMEM)]
        + [pl.BlockSpec(memory_space=pl.ANY)] * shards,
        out_specs=(vm, vm, vm, vm),
        scratch_shapes=[
            pltpu.VMEM((shards, SPARE, D), BF16),
            pltpu.SemaphoreType.DMA((shards, 2)),
        ],
        compiler_params=pltpu.CompilerParams(vmem_limit_bytes=24 * 2**20),
        name="prepare",
    )(me, *pieces)


def fwd_kernel(
    seq_rows, seq, len_ref, x_hbm, wk_ref, wqt_ref, wvt_ref, vec_ref,
    e_hbm, qt_hbm, mixt_hbm, inv_ref,
    rows, keys, vt, qpad, queries, mixed_t, ebuf, sems, io_sems,
):
    length = len_ref[seq]
    total = length + MEM
    load = pltpu.make_async_copy(x_hbm.at[seq], rows.at[pl.ds(0, seq_rows), :], io_sems.at[0])
    load.start()
    memory = memory_rows(vec_ref)
    vec_cols = vec_ref[...].astype(F32).T
    bias_q = vec_cols[:, MEM : MEM + 1]
    bias_v = vec_cols[:, MEM + 1 : MEM + 2]
    mixed_t[...] = jnp.zeros(mixed_t.shape, BF16)
    inv_ref[...] = jnp.zeros(inv_ref.shape, F32)
    for head in range(HEADS):
        spare = HDIM * (1 - head % 2)
        qpad[head, spare : spare + HDIM, :] = jnp.zeros((HDIM, qpad.shape[2]), BF16)
    vt[:, HDIM:, :] = jnp.ones((HEADS, VROWS - HDIM, vt.shape[2]), BF16)
    n_tiles = cdiv(length, TILE)
    chunks = cdiv(total, TILE)
    load.wait()

    rows[seq_rows:, :] = jnp.zeros((rows.shape[0] - seq_rows, D), BF16)
    pick_memory(rows, memory, length)

    def project(chunk, _):
        here = pl.ds(pl.multiple_of(chunk * TILE, TILE), TILE)
        joined = rows[here, :]
        key_rows = nn(joined, wk_ref[...]).astype(BF16)
        for pair in range(PAIRS):
            keys[pair, here, :] = key_rows[:, pair * 128 : pair * 128 + 128]
        values = (nt(wvt_ref[...], joined) + bias_v).astype(BF16)
        found = ((nt(wqt_ref[...], joined) + bias_q) * QSCALE).astype(BF16)
        queries[:, here] = found
        for head in range(HEADS):
            low = (head % 2) * HDIM
            vt[head, :HDIM, here] = values[head * HDIM : (head + 1) * HDIM]
            qpad[head, low : low + HDIM, here] = found[head * HDIM : (head + 1) * HDIM]
        return 0

    lax.fori_loop(0, chunks, project, 0)
    save = pltpu.make_async_copy(queries.at[:, pl.ds(0, seq_rows)], qt_hbm, io_sems.at[1])
    save.start()

    def attend(kr):
        tail = kr - TILE if kr % TILE == 0 else kr - kr % TILE
        row = lax.broadcasted_iota(jnp.int32, (kr - tail, TILE), 0) + tail
        mask = row < total

        def copies(tile, pair):
            return pltpu.make_async_copy(
                ebuf.at[pair, :, pl.ds(0, kr), :],
                e_hbm.at[tile, pl.ds(pair * 2, 2), pl.ds(0, kr), :],
                sems.at[pair],
            )

        turns = HEADS // BODY_HEADS

        def step(unit, _):
            tile, turn = unit // turns, unit % turns
            here = pl.ds(pl.multiple_of(tile * TILE, TILE), TILE)
            base = turn * BODY_HEADS

            def score(i):
                pair = turn * (BODY_HEADS // 2) + i // 2
                scores = nn(keys[pair, :kr, :], qpad[base + i, :, here])
                scores = jnp.concatenate(
                    [scores[:tail], jnp.where(mask, scores[tail:], -1e30)], 0
                )
                return scores, column_max(scores)

            live = {i: score(i) for i in range(AHEAD)}
            for i in range(BODY_HEADS):
                pair, sub = turn * (BODY_HEADS // 2) + i // 2, i % 2
                scores, top = live.pop(i)
                if sub == 0:
                    copies(tile, pair).wait()
                if i + AHEAD < BODY_HEADS:
                    live[i + AHEAD] = score(i + AHEAD)
                expo = jnp.exp2(scores - top).astype(BF16)
                ebuf[pair, sub, :kr, :] = expo
                mixed = nn(vt[base + i, :, :kr], expo)
                inverse = 1.0 / mixed[HDIM : HDIM + 1]
                spot = pl.ds(pl.multiple_of((base + i) * HDIM, HDIM), HDIM)
                mixed_t[spot, here] = (mixed[:HDIM] * inverse).astype(BF16)
                inv_ref[pl.ds(base + i, 1), here] = inverse
                if sub == 1:
                    copies(tile, pair).start()
            return 0

        for pair in range(PAIRS):
            copies(0, pair).start()
        lax.fori_loop(0, n_tiles * turns, step, 0)
        out = pltpu.make_async_copy(mixed_t, mixt_hbm, io_sems.at[2])
        out.start()
        for pair in range(PAIRS):
            copies(n_tiles - 1, pair).wait()
        save.wait()
        out.wait()

    for_size(seq_rows, total, attend)


def attention_forward(seq, lengths, x, w_qkv, wqt, wvt, vectors):
    seq_rows = x.shape[1]
    top = key_sizes(seq_rows)[-1]
    padded = cdiv(seq_rows + MEM, TILE) * TILE
    tiles = seq_rows // TILE
    vm = pl.BlockSpec(memory_space=pltpu.VMEM)
    hbm = pl.BlockSpec(memory_space=pl.ANY)
    return pl.pallas_call(
        partial(fwd_kernel, seq_rows, seq),
        out_shape=(
            jax.ShapeDtypeStruct((tiles, HEADS, top, TILE), BF16),
            jax.ShapeDtypeStruct((D, seq_rows), BF16),
            jax.ShapeDtypeStruct((D, seq_rows), BF16),
            jax.ShapeDtypeStruct((HEADS, seq_rows), F32),
        ),
        grid=(1,),
        in_specs=[
            pl.BlockSpec(memory_space=pltpu.SMEM),
            hbm,
            pl.BlockSpec((D, D), lambda i: (0, 1)),
            vm,
            vm,
            vm,
        ],
        out_specs=(hbm, hbm, hbm, vm),
        scratch_shapes=[
            pltpu.VMEM((padded, D), BF16),
            pltpu.VMEM((PAIRS, padded, 128), BF16),
            pltpu.VMEM((HEADS, VROWS, padded), BF16),
            pltpu.VMEM((HEADS, 128, padded), BF16),
            pltpu.VMEM((D, padded), BF16),
            pltpu.VMEM((D, seq_rows), BF16),
            pltpu.VMEM((PAIRS, 2, top, TILE), BF16),
            pltpu.SemaphoreType.DMA((PAIRS,)),
            pltpu.SemaphoreType.DMA((3,)),
        ],
        compiler_params=pltpu.CompilerParams(vmem_limit_bytes=40 * 2**20),
        cost_estimate=pl.CostEstimate(
            flops=8 * 10**9, bytes_accessed=24 * 10**6, transcendentals=8 * 10**6
        ),
        name="attention_forward",
    )(lengths, x, w_qkv, wqt, wvt, vectors)


def norm_forward(values):
    center = values - jnp.mean(values, axis=-1, keepdims=True)
    inverse = lax.rsqrt(jnp.mean(center * center, axis=-1, keepdims=True) + 1e-05)
    return center * inverse, inverse


def norm_backward(grad, normed, inverse):
    return inverse * (
        grad
        - jnp.mean(grad, axis=-1, keepdims=True)
        - normed * jnp.mean(grad * normed, axis=-1, keepdims=True)
    )


def col_sum(values):
    return jnp.sum(values, axis=0, keepdims=True)


GELU_A = math.sqrt(2.0 / math.pi)
GELU_B = GELU_A * 0.044715
BLOCKS = FF // D


def piece_order(shards):
    bits = shards.bit_length() - 1
    return [int(format(i, "b").zfill(bits)[::-1], 2) if bits else 0 for i in range(shards)]


def piece_spots(pair, shards, rows):
    half = max(shards // 2, 1)
    for index, m in enumerate(piece_order(shards)):
        yield m, pair[index // half], index % half * rows


def ffn_kernel(
    seq_rows, shards, len_ref, me_ref, x_hbm, cot_hbm, mixt0, mixt1, inv0, inv1, *refs,
):
    wi_p, wb_p = refs[:shards], refs[shards : 2 * shards]
    vec_ref, out_hbm, gh_hbm, dot_hbm = refs[2 * shards : 2 * shards + 4]
    grads = refs[2 * shards + 4 : 2 * shards + 8]
    (
        sums_ref, x_ref, cot_ref, mixt_ref, inv_ref, wo_ref, wi_ref, wb_ref,
        out_ref, gh_ref, dot_ref, acc_o, acc_i, acc_b, slopes, actives,
        s_normed1, s_first, s_gsecond, ups, sems, out_sems,
    ) = refs[2 * shards + 8 :]
    half = TILE // 2
    len0, len1 = len_ref[0], len_ref[1]
    me = me_ref[0]
    n0, n1 = cdiv(len0, half), cdiv(len1, half)
    full = seq_rows // half
    n_all = n0 + n1

    def rows_at(piece, rows):
        return pl.ds(pl.multiple_of((me ^ piece) * rows, rows), rows)

    loads = []

    def load(src, dst):
        copy = pltpu.make_async_copy(src, dst, sems.at[len(loads)])
        loads.append(copy)
        copy.start()
        return copy

    first_loads = [load(mixt0, mixt_ref.at[0]), load(mixt1, mixt_ref.at[1])]
    first_loads += [load(inv0, inv_ref.at[0]), load(inv1, inv_ref.at[1])]
    part = D // shards
    first_loads += [
        load(p.at[:, pl.ds(0, D)], wo_ref.at[rows_at(i, part), :]) for i, p in enumerate(wi_p)
    ]
    first_loads += [load(x_hbm.at[s], x_ref.at[s]) for s in range(2)]
    second_loads = [
        load(p.at[:, pl.ds(D, FF)], wi_ref.at[rows_at(i, part), :]) for i, p in enumerate(wi_p)
    ]
    second_loads += [load(p, wb_ref.at[rows_at(i, FF // shards), :]) for i, p in enumerate(wb_p)]
    third_loads = [load(cot_hbm.at[s], cot_ref.at[s]) for s in range(2)]

    out_ref[...] = jnp.zeros(out_ref.shape, BF16)
    gh_ref[...] = jnp.zeros(gh_ref.shape, BF16)
    dot_ref[...] = jnp.zeros(dot_ref.shape, BF16)
    acc_o[...] = jnp.zeros(acc_o.shape, F32)
    acc_i[...] = jnp.zeros(acc_i.shape, F32)
    acc_b[...] = jnp.zeros(acc_b.shape, F32)
    sums_ref[...] = jnp.zeros(sums_ref.shape, F32)

    def vec(index):
        return vec_ref[index : index + 1, :].astype(F32)

    bias_out = vec(MEM + 2)
    bias_back = vec(MEM + 3 + BLOCKS)
    gain_one = vec(MEM + 4 + BLOCKS)
    shift_one = vec(MEM + 5 + BLOCKS)
    gain_two = vec(MEM + 6 + BLOCKS)
    shift_two = vec(MEM + 7 + BLOCKS)

    spare_one = jnp.logical_and(n_all % 2 == 1, n1 < full)
    spare_zero = jnp.logical_and(n_all % 2 == 1, n1 >= full)

    def place(chunk):
        second = chunk >= n0
        inside = jnp.where(second, chunk - n0, chunk)
        spare = chunk >= n_all
        seq = jnp.where(spare, jnp.where(n1 < full, 1, 0), jnp.where(second, 1, 0))
        inside = jnp.where(spare, jnp.where(n1 < full, n1, n0), inside)
        return seq, pl.multiple_of(inside * half, half), jnp.where(seq == 1, len1, len0)

    def rows_of(ref, spots):
        return jnp.concatenate([ref[s, pl.ds(r, half), :] for s, r, _ in spots], 0)

    def lanes_of(ref, spots):
        return jnp.concatenate([ref[s, :, pl.ds(r, half)] for s, r, _ in spots], 1)

    def put_rows(ref, value, spots):
        for i, (s, r, _) in enumerate(spots):
            ref[s, pl.ds(r, half), :] = value[i * half : (i + 1) * half]

    def put_lanes(ref, value, spots):
        for i, (s, r, _) in enumerate(spots):
            ref[s, :, pl.ds(r, half)] = value[:, i * half : (i + 1) * half]

    def valid_of(spots):
        iota = lax.broadcasted_iota(jnp.int32, (half, 1), 0)
        return jnp.concatenate(
            [jnp.where(iota + r < count, 1.0, 0.0) for _, r, count in spots], 0
        )

    def add_sum(row, value):
        sums_ref[row : row + 1] += col_sum(value)

    def whole_tile(spots):
        count = half * len(spots)
        here = slice(0, count)
        valid = valid_of(spots)
        mixt = lanes_of(mixt_ref, spots)
        attn = nn(mixt.T, wo_ref[...]) + bias_out
        normed_one, inverse_one = norm_forward(rows_of(x_ref, spots).astype(F32) + attn)
        first = normed_one * gain_one + shift_one
        s_normed1[here] = normed_one
        low = first.astype(BF16)
        s_first[here] = low
        second = first + bias_back
        for j in range(BLOCKS):
            cols = slice(j * D, (j + 1) * D)
            up = nn(low, wi_ref[:, cols]) + vec(MEM + 3 + j)
            square = up * up
            bent = jnp.tanh(up * (GELU_A + GELU_B * square))
            gate = 0.5 + 0.5 * bent
            active = up * gate
            slopes[here, cols] = (
                gate + active * (1.0 - bent) * (GELU_A + 3.0 * GELU_B * square)
            ).astype(slopes.dtype)
            actives[here, cols] = active.astype(BF16)
        second = second + nn(actives[here, :], wb_ref[...])
        normed_two, inverse_two = norm_forward(second)
        put_rows(out_ref, ((normed_two * gain_two + shift_two) * valid).astype(BF16), spots)
        grad_out = rows_of(cot_ref, spots).astype(F32) * valid
        add_sum(MEM + 6 + BLOCKS, grad_out * normed_two)
        add_sum(MEM + 7 + BLOCKS, grad_out)
        grad_second = norm_backward(grad_out * gain_two, normed_two, inverse_two)
        s_gsecond[here] = grad_second
        down = grad_second.astype(BF16)
        add_sum(MEM + 3 + BLOCKS, down.astype(F32))
        low_t = s_first[here, :].T
        for j in range(BLOCKS):
            cols = slice(j * D, (j + 1) * D)
            grad_up = (
                nt(down, wb_ref[cols, :]) * slopes[here, cols].astype(F32)
            ).astype(BF16)
            ups[here, cols] = grad_up
            add_sum(MEM + 3 + j, grad_up.astype(F32))
        grad_first = s_gsecond[here] + nt(ups[here, :], wi_ref[...])
        for j in range(BLOCKS):
            cols = slice(j * D, (j + 1) * D)
            acc_b[cols, :] += tn(actives[here, cols], down)
            acc_i[:, cols] += nn(low_t, ups[here, cols])
        normed_one = s_normed1[here]
        add_sum(MEM + 4 + BLOCKS, grad_first * normed_one)
        add_sum(MEM + 5 + BLOCKS, grad_first)
        grad_one = norm_backward(grad_first * gain_one, normed_one, inverse_one)
        low = grad_one.astype(BF16)
        put_rows(gh_ref, low, spots)
        add_sum(MEM + 2, low.astype(F32))
        acc_o[...] += nn(mixt, low)
        grad_mixed = nt(wo_ref[...], low)
        inverse = lanes_of(inv_ref, spots)
        scaled = [
            grad_mixed[h * HDIM : (h + 1) * HDIM] * inverse[h : h + 1] for h in range(HEADS)
        ]
        put_lanes(dot_ref, jnp.concatenate(scaled, 0).astype(BF16), spots)

    def send(ref, hbm, sem, seq, row, lanes=False):
        here = pl.ds(row, half)
        src = ref.at[seq, :, here] if lanes else ref.at[seq, here, :]
        dst = hbm.at[seq, :, here] if lanes else hbm.at[seq, here, :]
        pltpu.make_async_copy(src, dst, out_sems.at[sem]).start()

    def send_all(seq, row):
        send(out_ref, out_hbm, 0, seq, row)
        send(gh_ref, gh_hbm, 1, seq, row)
        send(dot_ref, dot_hbm, 2, seq, row, True)

    for copy in first_loads + second_loads + third_loads:
        copy.wait()

    def step(index, _):
        spots = [place(index * 4 + i) for i in range(4)]
        whole_tile(spots)
        for seq, row, _ in spots:
            send_all(seq, row)
        return 0

    left = lax.rem(n_all, 4)
    bigs = n_all // 4 + jnp.where(left == 3, 1, 0)
    lax.fori_loop(0, bigs, step, 0)

    @pl.when(jnp.logical_or(left == 1, left == 2))
    def _():
        spots = [place(bigs * 4 + i) for i in range(2)]
        whole_tile(spots)
        for seq, row, _ in spots:
            send_all(seq, row)

    def rest(seq):
        def one(chunk, _):
            send_all(seq, pl.multiple_of(chunk * half, half))
            return 0

        return one

    lax.fori_loop(n0 + jnp.where(spare_zero, 1, 0), full, rest(0), 0)
    lax.fori_loop(n1 + jnp.where(spare_one, 1, 0), full, rest(1), 0)

    part = D // shards
    deep = FF // shards
    block = part * (1 + BLOCKS)
    for m, piece, row in piece_spots(grads[:2], shards, block):
        at = pl.multiple_of((me ^ m) * part, part)
        piece[row : row + part, :] = acc_o[pl.ds(at, part), :].astype(BF16)
        for j in range(BLOCKS):
            row += part
            piece[row : row + part, :] = acc_i[
                pl.ds(at, part), j * D : (j + 1) * D
            ].astype(BF16)
    for m, piece, row in piece_spots(grads[2:], shards, deep):
        at = pl.multiple_of((me ^ m) * deep, deep)
        piece[row : row + deep, :] = acc_b[pl.ds(at, deep), :].astype(BF16)
    for ref, hbm, sem in ((out_ref, out_hbm, 0), (gh_ref, gh_hbm, 1), (dot_ref, dot_hbm, 2)):
        pltpu.make_async_copy(ref, hbm, out_sems.at[sem]).wait()


def feed_forward(lengths, me, x, cot, mixts, invs, w_up, w_back, vectors):
    count, seq_rows = x.shape[:2]
    shards = len(w_up)
    vm = pl.BlockSpec(memory_space=pltpu.VMEM)
    hbm = pl.BlockSpec(memory_space=pl.ANY)
    smem = pl.BlockSpec(memory_space=pltpu.SMEM)
    return pl.pallas_call(
        partial(ffn_kernel, seq_rows, shards),
        out_shape=(
            jax.ShapeDtypeStruct((count, seq_rows, D), BF16),
            jax.ShapeDtypeStruct((count, seq_rows, D), BF16),
            jax.ShapeDtypeStruct((count, D, seq_rows), BF16),
            *[
                jax.ShapeDtypeStruct((rows, D), BF16)
                for rows in (D * (1 + BLOCKS) // 2, FF // 2)
                for _ in range(2)
            ],
            jax.ShapeDtypeStruct((32, D), F32),
        ),
        in_specs=[smem, smem] + [hbm] * (6 + 2 * shards) + [vm],
        out_specs=(hbm, hbm, hbm) + (vm,) * 5,
        scratch_shapes=[
            pltpu.VMEM((count, seq_rows, D), BF16),
            pltpu.VMEM((count, seq_rows, D), BF16),
            pltpu.VMEM((count, D, seq_rows), BF16),
            pltpu.VMEM((count, HEADS, seq_rows), F32),
            pltpu.VMEM((D, D), BF16),
            pltpu.VMEM((D, FF), BF16),
            pltpu.VMEM((FF, D), BF16),
            pltpu.VMEM((count, seq_rows, D), BF16),
            pltpu.VMEM((count, seq_rows, D), BF16),
            pltpu.VMEM((count, D, seq_rows), BF16),
            pltpu.VMEM((D, D), F32),
            pltpu.VMEM((D, FF), F32),
            pltpu.VMEM((FF, D), F32),
            pltpu.VMEM((2 * TILE, FF), BF16),
            pltpu.VMEM((2 * TILE, FF), BF16),
            pltpu.VMEM((2 * TILE, D), F32),
            pltpu.VMEM((2 * TILE, D), BF16),
            pltpu.VMEM((2 * TILE, D), F32),
            pltpu.VMEM((2 * TILE, FF), BF16),
            pltpu.SemaphoreType.DMA((8 + 3 * shards,)),
            pltpu.SemaphoreType.DMA((3,)),
        ],
        compiler_params=pltpu.CompilerParams(vmem_limit_bytes=48 * 2**20),
        cost_estimate=pl.CostEstimate(
            flops=27 * 10**9, bytes_accessed=24 * 10**6, transcendentals=4 * 10**6
        ),
        name="feed_forward",
    )(lengths, me, x, cot, *mixts, *invs, *w_up, *w_back, vectors)


def bwd_kernel(seq_rows, groups, group, seq, shards, chained, closing, waits, *refs):
    gp = PAIRS // groups
    gcols = gp * 128
    width = 3 * gcols
    refs = list(refs)
    len_ref, me_ref, wk_ref, wv_ref, vec_ref = refs[:5]
    x_hbm, dot_hbm, qt_hbm, mixt_hbm, e_hbm = refs[5:10]
    refs = refs[10:]
    acc_in, extra_in = (refs.pop(0), refs.pop(0)) if chained else (None, None)
    other_rows = [refs.pop(0) for _ in range(closing)]
    refs = refs[waits:]
    proj_hbm = refs.pop(0)
    last = chained
    if last:
        pieces = [refs.pop(0), refs.pop(0)]
    else:
        acc_hbm = refs.pop(0)
    extra_ref = None if closing else refs.pop(0)
    token = refs.pop(0)
    token[...] = jnp.zeros(token.shape, F32)
    (
        rows, qts, mixts, dots, wkt, kt, values, qpad, dpad, dqt, dk, dv, ebuf, acc, proj,
        extra, table, sems, io_sems, out_sem, acc_sem,
    ) = refs
    base = group * gcols
    mine = pl.ds(base, gcols)
    length = len_ref[seq]
    total = length + MEM
    n_tiles = cdiv(length, TILE)
    chunks = cdiv(total, TILE)
    pairs = [
        (x_hbm.at[seq], rows.at[pl.ds(0, seq_rows), :]),
        (qt_hbm.at[mine, :], qts),
        (mixt_hbm.at[mine, :], mixts),
        (dot_hbm.at[seq, mine, :], dots),
    ]
    loads = [pltpu.make_async_copy(a, b, io_sems.at[i]) for i, (a, b) in enumerate(pairs)]

    def copies_of(kr):
        def copies(tile, slot):
            return pltpu.make_async_copy(
                e_hbm.at[tile, pl.ds(group * gp * 2, gp * 2), pl.ds(0, kr), :],
                ebuf.at[slot, :, pl.ds(0, kr), :],
                sems.at[slot],
            )

        return copies

    for copy in loads:
        copy.start()
    if chained:
        fetch = pltpu.make_async_copy(acc_in, acc, acc_sem)
        fetch.start()
    for_size(seq_rows, total, lambda kr: copies_of(kr)(0, 0).start())
    memory = memory_rows(vec_ref)
    bias_v = vec_ref[MEM + 1 : MEM + 2, base : base + gcols].astype(F32)
    wkt[...] = wk_ref[...].T
    if chained:
        extra[...] = extra_in[...]
        for other in other_rows:
            extra[...] += other[...]
    else:
        acc[...] = jnp.zeros(acc.shape, F32)
        extra[...] = jnp.zeros(extra.shape, F32)
    for head in range(gp * 2):
        spare = HDIM * (1 - head % 2)
        qpad[head, spare : spare + HDIM, :] = jnp.zeros((HDIM, TILE), BF16)
        dpad[head, spare : spare + HDIM, :] = jnp.zeros((HDIM, TILE), BF16)
    rows[seq_rows:, :] = jnp.zeros((rows.shape[0] - seq_rows, D), BF16)
    loads[0].wait()
    edge = pl.multiple_of(length // 128 * 128, 128)
    fix = pl.ds(edge, TILE)
    pick_memory(rows, memory, length)

    def project(chunk, _):
        here = pl.ds(pl.multiple_of(chunk * TILE, TILE), TILE)
        joined = rows[here, :]
        value_rows = (nn(joined, wv_ref[...]) + bias_v).astype(BF16)
        for pair in range(gp):
            values[pair, here, :] = value_rows[:, pair * 128 : pair * 128 + 128]
            dk[pair, here, :] = jnp.zeros((TILE, 128), F32)
            dv[pair, here, :] = jnp.zeros((TILE, 128), F32)
        kt[:, here] = nt(wkt[...], joined).astype(BF16)
        dqt[:, here] = jnp.zeros((gcols, TILE), BF16)
        return 0

    lax.fori_loop(0, chunks, project, 0)
    for copy in loads[1:]:
        copy.wait()

    def attend(kr):
        copies = copies_of(kr)

        def step(tile, _):
            slot = lax.rem(tile, 2)
            here = pl.ds(pl.multiple_of(tile * TILE, TILE), TILE)

            @pl.when(tile + 1 < n_tiles)
            def _():
                copies(tile + 1, 1 - slot).start()

            copies(tile, slot).wait()
            inners = []
            for head in range(gp * 2):
                low = (head % 2) * HDIM
                local = slice(head * HDIM, (head + 1) * HDIM)
                outer = dots[local, here]
                dpad[head, low : low + HDIM, :] = outer
                qpad[head, low : low + HDIM, :] = qts[local, here]
                inners.append(col_sum(outer.astype(F32) * mixts[local, here].astype(F32)))

            def outer_product(head):
                return nn(values[head // 2, :kr, :], dpad[head])

            live = {head: outer_product(head) for head in range(AHEAD)}
            grads = []
            for head in range(gp * 2):
                pair = head // 2
                product = live.pop(head)
                if head + AHEAD < gp * 2:
                    live[head + AHEAD] = outer_product(head + AHEAD)
                local = slice(head * HDIM, (head + 1) * HDIM)
                grad = (
                    ebuf[slot, head, :kr, :].astype(F32) * (product - inners[head])
                ).astype(BF16)
                grads.append(grad)
                dqt[local, here] = (nn(kt[local, :kr], grad) * SCALE).astype(BF16)
                if head % 2:
                    both = [ebuf[slot, h, :kr, :] for h in (head - 1, head)]
                    dv[pair, :kr, :] += nt(
                        jnp.concatenate(both, 1),
                        jnp.concatenate([dpad[head - 1], dpad[head]], 1),
                    )
                    dk[pair, :kr, :] += nt(
                        jnp.concatenate(grads[-2:], 1),
                        jnp.concatenate([qpad[head - 1], qpad[head]], 1),
                    )
            return 0

        lax.fori_loop(0, n_tiles, step, 0)

    for_size(seq_rows, total, attend)
    if chained:
        fetch.wait()

    def send(chunk):
        here = pl.ds(pl.multiple_of(chunk * TILE, TILE), TILE)
        return pltpu.make_async_copy(proj.at[here, :], proj_hbm.at[here, :], out_sem)

    def finish(chunk, sums):
        here = pl.ds(pl.multiple_of(chunk * TILE, TILE), TILE)
        parts = [dqt[:, here].T]
        parts += [(dk[pair, here, :] * LN2).astype(BF16) for pair in range(gp)]
        parts += [dv[pair, here, :].astype(BF16) for pair in range(gp)]
        grad = jnp.concatenate(parts, 1)
        proj[here, :] = grad
        send(chunk).start()
        acc[...] += tn(rows[here, :], grad)
        return sums + col_sum(grad.astype(F32))

    sums = lax.fori_loop(0, chunks, finish, jnp.zeros((1, width), F32))
    if not last:
        store = pltpu.make_async_copy(acc, acc_hbm, acc_sem)
        store.start()
    extra[MEM : MEM + 1, base : base + gcols] += sums[:, :gcols]
    extra[MEM + 1 : MEM + 2, base : base + gcols] += sums[:, 2 * gcols :]
    turned = (
        lax.broadcasted_iota(jnp.int32, (32, TILE), 1) + (edge - length)
        == lax.broadcasted_iota(jnp.int32, (32, TILE), 0)
    )
    turned = jnp.logical_and(turned, lax.broadcasted_iota(jnp.int32, (32, TILE), 0) < MEM)
    turned = jnp.where(turned, 1.0, 0.0).astype(BF16)
    found_k = jnp.concatenate([dk[pair, fix, :] * LN2 for pair in range(gp)], 1)
    found_v = jnp.concatenate([dv[pair, fix, :] for pair in range(gp)], 1)
    grad_memory = nt(nn(turned, found_k.astype(BF16)).astype(BF16), wk_ref[...])
    grad_memory += nt(nn(turned, found_v.astype(BF16)).astype(BF16), wv_ref[...])
    extra[...] += grad_memory

    if last:
        me = me_ref[0]
        part, few = D // shards, 32 // shards
        if closing:
            for s in range(shards):
                table[s, :few, :] = extra[s * few : (s + 1) * few]
        for m, piece, row in piece_spots(pieces, shards, part):
            spot = slice(row, row + part)
            at = pl.multiple_of((me ^ m) * part, part)
            piece[spot, :width] = acc[pl.ds(at, part), :].astype(BF16)
            if closing:
                mine_rows = table[me ^ m]
                lanes = [mine_rows[:, j : j + 128] for j in range(0, D, 128)]
                empty = part - mine_rows.shape[0] * len(lanes)
                if empty:
                    lanes.append(jnp.zeros((empty, 128), F32))
                piece[spot, width:] = jnp.concatenate(lanes, 0).astype(BF16)
    else:
        store.wait()
    if extra_ref is not None:
        extra_ref[...] = extra[...]

    def drain(chunk, _):
        send(chunk).wait()
        return 0

    lax.fori_loop(0, chunks, drain, 0)


def attention_backward(
    seq, group, groups, shards, lengths, me, w_qkv, vectors, x, dot, qt, mixt, expo,
    chain=(), others=(), after=(),
):
    seq_rows = x.shape[1]
    top = key_sizes(seq_rows)[-1]
    padded = cdiv(seq_rows + MEM, TILE) * TILE
    gp = PAIRS // groups
    gcols = gp * 128
    width = 3 * gcols
    vm = pl.BlockSpec(memory_space=pltpu.VMEM)
    hbm = pl.BlockSpec(memory_space=pl.ANY)
    smem = pl.BlockSpec(memory_space=pltpu.SMEM)
    out_shape = [jax.ShapeDtypeStruct((padded, width), BF16)]
    out_specs = [hbm]
    if chain:
        wide = width + (128 if others else 0)
        out_shape += [jax.ShapeDtypeStruct((D // 2, wide), BF16)] * 2
        out_specs += [vm] * 2
    else:
        out_shape += [jax.ShapeDtypeStruct((D, width), F32)]
        out_specs += [hbm]
    if not others:
        out_shape += [jax.ShapeDtypeStruct((32, D), F32)]
        out_specs += [vm]
    out_shape += [jax.ShapeDtypeStruct((8, 128), F32)]
    out_specs += [vm]
    return pl.pallas_call(
        partial(
            bwd_kernel, seq_rows, groups, group, seq, shards, bool(chain), len(others),
            len(after),
        ),
        out_shape=tuple(out_shape),
        grid=(1,),
        in_specs=[
            smem,
            smem,
            pl.BlockSpec((D, gcols), lambda i: (0, groups + group)),
            pl.BlockSpec((D, gcols), lambda i: (0, 2 * groups + group)),
            vm,
        ]
        + [hbm] * 5
        + ([hbm, vm] if chain else [])
        + [vm] * len(others)
        + [hbm] * len(after),
        out_specs=tuple(out_specs),
        scratch_shapes=[
            pltpu.VMEM((padded, D), BF16),
            pltpu.VMEM((gcols, seq_rows), BF16),
            pltpu.VMEM((gcols, seq_rows), BF16),
            pltpu.VMEM((gcols, seq_rows), BF16),
            pltpu.VMEM((gcols, D), BF16),
            pltpu.VMEM((gcols, padded), BF16),
            pltpu.VMEM((gp, padded, 128), BF16),
            pltpu.VMEM((gp * 2, 128, TILE), BF16),
            pltpu.VMEM((gp * 2, 128, TILE), BF16),
            pltpu.VMEM((gcols, padded), BF16),
            pltpu.VMEM((gp, padded, 128), F32),
            pltpu.VMEM((gp, padded, 128), F32),
            pltpu.VMEM((2, gp * 2, top, TILE), BF16),
            pltpu.VMEM((D, width), F32),
            pltpu.VMEM((padded, width), BF16),
            pltpu.VMEM((32, D), F32),
            pltpu.VMEM((shards, max(8, 32 // shards), D), F32),
            pltpu.SemaphoreType.DMA((2,)),
            pltpu.SemaphoreType.DMA((4,)),
            pltpu.SemaphoreType.DMA,
            pltpu.SemaphoreType.DMA,
        ],
        compiler_params=pltpu.CompilerParams(vmem_limit_bytes=VMEM_LIMIT),
        cost_estimate=pl.CostEstimate(
            flops=8 * 10**9, bytes_accessed=15 * 10**6, transcendentals=0
        ),
        name="attention_backward",
    )(lengths, me, w_qkv, w_qkv, vectors, x, dot, qt, mixt, expo, *chain, *others, *after)


def input_kernel(seq_rows, groups, seq, len_ref, w_ref, gh_hbm, *refs):
    projs = refs[:groups]
    gx_hbm, token, gh, blocks, rows, sems, out_sem = refs[-7:]
    token[...] = jnp.zeros(token.shape, F32)
    gcols = D // groups
    length = len_ref[seq]
    chunks = cdiv(length, TILE)
    whole = seq_rows // TILE

    def spot(chunk):
        return pl.ds(pl.multiple_of(chunk * TILE, TILE), TILE)

    def fetch(chunk):
        here = spot(chunk)
        return [pltpu.make_async_copy(gh_hbm.at[seq, here, :], gh.at[here, :], sems.at[chunk, 0])] + [
            pltpu.make_async_copy(p.at[here, :], blocks.at[i, here, :], sems.at[chunk, 1 + i])
            for i, p in enumerate(projs)
        ]

    def send(chunk):
        here = spot(chunk)
        return pltpu.make_async_copy(rows.at[here, :], gx_hbm.at[seq, here, :], out_sem)

    def begin(chunk, _):
        for copy in fetch(chunk):
            copy.start()
        return 0

    lax.fori_loop(0, chunks, begin, 0)

    def empty(chunk, _):
        rows[spot(chunk), :] = jnp.zeros((TILE, D), BF16)
        send(chunk).start()
        return 0

    lax.fori_loop(chunks, whole, empty, 0)

    def step(chunk, _):
        here = spot(chunk)
        for copy in fetch(chunk):
            copy.wait()
        joint = jnp.concatenate(
            [
                blocks[g, here, kind * gcols : (kind + 1) * gcols]
                for kind in range(3)
                for g in range(groups)
            ],
            1,
        )
        grad = nt(joint, w_ref[...])
        row = lax.broadcasted_iota(jnp.int32, (TILE, 1), 0) + chunk * TILE
        rows[here, :] = jnp.where(row < length, grad + gh[here, :].astype(F32), 0.0).astype(BF16)
        send(chunk).start()
        return 0

    lax.fori_loop(0, chunks, step, 0)
    pltpu.make_async_copy(rows, gx_hbm.at[seq], out_sem).wait()


def input_gradient(seq, lengths, w_qkv, gh, projs, after=(), base=None):
    count, seq_rows = gh.shape[:2]
    groups = len(projs)
    hbm = pl.BlockSpec(memory_space=pl.ANY)
    vm = pl.BlockSpec(memory_space=pltpu.VMEM)
    base = () if base is None else (base,)
    return pl.pallas_call(
        partial(input_kernel, seq_rows, groups, seq),
        out_shape=(
            jax.ShapeDtypeStruct((count, seq_rows, D), BF16),
            jax.ShapeDtypeStruct((8, 128), F32),
        ),
        in_specs=[pl.BlockSpec(memory_space=pltpu.SMEM), vm]
        + [hbm] * (1 + groups + len(after) + len(base)),
        out_specs=(hbm, vm),
        input_output_aliases={3 + groups + len(after): 0} if base else {},
        scratch_shapes=[
            pltpu.VMEM((seq_rows, D), BF16),
            pltpu.VMEM((groups, seq_rows, 3 * D // groups), BF16),
            pltpu.VMEM((seq_rows, D), BF16),
            pltpu.SemaphoreType.DMA((seq_rows // TILE, 1 + groups)),
            pltpu.SemaphoreType.DMA,
        ],
        compiler_params=pltpu.CompilerParams(vmem_limit_bytes=VMEM_LIMIT),
        cost_estimate=pl.CostEstimate(
            flops=2 * 10**9, bytes_accessed=7 * 10**6, transcendentals=0
        ),
        name="input_gradient",
    )(lengths, w_qkv, gh, *projs, *after, *base)


GROUPS = 2


def powers(size):
    return [1 << i for i in range(size.bit_length() - 1)]


def exchange(value, axis, size, bit):
    return lax.ppermute(value, axis, [(i, i ^ bit) for i in range(size)])


def far_pieces(value, axis, size):
    pieces = {0: value}
    for bit in reversed(powers(size)[1:]):
        for mask in sorted(pieces):
            pieces[mask | bit] = exchange(pieces[mask], axis, size, bit)
    return pieces


def near_pieces(pieces, axis, size):
    pieces = dict(pieces)
    for mask in sorted(pieces):
        pieces[mask | 1] = exchange(pieces[mask], axis, size, 1)
    return [pieces[mask] for mask in range(size)]


def held_until(pieces, event):
    keys = list(pieces)
    return dict(zip(keys, lax.optimization_barrier((*[pieces[k] for k in keys], event))))


def combine_kernel(counts, modes, waits, carried, place_ref, *refs):
    refs = list(refs)
    arrays = [[[refs.pop(0) for _ in range(c)] for c in group] for group in counts]
    refs = refs[waits:]
    total = refs.pop()
    refs = refs[: len(refs) - carried]
    token = refs.pop()
    token[...] = jnp.zeros(token.shape, F32)
    place = place_ref[0]
    for groups, (mode, stacked, cols) in zip(arrays, modes):
        rows = sum(group[0].shape[0] for group in groups)
        if mode == "halves":
            half = rows // 2
            for side in range(2):
                add_rows(groups[0], side * half, half, refs.pop(0), 0, cols)
        elif mode == "parts":
            base = 0
            for group in groups:
                more = group[0].shape[0]
                add_rows(group, 0, more, total, base, cols)
                base += more
            one = rows // stacked
            part = one // GROUP
            for m in range(GROUP):
                target = refs.pop(0)
                at = pl.multiple_of((place ^ m) * part, part)
                for i in range(stacked):
                    target[i * part : (i + 1) * part, :] = total[
                        pl.ds(at + i * one, part), :cols
                    ].astype(BF16)
        else:
            add_rows(groups[0], 0, rows, refs.pop(0), 0, cols)


def add_rows(group, start, rows, target, base, cols):
    wide = group[0].shape[1]
    step = next((s for s in (64, 32, 16) if not (rows % s or start % s or base % s)), rows)

    def add(index, _):
        def at(first):
            if step == rows:
                return pl.ds(first, rows)
            return pl.ds(pl.multiple_of(first + index * step, step), step)

        value = group[0][at(start), :].astype(F32)
        for other in group[1:]:
            value = value + other[at(start), :].astype(F32)
        target[at(base), :wide] = value.astype(target.dtype)
        if wide < cols:
            target[at(base), wide:cols] = jnp.zeros((step, cols - wide), target.dtype)
        return 0

    lax.fori_loop(0, rows // step, add, 0)


def combine(place, items, after, carry=()):
    vm = pl.BlockSpec(memory_space=pltpu.VMEM)
    shapes, flat, modes, most = [], [], [], 0
    for groups, mode, stacked in items:
        rows = sum(arrays[0].shape[0] for arrays in groups)
        cols = max(arrays[0].shape[1] for arrays in groups)
        flat += [a for arrays in groups for a in arrays]
        modes.append((mode, stacked, cols))
        most = max(most, rows)
        if mode == "halves":
            shapes += [(rows // 2, cols)] * 2
        elif mode == "parts":
            shapes += [(rows // GROUP, cols)] * GROUP
        else:
            shapes += [(rows, cols)]
    size = sum(a.size for a in flat) * 2
    outs = pl.pallas_call(
        partial(
            combine_kernel,
            [[len(g) for g in i[0]] for i in items],
            modes,
            len(after) + len(carry),
            len(carry),
        ),
        out_shape=tuple(jax.ShapeDtypeStruct(s, BF16) for s in shapes)
        + (jax.ShapeDtypeStruct((8, 128), F32),)
        + tuple(jax.ShapeDtypeStruct(a.shape, a.dtype) for a in carry),
        in_specs=[pl.BlockSpec(memory_space=pltpu.SMEM)]
        + [vm] * len(flat)
        + [pl.BlockSpec(memory_space=pl.ANY)] * (len(after) + len(carry)),
        out_specs=(vm,) * (len(shapes) + 1)
        + (pl.BlockSpec(memory_space=pl.ANY),) * len(carry),
        input_output_aliases={
            1 + len(flat) + len(after) + i: len(shapes) + 1 + i for i in range(len(carry))
        },
        scratch_shapes=[pltpu.VMEM((most, max(m[2] for m in modes)), F32)],
        compiler_params=pltpu.CompilerParams(vmem_limit_bytes=24 * 2**20),
        cost_estimate=pl.CostEstimate(flops=size, bytes_accessed=2 * size, transcendentals=0),
        name="combine",
    )(place, *flat, *after, *carry)
    held = list(outs[len(shapes) + 1 :])
    outs, token, results = list(outs[: len(shapes)]), outs[len(shapes)], []
    for mode, _, _ in modes:
        taken = {"halves": 2, "parts": GROUP, "whole": 1}[mode]
        results.append([outs.pop(0) for _ in range(taken)])
    return results, [token, *held]


GROUP = 4


class Stream:
    def __init__(self, value, sizes, steps, stacked=None):
        self.value, self.steps = list(value), list(steps)
        self.reps, self.shards = sizes
        self.stacked = stacked or max(self.shards // 2, 1)

    def exchange(self):
        kind, bit = self.steps.pop(0)
        value = self.value
        if kind == "fold":
            arrays = [value[0], exchange(value[1], "shard", self.shards, bit)]
        elif kind == "group":
            arrays = [value[0]] + [
                exchange(value[j], "rep", self.reps, j) for j in range(1, GROUP)
            ]
        else:
            arrays = [value[0], exchange(value[0], "rep", self.reps, bit)]
        follow = self.steps[0][0] if self.steps else "end"
        item = ([arrays], {"fold": "halves", "group": "parts"}.get(follow, "whole"), self.stacked)
        if follow == "fold":
            self.stacked //= 2
        return item

    def alone(self, place, after=()):
        (self.value,), token = combine(place, [self.exchange()], after)
        return token


def advance(place, streams, items, after, carry=()):
    results, token = combine(place, items, after, carry)
    for stream, result in zip(streams, results):
        stream.value = result
    return token


def whole_parts(stream):
    own = stream.value[0]
    return [own] + [exchange(own, "rep", stream.reps, j) for j in range(1, GROUP)]


def spread_kernel(shards, place_ref, *refs):
    refs = list(refs)
    arrays = [[refs.pop(0) for _ in range(GROUP)] for _ in range(3)]
    qkv_ref, out_ref, in_ref, back_ref, vec_ref, table = refs
    place = place_ref[0]

    def put(target, parts, cols, first=0, count=None):
        part = count or parts[0].shape[0]
        for m in range(GROUP):
            at = pl.multiple_of((place ^ m) * part, part)
            target[pl.ds(at, part), :cols] = parts[m][first : first + part, :].astype(F32)

    part = D // shards
    put(back_ref, arrays[1], D)
    put(table, arrays[0], D)
    out_ref[...] = table[:part, :D]
    for j in range(BLOCKS):
        in_ref[:, j * D : (j + 1) * D] = table[(1 + j) * part : (2 + j) * part, :D]
    gcols = D // GROUPS
    for g in range(GROUPS):
        put(table, arrays[2], 3 * gcols + 128, g * part // GROUP, part // GROUP)
        for kind in range(3):
            at = kind * D + g * gcols
            qkv_ref[:, at : at + gcols] = table[:part, kind * gcols : (kind + 1) * gcols]
    few = 32 // shards
    width = 3 * gcols
    step = max(8, few)
    for j in range(D // 128):
        vec_ref[:, j * 128 : (j + 1) * 128] = table[j * step : j * step + few, width : width + 128]


def spread(place, shards, parts):
    part = D // shards
    vm = pl.BlockSpec(memory_space=pltpu.VMEM)
    shapes = ((part, 3 * D), (part, D), (part, FF), (FF // shards, D), (32 // shards, D))
    most = max(part * (1 + BLOCKS), part), max(p.shape[1] for p in parts)
    return pl.pallas_call(
        partial(spread_kernel, shards),
        out_shape=tuple(jax.ShapeDtypeStruct(s, F32) for s in shapes),
        in_specs=[pl.BlockSpec(memory_space=pltpu.SMEM)] + [vm] * len(parts),
        out_specs=(vm,) * len(shapes),
        scratch_shapes=[pltpu.VMEM(most, F32)],
        compiler_params=pltpu.CompilerParams(vmem_limit_bytes=24 * 2**20),
        name="spread",
    )(place, *parts)


def body(sizes, inputs, lengths, w_qkv, w_out, w_in, w_back, vectors, cotangent):
    reps, shards = sizes
    count = inputs.shape[0]
    me = lax.axis_index("shard").astype(jnp.int32).reshape(1)

    axis = ("shard", shards)
    far = far_pieces(pack(w_qkv, vectors), *axis)
    start = held_until(
        {0: jnp.concatenate([w_out, w_in], 1), 1: w_back}, far[max(far)]
    )
    far_up, far_back = far_pieces(start[0], *axis), far_pieces(start[1], *axis)
    whole, wqt, wvt, table = prepare(me, near_pieces(far, *axis))
    fwd = [
        attention_forward(s, lengths, inputs, whole, wqt, wvt, table) for s in range(count)
    ]
    far_up, far_back = held_until(far_up, fwd[-1][3]), held_until(far_back, fwd[-1][3])
    out, gh, dot, *grads, sums = feed_forward(
        lengths, me, inputs, cotangent, [f[2] for f in fwd], [f[3] for f in fwd],
        near_pieces(far_up, *axis), near_pieces(far_back, *axis), table,
    )
    place = (lax.axis_index("rep") % GROUP).astype(jnp.int32).reshape(1)
    folds = [("fold", bit) for bit in powers(shards)]
    group = [("group", 0)]
    rest = [("full", bit) for bit in powers(reps) if bit >= GROUP]
    tall = Stream(grads[:2], sizes, folds + group + rest)
    deep = Stream(grads[2:], sizes, folds[:1] + group + folds[1:] + rest)
    projs = [[None] * GROUPS for _ in range(count)]
    quarters = [None] * GROUPS
    extras, after, calls = [], [], []
    for g in range(GROUPS):
        chain = ()
        for s in range(count):
            closing = [sums] + extras if s == count - 1 and g == GROUPS - 1 else ()
            busy = [
                (tall, deep), (tall, deep), (tall, quarters[0]), (deep, quarters[0], tall)
            ][len(calls)]
            items = [stream.exchange() for stream in busy]
            res = attention_backward(
                s, g, GROUPS, shards, lengths, me, whole, table, inputs, dot, fwd[s][1],
                fwd[s][2], fwd[s][0], chain, closing, after,
            )
            chain = list(res[1:-1])
            carry = chain[1:2] if len(calls) == 3 else []
            after, *held = advance(place, busy, items, [res[-1]], carry)
            after = [after]
            chain[1 : 1 + len(held)] = held
            projs[s][g] = res[0]
            calls.append(res)
        quarters[g] = Stream(chain[:2], sizes, folds + [("stop", 0)])
        extras += chain[2:]
    early, last = quarters
    for stream, left in ((early, 1), (tall, 0), (deep, 1)):
        while len(stream.steps) > left:
            stream.alone(place)
    tall_parts = whole_parts(tall)
    end = deep.exchange()
    after = []
    while len(last.steps) > 2:
        after = last.alone(place)
    gx, token = input_gradient(0, lengths, whole, gh, projs[0], after)
    final = last.exchange()[0]
    both = Stream([], sizes, group + rest, stacked=GROUPS)
    after = advance(
        place, [both, deep], [([early.value] + final, "parts", GROUPS), end], [token]
    )
    for seq in range(1, count):
        gx, token = input_gradient(seq, lengths, whole, gh, projs[seq], after, gx)
    both.alone(place, [token] + tall_parts[1:])
    deep_parts = whole_parts(deep)
    while both.steps:
        both.alone(place)
    return (out, gx, *spread(place, shards, tall_parts + deep_parts + whole_parts(both)))


def solution(mesh):
    data = P(("rep", "shard"), None, None)
    rows = P("shard", None)
    return jax.shard_map(
        partial(body, (mesh.shape["rep"], mesh.shape["shard"])),
        mesh=mesh,
        in_specs=(data, P(("rep", "shard")), rows, rows, rows, rows, rows, data),
        out_specs=(data, data, rows, rows, rows, rows, rows),
        check_vma=False,
    )
```

```python
import math
from functools import partial

import jax
import jax.numpy as jnp
from jax import lax
from jax.experimental import pallas as pl
from jax.experimental.pallas import tpu as pltpu
from jax.sharding import PartitionSpec as P

D = 512
HEADS = 8
HDIM = 64
FF = 2048
MEM = 20
TILE = 256
PAIRS = HEADS // 2
SCALE = HDIM**-0.5
QSCALE = SCALE * math.log2(math.e)
LN2 = math.log(2.0)
F32 = jnp.float32
BF16 = jnp.bfloat16
VROWS = 80
VMEM_LIMIT = 62 * 2**20


def nn(a, b):
    return lax.dot_general(a, b, (((1,), (0,)), ((), ())), preferred_element_type=F32)


def nt(a, b):
    return lax.dot_general(a, b, (((1,), (1,)), ((), ())), preferred_element_type=F32)


def tn(a, b):
    return lax.dot_general(a, b, (((0,), (0,)), ((), ())), preferred_element_type=F32)


def key_sizes(seq_rows):
    top = -(-(seq_rows + MEM) // 32) * 32
    return [rows for rows in range(512, top, 256)] + [top]


def column_max(values):
    parts = [values[i : i + 128] for i in range(0, values.shape[0] - 127, 128)]
    while len(parts) > 1:
        odd = parts[len(parts) - len(parts) % 2 :]
        parts = [jnp.maximum(a, b) for a, b in zip(parts[::2], parts[1::2])] + odd
    top = jnp.max(parts[0], axis=0, keepdims=True)
    rest = values.shape[0] % 128
    if rest:
        top = jnp.maximum(top, jnp.max(values[-rest:], axis=0, keepdims=True))
    return top


AHEAD = 2
BODY_HEADS = 4


def cdiv(a, b):
    return (a + b - 1) // b


def pick_memory(rows_ref, memory, length):
    edge = pl.multiple_of(length // 128 * 128, 128)
    fix = pl.ds(edge, TILE)
    row = lax.broadcasted_iota(jnp.int32, (TILE, 1), 0) + edge
    lane = lax.broadcasted_iota(jnp.int32, (TILE, 32), 1)
    pick = lax.broadcasted_iota(jnp.int32, (TILE, 32), 0) + (edge - length) == lane
    placed = nn(jnp.where(pick, 1.0, 0.0).astype(BF16), memory)
    rows_ref[fix, :] = jnp.where(row < length, rows_ref[fix, :].astype(F32), placed).astype(BF16)


def memory_rows(vec_ref):
    inside = lax.broadcasted_iota(jnp.int32, (32, D), 0) < MEM
    return jnp.where(inside, vec_ref[...].astype(F32), 0.0).astype(BF16)


def for_size(seq_rows, total, run):
    sizes = key_sizes(seq_rows)
    for index, kr in enumerate(sizes):
        least = sizes[index - 1] if index else 0

        @pl.when(jnp.logical_and(total > least, total <= kr))
        def _(kr=kr):
            run(kr)


def prepare_kernel(shards, me_ref, *refs):
    pieces = refs[:shards]
    w_ref, wqt_ref, wvt_ref, vec_ref, few_rows, sems = refs[shards:]
    me = me_ref[0]
    part, few = D // shards, 32 // shards
    copies, small = [], []
    for m in range(shards):
        at = pl.multiple_of((me ^ m) * part, part)
        small.append(
            pltpu.make_async_copy(
                pieces[m].at[pl.ds(part, SPARE), pl.ds(0, D)], few_rows.at[m], sems.at[m, 1]
            )
        )
        copies.append(
            pltpu.make_async_copy(
                pieces[m].at[pl.ds(0, part), :], w_ref.at[pl.ds(at, part), :], sems.at[m, 0]
            )
        )
    for copy in small + copies:
        copy.start()
    for copy in small:
        copy.wait()
    owner = lax.broadcasted_iota(jnp.int32, (32, D), 0) // few
    rows = jnp.zeros((32, D), F32)
    for m in range(shards):
        values = few_rows[m].astype(F32)[:few]
        rows = jnp.where(owner == (me ^ m), jnp.concatenate([values] * shards, 0), rows)
    vec_ref[...] = rows.astype(BF16)
    for copy in copies:
        copy.wait()
    wqt_ref[...] = w_ref[:, :D].T
    wvt_ref[...] = w_ref[:, 2 * D :].T


SPARE = 16


def pack(w_qkv, vectors):
    below = ((0, SPARE - vectors.shape[0]), (0, w_qkv.shape[1] - vectors.shape[1]))
    return jnp.concatenate([w_qkv, jnp.pad(vectors, below)], 0)


def prepare(me, pieces):
    shards = len(pieces)
    vm = pl.BlockSpec(memory_space=pltpu.VMEM)
    return pl.pallas_call(
        partial(prepare_kernel, shards),
        out_shape=(
            jax.ShapeDtypeStruct((D, 3 * D), BF16),
            jax.ShapeDtypeStruct((D, D), BF16),
            jax.ShapeDtypeStruct((D, D), BF16),
            jax.ShapeDtypeStruct((32, D), BF16),
        ),
        in_specs=[pl.BlockSpec(memory_space=pltpu.SMEM)]
        + [pl.BlockSpec(memory_space=pl.ANY)] * shards,
        out_specs=(vm, vm, vm, vm),
        scratch_shapes=[
            pltpu.VMEM((shards, SPARE, D), BF16),
            pltpu.SemaphoreType.DMA((shards, 2)),
        ],
        compiler_params=pltpu.CompilerParams(vmem_limit_bytes=24 * 2**20),
        name="prepare",
    )(me, *pieces)


def fwd_kernel(
    seq_rows, seq, len_ref, x_hbm, wk_ref, wqt_ref, wvt_ref, vec_ref,
    e_hbm, qt_hbm, mixt_hbm, inv_ref,
    rows, keys, vt, qpad, queries, mixed_t, ebuf, sems, io_sems,
):
    length = len_ref[seq]
    total = length + MEM
    load = pltpu.make_async_copy(x_hbm.at[seq], rows.at[pl.ds(0, seq_rows), :], io_sems.at[0])
    load.start()
    memory = memory_rows(vec_ref)
    vec_cols = vec_ref[...].astype(F32).T
    bias_q = vec_cols[:, MEM : MEM + 1]
    bias_v = vec_cols[:, MEM + 1 : MEM + 2]
    mixed_t[...] = jnp.zeros(mixed_t.shape, BF16)
    inv_ref[...] = jnp.zeros(inv_ref.shape, F32)
    for head in range(HEADS):
        spare = HDIM * (1 - head % 2)
        qpad[head, spare : spare + HDIM, :] = jnp.zeros((HDIM, qpad.shape[2]), BF16)
    vt[:, HDIM:, :] = jnp.ones((HEADS, VROWS - HDIM, vt.shape[2]), BF16)
    n_tiles = cdiv(length, TILE)
    chunks = cdiv(total, TILE)
    load.wait()

    rows[seq_rows:, :] = jnp.zeros((rows.shape[0] - seq_rows, D), BF16)
    pick_memory(rows, memory, length)

    def project(chunk, _):
        here = pl.ds(pl.multiple_of(chunk * TILE, TILE), TILE)
        joined = rows[here, :]
        key_rows = nn(joined, wk_ref[...]).astype(BF16)
        for pair in range(PAIRS):
            keys[pair, here, :] = key_rows[:, pair * 128 : pair * 128 + 128]
        values = (nt(wvt_ref[...], joined) + bias_v).astype(BF16)
        found = ((nt(wqt_ref[...], joined) + bias_q) * QSCALE).astype(BF16)
        queries[:, here] = found
        for head in range(HEADS):
            low = (head % 2) * HDIM
            vt[head, :HDIM, here] = values[head * HDIM : (head + 1) * HDIM]
            qpad[head, low : low + HDIM, here] = found[head * HDIM : (head + 1) * HDIM]
        return 0

    lax.fori_loop(0, chunks, project, 0)
    save = pltpu.make_async_copy(queries.at[:, pl.ds(0, seq_rows)], qt_hbm, io_sems.at[1])
    save.start()

    def attend(kr):
        tail = kr - TILE if kr % TILE == 0 else kr - kr % TILE
        row = lax.broadcasted_iota(jnp.int32, (kr - tail, TILE), 0) + tail
        mask = row < total

        def copies(tile, pair):
            return pltpu.make_async_copy(
                ebuf.at[pair, :, pl.ds(0, kr), :],
                e_hbm.at[tile, pl.ds(pair * 2, 2), pl.ds(0, kr), :],
                sems.at[pair],
            )

        turns = HEADS // BODY_HEADS

        def step(unit, _):
            tile, turn = unit // turns, unit % turns
            here = pl.ds(pl.multiple_of(tile * TILE, TILE), TILE)
            base = turn * BODY_HEADS

            def score(i):
                pair = turn * (BODY_HEADS // 2) + i // 2
                scores = nn(keys[pair, :kr, :], qpad[base + i, :, here])
                scores = jnp.concatenate(
                    [scores[:tail], jnp.where(mask, scores[tail:], -1e30)], 0
                )
                return scores, column_max(scores)

            live = {i: score(i) for i in range(AHEAD)}
            for i in range(BODY_HEADS):
                pair, sub = turn * (BODY_HEADS // 2) + i // 2, i % 2
                scores, top = live.pop(i)
                if sub == 0:
                    copies(tile, pair).wait()
                if i + AHEAD < BODY_HEADS:
                    live[i + AHEAD] = score(i + AHEAD)
                expo = jnp.exp2(scores - top).astype(BF16)
                ebuf[pair, sub, :kr, :] = expo
                mixed = nn(vt[base + i, :, :kr], expo)
                inverse = 1.0 / mixed[HDIM : HDIM + 1]
                spot = pl.ds(pl.multiple_of((base + i) * HDIM, HDIM), HDIM)
                mixed_t[spot, here] = (mixed[:HDIM] * inverse).astype(BF16)
                inv_ref[pl.ds(base + i, 1), here] = inverse
                if sub == 1:
                    copies(tile, pair).start()
            return 0

        for pair in range(PAIRS):
            copies(0, pair).start()
        lax.fori_loop(0, n_tiles * turns, step, 0)
        out = pltpu.make_async_copy(mixed_t, mixt_hbm, io_sems.at[2])
        out.start()
        for pair in range(PAIRS):
            copies(n_tiles - 1, pair).wait()
        save.wait()
        out.wait()

    for_size(seq_rows, total, attend)


def attention_forward(seq, lengths, x, w_qkv, wqt, wvt, vectors):
    seq_rows = x.shape[1]
    top = key_sizes(seq_rows)[-1]
    padded = cdiv(seq_rows + MEM, TILE) * TILE
    tiles = seq_rows // TILE
    vm = pl.BlockSpec(memory_space=pltpu.VMEM)
    hbm = pl.BlockSpec(memory_space=pl.ANY)
    return pl.pallas_call(
        partial(fwd_kernel, seq_rows, seq),
        out_shape=(
            jax.ShapeDtypeStruct((tiles, HEADS, top, TILE), BF16),
            jax.ShapeDtypeStruct((D, seq_rows), BF16),
            jax.ShapeDtypeStruct((D, seq_rows), BF16),
            jax.ShapeDtypeStruct((HEADS, seq_rows), F32),
        ),
        grid=(1,),
        in_specs=[
            pl.BlockSpec(memory_space=pltpu.SMEM),
            hbm,
            pl.BlockSpec((D, D), lambda i: (0, 1)),
            vm,
            vm,
            vm,
        ],
        out_specs=(hbm, hbm, hbm, vm),
        scratch_shapes=[
            pltpu.VMEM((padded, D), BF16),
            pltpu.VMEM((PAIRS, padded, 128), BF16),
            pltpu.VMEM((HEADS, VROWS, padded), BF16),
            pltpu.VMEM((HEADS, 128, padded), BF16),
            pltpu.VMEM((D, padded), BF16),
            pltpu.VMEM((D, seq_rows), BF16),
            pltpu.VMEM((PAIRS, 2, top, TILE), BF16),
            pltpu.SemaphoreType.DMA((PAIRS,)),
            pltpu.SemaphoreType.DMA((3,)),
        ],
        compiler_params=pltpu.CompilerParams(vmem_limit_bytes=44 * 2**20),
        cost_estimate=pl.CostEstimate(
            flops=8 * 10**9, bytes_accessed=24 * 10**6, transcendentals=8 * 10**6
        ),
        name="attention_forward",
    )(lengths, x, w_qkv, wqt, wvt, vectors)


def norm_forward(values):
    center = values - jnp.mean(values, axis=-1, keepdims=True)
    inverse = lax.rsqrt(jnp.mean(center * center, axis=-1, keepdims=True) + 1e-05)
    return center * inverse, inverse


def norm_backward(grad, normed, inverse):
    return inverse * (
        grad
        - jnp.mean(grad, axis=-1, keepdims=True)
        - normed * jnp.mean(grad * normed, axis=-1, keepdims=True)
    )


def col_sum(values):
    return jnp.sum(values, axis=0, keepdims=True)


GELU_A = math.sqrt(2.0 / math.pi)
GELU_B = GELU_A * 0.044715
BLOCKS = FF // D


def piece_order(shards):
    bits = shards.bit_length() - 1
    return [int(format(i, "b").zfill(bits)[::-1], 2) if bits else 0 for i in range(shards)]


def piece_spots(pair, shards, rows):
    half = max(shards // 2, 1)
    for index, m in enumerate(piece_order(shards)):
        yield m, pair[index // half], index % half * rows


def ffn_kernel(
    seq_rows, shards, len_ref, me_ref, x_hbm, cot_hbm, mixt0, mixt1, inv0, inv1, *refs,
):
    wi_p, wb_p = refs[:shards], refs[shards : 2 * shards]
    vec_ref, out_hbm, gh_hbm, dot_hbm = refs[2 * shards : 2 * shards + 4]
    grads = refs[2 * shards + 4 : 2 * shards + 8]
    (
        sums_ref, x_ref, cot_ref, mixt_ref, inv_ref, wo_ref, wi_ref, wb_ref,
        out_ref, gh_ref, dot_ref, acc_o, acc_i, acc_b, slopes, actives,
        s_normed1, s_first, s_gsecond, ups, sems, out_sems,
    ) = refs[2 * shards + 8 :]
    half = TILE // 2
    len0, len1 = len_ref[0], len_ref[1]
    me = me_ref[0]
    n0, n1 = cdiv(len0, half), cdiv(len1, half)
    full = seq_rows // half
    n_all = n0 + n1

    def rows_at(piece, rows):
        return pl.ds(pl.multiple_of((me ^ piece) * rows, rows), rows)

    loads = []

    def load(src, dst):
        copy = pltpu.make_async_copy(src, dst, sems.at[len(loads)])
        loads.append(copy)
        copy.start()
        return copy

    first_loads = [load(mixt0, mixt_ref.at[0]), load(mixt1, mixt_ref.at[1])]
    first_loads += [load(inv0, inv_ref.at[0]), load(inv1, inv_ref.at[1])]
    part = D // shards
    first_loads += [
        load(p.at[:, pl.ds(0, D)], wo_ref.at[rows_at(i, part), :]) for i, p in enumerate(wi_p)
    ]
    first_loads += [load(x_hbm.at[s], x_ref.at[s]) for s in range(2)]
    second_loads = [
        load(p.at[:, pl.ds(D, FF)], wi_ref.at[rows_at(i, part), :]) for i, p in enumerate(wi_p)
    ]
    second_loads += [load(p, wb_ref.at[rows_at(i, FF // shards), :]) for i, p in enumerate(wb_p)]
    third_loads = [load(cot_hbm.at[s], cot_ref.at[s]) for s in range(2)]

    out_ref[...] = jnp.zeros(out_ref.shape, BF16)
    gh_ref[...] = jnp.zeros(gh_ref.shape, BF16)
    dot_ref[...] = jnp.zeros(dot_ref.shape, BF16)
    acc_o[...] = jnp.zeros(acc_o.shape, F32)
    acc_i[...] = jnp.zeros(acc_i.shape, F32)
    acc_b[...] = jnp.zeros(acc_b.shape, F32)
    sums_ref[...] = jnp.zeros(sums_ref.shape, F32)

    def vec(index):
        return vec_ref[index : index + 1, :].astype(F32)

    bias_out = vec(MEM + 2)
    bias_back = vec(MEM + 3 + BLOCKS)
    gain_one = vec(MEM + 4 + BLOCKS)
    shift_one = vec(MEM + 5 + BLOCKS)
    gain_two = vec(MEM + 6 + BLOCKS)
    shift_two = vec(MEM + 7 + BLOCKS)

    spare_one = jnp.logical_and(n_all % 2 == 1, n1 < full)
    spare_zero = jnp.logical_and(n_all % 2 == 1, n1 >= full)

    def place(chunk):
        second = chunk >= n0
        inside = jnp.where(second, chunk - n0, chunk)
        spare = chunk >= n_all
        seq = jnp.where(spare, jnp.where(n1 < full, 1, 0), jnp.where(second, 1, 0))
        inside = jnp.where(spare, jnp.where(n1 < full, n1, n0), inside)
        return seq, pl.multiple_of(inside * half, half), jnp.where(seq == 1, len1, len0)

    def rows_of(ref, spots):
        return jnp.concatenate([ref[s, pl.ds(r, half), :] for s, r, _ in spots], 0)

    def lanes_of(ref, spots):
        return jnp.concatenate([ref[s, :, pl.ds(r, half)] for s, r, _ in spots], 1)

    def put_rows(ref, value, spots):
        for i, (s, r, _) in enumerate(spots):
            ref[s, pl.ds(r, half), :] = value[i * half : (i + 1) * half]

    def put_lanes(ref, value, spots):
        for i, (s, r, _) in enumerate(spots):
            ref[s, :, pl.ds(r, half)] = value[:, i * half : (i + 1) * half]

    def valid_of(spots):
        iota = lax.broadcasted_iota(jnp.int32, (half, 1), 0)
        return jnp.concatenate(
            [jnp.where(iota + r < count, 1.0, 0.0) for _, r, count in spots], 0
        )

    def add_sum(row, value):
        sums_ref[row : row + 1] += col_sum(value)

    def whole_tile(spots):
        count = half * len(spots)
        here = slice(0, count)
        valid = valid_of(spots)
        mixt = lanes_of(mixt_ref, spots)
        attn = nn(mixt.T, wo_ref[...]) + bias_out
        normed_one, inverse_one = norm_forward(rows_of(x_ref, spots).astype(F32) + attn)
        first = normed_one * gain_one + shift_one
        s_normed1[here] = normed_one
        low = first.astype(BF16)
        s_first[here] = low
        second = first + bias_back
        for j in range(BLOCKS):
            cols = slice(j * D, (j + 1) * D)
            up = nn(low, wi_ref[:, cols]) + vec(MEM + 3 + j)
            square = up * up
            bent = jnp.tanh(up * (GELU_A + GELU_B * square))
            gate = 0.5 + 0.5 * bent
            active = up * gate
            slopes[here, cols] = (
                gate + active * (1.0 - bent) * (GELU_A + 3.0 * GELU_B * square)
            ).astype(slopes.dtype)
            actives[here, cols] = active.astype(BF16)
        second = second + nn(actives[here, :], wb_ref[...])
        normed_two, inverse_two = norm_forward(second)
        put_rows(out_ref, ((normed_two * gain_two + shift_two) * valid).astype(BF16), spots)
        grad_out = rows_of(cot_ref, spots).astype(F32) * valid
        add_sum(MEM + 6 + BLOCKS, grad_out * normed_two)
        add_sum(MEM + 7 + BLOCKS, grad_out)
        grad_second = norm_backward(grad_out * gain_two, normed_two, inverse_two)
        s_gsecond[here] = grad_second
        down = grad_second.astype(BF16)
        add_sum(MEM + 3 + BLOCKS, down.astype(F32))
        low_t = s_first[here, :].T
        for j in range(BLOCKS):
            cols = slice(j * D, (j + 1) * D)
            grad_up = (
                nt(down, wb_ref[cols, :]) * slopes[here, cols].astype(F32)
            ).astype(BF16)
            ups[here, cols] = grad_up
            add_sum(MEM + 3 + j, grad_up.astype(F32))
        grad_first = s_gsecond[here] + nt(ups[here, :], wi_ref[...])
        for j in range(BLOCKS):
            cols = slice(j * D, (j + 1) * D)
            acc_b[cols, :] += tn(actives[here, cols], down)
            acc_i[:, cols] += nn(low_t, ups[here, cols])
        normed_one = s_normed1[here]
        add_sum(MEM + 4 + BLOCKS, grad_first * normed_one)
        add_sum(MEM + 5 + BLOCKS, grad_first)
        grad_one = norm_backward(grad_first * gain_one, normed_one, inverse_one)
        low = grad_one.astype(BF16)
        put_rows(gh_ref, low, spots)
        add_sum(MEM + 2, low.astype(F32))
        acc_o[...] += nn(mixt, low)
        grad_mixed = nt(wo_ref[...], low)
        inverse = lanes_of(inv_ref, spots)
        scaled = [
            grad_mixed[h * HDIM : (h + 1) * HDIM] * inverse[h : h + 1] for h in range(HEADS)
        ]
        put_lanes(dot_ref, jnp.concatenate(scaled, 0).astype(BF16), spots)

    def send(ref, hbm, sem, seq, row, lanes=False):
        here = pl.ds(row, half)
        src = ref.at[seq, :, here] if lanes else ref.at[seq, here, :]
        dst = hbm.at[seq, :, here] if lanes else hbm.at[seq, here, :]
        pltpu.make_async_copy(src, dst, out_sems.at[sem]).start()

    def send_all(seq, row):
        send(out_ref, out_hbm, 0, seq, row)
        send(gh_ref, gh_hbm, 1, seq, row)
        send(dot_ref, dot_hbm, 2, seq, row, True)

    for copy in first_loads + second_loads + third_loads:
        copy.wait()

    def step(index, _):
        spots = [place(index * 4 + i) for i in range(4)]
        whole_tile(spots)
        for seq, row, _ in spots:
            send_all(seq, row)
        return 0

    left = lax.rem(n_all, 4)
    bigs = n_all // 4 + jnp.where(left == 3, 1, 0)
    lax.fori_loop(0, bigs, step, 0)

    @pl.when(jnp.logical_or(left == 1, left == 2))
    def _():
        spots = [place(bigs * 4 + i) for i in range(2)]
        whole_tile(spots)
        for seq, row, _ in spots:
            send_all(seq, row)

    def rest(seq):
        def one(chunk, _):
            send_all(seq, pl.multiple_of(chunk * half, half))
            return 0

        return one

    lax.fori_loop(n0 + jnp.where(spare_zero, 1, 0), full, rest(0), 0)
    lax.fori_loop(n1 + jnp.where(spare_one, 1, 0), full, rest(1), 0)

    part = D // shards
    deep = FF // shards
    block = part * (1 + BLOCKS)
    for m, piece, row in piece_spots(grads[:2], shards, block):
        at = pl.multiple_of((me ^ m) * part, part)
        piece[row : row + part, :] = acc_o[pl.ds(at, part), :].astype(BF16)
        for j in range(BLOCKS):
            row += part
            piece[row : row + part, :] = acc_i[
                pl.ds(at, part), j * D : (j + 1) * D
            ].astype(BF16)
    for m, piece, row in piece_spots(grads[2:], shards, deep):
        at = pl.multiple_of((me ^ m) * deep, deep)
        piece[row : row + deep, :] = acc_b[pl.ds(at, deep), :].astype(BF16)
    for ref, hbm, sem in ((out_ref, out_hbm, 0), (gh_ref, gh_hbm, 1), (dot_ref, dot_hbm, 2)):
        pltpu.make_async_copy(ref, hbm, out_sems.at[sem]).wait()


def feed_forward(lengths, me, x, cot, mixts, invs, w_up, w_back, vectors):
    count, seq_rows = x.shape[:2]
    shards = len(w_up)
    vm = pl.BlockSpec(memory_space=pltpu.VMEM)
    hbm = pl.BlockSpec(memory_space=pl.ANY)
    smem = pl.BlockSpec(memory_space=pltpu.SMEM)
    return pl.pallas_call(
        partial(ffn_kernel, seq_rows, shards),
        out_shape=(
            jax.ShapeDtypeStruct((count, seq_rows, D), BF16),
            jax.ShapeDtypeStruct((count, seq_rows, D), BF16),
            jax.ShapeDtypeStruct((count, D, seq_rows), BF16),
            *[
                jax.ShapeDtypeStruct((rows, D), BF16)
                for rows in (D * (1 + BLOCKS) // 2, FF // 2)
                for _ in range(2)
            ],
            jax.ShapeDtypeStruct((32, D), F32),
        ),
        in_specs=[smem, smem] + [hbm] * (6 + 2 * shards) + [vm],
        out_specs=(hbm, hbm, hbm) + (vm,) * 5,
        scratch_shapes=[
            pltpu.VMEM((count, seq_rows, D), BF16),
            pltpu.VMEM((count, seq_rows, D), BF16),
            pltpu.VMEM((count, D, seq_rows), BF16),
            pltpu.VMEM((count, HEADS, seq_rows), F32),
            pltpu.VMEM((D, D), BF16),
            pltpu.VMEM((D, FF), BF16),
            pltpu.VMEM((FF, D), BF16),
            pltpu.VMEM((count, seq_rows, D), BF16),
            pltpu.VMEM((count, seq_rows, D), BF16),
            pltpu.VMEM((count, D, seq_rows), BF16),
            pltpu.VMEM((D, D), F32),
            pltpu.VMEM((D, FF), F32),
            pltpu.VMEM((FF, D), F32),
            pltpu.VMEM((2 * TILE, FF), BF16),
            pltpu.VMEM((2 * TILE, FF), BF16),
            pltpu.VMEM((2 * TILE, D), F32),
            pltpu.VMEM((2 * TILE, D), BF16),
            pltpu.VMEM((2 * TILE, D), F32),
            pltpu.VMEM((2 * TILE, FF), BF16),
            pltpu.SemaphoreType.DMA((8 + 3 * shards,)),
            pltpu.SemaphoreType.DMA((3,)),
        ],
        compiler_params=pltpu.CompilerParams(vmem_limit_bytes=56 * 2**20),
        cost_estimate=pl.CostEstimate(
            flops=27 * 10**9, bytes_accessed=24 * 10**6, transcendentals=4 * 10**6
        ),
        name="feed_forward",
    )(lengths, me, x, cot, *mixts, *invs, *w_up, *w_back, vectors)


def bwd_kernel(seq_rows, groups, group, seq, shards, chained, closing, waits, *refs):
    gp = PAIRS // groups
    gcols = gp * 128
    width = 3 * gcols
    refs = list(refs)
    len_ref, me_ref, wk_ref, wv_ref, vec_ref = refs[:5]
    x_hbm, dot_hbm, qt_hbm, mixt_hbm, e_hbm = refs[5:10]
    refs = refs[10:]
    acc_in, extra_in = (refs.pop(0), refs.pop(0)) if chained else (None, None)
    other_rows = [refs.pop(0) for _ in range(closing)]
    refs = refs[waits:]
    proj_hbm = refs.pop(0)
    last = chained
    if last:
        pieces = [refs.pop(0), refs.pop(0)]
    else:
        acc_hbm = refs.pop(0)
    extra_ref = None if closing else refs.pop(0)
    token = refs.pop(0)
    token[...] = jnp.zeros(token.shape, F32)
    (
        rows, qts, mixts, dots, wkt, kt, values, qpad, dpad, dqt, dk, dv, ebuf, acc, proj,
        extra, table, sems, io_sems, out_sem, acc_sem,
    ) = refs
    base = group * gcols
    mine = pl.ds(base, gcols)
    length = len_ref[seq]
    total = length + MEM
    n_tiles = cdiv(length, TILE)
    chunks = cdiv(total, TILE)
    pairs = [
        (x_hbm.at[seq], rows.at[pl.ds(0, seq_rows), :]),
        (qt_hbm.at[mine, :], qts),
        (mixt_hbm.at[mine, :], mixts),
        (dot_hbm.at[seq, mine, :], dots),
    ]
    loads = [pltpu.make_async_copy(a, b, io_sems.at[i]) for i, (a, b) in enumerate(pairs)]

    def copies_of(kr):
        def copies(tile, slot):
            return pltpu.make_async_copy(
                e_hbm.at[tile, pl.ds(group * gp * 2, gp * 2), pl.ds(0, kr), :],
                ebuf.at[slot, :, pl.ds(0, kr), :],
                sems.at[slot],
            )

        return copies

    for copy in loads:
        copy.start()
    if chained:
        fetch = pltpu.make_async_copy(acc_in, acc, acc_sem)
        fetch.start()
    for_size(seq_rows, total, lambda kr: copies_of(kr)(0, 0).start())
    memory = memory_rows(vec_ref)
    bias_v = vec_ref[MEM + 1 : MEM + 2, base : base + gcols].astype(F32)
    wkt[...] = wk_ref[...].T
    if chained:
        extra[...] = extra_in[...]
        for other in other_rows:
            extra[...] += other[...]
    else:
        acc[...] = jnp.zeros(acc.shape, F32)
        extra[...] = jnp.zeros(extra.shape, F32)
    for head in range(gp * 2):
        spare = HDIM * (1 - head % 2)
        qpad[head, spare : spare + HDIM, :] = jnp.zeros((HDIM, TILE), BF16)
        dpad[head, spare : spare + HDIM, :] = jnp.zeros((HDIM, TILE), BF16)
    rows[seq_rows:, :] = jnp.zeros((rows.shape[0] - seq_rows, D), BF16)
    loads[0].wait()
    edge = pl.multiple_of(length // 128 * 128, 128)
    fix = pl.ds(edge, TILE)
    pick_memory(rows, memory, length)

    def project(chunk, _):
        here = pl.ds(pl.multiple_of(chunk * TILE, TILE), TILE)
        joined = rows[here, :]
        value_rows = (nn(joined, wv_ref[...]) + bias_v).astype(BF16)
        for pair in range(gp):
            values[pair, here, :] = value_rows[:, pair * 128 : pair * 128 + 128]
            dk[pair, here, :] = jnp.zeros((TILE, 128), F32)
            dv[pair, here, :] = jnp.zeros((TILE, 128), F32)
        kt[:, here] = nt(wkt[...], joined).astype(BF16)
        dqt[:, here] = jnp.zeros((gcols, TILE), BF16)
        return 0

    lax.fori_loop(0, chunks, project, 0)
    for copy in loads[1:]:
        copy.wait()

    def attend(kr):
        copies = copies_of(kr)

        def step(tile, _):
            slot = lax.rem(tile, 2)
            here = pl.ds(pl.multiple_of(tile * TILE, TILE), TILE)

            @pl.when(tile + 1 < n_tiles)
            def _():
                copies(tile + 1, 1 - slot).start()

            copies(tile, slot).wait()
            inners = []
            for head in range(gp * 2):
                low = (head % 2) * HDIM
                local = slice(head * HDIM, (head + 1) * HDIM)
                outer = dots[local, here]
                dpad[head, low : low + HDIM, :] = outer
                qpad[head, low : low + HDIM, :] = qts[local, here]
                inners.append(col_sum(outer.astype(F32) * mixts[local, here].astype(F32)))

            def outer_product(head):
                return nn(values[head // 2, :kr, :], dpad[head])

            live = {head: outer_product(head) for head in range(AHEAD)}
            grads = []
            for head in range(gp * 2):
                pair = head // 2
                product = live.pop(head)
                if head + AHEAD < gp * 2:
                    live[head + AHEAD] = outer_product(head + AHEAD)
                local = slice(head * HDIM, (head + 1) * HDIM)
                grad = (
                    ebuf[slot, head, :kr, :].astype(F32) * (product - inners[head])
                ).astype(BF16)
                grads.append(grad)
                dqt[local, here] = (nn(kt[local, :kr], grad) * SCALE).astype(BF16)
                if head % 2:
                    both = [ebuf[slot, h, :kr, :] for h in (head - 1, head)]
                    dv[pair, :kr, :] += nt(
                        jnp.concatenate(both, 1),
                        jnp.concatenate([dpad[head - 1], dpad[head]], 1),
                    )
                    dk[pair, :kr, :] += nt(
                        jnp.concatenate(grads[-2:], 1),
                        jnp.concatenate([qpad[head - 1], qpad[head]], 1),
                    )
            return 0

        lax.fori_loop(0, n_tiles, step, 0)

    for_size(seq_rows, total, attend)
    if chained:
        fetch.wait()

    def send(chunk):
        here = pl.ds(pl.multiple_of(chunk * TILE, TILE), TILE)
        return pltpu.make_async_copy(proj.at[here, :], proj_hbm.at[here, :], out_sem)

    def finish(chunk, sums):
        here = pl.ds(pl.multiple_of(chunk * TILE, TILE), TILE)
        parts = [dqt[:, here].T]
        parts += [(dk[pair, here, :] * LN2).astype(BF16) for pair in range(gp)]
        parts += [dv[pair, here, :].astype(BF16) for pair in range(gp)]
        grad = jnp.concatenate(parts, 1)
        proj[here, :] = grad
        send(chunk).start()
        acc[...] += tn(rows[here, :], grad)
        return sums + col_sum(grad.astype(F32))

    sums = lax.fori_loop(0, chunks, finish, jnp.zeros((1, width), F32))
    if not last:
        store = pltpu.make_async_copy(acc, acc_hbm, acc_sem)
        store.start()
    extra[MEM : MEM + 1, base : base + gcols] += sums[:, :gcols]
    extra[MEM + 1 : MEM + 2, base : base + gcols] += sums[:, 2 * gcols :]
    turned = (
        lax.broadcasted_iota(jnp.int32, (32, TILE), 1) + (edge - length)
        == lax.broadcasted_iota(jnp.int32, (32, TILE), 0)
    )
    turned = jnp.logical_and(turned, lax.broadcasted_iota(jnp.int32, (32, TILE), 0) < MEM)
    turned = jnp.where(turned, 1.0, 0.0).astype(BF16)
    found_k = jnp.concatenate([dk[pair, fix, :] * LN2 for pair in range(gp)], 1)
    found_v = jnp.concatenate([dv[pair, fix, :] for pair in range(gp)], 1)
    grad_memory = nt(nn(turned, found_k.astype(BF16)).astype(BF16), wk_ref[...])
    grad_memory += nt(nn(turned, found_v.astype(BF16)).astype(BF16), wv_ref[...])
    extra[...] += grad_memory

    if last:
        me = me_ref[0]
        part, few = D // shards, 32 // shards
        if closing:
            for s in range(shards):
                table[s, :few, :] = extra[s * few : (s + 1) * few]
        for m, piece, row in piece_spots(pieces, shards, part):
            spot = slice(row, row + part)
            at = pl.multiple_of((me ^ m) * part, part)
            piece[spot, :width] = acc[pl.ds(at, part), :].astype(BF16)
            if closing:
                mine_rows = table[me ^ m]
                lanes = [mine_rows[:, j : j + 128] for j in range(0, D, 128)]
                empty = part - mine_rows.shape[0] * len(lanes)
                if empty:
                    lanes.append(jnp.zeros((empty, 128), F32))
                piece[spot, width:] = jnp.concatenate(lanes, 0).astype(BF16)
    else:
        store.wait()
    if extra_ref is not None:
        extra_ref[...] = extra[...]

    def drain(chunk, _):
        send(chunk).wait()
        return 0

    lax.fori_loop(0, chunks, drain, 0)


def attention_backward(
    seq, group, groups, shards, lengths, me, w_qkv, vectors, x, dot, qt, mixt, expo,
    chain=(), others=(), after=(),
):
    seq_rows = x.shape[1]
    top = key_sizes(seq_rows)[-1]
    padded = cdiv(seq_rows + MEM, TILE) * TILE
    gp = PAIRS // groups
    gcols = gp * 128
    width = 3 * gcols
    vm = pl.BlockSpec(memory_space=pltpu.VMEM)
    hbm = pl.BlockSpec(memory_space=pl.ANY)
    smem = pl.BlockSpec(memory_space=pltpu.SMEM)
    out_shape = [jax.ShapeDtypeStruct((padded, width), BF16)]
    out_specs = [hbm]
    if chain:
        wide = width + (128 if others else 0)
        out_shape += [jax.ShapeDtypeStruct((D // 2, wide), BF16)] * 2
        out_specs += [vm] * 2
    else:
        out_shape += [jax.ShapeDtypeStruct((D, width), F32)]
        out_specs += [hbm]
    if not others:
        out_shape += [jax.ShapeDtypeStruct((32, D), F32)]
        out_specs += [vm]
    out_shape += [jax.ShapeDtypeStruct((8, 128), F32)]
    out_specs += [vm]
    return pl.pallas_call(
        partial(
            bwd_kernel, seq_rows, groups, group, seq, shards, bool(chain), len(others),
            len(after),
        ),
        out_shape=tuple(out_shape),
        grid=(1,),
        in_specs=[
            smem,
            smem,
            pl.BlockSpec((D, gcols), lambda i: (0, groups + group)),
            pl.BlockSpec((D, gcols), lambda i: (0, 2 * groups + group)),
            vm,
        ]
        + [hbm] * 5
        + ([hbm, vm] if chain else [])
        + [vm] * len(others)
        + [hbm] * len(after),
        out_specs=tuple(out_specs),
        scratch_shapes=[
            pltpu.VMEM((padded, D), BF16),
            pltpu.VMEM((gcols, seq_rows), BF16),
            pltpu.VMEM((gcols, seq_rows), BF16),
            pltpu.VMEM((gcols, seq_rows), BF16),
            pltpu.VMEM((gcols, D), BF16),
            pltpu.VMEM((gcols, padded), BF16),
            pltpu.VMEM((gp, padded, 128), BF16),
            pltpu.VMEM((gp * 2, 128, TILE), BF16),
            pltpu.VMEM((gp * 2, 128, TILE), BF16),
            pltpu.VMEM((gcols, padded), BF16),
            pltpu.VMEM((gp, padded, 128), F32),
            pltpu.VMEM((gp, padded, 128), F32),
            pltpu.VMEM((2, gp * 2, top, TILE), BF16),
            pltpu.VMEM((D, width), F32),
            pltpu.VMEM((padded, width), BF16),
            pltpu.VMEM((32, D), F32),
            pltpu.VMEM((shards, max(8, 32 // shards), D), F32),
            pltpu.SemaphoreType.DMA((2,)),
            pltpu.SemaphoreType.DMA((4,)),
            pltpu.SemaphoreType.DMA,
            pltpu.SemaphoreType.DMA,
        ],
        compiler_params=pltpu.CompilerParams(vmem_limit_bytes=62 * 2**20),
        cost_estimate=pl.CostEstimate(
            flops=8 * 10**9, bytes_accessed=15 * 10**6, transcendentals=0
        ),
        name="attention_backward",
    )(lengths, me, w_qkv, w_qkv, vectors, x, dot, qt, mixt, expo, *chain, *others, *after)


def input_kernel(seq_rows, groups, seq, len_ref, w_ref, gh_hbm, *refs):
    projs = refs[:groups]
    gx_hbm, token, gh, blocks, rows, sems, out_sem = refs[-7:]
    token[...] = jnp.zeros(token.shape, F32)
    gcols = D // groups
    length = len_ref[seq]
    chunks = cdiv(length, TILE)
    whole = seq_rows // TILE

    def spot(chunk):
        return pl.ds(pl.multiple_of(chunk * TILE, TILE), TILE)

    def fetch(chunk):
        here = spot(chunk)
        return [pltpu.make_async_copy(gh_hbm.at[seq, here, :], gh.at[here, :], sems.at[chunk, 0])] + [
            pltpu.make_async_copy(p.at[here, :], blocks.at[i, here, :], sems.at[chunk, 1 + i])
            for i, p in enumerate(projs)
        ]

    def send(chunk):
        here = spot(chunk)
        return pltpu.make_async_copy(rows.at[here, :], gx_hbm.at[seq, here, :], out_sem)

    def begin(chunk, _):
        for copy in fetch(chunk):
            copy.start()
        return 0

    lax.fori_loop(0, chunks, begin, 0)

    def empty(chunk, _):
        rows[spot(chunk), :] = jnp.zeros((TILE, D), BF16)
        send(chunk).start()
        return 0

    lax.fori_loop(chunks, whole, empty, 0)

    def step(chunk, _):
        here = spot(chunk)
        for copy in fetch(chunk):
            copy.wait()
        joint = jnp.concatenate(
            [
                blocks[g, here, kind * gcols : (kind + 1) * gcols]
                for kind in range(3)
                for g in range(groups)
            ],
            1,
        )
        grad = nt(joint, w_ref[...])
        row = lax.broadcasted_iota(jnp.int32, (TILE, 1), 0) + chunk * TILE
        rows[here, :] = jnp.where(row < length, grad + gh[here, :].astype(F32), 0.0).astype(BF16)
        send(chunk).start()
        return 0

    lax.fori_loop(0, chunks, step, 0)
    pltpu.make_async_copy(rows, gx_hbm.at[seq], out_sem).wait()


def input_gradient(seq, lengths, w_qkv, gh, projs, after=(), base=None):
    count, seq_rows = gh.shape[:2]
    groups = len(projs)
    hbm = pl.BlockSpec(memory_space=pl.ANY)
    vm = pl.BlockSpec(memory_space=pltpu.VMEM)
    base = () if base is None else (base,)
    return pl.pallas_call(
        partial(input_kernel, seq_rows, groups, seq),
        out_shape=(
            jax.ShapeDtypeStruct((count, seq_rows, D), BF16),
            jax.ShapeDtypeStruct((8, 128), F32),
        ),
        in_specs=[pl.BlockSpec(memory_space=pltpu.SMEM), vm]
        + [hbm] * (1 + groups + len(after) + len(base)),
        out_specs=(hbm, vm),
        input_output_aliases={3 + groups + len(after): 0} if base else {},
        scratch_shapes=[
            pltpu.VMEM((seq_rows, D), BF16),
            pltpu.VMEM((groups, seq_rows, 3 * D // groups), BF16),
            pltpu.VMEM((seq_rows, D), BF16),
            pltpu.SemaphoreType.DMA((seq_rows // TILE, 1 + groups)),
            pltpu.SemaphoreType.DMA,
        ],
        compiler_params=pltpu.CompilerParams(vmem_limit_bytes=VMEM_LIMIT),
        cost_estimate=pl.CostEstimate(
            flops=2 * 10**9, bytes_accessed=7 * 10**6, transcendentals=0
        ),
        name="input_gradient",
    )(lengths, w_qkv, gh, *projs, *after, *base)


GROUPS = 2


def powers(size):
    return [1 << i for i in range(size.bit_length() - 1)]


def exchange(value, axis, size, bit):
    return lax.ppermute(value, axis, [(i, i ^ bit) for i in range(size)])


def far_pieces(value, axis, size):
    pieces = {0: value}
    for bit in reversed(powers(size)[1:]):
        for mask in sorted(pieces):
            pieces[mask | bit] = exchange(pieces[mask], axis, size, bit)
    return pieces


def near_pieces(pieces, axis, size):
    pieces = dict(pieces)
    for mask in sorted(pieces):
        pieces[mask | 1] = exchange(pieces[mask], axis, size, 1)
    return [pieces[mask] for mask in range(size)]


def held_until(pieces, event):
    keys = list(pieces)
    return dict(zip(keys, lax.optimization_barrier((*[pieces[k] for k in keys], event))))


def combine_kernel(counts, modes, waits, carried, place_ref, *refs):
    refs = list(refs)
    arrays = [[[refs.pop(0) for _ in range(c)] for c in group] for group in counts]
    refs = refs[waits:]
    total = refs.pop()
    refs = refs[: len(refs) - carried]
    token = refs.pop()
    token[...] = jnp.zeros(token.shape, F32)
    place = place_ref[0]
    for groups, (mode, stacked, cols) in zip(arrays, modes):
        rows = sum(group[0].shape[0] for group in groups)
        if mode == "halves":
            half = rows // 2
            for side in range(2):
                add_rows(groups[0], side * half, half, refs.pop(0), 0, cols)
        elif mode == "parts":
            base = 0
            for group in groups:
                more = group[0].shape[0]
                add_rows(group, 0, more, total, base, cols)
                base += more
            one = rows // stacked
            part = one // GROUP
            for m in range(GROUP):
                target = refs.pop(0)
                at = pl.multiple_of((place ^ m) * part, part)
                for i in range(stacked):
                    target[i * part : (i + 1) * part, :] = total[
                        pl.ds(at + i * one, part), :cols
                    ].astype(BF16)
        else:
            add_rows(groups[0], 0, rows, refs.pop(0), 0, cols)


def add_rows(group, start, rows, target, base, cols):
    wide = group[0].shape[1]
    step = next((s for s in (64, 32, 16) if not (rows % s or start % s or base % s)), rows)

    def add(index, _):
        def at(first):
            if step == rows:
                return pl.ds(first, rows)
            return pl.ds(pl.multiple_of(first + index * step, step), step)

        value = group[0][at(start), :].astype(F32)
        for other in group[1:]:
            value = value + other[at(start), :].astype(F32)
        target[at(base), :wide] = value.astype(target.dtype)
        if wide < cols:
            target[at(base), wide:cols] = jnp.zeros((step, cols - wide), target.dtype)
        return 0

    lax.fori_loop(0, rows // step, add, 0)


def combine(place, items, after, carry=()):
    vm = pl.BlockSpec(memory_space=pltpu.VMEM)
    shapes, flat, modes, most = [], [], [], 0
    for groups, mode, stacked in items:
        rows = sum(arrays[0].shape[0] for arrays in groups)
        cols = max(arrays[0].shape[1] for arrays in groups)
        flat += [a for arrays in groups for a in arrays]
        modes.append((mode, stacked, cols))
        most = max(most, rows)
        if mode == "halves":
            shapes += [(rows // 2, cols)] * 2
        elif mode == "parts":
            shapes += [(rows // GROUP, cols)] * GROUP
        else:
            shapes += [(rows, cols)]
    size = sum(a.size for a in flat) * 2
    outs = pl.pallas_call(
        partial(
            combine_kernel,
            [[len(g) for g in i[0]] for i in items],
            modes,
            len(after) + len(carry),
            len(carry),
        ),
        out_shape=tuple(jax.ShapeDtypeStruct(s, BF16) for s in shapes)
        + (jax.ShapeDtypeStruct((8, 128), F32),)
        + tuple(jax.ShapeDtypeStruct(a.shape, a.dtype) for a in carry),
        in_specs=[pl.BlockSpec(memory_space=pltpu.SMEM)]
        + [vm] * len(flat)
        + [pl.BlockSpec(memory_space=pl.ANY)] * (len(after) + len(carry)),
        out_specs=(vm,) * (len(shapes) + 1)
        + (pl.BlockSpec(memory_space=pl.ANY),) * len(carry),
        input_output_aliases={
            1 + len(flat) + len(after) + i: len(shapes) + 1 + i for i in range(len(carry))
        },
        scratch_shapes=[pltpu.VMEM((most, max(m[2] for m in modes)), F32)],
        compiler_params=pltpu.CompilerParams(vmem_limit_bytes=24 * 2**20),
        cost_estimate=pl.CostEstimate(flops=size, bytes_accessed=2 * size, transcendentals=0),
        name="combine",
    )(place, *flat, *after, *carry)
    held = list(outs[len(shapes) + 1 :])
    outs, token, results = list(outs[: len(shapes)]), outs[len(shapes)], []
    for mode, _, _ in modes:
        taken = {"halves": 2, "parts": GROUP, "whole": 1}[mode]
        results.append([outs.pop(0) for _ in range(taken)])
    return results, [token, *held]


GROUP = 4


class Stream:
    def __init__(self, value, sizes, steps, stacked=None):
        self.value, self.steps = list(value), list(steps)
        self.reps, self.shards = sizes
        self.stacked = stacked or max(self.shards // 2, 1)

    def exchange(self):
        kind, bit = self.steps.pop(0)
        value = self.value
        if kind == "fold":
            arrays = [value[0], exchange(value[1], "shard", self.shards, bit)]
        elif kind == "group":
            arrays = [value[0]] + [
                exchange(value[j], "rep", self.reps, j) for j in range(1, GROUP)
            ]
        else:
            arrays = [value[0], exchange(value[0], "rep", self.reps, bit)]
        follow = self.steps[0][0] if self.steps else "end"
        item = ([arrays], {"fold": "halves", "group": "parts"}.get(follow, "whole"), self.stacked)
        if follow == "fold":
            self.stacked //= 2
        return item

    def alone(self, place, after=()):
        (self.value,), token = combine(place, [self.exchange()], after)
        return token


def advance(place, streams, items, after, carry=()):
    results, token = combine(place, items, after, carry)
    for stream, result in zip(streams, results):
        stream.value = result
    return token


def whole_parts(stream):
    own = stream.value[0]
    return [own] + [exchange(own, "rep", stream.reps, j) for j in range(1, GROUP)]


def spread_kernel(shards, place_ref, *refs):
    refs = list(refs)
    arrays = [[refs.pop(0) for _ in range(GROUP)] for _ in range(3)]
    qkv_ref, out_ref, in_ref, back_ref, vec_ref, table = refs
    place = place_ref[0]

    def put(target, parts, cols, first=0, count=None):
        part = count or parts[0].shape[0]
        for m in range(GROUP):
            at = pl.multiple_of((place ^ m) * part, part)
            target[pl.ds(at, part), :cols] = parts[m][first : first + part, :].astype(F32)

    part = D // shards
    put(back_ref, arrays[1], D)
    put(table, arrays[0], D)
    out_ref[...] = table[:part, :D]
    for j in range(BLOCKS):
        in_ref[:, j * D : (j + 1) * D] = table[(1 + j) * part : (2 + j) * part, :D]
    gcols = D // GROUPS
    for g in range(GROUPS):
        put(table, arrays[2], 3 * gcols + 128, g * part // GROUP, part // GROUP)
        for kind in range(3):
            at = kind * D + g * gcols
            qkv_ref[:, at : at + gcols] = table[:part, kind * gcols : (kind + 1) * gcols]
    few = 32 // shards
    width = 3 * gcols
    step = max(8, few)
    for j in range(D // 128):
        vec_ref[:, j * 128 : (j + 1) * 128] = table[j * step : j * step + few, width : width + 128]


def spread(place, shards, parts):
    part = D // shards
    vm = pl.BlockSpec(memory_space=pltpu.VMEM)
    shapes = ((part, 3 * D), (part, D), (part, FF), (FF // shards, D), (32 // shards, D))
    most = max(part * (1 + BLOCKS), part), max(p.shape[1] for p in parts)
    return pl.pallas_call(
        partial(spread_kernel, shards),
        out_shape=tuple(jax.ShapeDtypeStruct(s, F32) for s in shapes),
        in_specs=[pl.BlockSpec(memory_space=pltpu.SMEM)] + [vm] * len(parts),
        out_specs=(vm,) * len(shapes),
        scratch_shapes=[pltpu.VMEM(most, F32)],
        compiler_params=pltpu.CompilerParams(vmem_limit_bytes=24 * 2**20),
        name="spread",
    )(place, *parts)


def body(sizes, inputs, lengths, w_qkv, w_out, w_in, w_back, vectors, cotangent):
    reps, shards = sizes
    count = inputs.shape[0]
    me = lax.axis_index("shard").astype(jnp.int32).reshape(1)

    axis = ("shard", shards)
    far = far_pieces(pack(w_qkv, vectors), *axis)
    start = held_until(
        {0: jnp.concatenate([w_out, w_in], 1), 1: w_back}, far[max(far)]
    )
    far_up, far_back = far_pieces(start[0], *axis), far_pieces(start[1], *axis)
    whole, wqt, wvt, table = prepare(me, near_pieces(far, *axis))
    fwd = [
        attention_forward(s, lengths, inputs, whole, wqt, wvt, table) for s in range(count)
    ]
    far_up, far_back = held_until(far_up, fwd[-1][3]), held_until(far_back, fwd[-1][3])
    out, gh, dot, *grads, sums = feed_forward(
        lengths, me, inputs, cotangent, [f[2] for f in fwd], [f[3] for f in fwd],
        near_pieces(far_up, *axis), near_pieces(far_back, *axis), table,
    )
    place = (lax.axis_index("rep") % GROUP).astype(jnp.int32).reshape(1)
    folds = [("fold", bit) for bit in powers(shards)]
    group = [("group", 0)]
    rest = [("full", bit) for bit in powers(reps) if bit >= GROUP]
    tall = Stream(grads[:2], sizes, folds + group + rest)
    deep = Stream(grads[2:], sizes, folds[:1] + group + folds[1:] + rest)
    projs = [[None] * GROUPS for _ in range(count)]
    quarters = [None] * GROUPS
    extras, after, calls = [], [], []
    for g in range(GROUPS):
        chain = ()
        for s in range(count):
            closing = [sums] + extras if s == count - 1 and g == GROUPS - 1 else ()
            busy = [
                (tall, deep), (tall, deep), (tall, quarters[0]), (deep, quarters[0], tall)
            ][len(calls)]
            items = [stream.exchange() for stream in busy]
            res = attention_backward(
                s, g, GROUPS, shards, lengths, me, whole, table, inputs, dot, fwd[s][1],
                fwd[s][2], fwd[s][0], chain, closing, after,
            )
            chain = list(res[1:-1])
            carry = chain[1:2] if len(calls) == 3 else []
            after, *held = advance(place, busy, items, [res[-1]], carry)
            after = [after]
            chain[1 : 1 + len(held)] = held
            projs[s][g] = res[0]
            calls.append(res)
        quarters[g] = Stream(chain[:2], sizes, folds + [("stop", 0)])
        extras += chain[2:]
    early, last = quarters
    for stream, left in ((early, 1), (tall, 0), (deep, 1)):
        while len(stream.steps) > left:
            stream.alone(place)
    tall_parts = whole_parts(tall)
    end = deep.exchange()
    after = []
    while len(last.steps) > 2:
        after = last.alone(place)
    gx, token = input_gradient(0, lengths, whole, gh, projs[0], after)
    final = last.exchange()[0]
    both = Stream([], sizes, group + rest, stacked=GROUPS)
    after = advance(
        place, [both, deep], [([early.value] + final, "parts", GROUPS), end], [token]
    )
    for seq in range(1, count):
        gx, token = input_gradient(seq, lengths, whole, gh, projs[seq], after, gx)
    both.alone(place, [token] + tall_parts[1:])
    deep_parts = whole_parts(deep)
    while both.steps:
        both.alone(place)
    return (out, gx, *spread(place, shards, tall_parts + deep_parts + whole_parts(both)))


def solution(mesh):
    data = P(("rep", "shard"), None, None)
    rows = P("shard", None)
    return jax.shard_map(
        partial(body, (mesh.shape["rep"], mesh.shape["shard"])),
        mesh=mesh,
        in_specs=(data, P(("rep", "shard")), rows, rows, rows, rows, rows, data),
        out_specs=(data, data, rows, rows, rows, rows, rows),
        check_vma=False,
    )
```

```python
import math
from functools import partial

import jax
import jax.numpy as jnp
from jax import lax
from jax.experimental import pallas as pl
from jax.experimental.pallas import tpu as pltpu
from jax.sharding import PartitionSpec as P

D = 512
HEADS = 8
HDIM = 64
FF = 2048
MEM = 20
TILE = 256
PAIRS = HEADS // 2
SCALE = HDIM**-0.5
QSCALE = SCALE * math.log2(math.e)
LN2 = math.log(2.0)
F32 = jnp.float32
BF16 = jnp.bfloat16
VROWS = 80
VMEM_LIMIT = 62 * 2**20


def nn(a, b):
    return lax.dot_general(a, b, (((1,), (0,)), ((), ())), preferred_element_type=F32)


def nt(a, b):
    return lax.dot_general(a, b, (((1,), (1,)), ((), ())), preferred_element_type=F32)


def tn(a, b):
    return lax.dot_general(a, b, (((0,), (0,)), ((), ())), preferred_element_type=F32)


def key_sizes(seq_rows):
    top = -(-(seq_rows + MEM) // 32) * 32
    return [rows for rows in range(512, top, 256)] + [top]


def column_max(values):
    parts = [values[i : i + 128] for i in range(0, values.shape[0] - 127, 128)]
    while len(parts) > 1:
        odd = parts[len(parts) - len(parts) % 2 :]
        parts = [jnp.maximum(a, b) for a, b in zip(parts[::2], parts[1::2])] + odd
    top = jnp.max(parts[0], axis=0, keepdims=True)
    rest = values.shape[0] % 128
    if rest:
        top = jnp.maximum(top, jnp.max(values[-rest:], axis=0, keepdims=True))
    return top


AHEAD = 2
BODY_HEADS = 4


def cdiv(a, b):
    return (a + b - 1) // b


def pick_memory(rows_ref, memory, length):
    edge = pl.multiple_of(length // 128 * 128, 128)
    fix = pl.ds(edge, TILE)
    row = lax.broadcasted_iota(jnp.int32, (TILE, 1), 0) + edge
    lane = lax.broadcasted_iota(jnp.int32, (TILE, 32), 1)
    pick = lax.broadcasted_iota(jnp.int32, (TILE, 32), 0) + (edge - length) == lane
    placed = nn(jnp.where(pick, 1.0, 0.0).astype(BF16), memory)
    rows_ref[fix, :] = jnp.where(row < length, rows_ref[fix, :].astype(F32), placed).astype(BF16)


def memory_rows(vec_ref):
    inside = lax.broadcasted_iota(jnp.int32, (32, D), 0) < MEM
    return jnp.where(inside, vec_ref[...].astype(F32), 0.0).astype(BF16)


def for_size(seq_rows, total, run):
    sizes = key_sizes(seq_rows)
    for index, kr in enumerate(sizes):
        least = sizes[index - 1] if index else 0

        @pl.when(jnp.logical_and(total > least, total <= kr))
        def _(kr=kr):
            run(kr)


def prepare_kernel(shards, me_ref, *refs):
    pieces = refs[:shards]
    w_ref, wqt_ref, wvt_ref, vec_ref, few_rows, sems = refs[shards:]
    me = me_ref[0]
    part, few = D // shards, 32 // shards
    copies, small = [], []
    for m in range(shards):
        at = pl.multiple_of((me ^ m) * part, part)
        small.append(
            pltpu.make_async_copy(
                pieces[m].at[pl.ds(part, SPARE), pl.ds(0, D)], few_rows.at[m], sems.at[m, 1]
            )
        )
        copies.append(
            pltpu.make_async_copy(
                pieces[m].at[pl.ds(0, part), :], w_ref.at[pl.ds(at, part), :], sems.at[m, 0]
            )
        )
    for copy in small + copies:
        copy.start()
    for copy in small:
        copy.wait()
    owner = lax.broadcasted_iota(jnp.int32, (32, D), 0) // few
    rows = jnp.zeros((32, D), F32)
    for m in range(shards):
        values = few_rows[m].astype(F32)[:few]
        rows = jnp.where(owner == (me ^ m), jnp.concatenate([values] * shards, 0), rows)
    vec_ref[...] = rows.astype(BF16)
    for copy in copies:
        copy.wait()
    wqt_ref[...] = w_ref[:, :D].T
    wvt_ref[...] = w_ref[:, 2 * D :].T


SPARE = 16


def pack(w_qkv, vectors):
    below = ((0, SPARE - vectors.shape[0]), (0, w_qkv.shape[1] - vectors.shape[1]))
    return jnp.concatenate([w_qkv, jnp.pad(vectors, below)], 0)


def prepare(me, pieces):
    shards = len(pieces)
    vm = pl.BlockSpec(memory_space=pltpu.VMEM)
    return pl.pallas_call(
        partial(prepare_kernel, shards),
        out_shape=(
            jax.ShapeDtypeStruct((D, 3 * D), BF16),
            jax.ShapeDtypeStruct((D, D), BF16),
            jax.ShapeDtypeStruct((D, D), BF16),
            jax.ShapeDtypeStruct((32, D), BF16),
        ),
        in_specs=[pl.BlockSpec(memory_space=pltpu.SMEM)]
        + [pl.BlockSpec(memory_space=pl.ANY)] * shards,
        out_specs=(vm, vm, vm, vm),
        scratch_shapes=[
            pltpu.VMEM((shards, SPARE, D), BF16),
            pltpu.SemaphoreType.DMA((shards, 2)),
        ],
        compiler_params=pltpu.CompilerParams(vmem_limit_bytes=24 * 2**20),
        name="prepare",
    )(me, *pieces)


def fwd_kernel(
    seq_rows, seq, len_ref, x_hbm, wk_ref, wqt_ref, wvt_ref, vec_ref,
    e_hbm, qt_hbm, mixt_hbm, inv_ref,
    rows, keys, vt, qpad, queries, mixed_t, ebuf, sems, io_sems,
):
    length = len_ref[seq]
    total = length + MEM
    load = pltpu.make_async_copy(x_hbm.at[seq], rows.at[pl.ds(0, seq_rows), :], io_sems.at[0])
    load.start()
    memory = memory_rows(vec_ref)
    vec_cols = vec_ref[...].astype(F32).T
    bias_q = vec_cols[:, MEM : MEM + 1]
    bias_v = vec_cols[:, MEM + 1 : MEM + 2]
    mixed_t[...] = jnp.zeros(mixed_t.shape, BF16)
    inv_ref[...] = jnp.zeros(inv_ref.shape, F32)
    for head in range(HEADS):
        spare = HDIM * (1 - head % 2)
        qpad[head, spare : spare + HDIM, :] = jnp.zeros((HDIM, qpad.shape[2]), BF16)
    vt[:, HDIM:, :] = jnp.ones((HEADS, VROWS - HDIM, vt.shape[2]), BF16)
    n_tiles = cdiv(length, TILE)
    chunks = cdiv(total, TILE)
    load.wait()

    rows[seq_rows:, :] = jnp.zeros((rows.shape[0] - seq_rows, D), BF16)
    pick_memory(rows, memory, length)

    def project(chunk, _):
        here = pl.ds(pl.multiple_of(chunk * TILE, TILE), TILE)
        joined = rows[here, :]
        key_rows = nn(joined, wk_ref[...]).astype(BF16)
        for pair in range(PAIRS):
            keys[pair, here, :] = key_rows[:, pair * 128 : pair * 128 + 128]
        values = (nt(wvt_ref[...], joined) + bias_v).astype(BF16)
        found = ((nt(wqt_ref[...], joined) + bias_q) * QSCALE).astype(BF16)
        queries[:, here] = found
        for head in range(HEADS):
            low = (head % 2) * HDIM
            vt[head, :HDIM, here] = values[head * HDIM : (head + 1) * HDIM]
            qpad[head, low : low + HDIM, here] = found[head * HDIM : (head + 1) * HDIM]
        return 0

    lax.fori_loop(0, chunks, project, 0)
    save = pltpu.make_async_copy(queries.at[:, pl.ds(0, seq_rows)], qt_hbm, io_sems.at[1])
    save.start()

    def attend(kr):
        tail = kr - TILE if kr % TILE == 0 else kr - kr % TILE
        row = lax.broadcasted_iota(jnp.int32, (kr - tail, TILE), 0) + tail
        mask = row < total

        def copies(tile, pair):
            return pltpu.make_async_copy(
                ebuf.at[pair, :, pl.ds(0, kr), :],
                e_hbm.at[tile, pl.ds(pair * 2, 2), pl.ds(0, kr), :],
                sems.at[pair],
            )

        turns = HEADS // BODY_HEADS

        def step(unit, _):
            tile, turn = unit // turns, unit % turns
            here = pl.ds(pl.multiple_of(tile * TILE, TILE), TILE)
            base = turn * BODY_HEADS

            def score(i):
                pair = turn * (BODY_HEADS // 2) + i // 2
                scores = nn(keys[pair, :kr, :], qpad[base + i, :, here])
                scores = jnp.concatenate(
                    [scores[:tail], jnp.where(mask, scores[tail:], -1e30)], 0
                )
                return scores, column_max(scores)

            live = {i: score(i) for i in range(AHEAD)}
            for i in range(BODY_HEADS):
                pair, sub = turn * (BODY_HEADS // 2) + i // 2, i % 2
                scores, top = live.pop(i)
                if sub == 0:
                    copies(tile, pair).wait()
                if i + AHEAD < BODY_HEADS:
                    live[i + AHEAD] = score(i + AHEAD)
                expo = jnp.exp2(scores - top).astype(BF16)
                ebuf[pair, sub, :kr, :] = expo
                mixed = nn(vt[base + i, :, :kr], expo)
                inverse = 1.0 / mixed[HDIM : HDIM + 1]
                spot = pl.ds(pl.multiple_of((base + i) * HDIM, HDIM), HDIM)
                mixed_t[spot, here] = (mixed[:HDIM] * inverse).astype(BF16)
                inv_ref[pl.ds(base + i, 1), here] = inverse
                if sub == 1:
                    copies(tile, pair).start()
            return 0

        for pair in range(PAIRS):
            copies(0, pair).start()
        lax.fori_loop(0, n_tiles * turns, step, 0)
        out = pltpu.make_async_copy(mixed_t, mixt_hbm, io_sems.at[2])
        out.start()
        for pair in range(PAIRS):
            copies(n_tiles - 1, pair).wait()
        save.wait()
        out.wait()

    for_size(seq_rows, total, attend)


def attention_forward(seq, lengths, x, w_qkv, wqt, wvt, vectors):
    seq_rows = x.shape[1]
    top = key_sizes(seq_rows)[-1]
    padded = cdiv(seq_rows + MEM, TILE) * TILE
    tiles = seq_rows // TILE
    vm = pl.BlockSpec(memory_space=pltpu.VMEM)
    hbm = pl.BlockSpec(memory_space=pl.ANY)
    return pl.pallas_call(
        partial(fwd_kernel, seq_rows, seq),
        out_shape=(
            jax.ShapeDtypeStruct((tiles, HEADS, top, TILE), BF16),
            jax.ShapeDtypeStruct((D, seq_rows), BF16),
            jax.ShapeDtypeStruct((D, seq_rows), BF16),
            jax.ShapeDtypeStruct((HEADS, seq_rows), F32),
        ),
        grid=(1,),
        in_specs=[
            pl.BlockSpec(memory_space=pltpu.SMEM),
            hbm,
            pl.BlockSpec((D, D), lambda i: (0, 1)),
            vm,
            vm,
            vm,
        ],
        out_specs=(hbm, hbm, hbm, vm),
        scratch_shapes=[
            pltpu.VMEM((padded, D), BF16),
            pltpu.VMEM((PAIRS, padded, 128), BF16),
            pltpu.VMEM((HEADS, VROWS, padded), BF16),
            pltpu.VMEM((HEADS, 128, padded), BF16),
            pltpu.VMEM((D, padded), BF16),
            pltpu.VMEM((D, seq_rows), BF16),
            pltpu.VMEM((PAIRS, 2, top, TILE), BF16),
            pltpu.SemaphoreType.DMA((PAIRS,)),
            pltpu.SemaphoreType.DMA((3,)),
        ],
        compiler_params=pltpu.CompilerParams(vmem_limit_bytes=44 * 2**20),
        cost_estimate=pl.CostEstimate(
            flops=8 * 10**9, bytes_accessed=24 * 10**6, transcendentals=8 * 10**6
        ),
        name="attention_forward",
    )(lengths, x, w_qkv, wqt, wvt, vectors)


def norm_forward(values):
    center = values - jnp.mean(values, axis=-1, keepdims=True)
    inverse = lax.rsqrt(jnp.mean(center * center, axis=-1, keepdims=True) + 1e-05)
    return center * inverse, inverse


def norm_backward(grad, normed, inverse):
    return inverse * (
        grad
        - jnp.mean(grad, axis=-1, keepdims=True)
        - normed * jnp.mean(grad * normed, axis=-1, keepdims=True)
    )


def col_sum(values):
    return jnp.sum(values, axis=0, keepdims=True)


GELU_A = math.sqrt(2.0 / math.pi)
GELU_B = GELU_A * 0.044715
BLOCKS = FF // D


def piece_order(shards):
    bits = shards.bit_length() - 1
    return [int(format(i, "b").zfill(bits)[::-1], 2) if bits else 0 for i in range(shards)]


def piece_spots(pair, shards, rows):
    half = max(shards // 2, 1)
    for index, m in enumerate(piece_order(shards)):
        yield m, pair[index // half], index % half * rows


def ffn_kernel(
    seq_rows, shards, len_ref, me_ref, x_hbm, cot_hbm, mixt0, mixt1, inv0, inv1, *refs,
):
    wi_p, wb_p = refs[:shards], refs[shards : 2 * shards]
    vec_ref, out_hbm, gh_hbm, dot_hbm = refs[2 * shards : 2 * shards + 4]
    grads = refs[2 * shards + 4 : 2 * shards + 8]
    (
        sums_ref, x_ref, cot_ref, mixt_ref, inv_ref, wo_ref, wi_ref, wb_ref,
        out_ref, gh_ref, dot_ref, acc_o, acc_i, acc_b, slopes, actives,
        s_normed1, s_first, s_gsecond, ups, sems, out_sems,
    ) = refs[2 * shards + 8 :]
    half = TILE // 2
    len0, len1 = len_ref[0], len_ref[1]
    me = me_ref[0]
    n0, n1 = cdiv(len0, half), cdiv(len1, half)
    full = seq_rows // half
    n_all = n0 + n1

    def rows_at(piece, rows):
        return pl.ds(pl.multiple_of((me ^ piece) * rows, rows), rows)

    loads = []

    def load(src, dst):
        copy = pltpu.make_async_copy(src, dst, sems.at[len(loads)])
        loads.append(copy)
        copy.start()
        return copy

    first_loads = [load(mixt0, mixt_ref.at[0]), load(mixt1, mixt_ref.at[1])]
    first_loads += [load(inv0, inv_ref.at[0]), load(inv1, inv_ref.at[1])]
    part = D // shards
    first_loads += [
        load(p.at[:, pl.ds(0, D)], wo_ref.at[rows_at(i, part), :]) for i, p in enumerate(wi_p)
    ]
    first_loads += [load(x_hbm.at[s], x_ref.at[s]) for s in range(2)]
    second_loads = [
        load(p.at[:, pl.ds(D, FF)], wi_ref.at[rows_at(i, part), :]) for i, p in enumerate(wi_p)
    ]
    second_loads += [load(p, wb_ref.at[rows_at(i, FF // shards), :]) for i, p in enumerate(wb_p)]
    third_loads = [load(cot_hbm.at[s], cot_ref.at[s]) for s in range(2)]

    out_ref[...] = jnp.zeros(out_ref.shape, BF16)
    gh_ref[...] = jnp.zeros(gh_ref.shape, BF16)
    dot_ref[...] = jnp.zeros(dot_ref.shape, BF16)
    acc_o[...] = jnp.zeros(acc_o.shape, F32)
    acc_i[...] = jnp.zeros(acc_i.shape, F32)
    acc_b[...] = jnp.zeros(acc_b.shape, F32)
    sums_ref[...] = jnp.zeros(sums_ref.shape, F32)

    def vec(index):
        return vec_ref[index : index + 1, :].astype(F32)

    bias_out = vec(MEM + 2)
    bias_back = vec(MEM + 3 + BLOCKS)
    gain_one = vec(MEM + 4 + BLOCKS)
    shift_one = vec(MEM + 5 + BLOCKS)
    gain_two = vec(MEM + 6 + BLOCKS)
    shift_two = vec(MEM + 7 + BLOCKS)

    spare_one = jnp.logical_and(n_all % 2 == 1, n1 < full)
    spare_zero = jnp.logical_and(n_all % 2 == 1, n1 >= full)

    def place(chunk):
        second = chunk >= n0
        inside = jnp.where(second, chunk - n0, chunk)
        spare = chunk >= n_all
        seq = jnp.where(spare, jnp.where(n1 < full, 1, 0), jnp.where(second, 1, 0))
        inside = jnp.where(spare, jnp.where(n1 < full, n1, n0), inside)
        return seq, pl.multiple_of(inside * half, half), jnp.where(seq == 1, len1, len0)

    def rows_of(ref, spots):
        return jnp.concatenate([ref[s, pl.ds(r, half), :] for s, r, _ in spots], 0)

    def lanes_of(ref, spots):
        return jnp.concatenate([ref[s, :, pl.ds(r, half)] for s, r, _ in spots], 1)

    def put_rows(ref, value, spots):
        for i, (s, r, _) in enumerate(spots):
            ref[s, pl.ds(r, half), :] = value[i * half : (i + 1) * half]

    def put_lanes(ref, value, spots):
        for i, (s, r, _) in enumerate(spots):
            ref[s, :, pl.ds(r, half)] = value[:, i * half : (i + 1) * half]

    def valid_of(spots):
        iota = lax.broadcasted_iota(jnp.int32, (half, 1), 0)
        return jnp.concatenate(
            [jnp.where(iota + r < count, 1.0, 0.0) for _, r, count in spots], 0
        )

    def add_sum(row, value):
        sums_ref[row : row + 1] += col_sum(value)

    def whole_tile(spots):
        count = half * len(spots)
        here = slice(0, count)
        valid = valid_of(spots)
        mixt = lanes_of(mixt_ref, spots)
        attn = nn(mixt.T, wo_ref[...]) + bias_out
        normed_one, inverse_one = norm_forward(rows_of(x_ref, spots).astype(F32) + attn)
        first = normed_one * gain_one + shift_one
        s_normed1[here] = normed_one
        low = first.astype(BF16)
        s_first[here] = low
        second = first + bias_back
        for j in range(BLOCKS):
            cols = slice(j * D, (j + 1) * D)
            up = nn(low, wi_ref[:, cols]) + vec(MEM + 3 + j)
            square = up * up
            bent = jnp.tanh(up * (GELU_A + GELU_B * square))
            gate = 0.5 + 0.5 * bent
            active = up * gate
            slopes[here, cols] = (
                gate + active * (1.0 - bent) * (GELU_A + 3.0 * GELU_B * square)
            ).astype(slopes.dtype)
            actives[here, cols] = active.astype(BF16)
        second = second + nn(actives[here, :], wb_ref[...])
        normed_two, inverse_two = norm_forward(second)
        put_rows(out_ref, ((normed_two * gain_two + shift_two) * valid).astype(BF16), spots)
        grad_out = rows_of(cot_ref, spots).astype(F32) * valid
        add_sum(MEM + 6 + BLOCKS, grad_out * normed_two)
        add_sum(MEM + 7 + BLOCKS, grad_out)
        grad_second = norm_backward(grad_out * gain_two, normed_two, inverse_two)
        s_gsecond[here] = grad_second
        down = grad_second.astype(BF16)
        add_sum(MEM + 3 + BLOCKS, down.astype(F32))
        low_t = s_first[here, :].T
        for j in range(BLOCKS):
            cols = slice(j * D, (j + 1) * D)
            grad_up = (
                nt(down, wb_ref[cols, :]) * slopes[here, cols].astype(F32)
            ).astype(BF16)
            ups[here, cols] = grad_up
            add_sum(MEM + 3 + j, grad_up.astype(F32))
        grad_first = s_gsecond[here] + nt(ups[here, :], wi_ref[...])
        for j in range(BLOCKS):
            cols = slice(j * D, (j + 1) * D)
            acc_b[cols, :] += tn(actives[here, cols], down)
            acc_i[:, cols] += nn(low_t, ups[here, cols])
        normed_one = s_normed1[here]
        add_sum(MEM + 4 + BLOCKS, grad_first * normed_one)
        add_sum(MEM + 5 + BLOCKS, grad_first)
        grad_one = norm_backward(grad_first * gain_one, normed_one, inverse_one)
        low = grad_one.astype(BF16)
        put_rows(gh_ref, low, spots)
        add_sum(MEM + 2, low.astype(F32))
        acc_o[...] += nn(mixt, low)
        grad_mixed = nt(wo_ref[...], low)
        inverse = lanes_of(inv_ref, spots)
        scaled = [
            grad_mixed[h * HDIM : (h + 1) * HDIM] * inverse[h : h + 1] for h in range(HEADS)
        ]
        put_lanes(dot_ref, jnp.concatenate(scaled, 0).astype(BF16), spots)

    def send(ref, hbm, sem, seq, row, lanes=False):
        here = pl.ds(row, half)
        src = ref.at[seq, :, here] if lanes else ref.at[seq, here, :]
        dst = hbm.at[seq, :, here] if lanes else hbm.at[seq, here, :]
        pltpu.make_async_copy(src, dst, out_sems.at[sem]).start()

    def send_all(seq, row):
        send(out_ref, out_hbm, 0, seq, row)
        send(gh_ref, gh_hbm, 1, seq, row)
        send(dot_ref, dot_hbm, 2, seq, row, True)

    for copy in first_loads + second_loads + third_loads:
        copy.wait()

    def step(index, _):
        spots = [place(index * 4 + i) for i in range(4)]
        whole_tile(spots)
        for seq, row, _ in spots:
            send_all(seq, row)
        return 0

    left = lax.rem(n_all, 4)
    bigs = n_all // 4 + jnp.where(left == 3, 1, 0)
    lax.fori_loop(0, bigs, step, 0)

    @pl.when(jnp.logical_or(left == 1, left == 2))
    def _():
        spots = [place(bigs * 4 + i) for i in range(2)]
        whole_tile(spots)
        for seq, row, _ in spots:
            send_all(seq, row)

    def rest(seq):
        def one(chunk, _):
            send_all(seq, pl.multiple_of(chunk * half, half))
            return 0

        return one

    lax.fori_loop(n0 + jnp.where(spare_zero, 1, 0), full, rest(0), 0)
    lax.fori_loop(n1 + jnp.where(spare_one, 1, 0), full, rest(1), 0)

    part = D // shards
    deep = FF // shards
    block = part * (1 + BLOCKS)
    for m, piece, row in piece_spots(grads[:2], shards, block):
        at = pl.multiple_of((me ^ m) * part, part)
        piece[row : row + part, :] = acc_o[pl.ds(at, part), :].astype(BF16)
        for j in range(BLOCKS):
            row += part
            piece[row : row + part, :] = acc_i[
                pl.ds(at, part), j * D : (j + 1) * D
            ].astype(BF16)
    for m, piece, row in piece_spots(grads[2:], shards, deep):
        at = pl.multiple_of((me ^ m) * deep, deep)
        piece[row : row + deep, :] = acc_b[pl.ds(at, deep), :].astype(BF16)
    for ref, hbm, sem in ((out_ref, out_hbm, 0), (gh_ref, gh_hbm, 1), (dot_ref, dot_hbm, 2)):
        pltpu.make_async_copy(ref, hbm, out_sems.at[sem]).wait()


def feed_forward(lengths, me, x, cot, mixts, invs, w_up, w_back, vectors):
    count, seq_rows = x.shape[:2]
    shards = len(w_up)
    vm = pl.BlockSpec(memory_space=pltpu.VMEM)
    hbm = pl.BlockSpec(memory_space=pl.ANY)
    smem = pl.BlockSpec(memory_space=pltpu.SMEM)
    return pl.pallas_call(
        partial(ffn_kernel, seq_rows, shards),
        out_shape=(
            jax.ShapeDtypeStruct((count, seq_rows, D), BF16),
            jax.ShapeDtypeStruct((count, seq_rows, D), BF16),
            jax.ShapeDtypeStruct((count, D, seq_rows), BF16),
            *[
                jax.ShapeDtypeStruct((rows, D), BF16)
                for rows in (D * (1 + BLOCKS) // 2, FF // 2)
                for _ in range(2)
            ],
            jax.ShapeDtypeStruct((32, D), F32),
        ),
        in_specs=[smem, smem] + [hbm] * (6 + 2 * shards) + [vm],
        out_specs=(hbm, hbm, hbm) + (vm,) * 5,
        scratch_shapes=[
            pltpu.VMEM((count, seq_rows, D), BF16),
            pltpu.VMEM((count, seq_rows, D), BF16),
            pltpu.VMEM((count, D, seq_rows), BF16),
            pltpu.VMEM((count, HEADS, seq_rows), F32),
            pltpu.VMEM((D, D), BF16),
            pltpu.VMEM((D, FF), BF16),
            pltpu.VMEM((FF, D), BF16),
            pltpu.VMEM((count, seq_rows, D), BF16),
            pltpu.VMEM((count, seq_rows, D), BF16),
            pltpu.VMEM((count, D, seq_rows), BF16),
            pltpu.VMEM((D, D), F32),
            pltpu.VMEM((D, FF), F32),
            pltpu.VMEM((FF, D), F32),
            pltpu.VMEM((2 * TILE, FF), BF16),
            pltpu.VMEM((2 * TILE, FF), BF16),
            pltpu.VMEM((2 * TILE, D), F32),
            pltpu.VMEM((2 * TILE, D), BF16),
            pltpu.VMEM((2 * TILE, D), F32),
            pltpu.VMEM((2 * TILE, FF), BF16),
            pltpu.SemaphoreType.DMA((8 + 3 * shards,)),
            pltpu.SemaphoreType.DMA((3,)),
        ],
        compiler_params=pltpu.CompilerParams(vmem_limit_bytes=56 * 2**20),
        cost_estimate=pl.CostEstimate(
            flops=27 * 10**9, bytes_accessed=24 * 10**6, transcendentals=4 * 10**6
        ),
        name="feed_forward",
    )(lengths, me, x, cot, *mixts, *invs, *w_up, *w_back, vectors)


def bwd_kernel(seq_rows, groups, group, seq, shards, chained, closing, waits, *refs):
    gp = PAIRS // groups
    gcols = gp * 128
    width = 3 * gcols
    refs = list(refs)
    len_ref, me_ref, wk_ref, wv_ref, vec_ref = refs[:5]
    x_hbm, dot_hbm, qt_hbm, mixt_hbm, e_hbm = refs[5:10]
    refs = refs[10:]
    acc_in, extra_in = (refs.pop(0), refs.pop(0)) if chained else (None, None)
    other_rows = [refs.pop(0) for _ in range(closing)]
    refs = refs[waits:]
    proj_hbm = refs.pop(0)
    last = chained
    if last:
        pieces = [refs.pop(0), refs.pop(0)]
    else:
        acc_hbm = refs.pop(0)
    extra_ref = None if closing else refs.pop(0)
    token = refs.pop(0)
    token[...] = jnp.zeros(token.shape, F32)
    (
        rows, qts, mixts, dots, wkt, kt, values, qpad, dpad, dqt, dk, dv, ebuf, acc, proj,
        extra, table, sems, io_sems, out_sem, acc_sem,
    ) = refs
    base = group * gcols
    mine = pl.ds(base, gcols)
    length = len_ref[seq]
    total = length + MEM
    n_tiles = cdiv(length, TILE)
    chunks = cdiv(total, TILE)
    pairs = [
        (x_hbm.at[seq], rows.at[pl.ds(0, seq_rows), :]),
        (qt_hbm.at[mine, :], qts),
        (mixt_hbm.at[mine, :], mixts),
        (dot_hbm.at[seq, mine, :], dots),
    ]
    loads = [pltpu.make_async_copy(a, b, io_sems.at[i]) for i, (a, b) in enumerate(pairs)]

    def copies_of(kr):
        def copies(tile, slot):
            return pltpu.make_async_copy(
                e_hbm.at[tile, pl.ds(group * gp * 2, gp * 2), pl.ds(0, kr), :],
                ebuf.at[slot, :, pl.ds(0, kr), :],
                sems.at[slot],
            )

        return copies

    for copy in loads:
        copy.start()
    if chained:
        fetch = pltpu.make_async_copy(acc_in, acc, acc_sem)
        fetch.start()
    for_size(seq_rows, total, lambda kr: copies_of(kr)(0, 0).start())
    memory = memory_rows(vec_ref)
    bias_v = vec_ref[MEM + 1 : MEM + 2, base : base + gcols].astype(F32)
    wkt[...] = wk_ref[...].T
    if chained:
        extra[...] = extra_in[...]
        for other in other_rows:
            extra[...] += other[...]
    else:
        acc[...] = jnp.zeros(acc.shape, F32)
        extra[...] = jnp.zeros(extra.shape, F32)
    for head in range(gp * 2):
        spare = HDIM * (1 - head % 2)
        qpad[head, spare : spare + HDIM, :] = jnp.zeros((HDIM, TILE), BF16)
        dpad[head, spare : spare + HDIM, :] = jnp.zeros((HDIM, TILE), BF16)
    rows[seq_rows:, :] = jnp.zeros((rows.shape[0] - seq_rows, D), BF16)
    loads[0].wait()
    edge = pl.multiple_of(length // 128 * 128, 128)
    fix = pl.ds(edge, TILE)
    pick_memory(rows, memory, length)

    def project(chunk, _):
        here = pl.ds(pl.multiple_of(chunk * TILE, TILE), TILE)
        joined = rows[here, :]
        value_rows = (nn(joined, wv_ref[...]) + bias_v).astype(BF16)
        for pair in range(gp):
            values[pair, here, :] = value_rows[:, pair * 128 : pair * 128 + 128]
            dk[pair, here, :] = jnp.zeros((TILE, 128), F32)
            dv[pair, here, :] = jnp.zeros((TILE, 128), F32)
        kt[:, here] = nt(wkt[...], joined).astype(BF16)
        dqt[:, here] = jnp.zeros((gcols, TILE), BF16)
        return 0

    lax.fori_loop(0, chunks, project, 0)
    for copy in loads[1:]:
        copy.wait()

    def attend(kr):
        copies = copies_of(kr)

        def step(tile, _):
            slot = lax.rem(tile, 2)
            here = pl.ds(pl.multiple_of(tile * TILE, TILE), TILE)

            @pl.when(tile + 1 < n_tiles)
            def _():
                copies(tile + 1, 1 - slot).start()

            copies(tile, slot).wait()
            inners = []
            for head in range(gp * 2):
                low = (head % 2) * HDIM
                local = slice(head * HDIM, (head + 1) * HDIM)
                outer = dots[local, here]
                dpad[head, low : low + HDIM, :] = outer
                qpad[head, low : low + HDIM, :] = qts[local, here]
                inners.append(col_sum(outer.astype(F32) * mixts[local, here].astype(F32)))

            def outer_product(head):
                return nn(values[head // 2, :kr, :], dpad[head])

            live = {head: outer_product(head) for head in range(AHEAD)}
            grads = []
            for head in range(gp * 2):
                pair = head // 2
                product = live.pop(head)
                if head + AHEAD < gp * 2:
                    live[head + AHEAD] = outer_product(head + AHEAD)
                local = slice(head * HDIM, (head + 1) * HDIM)
                grad = (
                    ebuf[slot, head, :kr, :].astype(F32) * (product - inners[head])
                ).astype(BF16)
                grads.append(grad)
                dqt[local, here] = (nn(kt[local, :kr], grad) * SCALE).astype(BF16)
                if head % 2:
                    both = [ebuf[slot, h, :kr, :] for h in (head - 1, head)]
                    dv[pair, :kr, :] += nt(
                        jnp.concatenate(both, 1),
                        jnp.concatenate([dpad[head - 1], dpad[head]], 1),
                    )
                    dk[pair, :kr, :] += nt(
                        jnp.concatenate(grads[-2:], 1),
                        jnp.concatenate([qpad[head - 1], qpad[head]], 1),
                    )
            return 0

        lax.fori_loop(0, n_tiles, step, 0)

    for_size(seq_rows, total, attend)
    if chained:
        fetch.wait()

    def send(chunk):
        here = pl.ds(pl.multiple_of(chunk * TILE, TILE), TILE)
        return pltpu.make_async_copy(proj.at[here, :], proj_hbm.at[here, :], out_sem)

    def finish(chunk, sums):
        here = pl.ds(pl.multiple_of(chunk * TILE, TILE), TILE)
        parts = [dqt[:, here].T]
        parts += [(dk[pair, here, :] * LN2).astype(BF16) for pair in range(gp)]
        parts += [dv[pair, here, :].astype(BF16) for pair in range(gp)]
        grad = jnp.concatenate(parts, 1)
        proj[here, :] = grad
        send(chunk).start()
        acc[...] += tn(rows[here, :], grad)
        return sums + col_sum(grad.astype(F32))

    sums = lax.fori_loop(0, chunks, finish, jnp.zeros((1, width), F32))
    if not last:
        store = pltpu.make_async_copy(acc, acc_hbm, acc_sem)
        store.start()
    extra[MEM : MEM + 1, base : base + gcols] += sums[:, :gcols]
    extra[MEM + 1 : MEM + 2, base : base + gcols] += sums[:, 2 * gcols :]
    turned = (
        lax.broadcasted_iota(jnp.int32, (32, TILE), 1) + (edge - length)
        == lax.broadcasted_iota(jnp.int32, (32, TILE), 0)
    )
    turned = jnp.logical_and(turned, lax.broadcasted_iota(jnp.int32, (32, TILE), 0) < MEM)
    turned = jnp.where(turned, 1.0, 0.0).astype(BF16)
    found_k = jnp.concatenate([dk[pair, fix, :] * LN2 for pair in range(gp)], 1)
    found_v = jnp.concatenate([dv[pair, fix, :] for pair in range(gp)], 1)
    grad_memory = nt(nn(turned, found_k.astype(BF16)).astype(BF16), wk_ref[...])
    grad_memory += nt(nn(turned, found_v.astype(BF16)).astype(BF16), wv_ref[...])
    extra[...] += grad_memory

    if last:
        me = me_ref[0]
        part, few = D // shards, 32 // shards
        if closing:
            for s in range(shards):
                table[s, :few, :] = extra[s * few : (s + 1) * few]
        for m, piece, row in piece_spots(pieces, shards, part):
            spot = slice(row, row + part)
            at = pl.multiple_of((me ^ m) * part, part)
            piece[spot, :width] = acc[pl.ds(at, part), :].astype(BF16)
            if closing:
                mine_rows = table[me ^ m]
                lanes = [mine_rows[:, j : j + 128] for j in range(0, D, 128)]
                empty = part - mine_rows.shape[0] * len(lanes)
                if empty:
                    lanes.append(jnp.zeros((empty, 128), F32))
                piece[spot, width:] = jnp.concatenate(lanes, 0).astype(BF16)
    else:
        store.wait()
    if extra_ref is not None:
        extra_ref[...] = extra[...]

    def drain(chunk, _):
        send(chunk).wait()
        return 0

    lax.fori_loop(0, chunks, drain, 0)


def attention_backward(
    seq, group, groups, shards, lengths, me, w_qkv, vectors, x, dot, qt, mixt, expo,
    chain=(), others=(), after=(),
):
    seq_rows = x.shape[1]
    top = key_sizes(seq_rows)[-1]
    padded = cdiv(seq_rows + MEM, TILE) * TILE
    gp = PAIRS // groups
    gcols = gp * 128
    width = 3 * gcols
    vm = pl.BlockSpec(memory_space=pltpu.VMEM)
    hbm = pl.BlockSpec(memory_space=pl.ANY)
    smem = pl.BlockSpec(memory_space=pltpu.SMEM)
    out_shape = [jax.ShapeDtypeStruct((padded, width), BF16)]
    out_specs = [hbm]
    if chain:
        wide = width + (128 if others else 0)
        out_shape += [jax.ShapeDtypeStruct((D // 2, wide), BF16)] * 2
        out_specs += [vm] * 2
    else:
        out_shape += [jax.ShapeDtypeStruct((D, width), F32)]
        out_specs += [hbm]
    if not others:
        out_shape += [jax.ShapeDtypeStruct((32, D), F32)]
        out_specs += [vm]
    out_shape += [jax.ShapeDtypeStruct((8, 128), F32)]
    out_specs += [vm]
    return pl.pallas_call(
        partial(
            bwd_kernel, seq_rows, groups, group, seq, shards, bool(chain), len(others),
            len(after),
        ),
        out_shape=tuple(out_shape),
        grid=(1,),
        in_specs=[
            smem,
            smem,
            pl.BlockSpec((D, gcols), lambda i: (0, groups + group)),
            pl.BlockSpec((D, gcols), lambda i: (0, 2 * groups + group)),
            vm,
        ]
        + [hbm] * 5
        + ([hbm, vm] if chain else [])
        + [vm] * len(others)
        + [hbm] * len(after),
        out_specs=tuple(out_specs),
        scratch_shapes=[
            pltpu.VMEM((padded, D), BF16),
            pltpu.VMEM((gcols, seq_rows), BF16),
            pltpu.VMEM((gcols, seq_rows), BF16),
            pltpu.VMEM((gcols, seq_rows), BF16),
            pltpu.VMEM((gcols, D), BF16),
            pltpu.VMEM((gcols, padded), BF16),
            pltpu.VMEM((gp, padded, 128), BF16),
            pltpu.VMEM((gp * 2, 128, TILE), BF16),
            pltpu.VMEM((gp * 2, 128, TILE), BF16),
            pltpu.VMEM((gcols, padded), BF16),
            pltpu.VMEM((gp, padded, 128), F32),
            pltpu.VMEM((gp, padded, 128), F32),
            pltpu.VMEM((2, gp * 2, top, TILE), BF16),
            pltpu.VMEM((D, width), F32),
            pltpu.VMEM((padded, width), BF16),
            pltpu.VMEM((32, D), F32),
            pltpu.VMEM((shards, max(8, 32 // shards), D), F32),
            pltpu.SemaphoreType.DMA((2,)),
            pltpu.SemaphoreType.DMA((4,)),
            pltpu.SemaphoreType.DMA,
            pltpu.SemaphoreType.DMA,
        ],
        compiler_params=pltpu.CompilerParams(vmem_limit_bytes=62 * 2**20),
        cost_estimate=pl.CostEstimate(
            flops=8 * 10**9, bytes_accessed=15 * 10**6, transcendentals=0
        ),
        name="attention_backward",
    )(lengths, me, w_qkv, w_qkv, vectors, x, dot, qt, mixt, expo, *chain, *others, *after)


def input_kernel(seq_rows, groups, seq, len_ref, w_ref, gh_hbm, *refs):
    projs = refs[:groups]
    gx_hbm, token, gh, blocks, rows, sems, out_sem = refs[-7:]
    token[...] = jnp.zeros(token.shape, F32)
    gcols = D // groups
    length = len_ref[seq]
    chunks = cdiv(length, TILE)
    whole = seq_rows // TILE

    def spot(chunk):
        return pl.ds(pl.multiple_of(chunk * TILE, TILE), TILE)

    def fetch(chunk):
        here = spot(chunk)
        return [pltpu.make_async_copy(gh_hbm.at[seq, here, :], gh.at[here, :], sems.at[chunk, 0])] + [
            pltpu.make_async_copy(p.at[here, :], blocks.at[i, here, :], sems.at[chunk, 1 + i])
            for i, p in enumerate(projs)
        ]

    def send(chunk):
        here = spot(chunk)
        return pltpu.make_async_copy(rows.at[here, :], gx_hbm.at[seq, here, :], out_sem)

    def begin(chunk, _):
        for copy in fetch(chunk):
            copy.start()
        return 0

    lax.fori_loop(0, chunks, begin, 0)

    def empty(chunk, _):
        rows[spot(chunk), :] = jnp.zeros((TILE, D), BF16)
        send(chunk).start()
        return 0

    lax.fori_loop(chunks, whole, empty, 0)

    def step(chunk, _):
        here = spot(chunk)
        for copy in fetch(chunk):
            copy.wait()
        joint = jnp.concatenate(
            [
                blocks[g, here, kind * gcols : (kind + 1) * gcols]
                for kind in range(3)
                for g in range(groups)
            ],
            1,
        )
        grad = nt(joint, w_ref[...])
        row = lax.broadcasted_iota(jnp.int32, (TILE, 1), 0) + chunk * TILE
        rows[here, :] = jnp.where(row < length, grad + gh[here, :].astype(F32), 0.0).astype(BF16)
        send(chunk).start()
        return 0

    lax.fori_loop(0, chunks, step, 0)
    pltpu.make_async_copy(rows, gx_hbm.at[seq], out_sem).wait()


def input_gradient(seq, lengths, w_qkv, gh, projs, after=(), base=None):
    count, seq_rows = gh.shape[:2]
    groups = len(projs)
    hbm = pl.BlockSpec(memory_space=pl.ANY)
    vm = pl.BlockSpec(memory_space=pltpu.VMEM)
    base = () if base is None else (base,)
    return pl.pallas_call(
        partial(input_kernel, seq_rows, groups, seq),
        out_shape=(
            jax.ShapeDtypeStruct((count, seq_rows, D), BF16),
            jax.ShapeDtypeStruct((8, 128), F32),
        ),
        in_specs=[pl.BlockSpec(memory_space=pltpu.SMEM), vm]
        + [hbm] * (1 + groups + len(after) + len(base)),
        out_specs=(hbm, vm),
        input_output_aliases={3 + groups + len(after): 0} if base else {},
        scratch_shapes=[
            pltpu.VMEM((seq_rows, D), BF16),
            pltpu.VMEM((groups, seq_rows, 3 * D // groups), BF16),
            pltpu.VMEM((seq_rows, D), BF16),
            pltpu.SemaphoreType.DMA((seq_rows // TILE, 1 + groups)),
            pltpu.SemaphoreType.DMA,
        ],
        compiler_params=pltpu.CompilerParams(vmem_limit_bytes=VMEM_LIMIT),
        cost_estimate=pl.CostEstimate(
            flops=2 * 10**9, bytes_accessed=7 * 10**6, transcendentals=0
        ),
        name="input_gradient",
    )(lengths, w_qkv, gh, *projs, *after, *base)


GROUPS = 2


def powers(size):
    return [1 << i for i in range(size.bit_length() - 1)]


def exchange(value, axis, size, bit):
    return lax.ppermute(value, axis, [(i, i ^ bit) for i in range(size)])


def far_pieces(value, axis, size):
    pieces = {0: value}
    for bit in reversed(powers(size)[1:]):
        for mask in sorted(pieces):
            pieces[mask | bit] = exchange(pieces[mask], axis, size, bit)
    return pieces


def near_pieces(pieces, axis, size):
    pieces = dict(pieces)
    for mask in sorted(pieces):
        pieces[mask | 1] = exchange(pieces[mask], axis, size, 1)
    return [pieces[mask] for mask in range(size)]


def held_until(pieces, event):
    keys = list(pieces)
    return dict(zip(keys, lax.optimization_barrier((*[pieces[k] for k in keys], event))))


def combine_kernel(counts, modes, waits, carried, place_ref, *refs):
    refs = list(refs)
    arrays = [[[refs.pop(0) for _ in range(c)] for c in group] for group in counts]
    refs = refs[waits:]
    total = refs.pop()
    refs = refs[: len(refs) - carried]
    token = refs.pop()
    token[...] = jnp.zeros(token.shape, F32)
    place = place_ref[0]
    for groups, (mode, stacked, cols) in zip(arrays, modes):
        rows = sum(group[0].shape[0] for group in groups)
        if mode == "halves":
            half = rows // 2
            for side in range(2):
                add_rows(groups[0], side * half, half, refs.pop(0), 0, cols)
        elif mode == "parts":
            base = 0
            for group in groups:
                more = group[0].shape[0]
                add_rows(group, 0, more, total, base, cols)
                base += more
            one = rows // stacked
            part = one // GROUP
            for m in range(GROUP):
                target = refs.pop(0)
                at = pl.multiple_of((place ^ m) * part, part)
                for i in range(stacked):
                    target[i * part : (i + 1) * part, :] = total[
                        pl.ds(at + i * one, part), :cols
                    ].astype(BF16)
        else:
            add_rows(groups[0], 0, rows, refs.pop(0), 0, cols)


def add_rows(group, start, rows, target, base, cols):
    wide = group[0].shape[1]
    step = next((s for s in (64, 32, 16) if not (rows % s or start % s or base % s)), rows)

    def add(index, _):
        def at(first):
            if step == rows:
                return pl.ds(first, rows)
            return pl.ds(pl.multiple_of(first + index * step, step), step)

        value = group[0][at(start), :].astype(F32)
        for other in group[1:]:
            value = value + other[at(start), :].astype(F32)
        target[at(base), :wide] = value.astype(target.dtype)
        if wide < cols:
            target[at(base), wide:cols] = jnp.zeros((step, cols - wide), target.dtype)
        return 0

    lax.fori_loop(0, rows // step, add, 0)


def combine(place, items, after, carry=()):
    vm = pl.BlockSpec(memory_space=pltpu.VMEM)
    shapes, flat, modes, most = [], [], [], 0
    for groups, mode, stacked in items:
        rows = sum(arrays[0].shape[0] for arrays in groups)
        cols = max(arrays[0].shape[1] for arrays in groups)
        flat += [a for arrays in groups for a in arrays]
        modes.append((mode, stacked, cols))
        most = max(most, rows)
        if mode == "halves":
            shapes += [(rows // 2, cols)] * 2
        elif mode == "parts":
            shapes += [(rows // GROUP, cols)] * GROUP
        else:
            shapes += [(rows, cols)]
    size = sum(a.size for a in flat) * 2
    outs = pl.pallas_call(
        partial(
            combine_kernel,
            [[len(g) for g in i[0]] for i in items],
            modes,
            len(after) + len(carry),
            len(carry),
        ),
        out_shape=tuple(jax.ShapeDtypeStruct(s, BF16) for s in shapes)
        + (jax.ShapeDtypeStruct((8, 128), F32),)
        + tuple(jax.ShapeDtypeStruct(a.shape, a.dtype) for a in carry),
        in_specs=[pl.BlockSpec(memory_space=pltpu.SMEM)]
        + [vm] * len(flat)
        + [pl.BlockSpec(memory_space=pl.ANY)] * (len(after) + len(carry)),
        out_specs=(vm,) * (len(shapes) + 1)
        + (pl.BlockSpec(memory_space=pl.ANY),) * len(carry),
        input_output_aliases={
            1 + len(flat) + len(after) + i: len(shapes) + 1 + i for i in range(len(carry))
        },
        scratch_shapes=[pltpu.VMEM((most, max(m[2] for m in modes)), F32)],
        compiler_params=pltpu.CompilerParams(vmem_limit_bytes=24 * 2**20),
        cost_estimate=pl.CostEstimate(flops=size, bytes_accessed=2 * size, transcendentals=0),
        name="combine",
    )(place, *flat, *after, *carry)
    held = list(outs[len(shapes) + 1 :])
    outs, token, results = list(outs[: len(shapes)]), outs[len(shapes)], []
    for mode, _, _ in modes:
        taken = {"halves": 2, "parts": GROUP, "whole": 1}[mode]
        results.append([outs.pop(0) for _ in range(taken)])
    return results, [token, *held]


GROUP = 4


class Stream:
    def __init__(self, value, sizes, steps, stacked=None):
        self.value, self.steps = list(value), list(steps)
        self.reps, self.shards = sizes
        self.stacked = stacked or max(self.shards // 2, 1)

    def exchange(self):
        kind, bit = self.steps.pop(0)
        value = self.value
        if kind == "fold":
            arrays = [value[0], exchange(value[1], "shard", self.shards, bit)]
        elif kind == "group":
            arrays = [value[0]] + [
                exchange(value[j], "rep", self.reps, j) for j in range(1, GROUP)
            ]
        else:
            arrays = [value[0], exchange(value[0], "rep", self.reps, bit)]
        follow = self.steps[0][0] if self.steps else "end"
        item = ([arrays], {"fold": "halves", "group": "parts"}.get(follow, "whole"), self.stacked)
        if follow == "fold":
            self.stacked //= 2
        return item

    def alone(self, place, after=()):
        (self.value,), token = combine(place, [self.exchange()], after)
        return token


def advance(place, streams, items, after, carry=()):
    results, token = combine(place, items, after, carry)
    for stream, result in zip(streams, results):
        stream.value = result
    return token


def whole_parts(stream):
    own = stream.value[0]
    return [own] + [exchange(own, "rep", stream.reps, j) for j in range(1, GROUP)]


def spread_kernel(shards, place_ref, *refs):
    refs = list(refs)
    arrays = [[refs.pop(0) for _ in range(GROUP)] for _ in range(3)]
    qkv_ref, out_ref, in_ref, back_ref, vec_ref, table = refs
    place = place_ref[0]

    def put(target, parts, cols, first=0, count=None):
        part = count or parts[0].shape[0]
        for m in range(GROUP):
            at = pl.multiple_of((place ^ m) * part, part)
            target[pl.ds(at, part), :cols] = parts[m][first : first + part, :].astype(F32)

    part = D // shards
    put(back_ref, arrays[1], D)
    put(table, arrays[0], D)
    out_ref[...] = table[:part, :D]
    for j in range(BLOCKS):
        in_ref[:, j * D : (j + 1) * D] = table[(1 + j) * part : (2 + j) * part, :D]
    gcols = D // GROUPS
    for g in range(GROUPS):
        put(table, arrays[2], 3 * gcols + 128, g * part // GROUP, part // GROUP)
        for kind in range(3):
            at = kind * D + g * gcols
            qkv_ref[:, at : at + gcols] = table[:part, kind * gcols : (kind + 1) * gcols]
    few = 32 // shards
    width = 3 * gcols
    step = max(8, few)
    for j in range(D // 128):
        vec_ref[:, j * 128 : (j + 1) * 128] = table[j * step : j * step + few, width : width + 128]


def spread(place, shards, parts):
    part = D // shards
    vm = pl.BlockSpec(memory_space=pltpu.VMEM)
    shapes = ((part, 3 * D), (part, D), (part, FF), (FF // shards, D), (32 // shards, D))
    most = max(part * (1 + BLOCKS), part), max(p.shape[1] for p in parts)
    return pl.pallas_call(
        partial(spread_kernel, shards),
        out_shape=tuple(jax.ShapeDtypeStruct(s, F32) for s in shapes),
        in_specs=[pl.BlockSpec(memory_space=pltpu.SMEM)] + [vm] * len(parts),
        out_specs=(vm,) * len(shapes),
        scratch_shapes=[pltpu.VMEM(most, F32)],
        compiler_params=pltpu.CompilerParams(vmem_limit_bytes=24 * 2**20),
        name="spread",
    )(place, *parts)


def body(sizes, inputs, lengths, w_qkv, w_out, w_in, w_back, vectors, cotangent):
    reps, shards = sizes
    count = inputs.shape[0]
    me = lax.axis_index("shard").astype(jnp.int32).reshape(1)

    axis = ("shard", shards)
    far = far_pieces(pack(w_qkv, vectors), *axis)
    start = held_until({0: jnp.concatenate([w_out, w_in], 1)}, far[max(far)])
    far_up = far_pieces(start[0], *axis)
    whole, wqt, wvt, table = prepare(me, near_pieces(far, *axis))
    fwd = [
        attention_forward(s, lengths, inputs, whole, wqt, wvt, table) for s in range(count)
    ]
    far_up = held_until(far_up, fwd[-1][3])
    far_back = far_pieces(held_until({0: w_back}, fwd[-1][3])[0], *axis)
    far_back = held_until(far_back, fwd[0][3])
    out, gh, dot, *grads, sums = feed_forward(
        lengths, me, inputs, cotangent, [f[2] for f in fwd], [f[3] for f in fwd],
        near_pieces(far_up, *axis), near_pieces(far_back, *axis), table,
    )
    place = (lax.axis_index("rep") % GROUP).astype(jnp.int32).reshape(1)
    folds = [("fold", bit) for bit in powers(shards)]
    group = [("group", 0)]
    rest = [("full", bit) for bit in powers(reps) if bit >= GROUP]
    tall = Stream(grads[:2], sizes, folds + group + rest)
    deep = Stream(grads[2:], sizes, folds[:1] + group + folds[1:] + rest)
    projs = [[None] * GROUPS for _ in range(count)]
    quarters = [None] * GROUPS
    extras, after, calls = [], [], []
    for g in range(GROUPS):
        chain = ()
        for s in range(count):
            closing = [sums] + extras if s == count - 1 and g == GROUPS - 1 else ()
            busy = [
                (tall, deep), (tall, deep), (tall, quarters[0]), (deep, quarters[0], tall)
            ][len(calls)]
            items = [stream.exchange() for stream in busy]
            res = attention_backward(
                s, g, GROUPS, shards, lengths, me, whole, table, inputs, dot, fwd[s][1],
                fwd[s][2], fwd[s][0], chain, closing, after,
            )
            chain = list(res[1:-1])
            carry = chain[1:2] if len(calls) == 3 else []
            after, *held = advance(place, busy, items, [res[-1]], carry)
            after = [after]
            chain[1 : 1 + len(held)] = held
            projs[s][g] = res[0]
            calls.append(res)
        quarters[g] = Stream(chain[:2], sizes, folds + [("stop", 0)])
        extras += chain[2:]
    early, last = quarters
    for stream, left in ((early, 1), (tall, 0), (deep, 1)):
        while len(stream.steps) > left:
            stream.alone(place)
    tall_parts = whole_parts(tall)
    end = deep.exchange()
    after = []
    while len(last.steps) > 2:
        after = last.alone(place)
    gx, token = input_gradient(0, lengths, whole, gh, projs[0], after)
    final = last.exchange()[0]
    both = Stream([], sizes, group + rest, stacked=GROUPS)
    after = advance(
        place, [both, deep], [([early.value] + final, "parts", GROUPS), end], [token]
    )
    for seq in range(1, count):
        gx, token = input_gradient(seq, lengths, whole, gh, projs[seq], after, gx)
    both.alone(place, [token] + tall_parts[1:])
    deep_parts = whole_parts(deep)
    while both.steps:
        both.alone(place)
    return (out, gx, *spread(place, shards, tall_parts + deep_parts + whole_parts(both)))


def solution(mesh):
    data = P(("rep", "shard"), None, None)
    rows = P("shard", None)
    return jax.shard_map(
        partial(body, (mesh.shape["rep"], mesh.shape["shard"])),
        mesh=mesh,
        in_specs=(data, P(("rep", "shard")), rows, rows, rows, rows, rows, data),
        out_specs=(data, data, rows, rows, rows, rows, rows),
        check_vma=False,
    )
```

```python
import math
from functools import partial

import jax
import jax.numpy as jnp
from jax import lax
from jax.experimental import pallas as pl
from jax.experimental.pallas import tpu as pltpu
from jax.sharding import PartitionSpec as P

D = 512
HEADS = 8
HDIM = 64
FF = 2048
MEM = 20
TILE = 256
PAIRS = HEADS // 2
SCALE = HDIM**-0.5
QSCALE = SCALE * math.log2(math.e)
LN2 = math.log(2.0)
F32 = jnp.float32
BF16 = jnp.bfloat16
VROWS = 80
VMEM_LIMIT = 62 * 2**20


def nn(a, b):
    return lax.dot_general(a, b, (((1,), (0,)), ((), ())), preferred_element_type=F32)


def nt(a, b):
    return lax.dot_general(a, b, (((1,), (1,)), ((), ())), preferred_element_type=F32)


def tn(a, b):
    return lax.dot_general(a, b, (((0,), (0,)), ((), ())), preferred_element_type=F32)


def key_sizes(seq_rows):
    top = -(-(seq_rows + MEM) // 32) * 32
    return [rows for rows in range(512, top, 256)] + [top]


def column_max(values):
    parts = [values[i : i + 128] for i in range(0, values.shape[0] - 127, 128)]
    while len(parts) > 1:
        odd = parts[len(parts) - len(parts) % 2 :]
        parts = [jnp.maximum(a, b) for a, b in zip(parts[::2], parts[1::2])] + odd
    top = jnp.max(parts[0], axis=0, keepdims=True)
    rest = values.shape[0] % 128
    if rest:
        top = jnp.maximum(top, jnp.max(values[-rest:], axis=0, keepdims=True))
    return top


AHEAD = 2
BODY_HEADS = 4


def cdiv(a, b):
    return (a + b - 1) // b


def pick_memory(rows_ref, memory, length):
    edge = pl.multiple_of(length // 128 * 128, 128)
    fix = pl.ds(edge, TILE)
    row = lax.broadcasted_iota(jnp.int32, (TILE, 1), 0) + edge
    lane = lax.broadcasted_iota(jnp.int32, (TILE, 32), 1)
    pick = lax.broadcasted_iota(jnp.int32, (TILE, 32), 0) + (edge - length) == lane
    placed = nn(jnp.where(pick, 1.0, 0.0).astype(BF16), memory)
    rows_ref[fix, :] = jnp.where(row < length, rows_ref[fix, :].astype(F32), placed).astype(BF16)


def memory_rows(vec_ref):
    inside = lax.broadcasted_iota(jnp.int32, (32, D), 0) < MEM
    return jnp.where(inside, vec_ref[...].astype(F32), 0.0).astype(BF16)


def for_size(seq_rows, total, run):
    sizes = key_sizes(seq_rows)
    for index, kr in enumerate(sizes):
        least = sizes[index - 1] if index else 0

        @pl.when(jnp.logical_and(total > least, total <= kr))
        def _(kr=kr):
            run(kr)


def prepare_kernel(shards, me_ref, *refs):
    pieces = refs[:shards]
    w_ref, wqt_ref, wvt_ref, vec_ref, few_rows, sems = refs[shards:]
    me = me_ref[0]
    part, few = D // shards, 32 // shards
    copies, small = [], []
    for m in range(shards):
        at = pl.multiple_of((me ^ m) * part, part)
        small.append(
            pltpu.make_async_copy(
                pieces[m].at[pl.ds(part, SPARE), pl.ds(0, D)], few_rows.at[m], sems.at[m, 1]
            )
        )
        copies.append(
            pltpu.make_async_copy(
                pieces[m].at[pl.ds(0, part), :], w_ref.at[pl.ds(at, part), :], sems.at[m, 0]
            )
        )
    for copy in small + copies:
        copy.start()
    for copy in small:
        copy.wait()
    owner = lax.broadcasted_iota(jnp.int32, (32, D), 0) // few
    rows = jnp.zeros((32, D), F32)
    for m in range(shards):
        values = few_rows[m].astype(F32)[:few]
        rows = jnp.where(owner == (me ^ m), jnp.concatenate([values] * shards, 0), rows)
    vec_ref[...] = rows.astype(BF16)
    for copy in copies:
        copy.wait()
    wqt_ref[...] = w_ref[:, :D].T
    wvt_ref[...] = w_ref[:, 2 * D :].T


SPARE = 16


def pack(w_qkv, vectors):
    below = ((0, SPARE - vectors.shape[0]), (0, w_qkv.shape[1] - vectors.shape[1]))
    return jnp.concatenate([w_qkv, jnp.pad(vectors, below)], 0)


def prepare(me, pieces):
    shards = len(pieces)
    vm = pl.BlockSpec(memory_space=pltpu.VMEM)
    return pl.pallas_call(
        partial(prepare_kernel, shards),
        out_shape=(
            jax.ShapeDtypeStruct((D, 3 * D), BF16),
            jax.ShapeDtypeStruct((D, D), BF16),
            jax.ShapeDtypeStruct((D, D), BF16),
            jax.ShapeDtypeStruct((32, D), BF16),
        ),
        in_specs=[pl.BlockSpec(memory_space=pltpu.SMEM)]
        + [pl.BlockSpec(memory_space=pl.ANY)] * shards,
        out_specs=(vm, vm, vm, vm),
        scratch_shapes=[
            pltpu.VMEM((shards, SPARE, D), BF16),
            pltpu.SemaphoreType.DMA((shards, 2)),
        ],
        compiler_params=pltpu.CompilerParams(vmem_limit_bytes=24 * 2**20),
        name="prepare",
    )(me, *pieces)


def fwd_kernel(
    seq_rows, seq, len_ref, x_hbm, wk_ref, wqt_ref, wvt_ref, vec_ref,
    e_hbm, qt_hbm, mixt_hbm, inv_ref,
    rows, keys, vt, qpad, queries, mixed_t, ebuf, sems, io_sems,
):
    length = len_ref[seq]
    total = length + MEM
    load = pltpu.make_async_copy(x_hbm.at[seq], rows.at[pl.ds(0, seq_rows), :], io_sems.at[0])
    load.start()
    memory = memory_rows(vec_ref)
    vec_cols = vec_ref[...].astype(F32).T
    bias_q = vec_cols[:, MEM : MEM + 1]
    bias_v = vec_cols[:, MEM + 1 : MEM + 2]
    mixed_t[...] = jnp.zeros(mixed_t.shape, BF16)
    inv_ref[...] = jnp.zeros(inv_ref.shape, F32)
    for head in range(HEADS):
        spare = HDIM * (1 - head % 2)
        qpad[head, spare : spare + HDIM, :] = jnp.zeros((HDIM, qpad.shape[2]), BF16)
    vt[:, HDIM:, :] = jnp.ones((HEADS, VROWS - HDIM, vt.shape[2]), BF16)
    n_tiles = cdiv(length, TILE)
    chunks = cdiv(total, TILE)
    load.wait()

    rows[seq_rows:, :] = jnp.zeros((rows.shape[0] - seq_rows, D), BF16)
    pick_memory(rows, memory, length)

    def project(chunk, _):
        here = pl.ds(pl.multiple_of(chunk * TILE, TILE), TILE)
        joined = rows[here, :]
        key_rows = nn(joined, wk_ref[...]).astype(BF16)
        for pair in range(PAIRS):
            keys[pair, here, :] = key_rows[:, pair * 128 : pair * 128 + 128]
        values = (nt(wvt_ref[...], joined) + bias_v).astype(BF16)
        found = ((nt(wqt_ref[...], joined) + bias_q) * QSCALE).astype(BF16)
        queries[:, here] = found
        for head in range(HEADS):
            low = (head % 2) * HDIM
            vt[head, :HDIM, here] = values[head * HDIM : (head + 1) * HDIM]
            qpad[head, low : low + HDIM, here] = found[head * HDIM : (head + 1) * HDIM]
        return 0

    lax.fori_loop(0, chunks, project, 0)
    save = pltpu.make_async_copy(queries.at[:, pl.ds(0, seq_rows)], qt_hbm, io_sems.at[1])
    save.start()

    def attend(kr):
        tail = kr - TILE if kr % TILE == 0 else kr - kr % TILE
        row = lax.broadcasted_iota(jnp.int32, (kr - tail, TILE), 0) + tail
        mask = row < total

        def copies(tile, pair):
            return pltpu.make_async_copy(
                ebuf.at[pair, :, pl.ds(0, kr), :],
                e_hbm.at[tile, pl.ds(pair * 2, 2), pl.ds(0, kr), :],
                sems.at[pair],
            )

        turns = HEADS // BODY_HEADS

        def step(unit, _):
            tile, turn = unit // turns, unit % turns
            here = pl.ds(pl.multiple_of(tile * TILE, TILE), TILE)
            base = turn * BODY_HEADS

            def score(i):
                pair = turn * (BODY_HEADS // 2) + i // 2
                scores = nn(keys[pair, :kr, :], qpad[base + i, :, here])
                scores = jnp.concatenate(
                    [scores[:tail], jnp.where(mask, scores[tail:], -1e30)], 0
                )
                return scores, column_max(scores)

            live = {i: score(i) for i in range(AHEAD)}
            for i in range(BODY_HEADS):
                pair, sub = turn * (BODY_HEADS // 2) + i // 2, i % 2
                scores, top = live.pop(i)
                if sub == 0:
                    copies(tile, pair).wait()
                if i + AHEAD < BODY_HEADS:
                    live[i + AHEAD] = score(i + AHEAD)
                expo = jnp.exp2(scores - top).astype(BF16)
                ebuf[pair, sub, :kr, :] = expo
                mixed = nn(vt[base + i, :, :kr], expo)
                inverse = 1.0 / mixed[HDIM : HDIM + 1]
                spot = pl.ds(pl.multiple_of((base + i) * HDIM, HDIM), HDIM)
                mixed_t[spot, here] = (mixed[:HDIM] * inverse).astype(BF16)
                inv_ref[pl.ds(base + i, 1), here] = inverse
                if sub == 1:
                    copies(tile, pair).start()
            return 0

        for pair in range(PAIRS):
            copies(0, pair).start()
        lax.fori_loop(0, n_tiles * turns, step, 0)
        out = pltpu.make_async_copy(mixed_t, mixt_hbm, io_sems.at[2])
        out.start()
        for pair in range(PAIRS):
            copies(n_tiles - 1, pair).wait()
        save.wait()
        out.wait()

    for_size(seq_rows, total, attend)


def attention_forward(seq, lengths, x, w_qkv, wqt, wvt, vectors):
    seq_rows = x.shape[1]
    top = key_sizes(seq_rows)[-1]
    padded = cdiv(seq_rows + MEM, TILE) * TILE
    tiles = seq_rows // TILE
    vm = pl.BlockSpec(memory_space=pltpu.VMEM)
    hbm = pl.BlockSpec(memory_space=pl.ANY)
    return pl.pallas_call(
        partial(fwd_kernel, seq_rows, seq),
        out_shape=(
            jax.ShapeDtypeStruct((tiles, HEADS, top, TILE), BF16),
            jax.ShapeDtypeStruct((D, seq_rows), BF16),
            jax.ShapeDtypeStruct((D, seq_rows), BF16),
            jax.ShapeDtypeStruct((HEADS, seq_rows), F32),
        ),
        grid=(1,),
        in_specs=[
            pl.BlockSpec(memory_space=pltpu.SMEM),
            hbm,
            pl.BlockSpec((D, D), lambda i: (0, 1)),
            vm,
            vm,
            vm,
        ],
        out_specs=(hbm, hbm, hbm, vm),
        scratch_shapes=[
            pltpu.VMEM((padded, D), BF16),
            pltpu.VMEM((PAIRS, padded, 128), BF16),
            pltpu.VMEM((HEADS, VROWS, padded), BF16),
            pltpu.VMEM((HEADS, 128, padded), BF16),
            pltpu.VMEM((D, padded), BF16),
            pltpu.VMEM((D, seq_rows), BF16),
            pltpu.VMEM((PAIRS, 2, top, TILE), BF16),
            pltpu.SemaphoreType.DMA((PAIRS,)),
            pltpu.SemaphoreType.DMA((3,)),
        ],
        compiler_params=pltpu.CompilerParams(vmem_limit_bytes=44 * 2**20),
        cost_estimate=pl.CostEstimate(
            flops=8 * 10**9, bytes_accessed=24 * 10**6, transcendentals=8 * 10**6
        ),
        name="attention_forward",
    )(lengths, x, w_qkv, wqt, wvt, vectors)


def norm_forward(values):
    center = values - jnp.mean(values, axis=-1, keepdims=True)
    inverse = lax.rsqrt(jnp.mean(center * center, axis=-1, keepdims=True) + 1e-05)
    return center * inverse, inverse


def norm_backward(grad, normed, inverse):
    return inverse * (
        grad
        - jnp.mean(grad, axis=-1, keepdims=True)
        - normed * jnp.mean(grad * normed, axis=-1, keepdims=True)
    )


def col_sum(values):
    return jnp.sum(values, axis=0, keepdims=True)


GELU_A = math.sqrt(2.0 / math.pi)
GELU_B = GELU_A * 0.044715
BLOCKS = FF // D


def piece_order(shards):
    bits = shards.bit_length() - 1
    return [int(format(i, "b").zfill(bits)[::-1], 2) if bits else 0 for i in range(shards)]


def piece_spots(pair, shards, rows):
    half = max(shards // 2, 1)
    for index, m in enumerate(piece_order(shards)):
        yield m, pair[index // half], index % half * rows


def ffn_kernel(
    seq_rows, shards, len_ref, me_ref, x_hbm, cot_hbm, mixt0, mixt1, inv0, inv1, *refs,
):
    wi_p, wb_p = refs[:shards], refs[shards : 2 * shards]
    vec_ref, out_hbm, gh_hbm, dot_hbm = refs[2 * shards : 2 * shards + 4]
    grads = refs[2 * shards + 4 : 2 * shards + 8]
    (
        sums_ref, x_ref, cot_ref, mixt_ref, inv_ref, wo_ref, wi_ref, wb_ref,
        out_ref, gh_ref, dot_ref, acc_o, acc_i, acc_b, slopes, actives,
        s_normed1, s_first, s_gsecond, ups, sems, out_sems,
    ) = refs[2 * shards + 8 :]
    half = TILE // 2
    len0, len1 = len_ref[0], len_ref[1]
    me = me_ref[0]
    n0, n1 = cdiv(len0, half), cdiv(len1, half)
    full = seq_rows // half
    n_all = n0 + n1

    def rows_at(piece, rows):
        return pl.ds(pl.multiple_of((me ^ piece) * rows, rows), rows)

    loads = []

    def load(src, dst):
        copy = pltpu.make_async_copy(src, dst, sems.at[len(loads)])
        loads.append(copy)
        copy.start()
        return copy

    first_loads = [load(mixt0, mixt_ref.at[0]), load(mixt1, mixt_ref.at[1])]
    first_loads += [load(inv0, inv_ref.at[0]), load(inv1, inv_ref.at[1])]
    part = D // shards
    first_loads += [
        load(p.at[:, pl.ds(0, D)], wo_ref.at[rows_at(i, part), :]) for i, p in enumerate(wi_p)
    ]
    first_loads += [load(x_hbm.at[s], x_ref.at[s]) for s in range(2)]
    second_loads = [
        load(p.at[:, pl.ds(D, FF)], wi_ref.at[rows_at(i, part), :]) for i, p in enumerate(wi_p)
    ]
    second_loads += [load(p, wb_ref.at[rows_at(i, FF // shards), :]) for i, p in enumerate(wb_p)]
    third_loads = [load(cot_hbm.at[s], cot_ref.at[s]) for s in range(2)]

    out_ref[...] = jnp.zeros(out_ref.shape, BF16)
    gh_ref[...] = jnp.zeros(gh_ref.shape, BF16)
    dot_ref[...] = jnp.zeros(dot_ref.shape, BF16)
    acc_o[...] = jnp.zeros(acc_o.shape, F32)
    acc_i[...] = jnp.zeros(acc_i.shape, F32)
    acc_b[...] = jnp.zeros(acc_b.shape, F32)
    sums_ref[...] = jnp.zeros(sums_ref.shape, F32)

    def vec(index):
        return vec_ref[index : index + 1, :].astype(F32)

    bias_out = vec(MEM + 2)
    bias_back = vec(MEM + 3 + BLOCKS)
    gain_one = vec(MEM + 4 + BLOCKS)
    shift_one = vec(MEM + 5 + BLOCKS)
    gain_two = vec(MEM + 6 + BLOCKS)
    shift_two = vec(MEM + 7 + BLOCKS)

    spare_one = jnp.logical_and(n_all % 2 == 1, n1 < full)
    spare_zero = jnp.logical_and(n_all % 2 == 1, n1 >= full)

    def place(chunk):
        second = chunk >= n0
        inside = jnp.where(second, chunk - n0, chunk)
        spare = chunk >= n_all
        seq = jnp.where(spare, jnp.where(n1 < full, 1, 0), jnp.where(second, 1, 0))
        inside = jnp.where(spare, jnp.where(n1 < full, n1, n0), inside)
        return seq, pl.multiple_of(inside * half, half), jnp.where(seq == 1, len1, len0)

    def rows_of(ref, spots):
        return jnp.concatenate([ref[s, pl.ds(r, half), :] for s, r, _ in spots], 0)

    def lanes_of(ref, spots):
        return jnp.concatenate([ref[s, :, pl.ds(r, half)] for s, r, _ in spots], 1)

    def put_rows(ref, value, spots):
        for i, (s, r, _) in enumerate(spots):
            ref[s, pl.ds(r, half), :] = value[i * half : (i + 1) * half]

    def put_lanes(ref, value, spots):
        for i, (s, r, _) in enumerate(spots):
            ref[s, :, pl.ds(r, half)] = value[:, i * half : (i + 1) * half]

    def valid_of(spots):
        iota = lax.broadcasted_iota(jnp.int32, (half, 1), 0)
        return jnp.concatenate(
            [jnp.where(iota + r < count, 1.0, 0.0) for _, r, count in spots], 0
        )

    def add_sum(row, value):
        sums_ref[row : row + 1] += col_sum(value)

    def whole_tile(spots):
        count = half * len(spots)
        here = slice(0, count)
        valid = valid_of(spots)
        mixt = lanes_of(mixt_ref, spots)
        attn = nn(mixt.T, wo_ref[...]) + bias_out
        normed_one, inverse_one = norm_forward(rows_of(x_ref, spots).astype(F32) + attn)
        first = normed_one * gain_one + shift_one
        s_normed1[here] = normed_one
        low = first.astype(BF16)
        s_first[here] = low
        second = first + bias_back
        for j in range(BLOCKS):
            cols = slice(j * D, (j + 1) * D)
            up = nn(low, wi_ref[:, cols]) + vec(MEM + 3 + j)
            square = up * up
            bent = jnp.tanh(up * (GELU_A + GELU_B * square))
            gate = 0.5 + 0.5 * bent
            active = up * gate
            slopes[here, cols] = (
                gate + active * (1.0 - bent) * (GELU_A + 3.0 * GELU_B * square)
            ).astype(slopes.dtype)
            actives[here, cols] = active.astype(BF16)
        second = second + nn(actives[here, :], wb_ref[...])
        normed_two, inverse_two = norm_forward(second)
        put_rows(out_ref, ((normed_two * gain_two + shift_two) * valid).astype(BF16), spots)
        grad_out = rows_of(cot_ref, spots).astype(F32) * valid
        add_sum(MEM + 6 + BLOCKS, grad_out * normed_two)
        add_sum(MEM + 7 + BLOCKS, grad_out)
        grad_second = norm_backward(grad_out * gain_two, normed_two, inverse_two)
        s_gsecond[here] = grad_second
        down = grad_second.astype(BF16)
        add_sum(MEM + 3 + BLOCKS, down.astype(F32))
        low_t = s_first[here, :].T
        for j in range(BLOCKS):
            cols = slice(j * D, (j + 1) * D)
            grad_up = (
                nt(down, wb_ref[cols, :]) * slopes[here, cols].astype(F32)
            ).astype(BF16)
            ups[here, cols] = grad_up
            add_sum(MEM + 3 + j, grad_up.astype(F32))
        grad_first = s_gsecond[here] + nt(ups[here, :], wi_ref[...])
        for j in range(BLOCKS):
            cols = slice(j * D, (j + 1) * D)
            acc_b[cols, :] += tn(actives[here, cols], down)
            acc_i[:, cols] += nn(low_t, ups[here, cols])
        normed_one = s_normed1[here]
        add_sum(MEM + 4 + BLOCKS, grad_first * normed_one)
        add_sum(MEM + 5 + BLOCKS, grad_first)
        grad_one = norm_backward(grad_first * gain_one, normed_one, inverse_one)
        low = grad_one.astype(BF16)
        put_rows(gh_ref, low, spots)
        add_sum(MEM + 2, low.astype(F32))
        acc_o[...] += nn(mixt, low)
        grad_mixed = nt(wo_ref[...], low)
        inverse = lanes_of(inv_ref, spots)
        scaled = [
            grad_mixed[h * HDIM : (h + 1) * HDIM] * inverse[h : h + 1] for h in range(HEADS)
        ]
        put_lanes(dot_ref, jnp.concatenate(scaled, 0).astype(BF16), spots)

    def send(ref, hbm, sem, seq, row, lanes=False):
        here = pl.ds(row, half)
        src = ref.at[seq, :, here] if lanes else ref.at[seq, here, :]
        dst = hbm.at[seq, :, here] if lanes else hbm.at[seq, here, :]
        pltpu.make_async_copy(src, dst, out_sems.at[sem]).start()

    def send_all(seq, row):
        send(out_ref, out_hbm, 0, seq, row)
        send(gh_ref, gh_hbm, 1, seq, row)
        send(dot_ref, dot_hbm, 2, seq, row, True)

    for copy in first_loads + second_loads + third_loads:
        copy.wait()

    def step(index, _):
        spots = [place(index * 4 + i) for i in range(4)]
        whole_tile(spots)
        for seq, row, _ in spots:
            send_all(seq, row)
        return 0

    left = lax.rem(n_all, 4)
    bigs = n_all // 4 + jnp.where(left == 3, 1, 0)
    lax.fori_loop(0, bigs, step, 0)

    @pl.when(jnp.logical_or(left == 1, left == 2))
    def _():
        spots = [place(bigs * 4 + i) for i in range(2)]
        whole_tile(spots)
        for seq, row, _ in spots:
            send_all(seq, row)

    def rest(seq):
        def one(chunk, _):
            send_all(seq, pl.multiple_of(chunk * half, half))
            return 0

        return one

    lax.fori_loop(n0 + jnp.where(spare_zero, 1, 0), full, rest(0), 0)
    lax.fori_loop(n1 + jnp.where(spare_one, 1, 0), full, rest(1), 0)

    part = D // shards
    deep = FF // shards
    block = part * (1 + BLOCKS)
    for m, piece, row in piece_spots(grads[:2], shards, block):
        at = pl.multiple_of((me ^ m) * part, part)
        piece[row : row + part, :] = acc_o[pl.ds(at, part), :].astype(BF16)
        for j in range(BLOCKS):
            row += part
            piece[row : row + part, :] = acc_i[
                pl.ds(at, part), j * D : (j + 1) * D
            ].astype(BF16)
    for m, piece, row in piece_spots(grads[2:], shards, deep):
        at = pl.multiple_of((me ^ m) * deep, deep)
        piece[row : row + deep, :] = acc_b[pl.ds(at, deep), :].astype(BF16)
    for ref, hbm, sem in ((out_ref, out_hbm, 0), (gh_ref, gh_hbm, 1), (dot_ref, dot_hbm, 2)):
        pltpu.make_async_copy(ref, hbm, out_sems.at[sem]).wait()


def feed_forward(lengths, me, x, cot, mixts, invs, w_up, w_back, vectors):
    count, seq_rows = x.shape[:2]
    shards = len(w_up)
    vm = pl.BlockSpec(memory_space=pltpu.VMEM)
    hbm = pl.BlockSpec(memory_space=pl.ANY)
    smem = pl.BlockSpec(memory_space=pltpu.SMEM)
    return pl.pallas_call(
        partial(ffn_kernel, seq_rows, shards),
        out_shape=(
            jax.ShapeDtypeStruct((count, seq_rows, D), BF16),
            jax.ShapeDtypeStruct((count, seq_rows, D), BF16),
            jax.ShapeDtypeStruct((count, D, seq_rows), BF16),
            *[
                jax.ShapeDtypeStruct((rows, D), BF16)
                for rows in (D * (1 + BLOCKS) // 2, FF // 2)
                for _ in range(2)
            ],
            jax.ShapeDtypeStruct((32, D), F32),
        ),
        in_specs=[smem, smem] + [hbm] * (6 + 2 * shards) + [vm],
        out_specs=(hbm, hbm, hbm) + (vm,) * 5,
        scratch_shapes=[
            pltpu.VMEM((count, seq_rows, D), BF16),
            pltpu.VMEM((count, seq_rows, D), BF16),
            pltpu.VMEM((count, D, seq_rows), BF16),
            pltpu.VMEM((count, HEADS, seq_rows), F32),
            pltpu.VMEM((D, D), BF16),
            pltpu.VMEM((D, FF), BF16),
            pltpu.VMEM((FF, D), BF16),
            pltpu.VMEM((count, seq_rows, D), BF16),
            pltpu.VMEM((count, seq_rows, D), BF16),
            pltpu.VMEM((count, D, seq_rows), BF16),
            pltpu.VMEM((D, D), F32),
            pltpu.VMEM((D, FF), F32),
            pltpu.VMEM((FF, D), F32),
            pltpu.VMEM((2 * TILE, FF), BF16),
            pltpu.VMEM((2 * TILE, FF), BF16),
            pltpu.VMEM((2 * TILE, D), F32),
            pltpu.VMEM((2 * TILE, D), BF16),
            pltpu.VMEM((2 * TILE, D), F32),
            pltpu.VMEM((2 * TILE, FF), BF16),
            pltpu.SemaphoreType.DMA((8 + 3 * shards,)),
            pltpu.SemaphoreType.DMA((3,)),
        ],
        compiler_params=pltpu.CompilerParams(vmem_limit_bytes=56 * 2**20),
        cost_estimate=pl.CostEstimate(
            flops=27 * 10**9, bytes_accessed=24 * 10**6, transcendentals=4 * 10**6
        ),
        name="feed_forward",
    )(lengths, me, x, cot, *mixts, *invs, *w_up, *w_back, vectors)


def bwd_kernel(seq_rows, groups, group, seq, shards, chained, closing, waits, *refs):
    gp = PAIRS // groups
    gcols = gp * 128
    width = 3 * gcols
    refs = list(refs)
    len_ref, me_ref, wk_ref, wv_ref, vec_ref = refs[:5]
    x_hbm, dot_hbm, qt_hbm, mixt_hbm, e_hbm = refs[5:10]
    refs = refs[10:]
    acc_in, extra_in = (refs.pop(0), refs.pop(0)) if chained else (None, None)
    other_rows = [refs.pop(0) for _ in range(closing)]
    refs = refs[waits:]
    proj_hbm = refs.pop(0)
    last = chained
    if last:
        pieces = [refs.pop(0), refs.pop(0)]
    else:
        acc_hbm = refs.pop(0)
    extra_ref = None if closing else refs.pop(0)
    token = refs.pop(0)
    token[...] = jnp.zeros(token.shape, F32)
    (
        rows, qts, mixts, dots, wkt, kt, values, qpad, dpad, dqt, dk, dv, ebuf, acc, proj,
        extra, table, sems, io_sems, out_sem, acc_sem,
    ) = refs
    base = group * gcols
    mine = pl.ds(base, gcols)
    length = len_ref[seq]
    total = length + MEM
    n_tiles = cdiv(length, TILE)
    chunks = cdiv(total, TILE)
    pairs = [
        (x_hbm.at[seq], rows.at[pl.ds(0, seq_rows), :]),
        (qt_hbm.at[mine, :], qts),
        (mixt_hbm.at[mine, :], mixts),
        (dot_hbm.at[seq, mine, :], dots),
    ]
    loads = [pltpu.make_async_copy(a, b, io_sems.at[i]) for i, (a, b) in enumerate(pairs)]

    def copies_of(kr):
        def copies(tile, slot):
            return pltpu.make_async_copy(
                e_hbm.at[tile, pl.ds(group * gp * 2, gp * 2), pl.ds(0, kr), :],
                ebuf.at[slot, :, pl.ds(0, kr), :],
                sems.at[slot],
            )

        return copies

    for copy in loads:
        copy.start()
    if chained:
        fetch = pltpu.make_async_copy(acc_in, acc, acc_sem)
        fetch.start()
    for_size(seq_rows, total, lambda kr: copies_of(kr)(0, 0).start())
    memory = memory_rows(vec_ref)
    bias_v = vec_ref[MEM + 1 : MEM + 2, base : base + gcols].astype(F32)
    wkt[...] = wk_ref[...].T
    if chained:
        extra[...] = extra_in[...]
        for other in other_rows:
            extra[...] += other[...]
    else:
        acc[...] = jnp.zeros(acc.shape, F32)
        extra[...] = jnp.zeros(extra.shape, F32)
    for head in range(gp * 2):
        spare = HDIM * (1 - head % 2)
        qpad[head, spare : spare + HDIM, :] = jnp.zeros((HDIM, TILE), BF16)
        dpad[head, spare : spare + HDIM, :] = jnp.zeros((HDIM, TILE), BF16)
    rows[seq_rows:, :] = jnp.zeros((rows.shape[0] - seq_rows, D), BF16)
    loads[0].wait()
    edge = pl.multiple_of(length // 128 * 128, 128)
    fix = pl.ds(edge, TILE)
    pick_memory(rows, memory, length)

    def project(chunk, _):
        here = pl.ds(pl.multiple_of(chunk * TILE, TILE), TILE)
        joined = rows[here, :]
        value_rows = (nn(joined, wv_ref[...]) + bias_v).astype(BF16)
        for pair in range(gp):
            values[pair, here, :] = value_rows[:, pair * 128 : pair * 128 + 128]
            dk[pair, here, :] = jnp.zeros((TILE, 128), F32)
            dv[pair, here, :] = jnp.zeros((TILE, 128), F32)
        kt[:, here] = nt(wkt[...], joined).astype(BF16)
        dqt[:, here] = jnp.zeros((gcols, TILE), BF16)
        return 0

    lax.fori_loop(0, chunks, project, 0)
    for copy in loads[1:]:
        copy.wait()

    def attend(kr):
        copies = copies_of(kr)

        def step(tile, _):
            slot = lax.rem(tile, 2)
            here = pl.ds(pl.multiple_of(tile * TILE, TILE), TILE)

            @pl.when(tile + 1 < n_tiles)
            def _():
                copies(tile + 1, 1 - slot).start()

            copies(tile, slot).wait()
            inners = []
            for head in range(gp * 2):
                low = (head % 2) * HDIM
                local = slice(head * HDIM, (head + 1) * HDIM)
                outer = dots[local, here]
                dpad[head, low : low + HDIM, :] = outer
                qpad[head, low : low + HDIM, :] = qts[local, here]
                inners.append(col_sum(outer.astype(F32) * mixts[local, here].astype(F32)))

            def outer_product(head):
                return nn(values[head // 2, :kr, :], dpad[head])

            live = {head: outer_product(head) for head in range(AHEAD)}
            grads = []
            for head in range(gp * 2):
                pair = head // 2
                product = live.pop(head)
                if head + AHEAD < gp * 2:
                    live[head + AHEAD] = outer_product(head + AHEAD)
                local = slice(head * HDIM, (head + 1) * HDIM)
                grad = (
                    ebuf[slot, head, :kr, :].astype(F32) * (product - inners[head])
                ).astype(BF16)
                grads.append(grad)
                dqt[local, here] = (nn(kt[local, :kr], grad) * SCALE).astype(BF16)
                if head % 2:
                    both = [ebuf[slot, h, :kr, :] for h in (head - 1, head)]
                    dv[pair, :kr, :] += nt(
                        jnp.concatenate(both, 1),
                        jnp.concatenate([dpad[head - 1], dpad[head]], 1),
                    )
                    dk[pair, :kr, :] += nt(
                        jnp.concatenate(grads[-2:], 1),
                        jnp.concatenate([qpad[head - 1], qpad[head]], 1),
                    )
            return 0

        lax.fori_loop(0, n_tiles, step, 0)

    for_size(seq_rows, total, attend)
    if chained:
        fetch.wait()

    def send(chunk):
        here = pl.ds(pl.multiple_of(chunk * TILE, TILE), TILE)
        return pltpu.make_async_copy(proj.at[here, :], proj_hbm.at[here, :], out_sem)

    def finish(chunk, sums):
        here = pl.ds(pl.multiple_of(chunk * TILE, TILE), TILE)
        parts = [dqt[:, here].T]
        parts += [(dk[pair, here, :] * LN2).astype(BF16) for pair in range(gp)]
        parts += [dv[pair, here, :].astype(BF16) for pair in range(gp)]
        grad = jnp.concatenate(parts, 1)
        proj[here, :] = grad
        send(chunk).start()
        acc[...] += tn(rows[here, :], grad)
        return sums + col_sum(grad.astype(F32))

    sums = lax.fori_loop(0, chunks, finish, jnp.zeros((1, width), F32))
    if not last:
        store = pltpu.make_async_copy(acc, acc_hbm, acc_sem)
        store.start()
    extra[MEM : MEM + 1, base : base + gcols] += sums[:, :gcols]
    extra[MEM + 1 : MEM + 2, base : base + gcols] += sums[:, 2 * gcols :]
    turned = (
        lax.broadcasted_iota(jnp.int32, (32, TILE), 1) + (edge - length)
        == lax.broadcasted_iota(jnp.int32, (32, TILE), 0)
    )
    turned = jnp.logical_and(turned, lax.broadcasted_iota(jnp.int32, (32, TILE), 0) < MEM)
    turned = jnp.where(turned, 1.0, 0.0).astype(BF16)
    found_k = jnp.concatenate([dk[pair, fix, :] * LN2 for pair in range(gp)], 1)
    found_v = jnp.concatenate([dv[pair, fix, :] for pair in range(gp)], 1)
    grad_memory = nt(nn(turned, found_k.astype(BF16)).astype(BF16), wk_ref[...])
    grad_memory += nt(nn(turned, found_v.astype(BF16)).astype(BF16), wv_ref[...])
    extra[...] += grad_memory

    if last:
        me = me_ref[0]
        part, few = D // shards, 32 // shards
        if closing:
            for s in range(shards):
                table[s, :few, :] = extra[s * few : (s + 1) * few]
        for m, piece, row in piece_spots(pieces, shards, part):
            spot = slice(row, row + part)
            at = pl.multiple_of((me ^ m) * part, part)
            piece[spot, :width] = acc[pl.ds(at, part), :].astype(BF16)
            if closing:
                mine_rows = table[me ^ m]
                lanes = [mine_rows[:, j : j + 128] for j in range(0, D, 128)]
                empty = part - mine_rows.shape[0] * len(lanes)
                if empty:
                    lanes.append(jnp.zeros((empty, 128), F32))
                piece[spot, width:] = jnp.concatenate(lanes, 0).astype(BF16)
    else:
        store.wait()
    if extra_ref is not None:
        extra_ref[...] = extra[...]

    def drain(chunk, _):
        send(chunk).wait()
        return 0

    lax.fori_loop(0, chunks, drain, 0)


def attention_backward(
    seq, group, groups, shards, lengths, me, w_qkv, vectors, x, dot, qt, mixt, expo,
    chain=(), others=(), after=(),
):
    seq_rows = x.shape[1]
    top = key_sizes(seq_rows)[-1]
    padded = cdiv(seq_rows + MEM, TILE) * TILE
    gp = PAIRS // groups
    gcols = gp * 128
    width = 3 * gcols
    vm = pl.BlockSpec(memory_space=pltpu.VMEM)
    hbm = pl.BlockSpec(memory_space=pl.ANY)
    smem = pl.BlockSpec(memory_space=pltpu.SMEM)
    out_shape = [jax.ShapeDtypeStruct((padded, width), BF16)]
    out_specs = [hbm]
    if chain:
        wide = width + (128 if others else 0)
        out_shape += [jax.ShapeDtypeStruct((D // 2, wide), BF16)] * 2
        out_specs += [vm] * 2
    else:
        out_shape += [jax.ShapeDtypeStruct((D, width), F32)]
        out_specs += [hbm]
    if not others:
        out_shape += [jax.ShapeDtypeStruct((32, D), F32)]
        out_specs += [vm]
    out_shape += [jax.ShapeDtypeStruct((8, 128), F32)]
    out_specs += [vm]
    return pl.pallas_call(
        partial(
            bwd_kernel, seq_rows, groups, group, seq, shards, bool(chain), len(others),
            len(after),
        ),
        out_shape=tuple(out_shape),
        grid=(1,),
        in_specs=[
            smem,
            smem,
            pl.BlockSpec((D, gcols), lambda i: (0, groups + group)),
            pl.BlockSpec((D, gcols), lambda i: (0, 2 * groups + group)),
            vm,
        ]
        + [hbm] * 5
        + ([hbm, vm] if chain else [])
        + [vm] * len(others)
        + [hbm] * len(after),
        out_specs=tuple(out_specs),
        scratch_shapes=[
            pltpu.VMEM((padded, D), BF16),
            pltpu.VMEM((gcols, seq_rows), BF16),
            pltpu.VMEM((gcols, seq_rows), BF16),
            pltpu.VMEM((gcols, seq_rows), BF16),
            pltpu.VMEM((gcols, D), BF16),
            pltpu.VMEM((gcols, padded), BF16),
            pltpu.VMEM((gp, padded, 128), BF16),
            pltpu.VMEM((gp * 2, 128, TILE), BF16),
            pltpu.VMEM((gp * 2, 128, TILE), BF16),
            pltpu.VMEM((gcols, padded), BF16),
            pltpu.VMEM((gp, padded, 128), F32),
            pltpu.VMEM((gp, padded, 128), F32),
            pltpu.VMEM((2, gp * 2, top, TILE), BF16),
            pltpu.VMEM((D, width), F32),
            pltpu.VMEM((padded, width), BF16),
            pltpu.VMEM((32, D), F32),
            pltpu.VMEM((shards, max(8, 32 // shards), D), F32),
            pltpu.SemaphoreType.DMA((2,)),
            pltpu.SemaphoreType.DMA((4,)),
            pltpu.SemaphoreType.DMA,
            pltpu.SemaphoreType.DMA,
        ],
        compiler_params=pltpu.CompilerParams(vmem_limit_bytes=57 * 2**20),
        cost_estimate=pl.CostEstimate(
            flops=8 * 10**9, bytes_accessed=15 * 10**6, transcendentals=0
        ),
        name="attention_backward",
    )(lengths, me, w_qkv, w_qkv, vectors, x, dot, qt, mixt, expo, *chain, *others, *after)


def input_kernel(seq_rows, groups, seq, len_ref, w_ref, gh_hbm, *refs):
    projs = refs[:groups]
    gx_hbm, token, gh, blocks, rows, sems, out_sem = refs[-7:]
    token[...] = jnp.zeros(token.shape, F32)
    gcols = D // groups
    length = len_ref[seq]
    chunks = cdiv(length, TILE)
    whole = seq_rows // TILE

    def spot(chunk):
        return pl.ds(pl.multiple_of(chunk * TILE, TILE), TILE)

    def fetch(chunk):
        here = spot(chunk)
        return [pltpu.make_async_copy(gh_hbm.at[seq, here, :], gh.at[here, :], sems.at[chunk, 0])] + [
            pltpu.make_async_copy(p.at[here, :], blocks.at[i, here, :], sems.at[chunk, 1 + i])
            for i, p in enumerate(projs)
        ]

    def send(chunk):
        here = spot(chunk)
        return pltpu.make_async_copy(rows.at[here, :], gx_hbm.at[seq, here, :], out_sem)

    def begin(chunk, _):
        for copy in fetch(chunk):
            copy.start()
        return 0

    lax.fori_loop(0, chunks, begin, 0)

    def empty(chunk, _):
        rows[spot(chunk), :] = jnp.zeros((TILE, D), BF16)
        send(chunk).start()
        return 0

    lax.fori_loop(chunks, whole, empty, 0)

    def step(chunk, _):
        here = spot(chunk)
        for copy in fetch(chunk):
            copy.wait()
        joint = jnp.concatenate(
            [
                blocks[g, here, kind * gcols : (kind + 1) * gcols]
                for kind in range(3)
                for g in range(groups)
            ],
            1,
        )
        grad = nt(joint, w_ref[...])
        row = lax.broadcasted_iota(jnp.int32, (TILE, 1), 0) + chunk * TILE
        rows[here, :] = jnp.where(row < length, grad + gh[here, :].astype(F32), 0.0).astype(BF16)
        send(chunk).start()
        return 0

    lax.fori_loop(0, chunks, step, 0)
    pltpu.make_async_copy(rows, gx_hbm.at[seq], out_sem).wait()


def input_gradient(seq, lengths, w_qkv, gh, projs, after=(), base=None):
    count, seq_rows = gh.shape[:2]
    groups = len(projs)
    hbm = pl.BlockSpec(memory_space=pl.ANY)
    vm = pl.BlockSpec(memory_space=pltpu.VMEM)
    base = () if base is None else (base,)
    return pl.pallas_call(
        partial(input_kernel, seq_rows, groups, seq),
        out_shape=(
            jax.ShapeDtypeStruct((count, seq_rows, D), BF16),
            jax.ShapeDtypeStruct((8, 128), F32),
        ),
        in_specs=[pl.BlockSpec(memory_space=pltpu.SMEM), vm]
        + [hbm] * (1 + groups + len(after) + len(base)),
        out_specs=(hbm, vm),
        input_output_aliases={3 + groups + len(after): 0} if base else {},
        scratch_shapes=[
            pltpu.VMEM((seq_rows, D), BF16),
            pltpu.VMEM((groups, seq_rows, 3 * D // groups), BF16),
            pltpu.VMEM((seq_rows, D), BF16),
            pltpu.SemaphoreType.DMA((seq_rows // TILE, 1 + groups)),
            pltpu.SemaphoreType.DMA,
        ],
        compiler_params=pltpu.CompilerParams(vmem_limit_bytes=52 * 2**20),
        cost_estimate=pl.CostEstimate(
            flops=2 * 10**9, bytes_accessed=7 * 10**6, transcendentals=0
        ),
        name="input_gradient",
    )(lengths, w_qkv, gh, *projs, *after, *base)


GROUPS = 2


def powers(size):
    return [1 << i for i in range(size.bit_length() - 1)]


def exchange(value, axis, size, bit):
    return lax.ppermute(value, axis, [(i, i ^ bit) for i in range(size)])


def far_pieces(value, axis, size):
    pieces = {0: value}
    for bit in reversed(powers(size)[1:]):
        for mask in sorted(pieces):
            pieces[mask | bit] = exchange(pieces[mask], axis, size, bit)
    return pieces


def near_pieces(pieces, axis, size):
    pieces = dict(pieces)
    for mask in sorted(pieces):
        pieces[mask | 1] = exchange(pieces[mask], axis, size, 1)
    return [pieces[mask] for mask in range(size)]


def held_until(pieces, event):
    keys = list(pieces)
    return dict(zip(keys, lax.optimization_barrier((*[pieces[k] for k in keys], event))))


def combine_kernel(counts, modes, waits, carried, place_ref, *refs):
    refs = list(refs)
    arrays = [[[refs.pop(0) for _ in range(c)] for c in group] for group in counts]
    refs = refs[waits:]
    total = refs.pop()
    refs = refs[: len(refs) - carried]
    token = refs.pop()
    token[...] = jnp.zeros(token.shape, F32)
    place = place_ref[0]
    for groups, (mode, stacked, cols) in zip(arrays, modes):
        rows = sum(group[0].shape[0] for group in groups)
        if mode == "halves":
            half = rows // 2
            for side in range(2):
                add_rows(groups[0], side * half, half, refs.pop(0), 0, cols)
        elif mode == "parts":
            base = 0
            for group in groups:
                more = group[0].shape[0]
                add_rows(group, 0, more, total, base, cols)
                base += more
            one = rows // stacked
            part = one // GROUP
            for m in range(GROUP):
                target = refs.pop(0)
                at = pl.multiple_of((place ^ m) * part, part)
                for i in range(stacked):
                    target[i * part : (i + 1) * part, :] = total[
                        pl.ds(at + i * one, part), :cols
                    ].astype(BF16)
        else:
            add_rows(groups[0], 0, rows, refs.pop(0), 0, cols)


def add_rows(group, start, rows, target, base, cols):
    wide = group[0].shape[1]
    step = next((s for s in (64, 32, 16) if not (rows % s or start % s or base % s)), rows)

    def add(index, _):
        def at(first):
            if step == rows:
                return pl.ds(first, rows)
            return pl.ds(pl.multiple_of(first + index * step, step), step)

        value = group[0][at(start), :].astype(F32)
        for other in group[1:]:
            value = value + other[at(start), :].astype(F32)
        target[at(base), :wide] = value.astype(target.dtype)
        if wide < cols:
            target[at(base), wide:cols] = jnp.zeros((step, cols - wide), target.dtype)
        return 0

    lax.fori_loop(0, rows // step, add, 0)


def combine(place, items, after, carry=()):
    vm = pl.BlockSpec(memory_space=pltpu.VMEM)
    shapes, flat, modes, most = [], [], [], 0
    for groups, mode, stacked in items:
        rows = sum(arrays[0].shape[0] for arrays in groups)
        cols = max(arrays[0].shape[1] for arrays in groups)
        flat += [a for arrays in groups for a in arrays]
        modes.append((mode, stacked, cols))
        most = max(most, rows)
        if mode == "halves":
            shapes += [(rows // 2, cols)] * 2
        elif mode == "parts":
            shapes += [(rows // GROUP, cols)] * GROUP
        else:
            shapes += [(rows, cols)]
    size = sum(a.size for a in flat) * 2
    outs = pl.pallas_call(
        partial(
            combine_kernel,
            [[len(g) for g in i[0]] for i in items],
            modes,
            len(after) + len(carry),
            len(carry),
        ),
        out_shape=tuple(jax.ShapeDtypeStruct(s, BF16) for s in shapes)
        + (jax.ShapeDtypeStruct((8, 128), F32),)
        + tuple(jax.ShapeDtypeStruct(a.shape, a.dtype) for a in carry),
        in_specs=[pl.BlockSpec(memory_space=pltpu.SMEM)]
        + [vm] * len(flat)
        + [pl.BlockSpec(memory_space=pl.ANY)] * (len(after) + len(carry)),
        out_specs=(vm,) * (len(shapes) + 1)
        + (pl.BlockSpec(memory_space=pl.ANY),) * len(carry),
        input_output_aliases={
            1 + len(flat) + len(after) + i: len(shapes) + 1 + i for i in range(len(carry))
        },
        scratch_shapes=[pltpu.VMEM((most, max(m[2] for m in modes)), F32)],
        compiler_params=pltpu.CompilerParams(vmem_limit_bytes=24 * 2**20),
        cost_estimate=pl.CostEstimate(flops=size, bytes_accessed=2 * size, transcendentals=0),
        name="combine",
    )(place, *flat, *after, *carry)
    held = list(outs[len(shapes) + 1 :])
    outs, token, results = list(outs[: len(shapes)]), outs[len(shapes)], []
    for mode, _, _ in modes:
        taken = {"halves": 2, "parts": GROUP, "whole": 1}[mode]
        results.append([outs.pop(0) for _ in range(taken)])
    return results, [token, *held]


GROUP = 4


class Stream:
    def __init__(self, value, sizes, steps, stacked=None):
        self.value, self.steps = list(value), list(steps)
        self.reps, self.shards = sizes
        self.stacked = stacked or max(self.shards // 2, 1)

    def exchange(self):
        kind, bit = self.steps.pop(0)
        value = self.value
        if kind == "fold":
            arrays = [value[0], exchange(value[1], "shard", self.shards, bit)]
        elif kind == "group":
            arrays = [value[0]] + [
                exchange(value[j], "rep", self.reps, j) for j in range(1, GROUP)
            ]
        else:
            arrays = [value[0], exchange(value[0], "rep", self.reps, bit)]
        follow = self.steps[0][0] if self.steps else "end"
        item = ([arrays], {"fold": "halves", "group": "parts"}.get(follow, "whole"), self.stacked)
        if follow == "fold":
            self.stacked //= 2
        return item

    def alone(self, place, after=()):
        (self.value,), token = combine(place, [self.exchange()], after)
        return token


def advance(place, streams, items, after, carry=()):
    results, token = combine(place, items, after, carry)
    for stream, result in zip(streams, results):
        stream.value = result
    return token


def whole_parts(stream):
    own = stream.value[0]
    return [own] + [exchange(own, "rep", stream.reps, j) for j in range(1, GROUP)]


def spread_kernel(shards, place_ref, *refs):
    refs = list(refs)
    arrays = [[refs.pop(0) for _ in range(GROUP)] for _ in range(3)]
    qkv_ref, out_ref, in_ref, back_ref, vec_ref, table = refs
    place = place_ref[0]

    def put(target, parts, cols, first=0, count=None):
        part = count or parts[0].shape[0]
        for m in range(GROUP):
            at = pl.multiple_of((place ^ m) * part, part)
            target[pl.ds(at, part), :cols] = parts[m][first : first + part, :].astype(F32)

    part = D // shards
    put(back_ref, arrays[1], D)
    put(table, arrays[0], D)
    out_ref[...] = table[:part, :D]
    for j in range(BLOCKS):
        in_ref[:, j * D : (j + 1) * D] = table[(1 + j) * part : (2 + j) * part, :D]
    gcols = D // GROUPS
    for g in range(GROUPS):
        put(table, arrays[2], 3 * gcols + 128, g * part // GROUP, part // GROUP)
        for kind in range(3):
            at = kind * D + g * gcols
            qkv_ref[:, at : at + gcols] = table[:part, kind * gcols : (kind + 1) * gcols]
    few = 32 // shards
    width = 3 * gcols
    step = max(8, few)
    for j in range(D // 128):
        vec_ref[:, j * 128 : (j + 1) * 128] = table[j * step : j * step + few, width : width + 128]


def spread(place, shards, parts):
    part = D // shards
    vm = pl.BlockSpec(memory_space=pltpu.VMEM)
    shapes = ((part, 3 * D), (part, D), (part, FF), (FF // shards, D), (32 // shards, D))
    most = max(part * (1 + BLOCKS), part), max(p.shape[1] for p in parts)
    return pl.pallas_call(
        partial(spread_kernel, shards),
        out_shape=tuple(jax.ShapeDtypeStruct(s, F32) for s in shapes),
        in_specs=[pl.BlockSpec(memory_space=pltpu.SMEM)] + [vm] * len(parts),
        out_specs=(vm,) * len(shapes),
        scratch_shapes=[pltpu.VMEM(most, F32)],
        compiler_params=pltpu.CompilerParams(vmem_limit_bytes=24 * 2**20),
        name="spread",
    )(place, *parts)


def body(sizes, inputs, lengths, w_qkv, w_out, w_in, w_back, vectors, cotangent):
    reps, shards = sizes
    count = inputs.shape[0]
    me = lax.axis_index("shard").astype(jnp.int32).reshape(1)

    axis = ("shard", shards)
    far = far_pieces(pack(w_qkv, vectors), *axis)
    start = held_until({0: jnp.concatenate([w_out, w_in], 1)}, far[max(far)])
    far_up = far_pieces(start[0], *axis)
    whole, wqt, wvt, table = prepare(me, near_pieces(far, *axis))
    fwd = [
        attention_forward(s, lengths, inputs, whole, wqt, wvt, table) for s in range(count)
    ]
    far_up = held_until(far_up, fwd[-1][3])
    far_back = far_pieces(held_until({0: w_back}, fwd[-1][3])[0], *axis)
    far_back = held_until(far_back, fwd[0][3])
    out, gh, dot, *grads, sums = feed_forward(
        lengths, me, inputs, cotangent, [f[2] for f in fwd], [f[3] for f in fwd],
        near_pieces(far_up, *axis), near_pieces(far_back, *axis), table,
    )
    place = (lax.axis_index("rep") % GROUP).astype(jnp.int32).reshape(1)
    folds = [("fold", bit) for bit in powers(shards)]
    group = [("group", 0)]
    rest = [("full", bit) for bit in powers(reps) if bit >= GROUP]
    tall = Stream(grads[:2], sizes, folds + group + rest)
    deep = Stream(grads[2:], sizes, folds[:1] + group + folds[1:] + rest)
    projs = [[None] * GROUPS for _ in range(count)]
    quarters = [None] * GROUPS
    extras, after, calls = [], [], []
    for g in range(GROUPS):
        chain = ()
        for s in range(count):
            closing = [sums] + extras if s == count - 1 and g == GROUPS - 1 else ()
            busy = [
                (tall, deep), (tall, deep), (tall, quarters[0]), (deep, quarters[0], tall)
            ][len(calls)]
            items = [stream.exchange() for stream in busy]
            res = attention_backward(
                s, g, GROUPS, shards, lengths, me, whole, table, inputs, dot, fwd[s][1],
                fwd[s][2], fwd[s][0], chain, closing, after,
            )
            chain = list(res[1:-1])
            carry = chain[1:2] if len(calls) == 3 else []
            after, *held = advance(place, busy, items, [res[-1]], carry)
            after = [after]
            chain[1 : 1 + len(held)] = held
            projs[s][g] = res[0]
            calls.append(res)
        quarters[g] = Stream(chain[:2], sizes, folds + [("stop", 0)])
        extras += chain[2:]
    early, last = quarters
    for stream, left in ((early, 1), (tall, 0), (deep, 1)):
        while len(stream.steps) > left:
            stream.alone(place)
    tall_parts = whole_parts(tall)
    end = deep.exchange()
    after = []
    while len(last.steps) > 2:
        after = last.alone(place)
    gx, token = input_gradient(0, lengths, whole, gh, projs[0], after)
    final = last.exchange()[0]
    both = Stream([], sizes, group + rest, stacked=GROUPS)
    after = advance(
        place, [both, deep], [([early.value] + final, "parts", GROUPS), end], [token]
    )
    for seq in range(1, count):
        gx, token = input_gradient(seq, lengths, whole, gh, projs[seq], after, gx)
    both.alone(place, [token] + tall_parts[1:])
    deep_parts = whole_parts(deep)
    while both.steps:
        both.alone(place)
    return (out, gx, *spread(place, shards, tall_parts + deep_parts + whole_parts(both)))


def solution(mesh):
    data = P(("rep", "shard"), None, None)
    rows = P("shard", None)
    return jax.shard_map(
        partial(body, (mesh.shape["rep"], mesh.shape["shard"])),
        mesh=mesh,
        in_specs=(data, P(("rep", "shard")), rows, rows, rows, rows, rows, data),
        out_specs=(data, data, rows, rows, rows, rows, rows),
        check_vma=False,
    )
```
